32 devices in a mesh: row: 8 (over z, y), col: 4 (over x, core).
Axes of the slice: x: 2, y: 2, z: 4, core: 2. Of those that a mesh axis runs over, the one named last changes fastest.
Arguments:
- tokens: bfloat16 [8192, 1024], P('row', 'col'), may hold values from -6 to 6
- segment_ids: int32 [8, 1024], P('row'), may hold values from 0 to 7, never falling along the last dimension, each value on 1 to 512 neighbouring positions
- w_query: bfloat16 [1024, 1024], P('row', 'col'), may hold values from -0.1875 to 0.1875
- key_matrix: bfloat16 [1024, 512], P('row', 'col'), may hold values from -0.1875 to 0.1875
- value_matrix: bfloat16 [1024, 512], P('row', 'col'), may hold values from -0.1875 to 0.1875
- w_out: bfloat16 [1024, 1024], P('col', 'row'), may hold values from -0.75 to 0.75
- w_gate: bfloat16 [1024, 4608], P('row', 'col'), may hold values from -0.1875 to 0.1875
- w_up: bfloat16 [1024, 4608], P('row', 'col'), may hold values from -0.1875 to 0.1875
- w_down: bfloat16 [4608, 1024], P('col', 'row'), may hold values from -0.09375 to 0.09375
- norm_attn: float32 [1024], replicated, may hold values from 0.1 to 1.9
- norm_ffn: float32 [1024], replicated, may hold values from 0.1 to 1.9
- norm_query: float32 [64], replicated, may hold values from 0.1 to 1.9
- norm_key: float32 [64], replicated, may hold values from 0.1 to 1.9
- cotangent: bfloat16 [8192, 1024], P('row', 'col'), may hold values from -6 to 6
Outputs:
- layer_out: bfloat16 [8192, 1024], P('row', 'col')
- grad_tokens: float32 [8192, 1024], P('row', 'col')
- grad_w_query: float32 [1024, 1024], P('row', 'col')
- grad_w_key: float32 [1024, 512], P('row', 'col')
- grad_w_value: float32 [1024, 512], P('row', 'col')
- grad_w_out: float32 [1024, 1024], P('col', 'row')
- grad_w_gate: float32 [1024, 4608], P('row', 'col')
- grad_w_up: float32 [1024, 4608], P('row', 'col')
- grad_w_down: float32 [4608, 1024], P('col', 'row')
- grad_norm_attn: float32 [1024], replicated
- grad_norm_ffn: float32 [1024], replicated
- grad_norm_query: float32 [64], replicated
- grad_norm_key: float32 [64], replicated
The draws below stay inside these ranges and needn't reach their ends.
Inputs may be any that keep to these rules, and one draw needn't show every extreme that they name: `segment_ids`: within each sequence the ids never fall, and a document spans at most 512 tokens.
All inputs are finite; a program needn't handle non-finite values.
Results may differ from the reference program's by a relative error of at most 0.012.
The reference program's roundings to bfloat16 on the way count: a program that leaves them out, or rounds other values in their place, can miss the bound.
Values may be sent and summed in bfloat16 or wider, within the bound.
A program may use at most 192 MiB of HBM per device.

```python
import math
import jax
import jax.numpy as jnp
import numpy as np
from jax import lax

MODEL_WIDTH = 1024
QUERY_HEADS = 16
KEY_VALUE_HEADS = 8
HEAD_WIDTH = 64
FF = 4608
SEQ = 1024
DOCS = 8
SEQS = 8
TOKENS = 8192


def block_scale(key, shape, pieces, smallest, top_value):
    gain = 1.0
    for position, parts in pieces:
        heights = jax.random.uniform(jax.random.fold_in(jax.random.fold_in(key, 6), position), (parts,), jnp.float32, smallest / len(pieces), top_value / len(pieces))
        gain = gain * jnp.repeat(jnp.exp(heights), shape[position] // parts).reshape((-1,) + (1,) * (len(shape) - 1 - position))
    return gain


def split_up(count, total, most, lean):
    weights = [(1 << 20) // math.isqrt(standing ** lean) + 1 for standing in range(2, count + 1)]
    spare, given = total - most - (count - 1), [1] * (count - 1)
    while spare > 0:
        candidates = [i for i in range(count - 1) if given[i] < most]
        whole, left = sum([weights[i] for i in candidates]), spare
        for i in candidates:
            addition = min(most - given[i], max(1, left * weights[i] // whole), spare)
            given[i] = given[i] + addition
            spare = spare - addition
    return np.array([most] + given)


def ragged_sizes(rng, amount, total, limit, lean):
    if amount == 2:
        one = jax.random.randint(rng, (), max(1, total - limit), min(limit, total - 1) + 1)
        return jnp.stack([one, total - one])
    lengths = jnp.asarray(split_up(amount, total, limit, lean), jnp.int32)
    twos = (amount - 1) // 2
    source_of, sink = lengths[1:1 + 2 * twos:2], lengths[2:2 + 2 * twos:2]
    margin = jnp.minimum(source_of - 1, limit - sink)
    moved = jax.random.randint(jax.random.fold_in(rng, 1), (twos,), 0, 1 << 20) % (margin + 1)
    lengths = lengths.at[1:1 + 2 * twos:2].set(source_of - moved).at[2:2 + 2 * twos:2].set(sink + moved)
    return lengths[jax.random.permutation(jax.random.fold_in(rng, 2), amount)]


def bell_draw(stream_key, extent, width, limit, split=(), held_as=jnp.bfloat16):
    level = block_scale(stream_key, extent, split, -0.22, 0.18) if split else 1.0
    values = jax.random.normal(stream_key, extent, jnp.float32) * width * level
    return jnp.minimum(jnp.maximum(values, -limit), limit).astype(held_as)


def setup_inputs(seed: int = 0) -> dict:
    splits = jax.random.split(jax.random.key(seed), 15)
    return {
        "tokens": bell_draw(splits[0], (TOKENS, MODEL_WIDTH), 1.0, 6.0, ((0, 8), (1, 4))),
        "segment_ids": jax.vmap(lambda own: jnp.searchsorted(jnp.cumsum(ragged_sizes(own, DOCS, SEQ, SEQ // 2, 2)), jnp.arange(SEQ), side="right"))(jax.random.split(splits[1], SEQS)).reshape((SEQS, SEQ)).astype(jnp.int32),
        "w_query": bell_draw(splits[2], (MODEL_WIDTH, QUERY_HEADS * HEAD_WIDTH), MODEL_WIDTH ** -0.5, 0.1875, ((0, 8), (1, 4))),
        "key_matrix": bell_draw(splits[3], (MODEL_WIDTH, KEY_VALUE_HEADS * HEAD_WIDTH), MODEL_WIDTH ** -0.5, 0.1875, ((0, 8), (1, 4))),
        "value_matrix": bell_draw(splits[4], (MODEL_WIDTH, KEY_VALUE_HEADS * HEAD_WIDTH), MODEL_WIDTH ** -0.5, 0.1875, ((0, 8), (1, 4))),
        "w_out": bell_draw(splits[5], (QUERY_HEADS * HEAD_WIDTH, MODEL_WIDTH), (QUERY_HEADS * HEAD_WIDTH // 16) ** -0.5, 0.75, ((0, 4), (1, 8))),
        "w_gate": bell_draw(splits[6], (MODEL_WIDTH, FF), MODEL_WIDTH ** -0.5, 0.1875, ((0, 8), (1, 4))),
        "w_up": bell_draw(splits[7], (MODEL_WIDTH, FF), MODEL_WIDTH ** -0.5, 0.1875, ((0, 8), (1, 4))),
        "w_down": bell_draw(splits[8], (FF, MODEL_WIDTH), FF ** -0.5, 0.09375, ((0, 4), (1, 8))),
        "norm_attn": jnp.clip(1.0 + 0.18 * jax.random.normal(splits[9], (MODEL_WIDTH,), jnp.float32), 0.1, 1.9),
        "norm_ffn": jnp.clip(1.0 + 0.18 * jax.random.normal(splits[10], (MODEL_WIDTH,), jnp.float32), 0.1, 1.9),
        "norm_query": jnp.clip(1.0 + 0.18 * jax.random.normal(splits[11], (HEAD_WIDTH,), jnp.float32), 0.1, 1.9),
        "norm_key": jnp.clip(1.0 + 0.18 * jax.random.normal(splits[12], (HEAD_WIDTH,), jnp.float32), 0.1, 1.9),
        "cotangent": bell_draw(splits[13], (TOKENS, MODEL_WIDTH), 1.0, 6.0, ((0, 8), (1, 4))),
    }


epsilon = 1e-05
rope_base = 1000000.0

@jax.custom_vjp
def reduced_precision(v):
    return lax.optimization_barrier(v.astype(jnp.bfloat16)).astype(jnp.float32)

@jax.custom_vjp
def reduced_precision_backward(v):
    return v

def low_keep(v):
    return (reduced_precision(v), None)

def low_pass(kept, grad):
    return (grad,)

def back_keep(v):
    return (v, None)

def back_low(kept, grad):
    return (reduced_precision(grad),)
reduced_precision.defvjp(low_keep, low_pass)
reduced_precision_backward.defvjp(back_keep, back_low)

def matrix_product(left_mat, right_mat):
    return jnp.dot(left_mat, right_mat, precision=lax.Precision.HIGHEST)

def root_norm(operand):
    return operand * lax.rsqrt(lax.optimization_barrier(jnp.mean(operand * operand, axis=-1, keepdims=True)) + epsilon)

def doc_positions(segment_row):
    token_length = segment_row.shape[0]
    places = jnp.arange(token_length, dtype=jnp.int32)
    doc_starts = jnp.concatenate([jnp.ones((1,), dtype=bool), segment_row[1:] != segment_row[:-1]])
    first_place = lax.cummax(jnp.where(doc_starts, places, 0), axis=0)
    return places - first_place

def rotate(operand, positions):
    half_size = operand.shape[-1] // 2
    freq_steps = jnp.arange(half_size, dtype=jnp.float32) * (2.0 / operand.shape[-1])
    inverse_freq = jnp.exp(-freq_steps * math.log(rope_base))
    angles = positions.astype(jnp.float32)[:, None] * inverse_freq[None, :]
    cosine = jnp.cos(angles)[:, None, :]
    sine_val = jnp.sin(angles)[:, None, :]
    front_half = operand[..., :half_size]
    back_half = operand[..., half_size:]
    return jnp.concatenate([front_half * cosine - back_half * sine_val, back_half * cosine + front_half * sine_val], axis=-1)

def layer_step(tokens_row, segment_row, w_query, key_matrix, value_matrix, w_out, w_gate, w_up, w_down, norm_attn, norm_ffn, norm_query, norm_key):
    token_length = tokens_row.shape[0]
    positions = doc_positions(segment_row)
    places = jnp.arange(token_length, dtype=jnp.int32)
    allowed = (segment_row[:, None] == segment_row[None, :]) & (places[None, :] <= places[:, None])
    normalized_input = reduced_precision(root_norm(tokens_row) * norm_attn)
    query_pre = reduced_precision_backward(matrix_product(normalized_input, w_query)).reshape(token_length, QUERY_HEADS, HEAD_WIDTH)
    key_before_rotation = reduced_precision_backward(matrix_product(normalized_input, key_matrix)).reshape(token_length, KEY_VALUE_HEADS, HEAD_WIDTH)
    value_head_rows = reduced_precision(reduced_precision_backward(matrix_product(normalized_input, value_matrix))).reshape(token_length, KEY_VALUE_HEADS, HEAD_WIDTH)
    query_head_rows = reduced_precision(rotate(root_norm(query_pre) * norm_query, positions))
    key_heads = reduced_precision(rotate(root_norm(key_before_rotation) * norm_key, positions))
    heads_per_group = QUERY_HEADS // KEY_VALUE_HEADS
    score_scale = HEAD_WIDTH ** (-0.5)
    grouped_queries = query_head_rows.reshape(token_length, KEY_VALUE_HEADS, heads_per_group, HEAD_WIDTH).transpose(1, 2, 0, 3)

    def head_block(operands):
        query_part, key_part, value_part = operands
        raw_scores = jnp.einsum('gqd,kd->gqk', query_part, key_part, precision=lax.Precision.HIGHEST)
        scores = reduced_precision_backward(raw_scores * score_scale)
        masked = jnp.where(allowed[None], scores, -1e+30)
        row_top = lax.optimization_barrier(jnp.max(masked, axis=-1, keepdims=True))
        exponent = jnp.exp(masked - row_top)
        row_total = lax.optimization_barrier(jnp.sum(exponent, axis=-1, keepdims=True))
        weights = reduced_precision(exponent / row_total)
        return jnp.einsum('gqk,kd->gqd', weights, value_part, precision=lax.Precision.HIGHEST)
    mixed_out = lax.map(jax.checkpoint(head_block), (grouped_queries, key_heads.transpose(1, 0, 2), value_head_rows.transpose(1, 0, 2)))
    mixed_out = mixed_out.transpose(2, 0, 1, 3).reshape(token_length, QUERY_HEADS * HEAD_WIDTH)
    attended = reduced_precision_backward(matrix_product(reduced_precision(reduced_precision_backward(mixed_out)), w_out))
    residual = tokens_row + attended
    normed_ffn = reduced_precision(root_norm(residual) * norm_ffn)
    gate_act = reduced_precision_backward(matrix_product(normed_ffn, w_gate))
    up_act = reduced_precision_backward(matrix_product(normed_ffn, w_up))
    hidden = reduced_precision(jax.nn.silu(gate_act) * up_act)
    return residual + reduced_precision_backward(matrix_product(hidden, w_down))

def reference(tokens, segment_ids, w_query, key_matrix, value_matrix, w_out, w_gate, w_up, w_down, norm_attn, norm_ffn, norm_query, norm_key, cotangent):
    tokens_f32 = tokens.astype(jnp.float32).reshape(SEQS, SEQ, MODEL_WIDTH)
    weights_f32 = (w_query.astype(jnp.float32), key_matrix.astype(jnp.float32), value_matrix.astype(jnp.float32), w_out.astype(jnp.float32), w_gate.astype(jnp.float32), w_up.astype(jnp.float32), w_down.astype(jnp.float32), norm_attn.astype(jnp.float32), norm_ffn.astype(jnp.float32), norm_query.astype(jnp.float32), norm_key.astype(jnp.float32))

    def forward(tokens_all, wq, wk, wv, wo, wg, wu, wd, gain_attn, gain_ffn, gain_query, gain_key):

        def scan_step(carry_val, inputs):
            tokens_row, segment_row = inputs
            result = jax.checkpoint(layer_step)(tokens_row, segment_row, wq, wk, wv, wo, wg, wu, wd, gain_attn, gain_ffn, gain_query, gain_key)
            return (carry_val, result)
        unused, outputs = lax.scan(scan_step, None, (tokens_all, segment_ids))
        return outputs
    outputs, pull_back = jax.vjp(forward, tokens_f32, *weights_f32)
    gradients = pull_back(cotangent.astype(jnp.float32).reshape(SEQS, SEQ, MODEL_WIDTH))
    return (outputs.reshape(TOKENS, MODEL_WIDTH).astype(jnp.bfloat16), gradients[0].reshape(TOKENS, MODEL_WIDTH), gradients[1], gradients[2], gradients[3], gradients[4], gradients[5], gradients[6], gradients[7], gradients[8], gradients[9], gradients[10], gradients[11])
```

```python
import functools
import math

import jax
import jax.numpy as jnp
from jax import lax
from jax.experimental import pallas as pl
from jax.experimental.pallas import tpu as pltpu
from jax.sharding import PartitionSpec as P

epsilon = 1e-05
rope_base = 1000000.0
longest = 512
ids = 8
f32, bf16 = jnp.float32, jnp.bfloat16
MESH = pl.DeviceIdType.MESH
RB = 256


def dot_nn(a, b):
    return lax.dot_general(a, b, (((1,), (0,)), ((), ())), preferred_element_type=f32)


def dot_nt(a, b):
    return lax.dot_general(a, b, (((1,), (1,)), ((), ())), preferred_element_type=f32)


def rows(i, n):
    return pl.ds(pl.multiple_of(i * n, n), n)


def layer_kernel(
    nz,
    tok_h, seg_ref, wq_h, wk_h, wv_h, wot_h, wg_h, wu_h, wdt_h, ga_ref, gf_ref, gq_ref, gk_ref, cot_h,
    lo_h, gt_h, gattn_h, ggate_h, gup_h, gdown_h, gain_ref,
    W, G, RY, RZ, GF, Tk, Ct, Nm, R1, PRE, QS, KS, VS, KT, VT, DO, MX, PB, A0, B0, S0, RES, NF, GG, HID,
    CS, SN, BIAS, INV, DQ, DK, DV, AC, BC, SC, LO, LOC, VEC, VC, VX, VY, VZ,
    loc_sem, agz_s, agz_r, agy_s, agy_r, rsy_s, rsy_r, rsz_s, rsz_r,
    cag_s, cag_r, crs_s, crs_r, gn_s, gn_r, lo_s, lo_r, vec_s, vec_r, vz_s, vz_r, out_sem,
):
    T, D = Tk.shape
    br = RY.shape[1]
    QW, KW = PRE.shape[1] // 2, PRE.shape[1] // 4
    PW = 2 * QW + 2 * KW
    F = HID.shape[1]
    FC = F // 3
    nb = T // RB
    CW = D // 4
    row, col = lax.axis_index("row"), lax.axis_index("col")
    z, y = row // 2, row % 2
    x, c = col // 2, col % 2
    ypeer = (row + 1 - 2 * y, col)
    cpeer = (row, col + 1 - 2 * c)
    xpeer = (row, (1 - x) * 2 + c)
    dpeer = (row, (1 - x) * 2 + 1 - c)

    def zdev(zz):
        return (zz * 2 + y, col)

    def rc(src, dst, ss, rs, dev):
        return pltpu.make_async_remote_copy(
            src_ref=src, dst_ref=dst, send_sem=ss, recv_sem=rs, device_id=dev, device_id_type=MESH
        )

    def loop(n, body, first=0):
        def step(i, carry):
            body(i)
            return carry

        lax.fori_loop(first, n, step, 0)

    down0 = PW + 2 * F
    CH = [(0, PW)] + [(PW + 2 * FC * j, 2 * FC) for j in range(3)] + [(down0 + FC * j, FC) for j in range(3)]
    RCH = CH[4:7] + CH[1:4] + [(2 * QW, QW), (0, 2 * QW)]

    own = rows(row, br)
    mine = pl.ds(pl.multiple_of(col * CW, CW), CW)
    local = [
        (wq_h, W.at[own, pl.ds(0, QW)]),
        (wk_h, W.at[own, pl.ds(QW, KW)]),
        (wv_h, W.at[own, pl.ds(QW + KW, KW)]),
        (wot_h, W.at[own, pl.ds(2 * QW, QW)]),
        (tok_h, Tk.at[:, mine]),
        (cot_h, Ct.at[:, mine]),
    ]
    for j in range(3):
        local.append((wg_h.at[:, pl.ds(FC * j, FC)], W.at[own, pl.ds(PW + 2 * FC * j, FC)]))
        local.append((wu_h.at[:, pl.ds(FC * j, FC)], W.at[own, pl.ds(PW + 2 * FC * j + FC, FC)]))
    local.append((wdt_h, W.at[own, pl.ds(down0, F)]))
    local = [pltpu.make_async_copy(s, d, loc_sem.at[i]) for i, (s, d) in enumerate(local)]
    for copy in local:
        copy.start()

    bar = pltpu.get_barrier_semaphore()
    for dev in (ypeer, cpeer, xpeer, dpeer):
        pl.semaphore_signal(bar, inc=1, device_id=dev, device_id_type=MESH)

    def greet(k):
        pl.semaphore_signal(bar, inc=1, device_id=zdev((z + k) % nz), device_id_type=MESH)

    loop(nz, greet, 1)
    pl.semaphore_wait(bar, 4 + nz - 1)

    def wblk(ch, zz, yy):
        start, width = CH[ch]
        return W.at[rows(zz * 2 + yy, br), pl.ds(start, width)]

    def ag_z(ch, k, src):
        b = wblk(ch, src, y)
        return rc(b, b, agz_s.at[ch, k], agz_r.at[ch, k], zdev((z + k) % nz))

    def ag_y(ch, k, src, yy):
        b = wblk(ch, src, yy)
        return rc(b, b, agy_s.at[ch, k], agy_r.at[ch, k], ypeer)

    def ag_own(ch):
        ag_y(ch, 0, z, y).start()
        loop(nz, lambda k: ag_z(ch, k, z).start(), 1)

    def ag_fwd(ch):
        def step(k):
            src = (z + nz - k) % nz
            ag_z(ch, k, src).wait_recv()
            ag_y(ch, k, src, y).start()

        loop(nz, step, 1)

    def ag_wait(ch):
        loop(nz, lambda k: ag_y(ch, k, (z + nz - k) % nz, 1 - y).wait_recv())

    def ag_done(ch):
        loop(nz, lambda k: ag_y(ch, k, (z + nz - k) % nz, y).wait_send())
        loop(nz, lambda k: ag_z(ch, k, z).wait_send(), 1)

    def cag(n, block):
        def copy(i, d, dev):
            return rc(block(d), block(d), cag_s.at[n, i], cag_r.at[n, i], dev)

        def start():
            copy(0, col, cpeer).start()
            copy(1, col, xpeer).start()

        def forward():
            copy(1, (1 - x) * 2 + c, xpeer).wait_recv()
            copy(2, (1 - x) * 2 + c, cpeer).start()

        def wait():
            copy(0, x * 2 + 1 - c, cpeer).wait_recv()
            copy(2, (1 - x) * 2 + 1 - c, cpeer).wait_recv()

        def done():
            copy(0, col, cpeer).wait_send()
            copy(1, col, xpeer).wait_send()
            copy(2, (1 - x) * 2 + c, cpeer).wait_send()

        return start, forward, wait, done

    def col_block(ref):
        return lambda d: ref.at[:, pl.ds(pl.multiple_of(d * CW, CW), CW)]

    def row_block(ref):
        return lambda d: ref.at[rows(d, RB), :]

    tok_start, tok_forward, tok_wait, tok_done = cag(0, col_block(Tk))
    cot_start, cot_forward, cot_wait, cot_done = cag(1, col_block(Ct))
    nf_start, nf_forward, nf_wait, nf_done = cag(2, row_block(NF))
    rl_start, rl_forward, rl_wait, rl_done = cag(3, row_block(Ct))

    def crs(n, A, B, S):
        def to_core(i, xx, cc):
            return rc(PB.at[rows(xx * 2 + cc, RB), :], A(xx), crs_s.at[n, i], crs_r.at[n, i], cpeer)

        def to_x():
            return rc(S, B, crs_s.at[n, 2], crs_r.at[n, 2], xpeer)

        def produce(part):
            def step(i):
                xx = jnp.where(i < 2, 1 - x, x)
                cc = jnp.where(i % 2 == 0, 1 - c, c)
                PB[rows(xx * 2 + cc, RB), :] = part(xx * 2 + cc).astype(bf16)

                @pl.when(i % 2 == 0)
                def _():
                    to_core(i // 2, xx, 1 - c).start()

            loop(4, step)

        def middle():
            to_core(0, 1 - x, c).wait_recv()

            def step(i):
                r = rows(i, 32)
                block = PB[pl.ds(pl.multiple_of(((1 - x) * 2 + c) * RB + i * 32, 32), 32), :]
                S[r, :] = (block.astype(f32) + A(1 - x)[r, :].astype(f32)).astype(bf16)

            loop(RB // 32, step)
            to_x().start()

        def wait():
            to_core(1, x, c).wait_recv()
            to_x().wait_recv()

        def total(i, n):
            r = rows(i, n)
            block = PB[pl.ds(pl.multiple_of(col * RB + i * n, n), n), :].astype(f32)
            return block + A(x)[r, :].astype(f32) + B[r, :].astype(f32)

        def done():
            to_core(0, 1 - x, 1 - c).wait_send()
            to_core(1, x, 1 - c).wait_send()
            to_x().wait_send()

        return produce, middle, wait, total, done

    def gcol(ch):
        start, width = RCH[ch]
        return (G, start - PW, width) if start >= PW else (W, down0 + start, width)

    def gblk(ch, zz, yy):
        ref, start, width = gcol(ch)
        return ref.at[rows(zz * 2 + yy, br), pl.ds(start, width)]

    def rs_y(ch, zz, yy):
        start, width = RCH[ch]
        return rc(
            gblk(ch, zz, yy), RY.at[zz, :, pl.ds(start, width)], rsy_s.at[ch, zz], rsy_r.at[ch, zz], ypeer
        )

    def rs_z(ch, k):
        start, width = RCH[ch]
        part = pl.ds(start, width)
        zz = (z + k) % nz
        return rc(RY.at[zz, :, part], RZ.at[k - 1, :, part], rsz_s.at[ch, k], rsz_r.at[ch, k], zdev(zz))

    zper = RB // (2 * br)

    def grad_step(i):
        return (row * br // RB + 1 + i) % (D // RB)

    def rs_send(ch, dblk):
        loop(zper, lambda s: rs_y(ch, dblk * zper + s, 1 - y).start())

    def rs_mid(ch):
        ref, gstart, width = gcol(ch)
        start = RCH[ch][0]

        def step(k):
            zz = (z + k) % nz
            rs_y(ch, zz, y).wait_recv()

            def add(i):
                r = rows(i, 16)
                g = ref[pl.ds(pl.multiple_of((zz * 2 + y) * br + i * 16, 16), 16), pl.ds(gstart, width)]
                t = RY[zz, r, pl.ds(start, width)]
                RY[zz, r, pl.ds(start, width)] = (g.astype(f32) + t.astype(f32)).astype(bf16)

            loop(br // 16, add)
            rs_z(ch, k).start()

        loop(nz, step, 1)

    def outs(ch):
        start, width = RCH[ch]
        if start >= down0:
            pairs = [(start, width, gdown_h, start - down0)]
        elif start >= PW:
            j = (start - PW) // (2 * FC)
            pairs = [(start, FC, ggate_h, FC * j), (start + FC, FC, gup_h, FC * j)]
        else:
            pairs = [(start, width, gattn_h, start)]
        return [
            pltpu.make_async_copy(GF.at[:, pl.ds(s, w)], ref.at[:, pl.ds(at, w)], out_sem.at[2 * ch + i])
            for i, (s, w, ref, at) in enumerate(pairs)
        ]

    def rs_fin(ch):
        ref, gstart, width = gcol(ch)
        part = pl.ds(RCH[ch][0], width)
        rs_y(ch, z, y).wait_recv()
        loop(nz, lambda k: rs_z(ch, k).wait_recv(), 1)

        def add(i):
            r = rows(i, 16)
            g = ref[pl.ds(pl.multiple_of(row * br + i * 16, 16), 16), pl.ds(gstart, width)]
            total = g.astype(f32) + RY[z, r, part].astype(f32)
            total = lax.fori_loop(0, nz - 1, lambda k, t: t + RZ[k, r, part].astype(f32), total)
            GF[r, part] = total

        loop(br // 16, add)
        for copy in outs(ch):
            copy.start()

    def rs_done(ch):
        loop(nz, lambda zz: rs_y(ch, zz, 1 - y).wait_send())
        loop(nz, lambda k: rs_z(ch, k).wait_send(), 1)
        for copy in outs(ch):
            copy.wait()

    for i in range(4):
        local[i].wait()
    ag_own(0)
    local[4].wait()
    tok_start()

    seg = seg_ref[...]
    first = jnp.zeros((1, T), jnp.int32)
    for d in range(ids):
        count = jnp.sum((seg == d).astype(f32), axis=1, keepdims=True).astype(jnp.int32)
        first = first + jnp.where(seg > d, count, 0)
    place = lax.broadcasted_iota(jnp.int32, (1, T), 1)
    lane = lax.broadcasted_iota(jnp.int32, (1, 128), 1)
    inverse_freq = jnp.exp((lane % 32).astype(f32) * (-2.0 / 64 * math.log(rope_base)))
    CS[...] = jnp.transpose(jnp.broadcast_to((place - first).astype(f32), (128, T)))

    def tables(i):
        angle = CS[rows(i, 128), :] * inverse_freq
        sine = jnp.sin(angle)
        CS[rows(i, 128), :] = jnp.cos(angle)
        SN[rows(i, 128), :] = jnp.where(lane % 64 < 32, -sine, sine)

    loop(T // 128, tables)
    windows = []
    at = 0
    for i in range(nb):
        start = max(0, RB * i - longest)
        width = RB * (i + 1) - start
        windows.append((start, width, at))
        key_place = lax.broadcasted_iota(jnp.int32, (width, RB), 0) + start
        q_place, q_first = place[:, RB * i : RB * (i + 1)], first[:, RB * i : RB * (i + 1)]
        seen = (key_place <= q_place) & (key_place >= q_first)
        BIAS[pl.ds(at, width), :] = jnp.where(seen, 0.0, -1e30).astype(bf16)
        at += width
    half_a = lax.broadcasted_iota(jnp.int32, (128, 128), 0) // 64
    half_b = lax.broadcasted_iota(jnp.int32, (128, 128), 1) // 64
    mean_matrix = jnp.where(half_a == half_b, 1.0 / 64, 0.0).astype(bf16)

    def head_mean(v):
        high = v.astype(bf16)
        low = (v - high.astype(f32)).astype(bf16)
        return dot_nn(high, mean_matrix) + dot_nn(low, mean_matrix)

    def turn(v):
        return jnp.where(lane % 64 < 32, pltpu.roll(v, 96, 1), pltpu.roll(v, 32, 1))

    gain_q = jnp.concatenate([gq_ref[...], gq_ref[...]], axis=1)
    gain_k = jnp.concatenate([gk_ref[...], gk_ref[...]], axis=1)
    ga = ga_ref[...]
    gf = gf_ref[...]

    for i in range(6, 12):
        local[i].wait()
    ag_own(1)
    tok_forward()
    local[5].wait()
    cot_start()
    tok_wait()

    def norm_tokens(i):
        t = Tk[rows(i, 128), :].astype(f32)
        r = lax.rsqrt(jnp.mean(t * t, axis=1, keepdims=True) + epsilon)
        R1[rows(i, 128), :] = jnp.broadcast_to(r, (128, 128))
        Nm[rows(i, 128), :] = (t * r * ga).astype(bf16)

    loop(T // 128, norm_tokens)
    ag_fwd(0)
    local[12].wait()
    ag_own(2)
    ag_wait(0)

    def project(i):
        r = rows(i, RB)
        PRE[r, :] = dot_nn(Nm[r, :], W[:, pl.ds(0, 2 * QW)])
        cos, sin = CS[r, :], SN[r, :]
        for p in range(3):
            v = PRE[r, pl.ds(128 * p, 128)]
            n = v * lax.rsqrt(head_mean(v * v) + epsilon)
            u = n * (gain_q if p < 2 else gain_k)
            u = (u * cos + turn(u) * sin).astype(bf16)
            if p < 2:
                u = u * jnp.asarray(0.125, bf16)
                QS[p, 0, r, :] = u[:, :64]
                QS[p, 1, r, :] = u[:, 64:]
            else:
                KS[0, r, :] = u[:, :64]
                KS[1, r, :] = u[:, 64:]
                ut = jnp.transpose(u)
                KT[0, :, r] = ut[:64, :]
                KT[1, :, r] = ut[64:, :]
        v = PRE[r, pl.ds(384, 128)].astype(bf16)
        VS[0, r, :] = v[:, :64]
        VS[1, r, :] = v[:, 64:]
        vt = jnp.transpose(v)
        VT[0, :, r] = vt[:64, :]
        VT[1, :, r] = vt[64:, :]

    loop(nb, project)

    def attend(i):
        start, width, at = windows[i]
        keys = pl.ds(start, width)
        r = pl.ds(RB * i, RB)

        def step(h):
            q = QS[h, :, r, :].reshape(2 * RB, 64)
            bias = BIAS[pl.ds(at, width), :].astype(f32)
            s = dot_nt(KS[h, keys, :], q) + jnp.concatenate([bias, bias], axis=1)
            e = jnp.exp(s)
            inv = 1.0 / jnp.sum(e, axis=0, keepdims=True)
            INV[h, pl.ds(i, 1), :] = inv
            o = dot_nn(VT[h, :, keys], (e * inv).astype(bf16))
            o = jnp.concatenate([o[:, :RB], o[:, RB:]], axis=0)
            MX[r, pl.ds(pl.multiple_of(h * 128, 128), 128)] = jnp.transpose(o).astype(bf16)

        loop(2, step)

    attend(0)
    attend(1)
    ag_fwd(1)
    ag_own(3)
    cot_forward()
    attend(2)
    attend(3)
    a_produce, a_middle, a_wait, a_total, a_done = crs(0, lambda i: A0.at[i], B0, S0)
    a_produce(lambda d: dot_nt(MX[rows(d, RB), :], W[:, pl.ds(2 * QW, QW)]))
    a_middle()
    ag_fwd(2)
    ag_own(4)
    a_wait()

    def after_attention(i):
        r = rows(i, 32)
        mine_rows = pl.ds(pl.multiple_of(col * RB + i * 32, 32), 32)
        v = Tk[mine_rows, :].astype(f32) + a_total(i, 32)
        RES[r, :] = v
        n = v * lax.rsqrt(jnp.mean(v * v, axis=1, keepdims=True) + epsilon)
        NF[mine_rows, :] = (n * gf).astype(bf16)

    loop(RB // 32, after_attention)
    nf_start()
    a_done()
    cot_wait()
    cot_done()
    ag_own(5)
    ag_own(6)
    nf_forward()
    nf_wait()
    nf_done()

    def ffn(j):
        def step(i):
            r = rows(i, RB)
            n = NF[r, :]
            gate = dot_nn(n, W[:, pl.ds(PW + 2 * FC * j, FC)])
            up = dot_nn(n, W[:, pl.ds(PW + 2 * FC * j + FC, FC)])
            sig = 1.0 / (1.0 + jnp.exp(-gate))
            act = gate * sig
            HID[r, pl.ds(FC * j, FC)] = (act * up).astype(bf16)
            GG[r, pl.ds(2 * FC * j, FC)] = (up * (sig + act * (1.0 - sig))).astype(bf16)
            GG[r, pl.ds(2 * FC * j + FC, FC)] = act.astype(bf16)

        loop(nb, step)

    def weight_grad(left, pieces):
        def step(i):
            d = grad_step(i)
            lt = jnp.transpose(left[:, rows(d, RB)])
            for ch, right in pieces:
                ref, start, width = gcol(ch)
                ref[rows(d, RB), pl.ds(start, width)] = dot_nn(lt, right[...]).astype(bf16)
                rs_send(ch, d)

        loop(D // RB, step)

    for j in range(3):
        ag_wait(1 + j)
        ffn(j)
        if j == 0:
            ag_fwd(3)
        else:
            ag_fwd(3 + j)
        weight_grad(Ct, [(j, HID.at[:, pl.ds(FC * j, FC)])])
        if j > 0:
            rs_mid(j - 1)
    ag_fwd(6)
    for j in range(3):
        ag_wait(4 + j)

        def grad_hidden(i, j=j):
            r = rows(i, RB)
            gh = dot_nn(Ct[r, :], W[:, pl.ds(down0 + FC * j, FC)])
            a, b = pl.ds(2 * FC * j, FC), pl.ds(2 * FC * j + FC, FC)
            GG[r, a] = (gh * GG[r, a].astype(f32)).astype(bf16)
            GG[r, b] = (gh * GG[r, b].astype(f32)).astype(bf16)

        loop(nb, grad_hidden)
    n_produce, n_middle, n_wait, n_total, n_done = crs(1, lambda i: A0.at[i], B0, S0)
    n_produce(lambda d: dot_nt(GG[rows(d, RB), :], W[:, pl.ds(PW, 2 * F)]))
    n_middle()
    rs_mid(2)
    weight_grad(NF, [(3 + j, GG.at[:, pl.ds(2 * FC * j, 2 * FC)]) for j in range(3)])
    n_wait()
    VEC[...] = jnp.zeros(VEC.shape, f32)

    def after_ffn(i):
        r = rows(i, 32)
        mine_rows = pl.ds(pl.multiple_of(col * RB + i * 32, 32), 32)
        gy = n_total(i, 32)
        v = RES[r, :]
        inv = lax.rsqrt(jnp.mean(v * v, axis=1, keepdims=True) + epsilon)
        n = v * inv
        VEC[1:2, :] += jnp.sum(gy * n, axis=0, keepdims=True)
        g = gy * gf
        g = inv * (g - n * jnp.mean(g * n, axis=1, keepdims=True))
        Ct[mine_rows, :] = (Ct[mine_rows, :].astype(f32) + g).astype(bf16)

    loop(RB // 32, after_ffn)
    rl_start()
    n_done()
    rs_mid(3)
    rl_forward()
    rl_wait()

    def grad_mixed(i):
        r = rows(i, RB)
        g = dot_nn(Ct[r, :], W[:, pl.ds(2 * QW, QW)]).astype(bf16)
        for p in range(2):
            DO[p, 0, r, :] = g[:, 128 * p : 128 * p + 64]
            DO[p, 1, r, :] = g[:, 128 * p + 64 : 128 * p + 128]

    loop(nb, grad_mixed)
    b_produce, b_middle, b_wait, b_total, b_done = crs(
        2, lambda i: NF.at[rows(i, RB), :], NF.at[pl.ds(2 * RB, RB), :], NF.at[pl.ds(3 * RB, RB), :]
    )
    b_produce(lambda d: dot_nt(HID[rows(d, RB), :], W[:, pl.ds(down0, F)]))
    b_middle()
    for ch in range(7):
        ag_done(ch)
    weight_grad(Ct, [(6, MX)])
    rs_mid(4)
    DK[...] = jnp.zeros(DK.shape, f32)
    DV[...] = jnp.zeros(DV.shape, f32)

    def attend_back(i):
        start, width, at = windows[i]
        keys = pl.ds(start, width)
        r = pl.ds(RB * i, RB)

        def step(h):
            q = QS[h, :, r, :].reshape(2 * RB, 64)
            do = DO[h, :, r, :].reshape(2 * RB, 64)
            bias = BIAS[pl.ds(at, width), :].astype(f32)
            s = dot_nt(KS[h, keys, :], q) + jnp.concatenate([bias, bias], axis=1)
            p = jnp.exp(s) * INV[h, pl.ds(i, 1), :]
            dp = dot_nt(VS[h, keys, :], do)
            DV[h, keys, :] += dot_nn(p.astype(bf16), do)
            ds = (p * (dp - jnp.sum(p * dp, axis=0, keepdims=True))).astype(bf16)
            DK[h, keys, :] += dot_nn(ds, q)
            g = dot_nn(KT[h, :, keys], ds) * 0.125
            g = jnp.concatenate([g[:, :RB], g[:, RB:]], axis=0)
            DQ[r, pl.ds(pl.multiple_of(h * 128, 128), 128)] = jnp.transpose(g)

        loop(2, step)

    attend_back(0)
    attend_back(1)
    rs_mid(5)
    b_wait()

    def finish(i):
        LO[rows(i, 32), :] = (RES[rows(i, 32), :] + b_total(i, 32)).astype(bf16)

    loop(RB // 32, finish)

    def lo_copy(i, d, dev):
        return rc(
            LO.at[:, pl.ds(pl.multiple_of(d * CW, CW), CW)], LOC.at[rows(col, RB), :], lo_s.at[i], lo_r.at[i], dev
        )

    others = [(0, x * 2 + 1 - c, cpeer), (1, (1 - x) * 2 + c, xpeer), (2, (1 - x) * 2 + 1 - c, dpeer)]
    for i, d, dev in others:
        lo_copy(i, d, dev).start()
    LOC[rows(col, RB), :] = LO[:, mine]
    attend_back(2)
    rs_mid(6)
    attend_back(3)

    def project_back(i):
        r = rows(i, RB)
        cos, sin = CS[r, :], SN[r, :]
        for p in range(3):
            g = DQ[r, pl.ds(128 * p, 128)] if p < 2 else jnp.concatenate([DK[0, r, :], DK[1, r, :]], axis=1)
            g = g * cos - turn(g) * sin
            v = PRE[r, pl.ds(128 * p, 128)]
            inv = lax.rsqrt(head_mean(v * v) + epsilon)
            n = v * inv
            s = pl.ds(0 if p < 2 else 128, 128)
            VEC[2:3, s] += jnp.sum(g * n, axis=0, keepdims=True)
            g = g * (gain_q if p < 2 else gain_k)
            HID[r, pl.ds(128 * p, 128)] = (inv * (g - n * head_mean(g * n))).astype(bf16)
        HID[r, pl.ds(384, 128)] = jnp.concatenate([DV[0, r, :], DV[1, r, :]], axis=1).astype(bf16)

    loop(nb, project_back)
    weight_grad(Nm, [(7, HID.at[:, pl.ds(0, 2 * QW)])])

    def gn_core(i, k, xx, cc):
        d = xx * 2 + cc
        return rc(
            PB.at[rows(i, RB), pl.ds(pl.multiple_of(d * CW, CW), CW)],
            AC.at[rows(i, RB), pl.ds(pl.multiple_of(xx * CW, CW), CW)],
            gn_s.at[i, k], gn_r.at[i, k], cpeer,
        )

    def gn_x(i):
        return rc(SC.at[rows(i, RB), :], BC.at[rows(i, RB), :], gn_s.at[i, 2], gn_r.at[i, 2], xpeer)

    b_done()

    def gn_produce(i):
        r = rows(i, RB)
        g = dot_nt(HID[r, pl.ds(0, 2 * QW)], W[:, pl.ds(0, 2 * QW)])
        PB[r, :] = g.astype(bf16)
        gn_core(i, 0, 1 - x, 1 - c).start()
        gn_core(i, 1, x, 1 - c).start()
        g = g * (Tk[r, :].astype(f32) * R1[r, pl.ds(0, 1)])
        VEC[0:1, :] += jnp.sum(g, axis=0, keepdims=True)
        s = jnp.sum(g * ga, axis=1, keepdims=True)
        VEC[3:4, r] = jnp.transpose(jnp.broadcast_to(s, (RB, 128)))[0:1, :]

    loop(nb, gn_produce)

    def vec_copy(i, src, dst, dev):
        return rc(src, dst, vec_s.at[i], vec_r.at[i], dev)

    vec_c = vec_copy(0, VEC, VC, cpeer)
    vec_c.start()

    def gn_middle(i):
        r = rows(i, RB)
        gn_core(i, 0, 1 - x, c).wait_recv()
        a = PB[r, pl.ds(pl.multiple_of(((1 - x) * 2 + c) * CW, CW), CW)].astype(f32)
        b = AC[r, pl.ds(pl.multiple_of((1 - x) * CW, CW), CW)].astype(f32)
        SC[r, :] = (a + b).astype(bf16)
        gn_x(i).start()

    loop(nb, gn_middle)
    vec_c.wait_recv()
    vec_c.wait_send()
    VEC[...] += VC[...]
    vec_x = vec_copy(1, VEC, VX, xpeer)
    vec_x.start()
    rs_fin(0)
    rs_fin(1)
    rs_fin(2)
    rs_mid(7)
    vec_x.wait_recv()
    vec_x.wait_send()
    VEC[...] += VX[...]
    vec_y = vec_copy(2, VEC, VY, ypeer)
    vec_y.start()

    def gn_finish(i):
        r = rows(i, RB)
        gn_core(i, 1, x, c).wait_recv()
        gn_x(i).wait_recv()
        g = PB[r, mine].astype(f32) + AC[r, pl.ds(pl.multiple_of(x * CW, CW), CW)].astype(f32) + BC[r, :].astype(f32)
        g = g * ga_ref[:, mine]
        inv = R1[r, pl.ds(0, 1)]
        s = jnp.transpose(jnp.broadcast_to(VEC[3:4, r], (128, RB)))[:, 0:1] * (1.0 / D)
        n = Tk[r, mine].astype(f32) * inv
        DQ[r, :] = Ct[r, mine].astype(f32) + inv * (g - n * s)

    loop(nb, gn_finish)
    gt_copy = pltpu.make_async_copy(DQ, gt_h, out_sem.at[16])
    gt_copy.start()
    vec_y.wait_recv()
    vec_y.wait_send()
    VZ[z] = VEC[...] + VY[...]

    def vz_copy(k, src):
        return rc(VZ.at[src], VZ.at[src], vz_s.at[k], vz_r.at[k], zdev((z + k) % nz))

    loop(nz, lambda k: vz_copy(k, z).start(), 1)
    for i, d, dev in others:
        lo_copy(i, d, dev).wait_recv()
    lo_out = pltpu.make_async_copy(LOC, lo_h, out_sem.at[17])
    lo_out.start()
    for ch in range(3, 8):
        rs_fin(ch)
    loop(nz, lambda k: vz_copy(k, (z + nz - k) % nz).wait_recv(), 1)
    gain_ref[...] = lax.fori_loop(1, nz, lambda k, t: t + VZ[k], VZ[0])

    tok_done()
    rl_done()
    for i, d, dev in others:
        lo_copy(i, d, dev).wait_send()

    def gn_done(i):
        gn_core(i, 0, 1 - x, 1 - c).wait_send()
        gn_core(i, 1, x, 1 - c).wait_send()
        gn_x(i).wait_send()

    loop(nb, gn_done)
    loop(nz, lambda k: vz_copy(k, z).wait_send(), 1)
    for ch in range(8):
        rs_done(ch)
    gt_copy.wait()
    lo_out.wait()


def per_device(
    n_row, tokens, segment_ids, w_query, key_matrix, value_matrix, w_out, w_gate, w_up, w_down,
    norm_attn, norm_ffn, norm_query, norm_key, cotangent,
):
    T, CW = tokens.shape
    br, QW = w_query.shape
    KW = key_matrix.shape[1]
    F = w_gate.shape[1]
    D = br * n_row
    nz = n_row // 2
    PW = 2 * QW + 2 * KW
    WW = PW + 3 * F
    nb = T // RB
    area = sum(RB * (i + 1) - max(0, RB * i - longest) for i in range(nb))
    vm, sem = pltpu.VMEM, pltpu.SemaphoreType.DMA
    scratch = [
        vm((D, WW), bf16), vm((D, 3 * F), bf16), vm((nz, br, WW), bf16), vm((nz - 1, br, WW), bf16),
        vm((br, WW), f32), vm((T, D), bf16), vm((T, D), bf16), vm((T, D), bf16), vm((T, 128), f32),
        vm((T, 2 * QW), f32), vm((2, 2, T, 64), bf16), vm((2, T, 64), bf16), vm((2, T, 64), bf16),
        vm((2, 64, T), bf16), vm((2, 64, T), bf16), vm((2, 2, T, 64), bf16), vm((T, QW), bf16),
        vm((T, D), bf16), vm((2, RB, D), bf16), vm((RB, D), bf16), vm((RB, D), bf16), vm((RB, D), f32),
        vm((T, D), bf16), vm((T, 2 * F), bf16), vm((T, F), bf16),
        vm((T, 128), f32), vm((T, 128), f32), vm((area, RB), bf16), vm((2, 8, 2 * RB), f32),
        vm((T, QW), f32), vm((2, T, 64), f32), vm((2, T, 64), f32),
        vm((T, 2 * CW), bf16), vm((T, CW), bf16), vm((T, CW), bf16), vm((RB, D), bf16), vm((T, CW), bf16),
        vm((8, D), f32), vm((8, D), f32), vm((8, D), f32), vm((8, D), f32), vm((nz, 8, D), f32),
        sem((13,)), sem((7, nz)), sem((7, nz)), sem((7, nz)), sem((7, nz)),
        sem((8, nz)), sem((8, nz)), sem((8, nz)), sem((8, nz)),
        sem((4, 3)), sem((4, 3)), sem((3, 3)), sem((3, 3)), sem((nb, 3)), sem((nb, 3)), sem((3,)), sem((3,)),
        sem((3,)), sem((3,)), sem((nz,)), sem((nz,)), sem((18,)),
    ]
    whole, hbm = pl.BlockSpec(memory_space=pltpu.VMEM), pl.BlockSpec(memory_space=pl.ANY)
    shape = jax.ShapeDtypeStruct
    outs = pl.pallas_call(
        functools.partial(layer_kernel, nz),
        out_shape=(
            shape((T, CW), bf16), shape((T, CW), f32), shape((br, PW), f32), shape((br, F), f32),
            shape((br, F), f32), shape((br, F), f32), shape((8, D), f32),
        ),
        in_specs=[hbm, whole] + [hbm] * 7 + [whole] * 4 + [hbm],
        out_specs=(hbm,) * 6 + (whole,),
        scratch_shapes=scratch,
        compiler_params=pltpu.CompilerParams(
            collective_id=0, has_side_effects=True, vmem_limit_bytes=64 * 2**20
        ),
        name="layer",
    )(
        tokens, segment_ids, w_query, key_matrix, value_matrix, w_out.T, w_gate, w_up, w_down.T,
        norm_attn[None], norm_ffn[None], norm_query[None], norm_key[None], cotangent,
    )
    layer_out, grad_tokens, g_attn, g_gate, g_up, g_down, gains = outs
    return (
        layer_out, grad_tokens, g_attn[:, :QW], g_attn[:, QW : QW + KW], g_attn[:, QW + KW : 2 * QW],
        g_attn[:, 2 * QW :].T, g_gate, g_up, g_down.T, gains[0], gains[1],
        gains[2, :64] + gains[2, 64:128], gains[2, 128:192] + gains[2, 192:256],
    )


def solution(mesh):
    in_specs = (
        P("row", "col"), P("row", None), P("row", "col"), P("row", "col"), P("row", "col"), P("col", "row"),
        P("row", "col"), P("row", "col"), P("col", "row"), P(), P(), P(), P(), P("row", "col"),
    )
    out_specs = (
        P("row", "col"), P("row", "col"), P("row", "col"), P("row", "col"), P("row", "col"), P("col", "row"),
        P("row", "col"), P("row", "col"), P("col", "row"), P(), P(), P(), P(),
    )
    return jax.shard_map(
        functools.partial(per_device, mesh.shape["row"]),
        mesh=mesh, in_specs=in_specs, out_specs=out_specs, check_vma=False,
    )
```

```python
import functools
import math

import jax
import jax.numpy as jnp
from jax import lax
from jax.experimental import pallas as pl
from jax.experimental.pallas import tpu as pltpu
from jax.sharding import PartitionSpec as P

epsilon = 1e-05
rope_base = 1000000.0
longest = 512
ids = 8
f32, bf16 = jnp.float32, jnp.bfloat16
MESH = pl.DeviceIdType.MESH
RB = 256


def dot_nn(a, b):
    return lax.dot_general(a, b, (((1,), (0,)), ((), ())), preferred_element_type=f32)


def dot_nt(a, b):
    return lax.dot_general(a, b, (((1,), (1,)), ((), ())), preferred_element_type=f32)


def rows(i, n):
    return pl.ds(pl.multiple_of(i * n, n), n)


def layer_kernel(
    nz,
    tok_h, seg_ref, wq_h, wk_h, wv_h, wo_h, wg_h, wu_h, wd_h, ga_ref, gf_ref, gq_ref, gk_ref, cot_h,
    lo_h, gt_h, gquery_h, gkey_h, gvalue_h, gout_h, ggate_h, gup_h, gdown_h, gain_ref,
    W, WO, WD, GFO, GFD, G, RY, RZ, GF, Tk, Ct, Nm, R1, PRE, QS, KS, VS, KT, VT, DO, MX, PB, A0, B0, S0, RES, NF, GG, HID,
    CS, SN, BIAS, INV, DQ, DK, DV, AC, BC, SC, LOC, VEC, VC, VX, VY, VZ,
    loc_sem, agz_s, agz_r, agy_s, agy_r, rsy_s, rsy_r, rsz_s, rsz_r,
    cag_s, cag_r, crs_s, crs_r, gn_s, gn_r, lo_s, lo_r, vec_s, vec_r, vz_s, vz_r, out_sem,
):
    T, D = Tk.shape
    br = RY.shape[1]
    QW, KW = PRE.shape[1] // 2, PRE.shape[1] // 4
    PW = 2 * QW + 2 * KW
    F = HID.shape[1]
    FC = F // 3
    nb = T // RB
    CW = D // 4
    row, col = lax.axis_index("row"), lax.axis_index("col")
    z, y = row // 2, row % 2
    x, c = col // 2, col % 2
    ypeer = (row + 1 - 2 * y, col)
    cpeer = (row, col + 1 - 2 * c)
    xpeer = (row, (1 - x) * 2 + c)
    dpeer = (row, (1 - x) * 2 + 1 - c)
    tree = nz == 4
    partner = z + 1 - 2 * (z % 2)
    is_middle = (z == 1) | (z == 2)
    near, far = 2 - z // 2, 3 - 3 * (z // 2)

    def zdev(zz):
        return (zz * 2 + y, col)

    def zsrc(k):
        if tree:
            return jnp.where(k == 0, z, jnp.where(k == 1, partner, jnp.where(k == 2, near, far)))
        return (z + nz - k) % nz

    def zorder(i):
        if tree:
            return zsrc(jnp.where(i == 3, 0, jnp.where(i == 2, 1, i + 2)))
        return (z + 1 + i) % nz

    def rc(src, dst, ss, rs, dev):
        return pltpu.make_async_remote_copy(
            src_ref=src, dst_ref=dst, send_sem=ss, recv_sem=rs, device_id=dev, device_id_type=MESH
        )

    def loop(n, body, first=0):
        def step(i, carry):
            body(i)
            return carry

        lax.fori_loop(first, n, step, 0)

    down0 = PW + 2 * F
    CH = [(0, PW)] + [(PW + 2 * FC * j, 2 * FC) for j in range(3)] + [(down0 + FC * j, FC) for j in range(3)]
    RCH = CH[4:7] + CH[1:4] + [(2 * QW, QW), (0, 2 * QW)]

    own = rows(row, br)
    mine = pl.ds(pl.multiple_of(col * CW, CW), CW)
    local = [
        (wq_h, W.at[own, pl.ds(0, QW)]),
        (wk_h, W.at[own, pl.ds(QW, KW)]),
        (wv_h, W.at[own, pl.ds(QW + KW, KW)]),
        (wo_h, WO),
        (tok_h, Tk.at[:, mine]),
        (cot_h, Ct.at[:, mine]),
    ]
    for j in range(3):
        local.append((wg_h.at[:, pl.ds(FC * j, FC)], W.at[own, pl.ds(PW + 2 * FC * j, FC)]))
        local.append((wu_h.at[:, pl.ds(FC * j, FC)], W.at[own, pl.ds(PW + 2 * FC * j + FC, FC)]))
    local.append((wd_h, WD))
    local = [pltpu.make_async_copy(s, d, loc_sem.at[i]) for i, (s, d) in enumerate(local)]
    for copy in local:
        copy.start()

    bar = pltpu.get_barrier_semaphore()
    for dev in (ypeer, cpeer, xpeer, dpeer):
        pl.semaphore_signal(bar, inc=1, device_id=dev, device_id_type=MESH)

    def greet(k):
        pl.semaphore_signal(bar, inc=1, device_id=zdev((z + k) % nz), device_id_type=MESH)

    loop(nz, greet, 1)
    pl.semaphore_wait(bar, 4 + nz - 1)

    def wblk(ch, zz, yy):
        start, width = CH[ch]
        return W.at[rows(zz * 2 + yy, br), pl.ds(start, width)]

    def ag_z(ch, k, src, slot, dev):
        b = wblk(ch, src, y)
        return rc(b, b, agz_s.at[ch, k], agz_r.at[ch, slot], zdev(dev))

    def ag_y(ch, k, src, yy):
        b = wblk(ch, src, yy)
        return rc(b, b, agy_s.at[ch, k], agy_r.at[ch, k], ypeer)

    def ag_own(ch):
        ag_y(ch, 0, z, y).start()
        if tree:
            ag_z(ch, 0, z, 1, partner).start()
            ag_z(ch, 1, z, jnp.where(is_middle, 2, 3), near).start()
        else:
            loop(nz, lambda k: ag_z(ch, k, z, k, (z + k) % nz).start(), 1)

    def ag_fwd(ch, only=None):
        def step(k):
            src = zsrc(k)
            ag_z(ch, k, src, k, partner).wait_recv()
            if tree:

                @pl.when((k >= 2) & is_middle)
                def _():
                    ag_z(ch, k, src, k, partner).start()

            ag_y(ch, k, src, y).start()

        if only is None:
            loop(nz, step, 1)
        else:
            loop(only[1], step, only[0])

    def ag_wait(ch):
        loop(nz, lambda k: ag_y(ch, k, zsrc(k), 1 - y).wait_recv())

    def ag_done(ch):
        loop(nz, lambda k: ag_y(ch, k, zsrc(k), y).wait_send())
        if tree:
            ag_z(ch, 0, z, 1, partner).wait_send()
            ag_z(ch, 1, z, 2, near).wait_send()

            @pl.when(is_middle)
            def _():
                ag_z(ch, 2, near, 2, partner).wait_send()
                ag_z(ch, 3, far, 3, partner).wait_send()

        else:
            loop(nz, lambda k: ag_z(ch, k, z, k, z).wait_send(), 1)

    def cag(n, block):
        def copy(i, d, dev):
            return rc(block(d), block(d), cag_s.at[n, i], cag_r.at[n, i], dev)

        def start():
            copy(0, col, cpeer).start()
            copy(1, col, xpeer).start()

        def forward():
            copy(1, (1 - x) * 2 + c, xpeer).wait_recv()
            copy(2, (1 - x) * 2 + c, cpeer).start()

        def wait():
            copy(0, x * 2 + 1 - c, cpeer).wait_recv()
            copy(2, (1 - x) * 2 + 1 - c, cpeer).wait_recv()

        def done():
            copy(0, col, cpeer).wait_send()
            copy(1, col, xpeer).wait_send()
            copy(2, (1 - x) * 2 + c, cpeer).wait_send()

        return start, forward, wait, done

    def col_block(ref):
        return lambda d: ref.at[:, pl.ds(pl.multiple_of(d * CW, CW), CW)]

    def row_block(ref):
        return lambda d: ref.at[rows(d, RB), :]

    tok_start, tok_forward, tok_wait, tok_done = cag(0, col_block(Tk))
    cot_start, cot_forward, cot_wait, cot_done = cag(1, col_block(Ct))
    nf_start, nf_forward, nf_wait, nf_done = cag(2, row_block(NF))
    rl_start, rl_forward, rl_wait, rl_done = cag(3, row_block(Ct))

    def crs(n, A, B, S):
        def to_core(i, xx, cc):
            return rc(PB.at[rows(xx * 2 + cc, RB), :], A(xx), crs_s.at[n, i], crs_r.at[n, i], cpeer)

        def to_x():
            return rc(S, B, crs_s.at[n, 2], crs_r.at[n, 2], xpeer)

        def produce(part):
            def step(i):
                xx = jnp.where(i < 2, 1 - x, x)
                cc = jnp.where(i % 2 == 0, 1 - c, c)
                PB[rows(xx * 2 + cc, RB), :] = part(xx * 2 + cc).astype(bf16)

                @pl.when(i % 2 == 0)
                def _():
                    to_core(i // 2, xx, 1 - c).start()

            loop(4, step)

        def middle():
            to_core(0, 1 - x, c).wait_recv()

            def step(i):
                r = rows(i, 32)
                block = PB[pl.ds(pl.multiple_of(((1 - x) * 2 + c) * RB + i * 32, 32), 32), :]
                S[r, :] = (block.astype(f32) + A(1 - x)[r, :].astype(f32)).astype(bf16)

            loop(RB // 32, step)
            to_x().start()

        def wait():
            to_core(1, x, c).wait_recv()
            to_x().wait_recv()

        def total(i, n):
            r = rows(i, n)
            block = PB[pl.ds(pl.multiple_of(col * RB + i * n, n), n), :].astype(f32)
            return block + A(x)[r, :].astype(f32) + B[r, :].astype(f32)

        def done():
            to_core(0, 1 - x, 1 - c).wait_send()
            to_core(1, x, 1 - c).wait_send()
            to_x().wait_send()

        return produce, middle, wait, total, done

    def gcol(ch):
        start, width = RCH[ch]
        return (G, start - PW, width) if start >= PW else (W, down0 + start, width)

    def gblk(ch, zz, yy):
        ref, start, width = gcol(ch)
        return ref.at[rows(zz * 2 + yy, br), pl.ds(start, width)]

    def rs_y(ch, zz, yy):
        start, width = RCH[ch]
        return rc(
            gblk(ch, zz, yy), RY.at[zz, :, pl.ds(start, width)], rsy_s.at[ch, zz], rsy_r.at[ch, zz], ypeer
        )

    def rs_z(ch, k, zz, slot, dev):
        part = pl.ds(RCH[ch][0], RCH[ch][1])
        return rc(RY.at[zz, :, part], RZ.at[slot, :, part], rsz_s.at[ch, k], rsz_r.at[ch, slot], zdev(dev))

    zper = RB // (2 * br)

    def grad_step(i):
        return zorder(i) if tree else (row * br // RB + 1 + i) % (D // RB)

    def rs_send(ch, dblk):
        loop(zper, lambda s: rs_y(ch, dblk * zper + s, 1 - y).start())

    def rs_add(ch, zz, what):
        start, width = RCH[ch]

        def add(i):
            r = rows(i, 16)
            t = RY[zz, r, pl.ds(start, width)].astype(f32)
            RY[zz, r, pl.ds(start, width)] = (what(i).astype(f32) + t).astype(bf16)

        loop(br // 16, add)

    def rs_mid(ch):
        ref, gstart, width = gcol(ch)

        def step(i):
            zz = zorder(i)
            rs_y(ch, zz, y).wait_recv()
            rs_add(
                ch, zz,
                lambda j: ref[pl.ds(pl.multiple_of((zz * 2 + y) * br + j * 16, 16), 16), pl.ds(gstart, width)],
            )
            if tree:

                @pl.when((i == 2) | jnp.logical_not(is_middle))
                def _():
                    rs_z(ch, i, zz, i, partner).start()

            else:
                rs_z(ch, i, zz, i, zz).start()

        loop(nz - 1, step)

    def rs_relay(ch):
        if tree:

            @pl.when(is_middle)
            def _():
                def step(i):
                    zz = zorder(i)
                    rs_z(ch, i, zz, i, partner).wait_recv()
                    rs_add(ch, zz, lambda j: RZ[i, rows(j, 16), pl.ds(RCH[ch][0], RCH[ch][1])])
                    rs_z(ch, i, zz, 3, zz).start()

                loop(2, step)

    def outs(ch):
        start, width = RCH[ch]
        if start >= down0:
            pairs = [(GFD.at[pl.ds(start - down0, width), :], gdown_h.at[pl.ds(start - down0, width), :])]
        elif start >= PW:
            at = pl.ds((start - PW) // 2, FC)
            pairs = [
                (GF.at[:, pl.ds(start - 2 * KW, FC)], ggate_h.at[:, at]),
                (GF.at[:, pl.ds(start - 2 * KW + FC, FC)], gup_h.at[:, at]),
            ]
        elif start == 2 * QW:
            pairs = [(GFO, gout_h)]
        else:
            pairs = [
                (GF.at[:, pl.ds(0, QW)], gquery_h),
                (GF.at[:, pl.ds(QW, KW)], gkey_h),
                (GF.at[:, pl.ds(QW + KW, KW)], gvalue_h),
            ]
        return [pltpu.make_async_copy(a, b, out_sem.at[3 * ch + i]) for i, (a, b) in enumerate(pairs)]

    def rs_fin(ch):
        ref, gstart, width = gcol(ch)
        start = RCH[ch][0]
        rs_y(ch, z, y).wait_recv()
        slots = (2, 3) if tree else (0, nz - 2)
        loop(slots[1] + 1, lambda k: rs_z(ch, 0, z, k, z).wait_recv(), slots[0])

        def total(r0, rn, c0, cn):
            r = pl.ds(r0, rn)
            g = ref[pl.ds(pl.multiple_of(row * br + r0, 16), rn), pl.ds(gstart + c0, cn)]
            part = pl.ds(start + c0, cn)
            t = g.astype(f32) + RY[z, r, part].astype(f32)
            return lax.fori_loop(slots[0], slots[1] + 1, lambda k, t: t + RZ[k, r, part].astype(f32), t)

        if start >= down0 or start == 2 * QW:
            for c0 in range(0, width, 128):
                t = jnp.transpose(total(0, br, c0, 128))
                if start >= down0:
                    GFD[pl.ds(start - down0 + c0, 128), :] = t
                else:
                    GFO[pl.ds(c0, 128), :] = t
        else:
            at = start - 2 * KW if start >= PW else start

            def add(i):
                r0 = pl.multiple_of(i * 16, 16)
                GF[pl.ds(r0, 16), pl.ds(at, width)] = total(r0, 16, 0, width)

            loop(br // 16, add)
        for copy in outs(ch):
            copy.start()

    def rs_done(ch):
        loop(nz, lambda zz: rs_y(ch, zz, 1 - y).wait_send())
        loop(nz - 1, lambda k: rs_z(ch, k, z, 0, z).wait_send())
        for copy in outs(ch):
            copy.wait()

    for i in range(4):
        local[i].wait()
    W[own, pl.ds(2 * QW, QW)] = jnp.transpose(WO[...])
    ag_own(0)
    local[4].wait()
    tok_start()
    for i in range(6, 12):
        local[i].wait()
    ag_own(1)
    local[12].wait()
    W[own, pl.ds(down0, F)] = jnp.transpose(WD[...])
    local[5].wait()
    cot_start()

    seg = seg_ref[...]
    first = jnp.zeros((1, T), jnp.int32)
    for d in range(ids):
        count = jnp.sum((seg == d).astype(f32), axis=1, keepdims=True).astype(jnp.int32)
        first = first + jnp.where(seg > d, count, 0)
    place = lax.broadcasted_iota(jnp.int32, (1, T), 1)
    lane = lax.broadcasted_iota(jnp.int32, (1, 128), 1)
    inverse_freq = jnp.exp((lane % 32).astype(f32) * (-2.0 / 64 * math.log(rope_base)))
    CS[...] = jnp.transpose(jnp.broadcast_to((place - first).astype(f32), (128, T)))

    def tables(i):
        angle = CS[rows(i, 128), :] * inverse_freq
        sine = jnp.sin(angle)
        CS[rows(i, 128), :] = jnp.cos(angle)
        SN[rows(i, 128), :] = jnp.where(lane % 64 < 32, -sine, sine)

    loop(T // 128, tables)
    windows = []
    at = 0
    for i in range(nb):
        start = max(0, RB * i - longest)
        width = RB * (i + 1) - start
        windows.append((start, width, at))
        key_place = lax.broadcasted_iota(jnp.int32, (width, RB), 0) + start
        q_place, q_first = place[:, RB * i : RB * (i + 1)], first[:, RB * i : RB * (i + 1)]
        seen = (key_place <= q_place) & (key_place >= q_first)
        BIAS[pl.ds(at, width), :] = jnp.where(seen, 0.0, -1e30).astype(bf16)
        at += width
    half_a = lax.broadcasted_iota(jnp.int32, (128, 128), 0) // 64
    half_b = lax.broadcasted_iota(jnp.int32, (128, 128), 1) // 64
    mean_matrix = jnp.where(half_a == half_b, 1.0 / 64, 0.0).astype(bf16)

    def head_mean(v):
        high = v.astype(bf16)
        low = (v - high.astype(f32)).astype(bf16)
        return dot_nn(high, mean_matrix) + dot_nn(low, mean_matrix)

    def turn(v):
        return jnp.where(lane % 64 < 32, pltpu.roll(v, 96, 1), pltpu.roll(v, 32, 1))

    gain_q = jnp.concatenate([gq_ref[...], gq_ref[...]], axis=1)
    gain_k = jnp.concatenate([gk_ref[...], gk_ref[...]], axis=1)
    ga = ga_ref[...]
    gf = gf_ref[...]

    ag_fwd(0, (1, 3))
    if tree:

        @pl.when(is_middle)
        def _():
            ag_fwd(0, (3, 4))

    tok_forward()
    tok_wait()

    def norm_tokens(i):
        t = Tk[rows(i, 128), :].astype(f32)
        r = lax.rsqrt(jnp.mean(t * t, axis=1, keepdims=True) + epsilon)
        R1[rows(i, 128), :] = jnp.broadcast_to(r, (128, 128))
        Nm[rows(i, 128), :] = (t * r * ga).astype(bf16)

    loop(T // 128, norm_tokens)
    if tree:

        @pl.when(jnp.logical_not(is_middle))
        def _():
            ag_fwd(0, (3, 4))

    else:
        ag_fwd(0, (3, nz))
    ag_own(2)
    ag_wait(0)

    def project(i):
        r = rows(i, RB)
        PRE[r, :] = dot_nn(Nm[r, :], W[:, pl.ds(0, 2 * QW)])
        cos, sin = CS[r, :], SN[r, :]
        for p in range(3):
            v = PRE[r, pl.ds(128 * p, 128)]
            n = v * lax.rsqrt(head_mean(v * v) + epsilon)
            u = n * (gain_q if p < 2 else gain_k)
            u = (u * cos + turn(u) * sin).astype(bf16)
            if p < 2:
                u = u * jnp.asarray(0.125, bf16)
                QS[p, 0, r, :] = u[:, :64]
                QS[p, 1, r, :] = u[:, 64:]
            else:
                KS[0, r, :] = u[:, :64]
                KS[1, r, :] = u[:, 64:]
                ut = jnp.transpose(u)
                KT[0, :, r] = ut[:64, :]
                KT[1, :, r] = ut[64:, :]
        v = PRE[r, pl.ds(384, 128)].astype(bf16)
        VS[0, r, :] = v[:, :64]
        VS[1, r, :] = v[:, 64:]
        vt = jnp.transpose(v)
        VT[0, :, r] = vt[:64, :]
        VT[1, :, r] = vt[64:, :]

    loop(nb, project)

    def attend(i):
        start, width, at = windows[i]
        keys = pl.ds(start, width)
        r = pl.ds(RB * i, RB)

        def step(h):
            q = QS[h, :, r, :].reshape(2 * RB, 64)
            bias = BIAS[pl.ds(at, width), :].astype(f32)
            s = dot_nt(KS[h, keys, :], q) + jnp.concatenate([bias, bias], axis=1)
            e = jnp.exp(s)
            inv = 1.0 / jnp.sum(e, axis=0, keepdims=True)
            INV[h, pl.ds(i, 1), :] = inv
            o = dot_nn(VT[h, :, keys], (e * inv).astype(bf16))
            o = jnp.concatenate([o[:, :RB], o[:, RB:]], axis=0)
            MX[r, pl.ds(pl.multiple_of(h * 128, 128), 128)] = jnp.transpose(o).astype(bf16)

        loop(2, step)

    ag_fwd(1)
    ag_own(3)
    attend(0)
    attend(1)
    cot_forward()
    attend(2)
    attend(3)
    a_produce, a_middle, a_wait, a_total, a_done = crs(0, lambda i: A0.at[i], B0, S0)
    a_produce(lambda d: dot_nt(MX[rows(d, RB), :], W[:, pl.ds(2 * QW, QW)]))
    a_middle()
    ag_fwd(2)
    ag_own(4)
    a_wait()

    def after_attention(i):
        r = rows(i, 32)
        mine_rows = pl.ds(pl.multiple_of(col * RB + i * 32, 32), 32)
        v = Tk[mine_rows, :].astype(f32) + a_total(i, 32)
        RES[r, :] = v
        n = v * lax.rsqrt(jnp.mean(v * v, axis=1, keepdims=True) + epsilon)
        NF[mine_rows, :] = (n * gf).astype(bf16)

    loop(RB // 32, after_attention)
    nf_start()
    a_done()
    cot_wait()
    cot_done()
    ag_fwd(3)
    ag_own(5)
    nf_forward()
    nf_wait()
    nf_done()

    def ffn(j):
        def step(i):
            r = rows(i, RB)
            n = NF[r, :]
            gate = dot_nn(n, W[:, pl.ds(PW + 2 * FC * j, FC)])
            up = dot_nn(n, W[:, pl.ds(PW + 2 * FC * j + FC, FC)])
            sig = 1.0 / (1.0 + jnp.exp(-gate))
            act = gate * sig
            HID[r, pl.ds(FC * j, FC)] = (act * up).astype(bf16)
            GG[r, pl.ds(2 * FC * j, FC)] = (up * (sig + act * (1.0 - sig))).astype(bf16)
            GG[r, pl.ds(2 * FC * j + FC, FC)] = act.astype(bf16)

        loop(nb, step)

    def weight_grad(left, pieces):
        def step(i):
            d = grad_step(i)
            lt = jnp.transpose(left[:, rows(d, RB)])
            for ch, right in pieces:
                ref, start, width = gcol(ch)
                ref[rows(d, RB), pl.ds(start, width)] = dot_nn(lt, right[...]).astype(bf16)
                rs_send(ch, d)

        loop(D // RB, step)

    for j in range(3):
        ag_wait(1 + j)
        ffn(j)
        ag_fwd(4 + j)
        if j == 0:
            ag_own(6)
        weight_grad(Ct, [(j, HID.at[:, pl.ds(FC * j, FC)])])
        if j > 0:
            rs_mid(j - 1)
        if j > 1:
            rs_relay(j - 2)
    for j in range(3):
        ag_wait(4 + j)

        def grad_hidden(i, j=j):
            r = rows(i, RB)
            gh = dot_nn(Ct[r, :], W[:, pl.ds(down0 + FC * j, FC)])
            a, b = pl.ds(2 * FC * j, FC), pl.ds(2 * FC * j + FC, FC)
            GG[r, a] = (gh * GG[r, a].astype(f32)).astype(bf16)
            GG[r, b] = (gh * GG[r, b].astype(f32)).astype(bf16)

        loop(nb, grad_hidden)
    n_produce, n_middle, n_wait, n_total, n_done = crs(1, lambda i: A0.at[i], B0, S0)
    n_produce(lambda d: dot_nt(GG[rows(d, RB), :], W[:, pl.ds(PW, 2 * F)]))
    n_middle()
    rs_relay(1)
    rs_mid(2)
    weight_grad(NF, [(3 + j, GG.at[:, pl.ds(2 * FC * j, 2 * FC)]) for j in range(3)])
    rs_relay(2)
    n_wait()
    VEC[...] = jnp.zeros(VEC.shape, f32)

    def after_ffn(i):
        r = rows(i, 32)
        mine_rows = pl.ds(pl.multiple_of(col * RB + i * 32, 32), 32)
        gy = n_total(i, 32)
        v = RES[r, :]
        inv = lax.rsqrt(jnp.mean(v * v, axis=1, keepdims=True) + epsilon)
        n = v * inv
        VEC[1:2, :] += jnp.sum(gy * n, axis=0, keepdims=True)
        g = gy * gf
        g = inv * (g - n * jnp.mean(g * n, axis=1, keepdims=True))
        Ct[mine_rows, :] = (Ct[mine_rows, :].astype(f32) + g).astype(bf16)

    loop(RB // 32, after_ffn)
    rl_start()
    n_done()
    rs_mid(3)
    rl_forward()
    rl_wait()

    def grad_mixed(i):
        r = rows(i, RB)
        g = dot_nn(Ct[r, :], W[:, pl.ds(2 * QW, QW)]).astype(bf16)
        for p in range(2):
            DO[p, 0, r, :] = g[:, 128 * p : 128 * p + 64]
            DO[p, 1, r, :] = g[:, 128 * p + 64 : 128 * p + 128]

    loop(nb, grad_mixed)
    b_produce, b_middle, b_wait, b_total, b_done = crs(
        2, lambda i: NF.at[rows(i, RB), :], NF.at[pl.ds(2 * RB, RB), :], NF.at[pl.ds(3 * RB, RB), :]
    )
    b_produce(lambda d: dot_nt(HID[rows(d, RB), :], W[:, pl.ds(down0, F)]))
    b_middle()
    for ch in range(7):
        ag_done(ch)
    weight_grad(Ct, [(6, MX)])
    rs_mid(4)
    rs_relay(3)
    DK[...] = jnp.zeros(DK.shape, f32)
    DV[...] = jnp.zeros(DV.shape, f32)

    def attend_back(i):
        start, width, at = windows[i]
        keys = pl.ds(start, width)
        r = pl.ds(RB * i, RB)

        def step(h):
            q = QS[h, :, r, :].reshape(2 * RB, 64)
            do = DO[h, :, r, :].reshape(2 * RB, 64)
            bias = BIAS[pl.ds(at, width), :].astype(f32)
            s = dot_nt(KS[h, keys, :], q) + jnp.concatenate([bias, bias], axis=1)
            p = jnp.exp(s) * INV[h, pl.ds(i, 1), :]
            dp = dot_nt(VS[h, keys, :], do)
            DV[h, keys, :] += dot_nn(p.astype(bf16), do)
            ds = (p * (dp - jnp.sum(p * dp, axis=0, keepdims=True))).astype(bf16)
            DK[h, keys, :] += dot_nn(ds, q)
            g = dot_nn(KT[h, :, keys], ds) * 0.125
            g = jnp.concatenate([g[:, :RB], g[:, RB:]], axis=0)
            DQ[r, pl.ds(pl.multiple_of(h * 128, 128), 128)] = jnp.transpose(g)

        loop(2, step)

    attend_back(0)
    attend_back(1)
    rs_mid(5)
    rs_relay(4)
    b_wait()
    LO = S0

    def finish(i):
        LO[rows(i, 32), :] = (RES[rows(i, 32), :] + b_total(i, 32)).astype(bf16)

    loop(RB // 32, finish)

    def lo_copy(i, d, dev):
        return rc(
            LO.at[:, pl.ds(pl.multiple_of(d * CW, CW), CW)], LOC.at[rows(col, RB), :], lo_s.at[i], lo_r.at[i], dev
        )

    others = [(0, x * 2 + 1 - c, cpeer), (1, (1 - x) * 2 + c, xpeer), (2, (1 - x) * 2 + 1 - c, dpeer)]
    for i, d, dev in others:
        lo_copy(i, d, dev).start()
    LOC[rows(col, RB), :] = LO[:, mine]
    attend_back(2)
    rs_relay(5)
    rs_mid(6)
    attend_back(3)
    rs_relay(6)

    def project_back(i):
        r = rows(i, RB)
        cos, sin = CS[r, :], SN[r, :]
        for p in range(3):
            g = DQ[r, pl.ds(128 * p, 128)] if p < 2 else jnp.concatenate([DK[0, r, :], DK[1, r, :]], axis=1)
            g = g * cos - turn(g) * sin
            v = PRE[r, pl.ds(128 * p, 128)]
            inv = lax.rsqrt(head_mean(v * v) + epsilon)
            n = v * inv
            s = pl.ds(0 if p < 2 else 128, 128)
            VEC[2:3, s] += jnp.sum(g * n, axis=0, keepdims=True)
            g = g * (gain_q if p < 2 else gain_k)
            HID[r, pl.ds(128 * p, 128)] = (inv * (g - n * head_mean(g * n))).astype(bf16)
        HID[r, pl.ds(384, 128)] = jnp.concatenate([DV[0, r, :], DV[1, r, :]], axis=1).astype(bf16)

    loop(nb, project_back)
    weight_grad(Nm, [(7, HID.at[:, pl.ds(0, 2 * QW)])])

    def gn_core(i, k, xx, cc):
        d = xx * 2 + cc
        return rc(
            PB.at[rows(i, RB), pl.ds(pl.multiple_of(d * CW, CW), CW)],
            AC.at[rows(i, RB), pl.ds(pl.multiple_of(xx * CW, CW), CW)],
            gn_s.at[i, k], gn_r.at[i, k], cpeer,
        )

    def gn_x(i):
        return rc(SC.at[rows(i, RB), :], BC.at[rows(i, RB), :], gn_s.at[i, 2], gn_r.at[i, 2], xpeer)

    b_done()

    def gn_produce(i):
        r = rows(i, RB)
        g = dot_nt(HID[r, pl.ds(0, 2 * QW)], W[:, pl.ds(0, 2 * QW)])
        PB[r, :] = g.astype(bf16)
        gn_core(i, 0, 1 - x, 1 - c).start()
        gn_core(i, 1, x, 1 - c).start()
        g = g * (Tk[r, :].astype(f32) * R1[r, pl.ds(0, 1)])
        VEC[0:1, :] += jnp.sum(g, axis=0, keepdims=True)
        s = jnp.sum(g * ga, axis=1, keepdims=True)
        VEC[3:4, r] = jnp.transpose(jnp.broadcast_to(s, (RB, 128)))[0:1, :]

    loop(nb, gn_produce)

    def vec_copy(i, src, dst, dev):
        return rc(src, dst, vec_s.at[i], vec_r.at[i], dev)

    vec_c = vec_copy(0, VEC, VC, cpeer)
    vec_c.start()

    def gn_middle(i):
        r = rows(i, RB)
        gn_core(i, 0, 1 - x, c).wait_recv()
        a = PB[r, pl.ds(pl.multiple_of(((1 - x) * 2 + c) * CW, CW), CW)].astype(f32)
        b = AC[r, pl.ds(pl.multiple_of((1 - x) * CW, CW), CW)].astype(f32)
        SC[r, :] = (a + b).astype(bf16)
        gn_x(i).start()

    loop(nb, gn_middle)
    vec_c.wait_recv()
    vec_c.wait_send()
    VEC[...] += VC[...]
    vec_x = vec_copy(1, VEC, VX, xpeer)
    vec_x.start()
    rs_fin(0)
    rs_fin(1)
    rs_fin(2)
    rs_mid(7)
    rs_relay(7)
    vec_x.wait_recv()
    vec_x.wait_send()
    VEC[...] += VX[...]
    vec_y = vec_copy(2, VEC, VY, ypeer)
    vec_y.start()

    def gn_finish(i):
        r = rows(i, RB)
        gn_core(i, 1, x, c).wait_recv()
        gn_x(i).wait_recv()
        g = PB[r, mine].astype(f32) + AC[r, pl.ds(pl.multiple_of(x * CW, CW), CW)].astype(f32) + BC[r, :].astype(f32)
        g = g * ga_ref[:, mine]
        inv = R1[r, pl.ds(0, 1)]
        s = jnp.transpose(jnp.broadcast_to(VEC[3:4, r], (128, RB)))[:, 0:1] * (1.0 / D)
        n = Tk[r, mine].astype(f32) * inv
        DQ[r, :] = Ct[r, mine].astype(f32) + inv * (g - n * s)

    loop(nb, gn_finish)
    gt_copy = pltpu.make_async_copy(DQ, gt_h, out_sem.at[24])
    gt_copy.start()
    vec_y.wait_recv()
    vec_y.wait_send()
    VZ[z] = VEC[...] + VY[...]

    def vz_copy(k, src):
        return rc(VZ.at[src], VZ.at[src], vz_s.at[k], vz_r.at[k], zdev((z + k) % nz))

    loop(nz, lambda k: vz_copy(k, z).start(), 1)
    for i, d, dev in others:
        lo_copy(i, d, dev).wait_recv()
    lo_out = pltpu.make_async_copy(LOC, lo_h, out_sem.at[25])
    lo_out.start()
    for ch in range(3, 8):
        rs_fin(ch)
    loop(nz, lambda k: vz_copy(k, (z + nz - k) % nz).wait_recv(), 1)
    gain_ref[...] = lax.fori_loop(1, nz, lambda k, t: t + VZ[k], VZ[0])

    tok_done()
    rl_done()
    for i, d, dev in others:
        lo_copy(i, d, dev).wait_send()

    def gn_done(i):
        gn_core(i, 0, 1 - x, 1 - c).wait_send()
        gn_core(i, 1, x, 1 - c).wait_send()
        gn_x(i).wait_send()

    loop(nb, gn_done)
    loop(nz, lambda k: vz_copy(k, z).wait_send(), 1)
    for ch in range(8):
        rs_done(ch)
    gt_copy.wait()
    lo_out.wait()


def hand_out(*refs):
    sources, gains, targets, held, sem = refs[:9], refs[9], refs[10:19], refs[23:32], refs[32]
    loads = [pltpu.make_async_copy(a, b, sem.at[0, i]) for i, (a, b) in enumerate(zip(sources, held))]
    stores = [pltpu.make_async_copy(a, b, sem.at[1, i]) for i, (a, b) in enumerate(zip(held, targets))]
    for copy in loads:
        copy.start()
    attn, ffn, query, key = refs[19:23]
    attn[...] = gains[0:1, :]
    ffn[...] = gains[1:2, :]
    query[...] = gains[2:3, 0:64] + gains[2:3, 64:128]
    key[...] = gains[2:3, 128:192] + gains[2:3, 192:256]
    for load, store in zip(loads, stores):
        load.wait()
        store.start()
    for store in stores:
        store.wait()


def per_device(
    n_row, tokens, segment_ids, w_query, key_matrix, value_matrix, w_out, w_gate, w_up, w_down,
    norm_attn, norm_ffn, norm_query, norm_key, cotangent,
):
    T, CW = tokens.shape
    br, QW = w_query.shape
    KW = key_matrix.shape[1]
    F = w_gate.shape[1]
    D = br * n_row
    nz = n_row // 2
    PW = 2 * QW + 2 * KW
    WW = PW + 3 * F
    nb = T // RB
    area = sum(RB * (i + 1) - max(0, RB * i - longest) for i in range(nb))
    vm, sem = pltpu.VMEM, pltpu.SemaphoreType.DMA
    scratch = [
        vm((D, WW), bf16), vm((QW, br), bf16), vm((F, br), bf16), vm((QW, br), f32), vm((F, br), f32),
        vm((D, 3 * F), bf16), vm((nz, br, WW), bf16), vm((4 if nz == 4 else nz - 1, br, WW), bf16),
        vm((br, 2 * QW + 2 * F), f32), vm((T, D), bf16), vm((T, D), bf16), vm((T, D), bf16), vm((T, 128), f32),
        vm((T, 2 * QW), f32), vm((2, 2, T, 64), bf16), vm((2, T, 64), bf16), vm((2, T, 64), bf16),
        vm((2, 64, T), bf16), vm((2, 64, T), bf16), vm((2, 2, T, 64), bf16), vm((T, QW), bf16),
        vm((T, D), bf16), vm((2, RB, D), bf16), vm((RB, D), bf16), vm((RB, D), bf16), vm((RB, D), f32),
        vm((T, D), bf16), vm((T, 2 * F), bf16), vm((T, F), bf16),
        vm((T, 128), f32), vm((T, 128), f32), vm((area, RB), bf16), vm((2, 8, 2 * RB), f32),
        vm((T, QW), f32), vm((2, T, 64), f32), vm((2, T, 64), f32),
        vm((T, 2 * CW), bf16), vm((T, CW), bf16), vm((T, CW), bf16), vm((T, CW), bf16),
        vm((8, D), f32), vm((8, D), f32), vm((8, D), f32), vm((8, D), f32), vm((nz, 8, D), f32),
        sem((13,)), sem((7, nz)), sem((7, nz)), sem((7, nz)), sem((7, nz)),
        sem((8, nz)), sem((8, nz)), sem((8, nz)), sem((8, nz)),
        sem((4, 3)), sem((4, 3)), sem((3, 3)), sem((3, 3)), sem((nb, 3)), sem((nb, 3)), sem((3,)), sem((3,)),
        sem((3,)), sem((3,)), sem((nz,)), sem((nz,)), sem((26,)),
    ]
    whole, hbm = pl.BlockSpec(memory_space=pltpu.VMEM), pl.BlockSpec(memory_space=pl.ANY)
    shape = jax.ShapeDtypeStruct
    results = (
        shape((T, CW), bf16), shape((T, CW), f32), shape((br, QW), f32), shape((br, KW), f32), shape((br, KW), f32),
        shape((QW, br), f32), shape((br, F), f32), shape((br, F), f32), shape((F, br), f32),
    )
    outs = pl.pallas_call(
        functools.partial(layer_kernel, nz),
        out_shape=results + (shape((8, D), f32),),
        in_specs=[hbm, whole] + [hbm] * 7 + [whole] * 4 + [hbm],
        out_specs=(hbm,) * 9 + (whole,),
        scratch_shapes=scratch,
        compiler_params=pltpu.CompilerParams(
            collective_id=0, has_side_effects=True, vmem_limit_bytes=64 * 2**20
        ),
        name="layer",
    )(
        tokens, segment_ids, w_query, key_matrix, value_matrix, w_out, w_gate, w_up, w_down,
        norm_attn[None], norm_ffn[None], norm_query[None], norm_key[None], cotangent,
    )
    gain = shape((1, D), f32)
    head_gain = shape((1, norm_query.shape[0]), f32)
    outs = pl.pallas_call(
        hand_out,
        out_shape=results + (gain, gain, head_gain, head_gain),
        in_specs=[pl.BlockSpec(memory_space=pltpu.HBM)] * 9 + [whole],
        out_specs=(pl.BlockSpec(memory_space=pltpu.HBM),) * 9 + (whole,) * 4,
        scratch_shapes=[vm(v.shape, v.dtype) for v in results] + [sem((2, 9))],
        compiler_params=pltpu.CompilerParams(vmem_limit_bytes=63 * 2**20),
        name="hand_out",
    )(*outs)
    return outs[:9] + tuple(v[0] for v in outs[9:])


def solution(mesh):
    in_specs = (
        P("row", "col"), P("row", None), P("row", "col"), P("row", "col"), P("row", "col"), P("col", "row"),
        P("row", "col"), P("row", "col"), P("col", "row"), P(), P(), P(), P(), P("row", "col"),
    )
    out_specs = (
        P("row", "col"), P("row", "col"), P("row", "col"), P("row", "col"), P("row", "col"), P("col", "row"),
        P("row", "col"), P("row", "col"), P("col", "row"), P(), P(), P(), P(),
    )
    return jax.shard_map(
        functools.partial(per_device, mesh.shape["row"]),
        mesh=mesh, in_specs=in_specs, out_specs=out_specs, check_vma=False,
    )
```

```python
import functools
import math

import jax
import jax.numpy as jnp
from jax import lax
from jax.experimental import pallas as pl
from jax.experimental.pallas import tpu as pltpu
from jax.sharding import PartitionSpec as P

epsilon = 1e-05
rope_base = 1000000.0
longest = 512
ids = 8
f32, bf16 = jnp.float32, jnp.bfloat16
MESH = pl.DeviceIdType.MESH
RB = 256


def dot_nn(a, b):
    return lax.dot_general(a, b, (((1,), (0,)), ((), ())), preferred_element_type=f32)


def dot_nt(a, b):
    return lax.dot_general(a, b, (((1,), (1,)), ((), ())), preferred_element_type=f32)


def rows(i, n):
    return pl.ds(pl.multiple_of(i * n, n), n)


AG_PAIRS, RS_PAIRS = (5, 6), (0, 1)
ORDER = [
    ("owny", 0, "a"), ("gate_up", "a"), ("owny", 2, "a"), ("ownz", 0, "a"), ("owny", 1, "a"), ("fwd", 0, 1, "e"),
    ("ownz", 1, "a"), ("ownz", 2, "a"), ("toks", "a"), ("owny", 3, "a"), ("ownz", 3, "a"), ("fwd", 0, 1, "m"),
    ("fwd", 1, 1, "m"), ("cots", "a"), ("fwd", 1, 2, "m"), ("fwd", 0, 2, "m"), ("tables", "a"), ("fwd", 0, 3, "m"),
    ("owny", 4, "a"), ("fwd", 0, 2, "e"), ("fwd", 0, 3, "e"), ("ownz", 4, "a"), ("down", "a"), ("owny", 5, "a"),
    ("owny", 6, "a"), ("tokf", "a"), ("fwd", 1, 3, "m"), ("fwd", 2, 1, "m"), ("owny", 7, "a"), ("fwd", 3, 1, "m"),
    ("norm", "a"), ("fwd", 1, 1, "e"), ("fwd", 1, 2, "e"), ("fwd", 2, 2, "m"), ("project", "a"), ("fwd", 2, 3, "m"),
    ("att", 0, "a"), ("att", 1, "a"), ("fwd", 1, 3, "e"), ("fwd", 4, 1, "m"), ("fwd", 2, 1, "e"),
    ("fwd", 3, 2, "m"), ("cotf", "a"), ("ownz", 5, "a"), ("fwd", 3, 1, "e"), ("fwd", 3, 3, "m"), ("att", 2, "a"),
    ("ownz", 7, "a"), ("fwd", 2, 2, "e"), ("att", 3, "a"), ("aprod", "a"), ("fwd", 4, 2, "m"), ("fwd", 2, 3, "e"),
    ("ownz", 6, "a"), ("fwd", 6, 1, "e"), ("fwd", 5, 1, "m"), ("amid", "a"), ("aft", 0, "a"), ("fwd", 7, 1, "e"),
    ("fwd", 3, 2, "e"), ("fwd", 4, 3, "m"), ("fwd", 7, 1, "m"), ("fwd", 5, 2, "m"), ("aft", 1, "a"),
    ("fwd", 5, 1, "e"), ("fwd", 4, 1, "e"), ("fwd", 3, 3, "e"), ("fwd", 6, 1, "m"), ("fwd", 7, 2, "m"),
    ("nff", 0, "a"), ("fwd", 5, 2, "e"), ("fwd", 7, 3, "m"), ("fwd", 5, 3, "m"), ("fwd", 6, 2, "m"),
    ("nff", 1, "a"), ("fwd", 4, 2, "e"), ("fwd", 4, 3, "e"), ("ffn", 0, "a"), ("ffn", 1, "a"), ("fwd", 6, 2, "e"),
    ("fwd", 6, 3, "m"), ("fwd", 7, 2, "e"), ("wg", 0, "a"), ("wg", 1, "a"), ("fwd", 7, 3, "e"), ("ffn", 2, "a"),
    ("wg", 2, "a"), ("fwd", 5, 3, "e"), ("fwd", 6, 3, "e"), ("gh", 0, "a"), ("gh", 1, "a"), ("gh", 2, "a"),
    ("mid", 2, 0, "m"), ("wg", 3, "a"), ("gnfp", "a"), ("relay", 0, 0, "m"), ("gnfm", "a"), ("mid", 2, 0, "e"),
    ("mid", 3, 0, "e"), ("relay", 0, 1, "m"), ("mid", 3, 0, "m"), ("mid", 4, 0, "e"), ("naft", 0, "a"),
    ("mid", 4, 0, "m"), ("mid", 3, 1, "e"), ("mid", 4, 1, "e"), ("mid", 2, 1, "m"), ("mid", 5, 0, "m"),
    ("mid", 5, 0, "e"), ("naft", 1, "a"), ("relay", 3, 0, "m"), ("relay", 1, 0, "m"), ("mid", 2, 2, "m"),
    ("mid", 2, 1, "e"), ("mid", 3, 1, "m"), ("mid", 4, 1, "m"), ("mid", 3, 2, "m"), ("relay", 1, 1, "m"),
    ("relay", 4, 0, "m"), ("rlf", 0, "a"), ("mid", 3, 2, "e"), ("relay", 3, 1, "m"), ("rlf", 1, "a"),
    ("mid", 4, 2, "e"), ("mid", 2, 2, "e"), ("mid", 5, 1, "e"), ("relay", 2, 0, "m"), ("mid", 5, 1, "m"),
    ("gmix", "a"), ("brp", "a"), ("ab", 0, "a"), ("relay", 4, 1, "m"), ("relay", 2, 1, "m"), ("ab", 1, "a"),
    ("mid", 4, 2, "m"), ("wg", 6, "a"), ("brm", "a"), ("relay", 5, 0, "m"), ("mid", 5, 2, "m"), ("mid", 5, 2, "e"),
    ("ab", 2, "a"), ("ab", 3, "a"), ("pb", "a"), ("gnp", "a"), ("wg", 7, "a"), ("relay", 5, 1, "m"),
    ("mid", 6, 0, "m"), ("vc", "a"), ("gnm", "a"), ("mid", 6, 1, "m"), ("pre", 1, "e"), ("mid", 6, 0, "e"),
    ("mid", 7, 0, "e"), ("brf", "a"), ("pre", 1, "m"), ("mid", 7, 1, "e"), ("mid", 6, 1, "e"), ("fin", 5, "a"),
    ("mid", 7, 0, "m"), ("mid", 7, 1, "m"), ("mid", 7, 2, "e"), ("relay", 6, 0, "m"), ("relay", 7, 0, "m"),
    ("mid", 6, 2, "e"), ("mid", 7, 2, "m"), ("fin", 3, "a"), ("vx", "a"), ("mid", 6, 2, "m"), ("pre", 0, "m"),
    ("relay", 7, 1, "m"), ("pre", 0, "e"), ("relay", 6, 1, "m"), ("gnfin", "a"), ("vy", "a"), ("fin", 4, "a"),
    ("fin", 6, "a"), ("fin", 7, "a"), ("fin", 2, "a"), ("fin", 0, "a"), ("fin", 1, "a"), ("lof", "a"), ("end", "a"),
]


def layer_kernel(
    plan,
    tok_h, seg_ref, wq_h, wk_h, wv_h, wo_h, wg_h, wu_h, wd_h, ga_ref, gf_ref, gq_ref, gk_ref, cot_h,
    lo_h, gt_h, gquery_h, gkey_h, gvalue_h, gout_h, ggate_h, gup_h, gdown_h, gain_ref,
    W, WO, WD, GFO, GFD, G, RY, RZ, RYP, RZP, GF, Tk, Ct, Nm, R1, PRE, QS, KS, VS, KT, VT, DO, MX, PB, A0, B0, S0,
    RES, NF, GG, HID, CS, SN, BIAS, INV, DQ, DKV, AC, BC, SC, LOC, VEC, VC, VX, VY, VZ,
    loc_sem, agz_s, agz_r, agy_s, agy_r, rsy_s, rsy_r, rsz_s, rsz_r,
    cag_s, cag_r, crs_s, crs_r, gn_s, gn_r, lo_s, lo_r, vec_s, vec_r, vz_s, vz_r, out_sem,
):
    nz, tree, CH, RCH, ag_pairs, rs_pairs, place = plan
    T, D = Tk.shape
    br = RY.shape[1]
    QW, KW = PRE.shape[1] // 2, PRE.shape[1] // 4
    PW = 2 * QW + 2 * KW
    F = HID.shape[1]
    FC = F // 3
    HB = RB // 2
    down0 = PW + 2 * F
    nb = T // RB
    CW = D // 4
    GQ = GG.at[:, pl.ds(PW, 2 * QW)]
    PN = GG.at[:, pl.ds(PW + 2 * QW, D)]
    row, col = lax.axis_index("row"), lax.axis_index("col")
    z, y = row // 2, row % 2
    x, c = col // 2, col % 2
    ypeer = (row + 1 - 2 * y, col)
    cpeer = (row, col + 1 - 2 * c)
    xpeer = (row, (1 - x) * 2 + c)
    dpeer = (row, (1 - x) * 2 + 1 - c)
    partner = z + 1 - 2 * (z % 2)
    is_middle = (z == 1) | (z == 2)
    near, far = 2 - z // 2, 3 - 3 * (z // 2)

    def zdev(zz):
        return (zz * 2 + y, col)

    def zsrc(k):
        return [z, partner, near, far][k] if tree else (z + nz - k) % nz

    def zto(i):
        return [near, far, partner, z][i]

    def rc(src, dst, ss, rs, dev):
        return pltpu.make_async_remote_copy(
            src_ref=src, dst_ref=dst, send_sem=ss, recv_sem=rs, device_id=dev, device_id_type=MESH
        )

    def loop(n, body, first=0):
        def step(i, carry):
            body(i)
            return carry

        lax.fori_loop(first, n, step, 0)

    own = rows(row, br)
    mine = pl.ds(pl.multiple_of(col * CW, CW), CW)
    local = [
        (wq_h, W.at[own, pl.ds(0, QW)]),
        (wk_h, W.at[own, pl.ds(QW, KW)]),
        (wv_h, W.at[own, pl.ds(QW + KW, KW)]),
        (wo_h, WO),
        (tok_h, Tk.at[:, mine]),
        (cot_h, Ct.at[:, mine]),
    ]
    for j in range(3):
        local.append((wg_h.at[:, pl.ds(FC * j, FC)], W.at[own, pl.ds(PW + 2 * FC * j, FC)]))
        local.append((wu_h.at[:, pl.ds(FC * j, FC)], W.at[own, pl.ds(PW + 2 * FC * j + FC, FC)]))
    local.append((wd_h, WD))
    local = [pltpu.make_async_copy(s, d, loc_sem.at[i]) for i, (s, d) in enumerate(local)]

    def wblk(ch, zz, yy):
        start, width = CH[ch]
        return W.at[rows(zz * 2 + yy, br), pl.ds(start, width)]

    def wpair(ch, zz):
        start, width = CH[ch]
        return W.at[rows(zz, 2 * br), pl.ds(start, width)]

    def ag_z(ch, k, src, slot, dev):
        b = wpair(ch, src) if ch in ag_pairs else wblk(ch, src, y)
        return rc(b, b, agz_s.at[ch, k], agz_r.at[ch, slot], zdev(dev))

    def ag_y(ch, k, src, yy):
        b = wblk(ch, src, yy)
        return rc(b, b, agy_s.at[ch, k], agy_r.at[ch, k], ypeer)

    def own_y(ch):
        ag_y(ch, 0, z, y).start()

    def own_z(ch):
        if ch in ag_pairs:
            ag_y(ch, 0, z, 1 - y).wait_recv()
        if tree:
            ag_z(ch, 0, z, 1, partner).start()
            ag_z(ch, 1, z, jnp.where(is_middle, 2, 3), near).start()
        else:
            loop(nz, lambda k: ag_z(ch, k, z, k, (z + k) % nz).start(), 1)

    def forward(ch, k, middle):
        if not tree:
            if k == 3 and middle:

                def step(k):
                    ag_z(ch, k, zsrc(k), k, z).wait_recv()
                    ag_y(ch, k, zsrc(k), y).start()

                loop(nz, step, 1)
            return
        relayed = middle and k >= 2
        if ch in ag_pairs and not relayed:
            return
        ag_z(ch, k, zsrc(k), k, partner).wait_recv()
        if relayed:
            ag_z(ch, k, zsrc(k), k, partner).start()
        if ch not in ag_pairs:
            ag_y(ch, k, zsrc(k), y).start()

    def ag_wait(ch):
        if not tree:
            loop(nz, lambda k: ag_y(ch, k, zsrc(k), 1 - y).wait_recv())
        elif ch in ag_pairs:
            ag_z(ch, 0, partner, 1, partner).wait_recv()

            @pl.when(jnp.logical_not(is_middle))
            def _():
                ag_z(ch, 0, near, 2, partner).wait_recv()
                ag_z(ch, 0, far, 3, partner).wait_recv()

        else:
            for k in range(4):
                ag_y(ch, k, zsrc(k), 1 - y).wait_recv()

    def ag_done(ch):
        if not tree:
            loop(nz, lambda k: ag_y(ch, k, zsrc(k), y).wait_send())
            loop(nz, lambda k: ag_z(ch, k, z, k, z).wait_send(), 1)
            return
        for k in range(1 if ch in ag_pairs else 4):
            ag_y(ch, k, zsrc(k), y).wait_send()
        ag_z(ch, 0, z, 1, partner).wait_send()
        ag_z(ch, 1, z, 2, near).wait_send()

        @pl.when(is_middle)
        def _():
            ag_z(ch, 2, near, 2, partner).wait_send()
            ag_z(ch, 3, far, 3, partner).wait_send()

    def cag(n, block, parts=1):
        def copy(i, d, dev, h):
            return rc(block(d, h), block(d, h), cag_s.at[n, h, i], cag_r.at[n, h, i], dev)

        def start(h=0):
            copy(0, col, cpeer, h).start()
            copy(1, col, xpeer, h).start()

        def forward(h=0):
            copy(1, (1 - x) * 2 + c, xpeer, h).wait_recv()
            copy(2, (1 - x) * 2 + c, cpeer, h).start()

        def wait():
            for h in range(parts):
                copy(0, x * 2 + 1 - c, cpeer, h).wait_recv()
                copy(2, (1 - x) * 2 + 1 - c, cpeer, h).wait_recv()

        def done():
            for h in range(parts):
                copy(0, col, cpeer, h).wait_send()
                copy(1, col, xpeer, h).wait_send()
                copy(2, (1 - x) * 2 + c, cpeer, h).wait_send()

        return start, forward, wait, done

    def col_block(ref):
        return lambda d, h: ref.at[:, pl.ds(pl.multiple_of(d * CW, CW), CW)]

    def row_block(ref):
        return lambda d, h: ref.at[rows(d * 2 + h, HB), :]

    tok_start, tok_forward, tok_wait, tok_done = cag(0, col_block(Tk))
    cot_start, cot_forward, cot_wait, cot_done = cag(1, col_block(Ct))
    nf_start, nf_forward, nf_wait, nf_done = cag(2, row_block(NF), 2)
    rl_start, rl_forward, rl_wait, rl_done = cag(3, row_block(Ct), 2)

    def crs(n, A, B, S):
        def to_core(i, xx, cc):
            return rc(PB.at[rows(xx * 2 + cc, RB), :], A(xx), crs_s.at[n, i], crs_r.at[n, i], cpeer)

        def to_x(h):
            half = rows(h, HB)
            return rc(S.at[half, :], B.at[half, :], crs_s.at[n, 2 + h], crs_r.at[n, 2 + h], xpeer)

        def produce(part):
            def step(i):
                xx = jnp.where(i < 2, 1 - x, x)
                cc = jnp.where(i % 2 == 0, 1 - c, c)
                PB[rows(xx * 2 + cc, RB), :] = part(xx * 2 + cc).astype(bf16)

                @pl.when(i % 2 == 0)
                def _():
                    to_core(i // 2, xx, 1 - c).start()

            loop(4, step)

        def middle():
            to_core(0, 1 - x, c).wait_recv()

            def step(i):
                r = rows(i, 32)
                block = PB[pl.ds(pl.multiple_of(((1 - x) * 2 + c) * RB + i * 32, 32), 32), :]
                S[r, :] = (block.astype(f32) + A(1 - x)[r, :].astype(f32)).astype(bf16)

            for h in range(2):
                loop(HB // 32 * (h + 1), step, HB // 32 * h)
                to_x(h).start()

        def total(h, use):
            if h == 0:
                to_core(1, x, c).wait_recv()
            to_x(h).wait_recv()

            def step(i):
                r = rows(i, 32)
                at = pl.ds(pl.multiple_of(col * RB + i * 32, 32), 32)
                use(r, at, PB[at, :].astype(f32) + A(x)[r, :].astype(f32) + B[r, :].astype(f32))

            loop(HB // 32 * (h + 1), step, HB // 32 * h)

        def done():
            to_core(0, 1 - x, 1 - c).wait_send()
            to_core(1, x, 1 - c).wait_send()
            to_x(0).wait_send()
            to_x(1).wait_send()

        return produce, middle, total, done

    a_produce, a_middle, a_total, a_done = crs(0, lambda i: A0.at[i], B0, S0)
    n_produce, n_middle, n_total, n_done = crs(1, lambda i: A0.at[i], B0, S0)
    b_produce, b_middle, b_total, b_done = crs(
        2, lambda i: NF.at[rows(i, RB), :], NF.at[pl.ds(2 * RB, RB), :], NF.at[pl.ds(3 * RB, RB), :]
    )

    def gcol(ch):
        start, width = RCH[ch]
        return (G, start - PW, width) if start >= PW else (GG, start, width)

    def gblk(ch, zz, yy):
        ref, start, width = gcol(ch)
        return ref.at[rows(zz * 2 + yy, br), pl.ds(start, width)]

    def part_of(ch):
        return pl.ds(place[ch], RCH[ch][1])

    def rs_y(ch, zz, yy):
        landing = RYP.at[:, part_of(ch)] if ch in rs_pairs else RY.at[zz, :, part_of(ch)]
        return rc(gblk(ch, zz, yy), landing, rsy_s.at[ch, zz], rsy_r.at[ch, zz], ypeer)

    def rs_z(ch, k, zz, slot, dev):
        if ch in rs_pairs:
            ref, start, width = gcol(ch)
            src, dst = ref.at[rows(zz, 2 * br), pl.ds(start, width)], RZP.at[slot, :, part_of(ch)]
        else:
            src, dst = RY.at[zz, :, part_of(ch)], RZ.at[slot, :, part_of(ch)]
        return rc(src, dst, rsz_s.at[ch, k], rsz_r.at[ch, slot], zdev(dev))

    zper = RB // (2 * br)

    def weight_grad(left, pieces):
        def one(i, d):
            lt = jnp.transpose(left[:, rows(d, RB)])
            for ch, right in pieces:
                ref, start, width = gcol(ch)
                ref[rows(d, RB), pl.ds(start, width)] = dot_nn(lt, right[...]).astype(bf16)
                if ch not in rs_pairs:
                    loop(zper, lambda s: rs_y(ch, d * zper + s, 1 - y).start())
                elif i == 2:
                    rs_z(ch, 2, d, 2, partner).start()
                elif i < 2:

                    @pl.when(jnp.logical_not(is_middle))
                    def _():
                        rs_z(ch, i, d, i, partner).start()

        if any(ch in rs_pairs for ch, _ in pieces):
            for i in range(4):
                one(i, zto(i))
        elif tree:

            def step(i):
                one(i, jnp.where(i == 0, near, jnp.where(i == 1, far, jnp.where(i == 2, partner, z))))

            loop(4, step)
        else:
            loop(D // RB, lambda i: one(i, (row * br // RB + 1 + i) % (D // RB)))

    def rs_mid(ch, i, middle):
        ref, gstart, width = gcol(ch)

        def one(zz):
            rs_y(ch, zz, y).wait_recv()

            def add(j):
                r = rows(j, 16)
                g = ref[pl.ds(pl.multiple_of((zz * 2 + y) * br + j * 16, 16), 16), pl.ds(gstart, width)]
                t = RY[zz, r, part_of(ch)]
                RY[zz, r, part_of(ch)] = (g.astype(f32) + t.astype(f32)).astype(bf16)

            loop(br // 16, add)

        if not tree:
            if i == 2 and middle:

                def step(k):
                    zz = (z + k) % nz
                    one(zz)
                    rs_z(ch, k, zz, k - 1, zz).start()

                loop(nz, step, 1)
        elif ch not in rs_pairs:
            one(zto(i))
            if i == 2 or not middle:
                rs_z(ch, i, zto(i), i, partner).start()

    def rs_relay(ch, i):
        if not tree:
            return
        zz = zto(i)
        rs_z(ch, i, zz, i, partner).wait_recv()
        ref, gstart, width = gcol(ch)

        def add(j):
            r = rows(j, 16)
            if ch in rs_pairs:
                at = pl.ds(pl.multiple_of(zz * 2 * br + j * 16, 16), 16)
                t = ref[at, pl.ds(gstart, width)].astype(f32) + RZP[i, r, part_of(ch)].astype(f32)
                ref[at, pl.ds(gstart, width)] = t.astype(bf16)
            else:
                t = RY[zz, r, part_of(ch)].astype(f32) + RZ[i, r, part_of(ch)].astype(f32)
                RY[zz, r, part_of(ch)] = t.astype(bf16)

        loop((2 * br if ch in rs_pairs else br) // 16, add)
        rs_z(ch, i, zz, 3, zz).start()

    def rs_pre(ch):
        if ch not in rs_pairs:
            return
        for slot in (2, 3):
            rs_z(ch, 2, z, slot, partner).wait_recv()
        ref, gstart, width = gcol(ch)

        def add(j):
            at = pl.ds(pl.multiple_of((z * 2 + 1 - y) * br + j * 16, 16), 16)
            r = pl.ds(pl.multiple_of((1 - y) * br + j * 16, 16), 16)
            t = ref[at, pl.ds(gstart, width)].astype(f32)
            t = t + RZP[2, r, part_of(ch)].astype(f32) + RZP[3, r, part_of(ch)].astype(f32)
            ref[at, pl.ds(gstart, width)] = t.astype(bf16)

        loop(br // 16, add)
        rs_y(ch, z, 1 - y).start()

    def outs(ch):
        start, width = RCH[ch]
        if start >= down0:
            pairs = [(GFD.at[pl.ds(start - down0, width), :], gdown_h.at[pl.ds(start - down0, width), :])]
        elif start >= PW:
            at = pl.ds((start - PW) // 2, FC)
            pairs = [
                (GF.at[:, pl.ds(start - 2 * KW, FC)], ggate_h.at[:, at]),
                (GF.at[:, pl.ds(start - 2 * KW + FC, FC)], gup_h.at[:, at]),
            ]
        elif start == 2 * QW:
            pairs = [(GFO, gout_h)]
        else:
            pairs = [
                (GF.at[:, pl.ds(0, QW)], gquery_h),
                (GF.at[:, pl.ds(QW, KW)], gkey_h),
                (GF.at[:, pl.ds(QW + KW, KW)], gvalue_h),
            ]
        return [pltpu.make_async_copy(a, b, out_sem.at[3 * ch + i]) for i, (a, b) in enumerate(pairs)]

    def rs_fin(ch):
        ref, gstart, width = gcol(ch)
        start = RCH[ch][0]
        paired = ch in rs_pairs
        rs_y(ch, z, y).wait_recv()
        if not tree:
            loop(nz - 1, lambda k: rs_z(ch, 0, z, k, z).wait_recv())
        elif not paired:
            for slot in (2, 3):
                rs_z(ch, 0, z, slot, z).wait_recv()

        def total(r0, rn, c0, cn):
            r = pl.ds(r0, rn)
            g = ref[pl.ds(pl.multiple_of(row * br + r0, 16), rn), pl.ds(gstart + c0, cn)]
            part = pl.ds(place[ch] + c0, cn)
            if paired:
                rp = pl.ds(pl.multiple_of(y * br + r0, 16), rn)
                t = RZP[2, rp, part].astype(f32) + RZP[3, rp, part].astype(f32)
                return g.astype(f32) + t + RYP[r, part].astype(f32)
            t = g.astype(f32) + RY[z, r, part].astype(f32)
            if tree:
                return t + (RZ[2, r, part].astype(f32) + RZ[3, r, part].astype(f32))
            return lax.fori_loop(0, nz - 1, lambda k, t: t + RZ[k, r, part].astype(f32), t)

        if start >= down0 or start == 2 * QW:
            for c0 in range(0, width, 128):
                t = jnp.transpose(total(0, br, c0, 128))
                if start >= down0:
                    GFD[pl.ds(start - down0 + c0, 128), :] = t
                else:
                    GFO[pl.ds(c0, 128), :] = t
        else:
            at = start - 2 * KW if start >= PW else start

            def add(i):
                r0 = pl.multiple_of(i * 16, 16)
                GF[pl.ds(r0, 16), pl.ds(at, width)] = total(r0, 16, 0, width)

            loop(br // 16, add)
        for copy in outs(ch):
            copy.start()

    def rs_done(ch):
        if ch in rs_pairs:
            rs_y(ch, z, 1 - y).wait_send()
        else:
            loop(nz, lambda zz: rs_y(ch, zz, 1 - y).wait_send())
        if tree:
            for i in range(3):
                rs_z(ch, i, zto(i), 0, partner).wait_send()
        else:
            loop(nz, lambda k: rs_z(ch, k, z, 0, z).wait_send(), 1)
        for copy in outs(ch):
            copy.wait()

    for copy in local:
        copy.start()
    bar = pltpu.get_barrier_semaphore()
    for dev in (ypeer, cpeer, xpeer, dpeer):
        pl.semaphore_signal(bar, inc=1, device_id=dev, device_id_type=MESH)

    def greet(k):
        pl.semaphore_signal(bar, inc=1, device_id=zdev((z + k) % nz), device_id_type=MESH)

    loop(nz, greet, 1)
    for i in range(4):
        local[i].wait()
    W[own, pl.ds(2 * QW, QW)] = jnp.transpose(WO[...])
    pl.semaphore_wait(bar, 4 + nz - 1)

    def load_gate_up():
        for i in range(6, 12):
            local[i].wait()

    def load_down():
        local[12].wait()
        W[own, pl.ds(down0, F)] = jnp.transpose(WD[...])

    def start_tokens():
        local[4].wait()
        tok_start()

    def start_cotangent():
        local[5].wait()
        cot_start()

    lane = lax.broadcasted_iota(jnp.int32, (1, 128), 1)
    gain_q = jnp.concatenate([gq_ref[...], gq_ref[...]], axis=1)
    gain_k = jnp.concatenate([gk_ref[...], gk_ref[...]], axis=1)
    windows = []
    for i in range(nb):
        start = max(0, RB * i - longest)
        windows.append((start, RB * (i + 1) - start, sum(w for _, w, _ in windows)))

    def tables():
        VEC[...] = jnp.zeros(VEC.shape, f32)
        seg = seg_ref[...]
        first = jnp.zeros((1, T), jnp.int32)
        for d in range(ids):
            count = jnp.sum((seg == d).astype(f32), axis=1, keepdims=True).astype(jnp.int32)
            first = first + jnp.where(seg > d, count, 0)
        place = lax.broadcasted_iota(jnp.int32, (1, T), 1)
        inverse_freq = jnp.exp((lane % 32).astype(f32) * (-2.0 / 64 * math.log(rope_base)))
        CS[...] = jnp.transpose(jnp.broadcast_to((place - first).astype(f32), (128, T)))

        def fill(i):
            angle = CS[rows(i, 128), :] * inverse_freq
            sine = jnp.sin(angle)
            CS[rows(i, 128), :] = jnp.cos(angle)
            SN[rows(i, 128), :] = jnp.where(lane % 64 < 32, -sine, sine)

        loop(T // 128, fill)
        for i, (start, width, at) in enumerate(windows):
            key_place = lax.broadcasted_iota(jnp.int32, (width, RB), 0) + start
            q_place, q_first = place[:, RB * i : RB * (i + 1)], first[:, RB * i : RB * (i + 1)]
            seen = (key_place <= q_place) & (key_place >= q_first)
            BIAS[pl.ds(at, width), :] = jnp.where(seen, 0.0, -1e30).astype(bf16)

    def head_mean(v):
        half_a = lax.broadcasted_iota(jnp.int32, (128, 128), 0) // 64
        half_b = lax.broadcasted_iota(jnp.int32, (128, 128), 1) // 64
        mean_matrix = jnp.where(half_a == half_b, 1.0 / 64, 0.0).astype(bf16)
        high = v.astype(bf16)
        low = (v - high.astype(f32)).astype(bf16)
        return dot_nn(high, mean_matrix) + dot_nn(low, mean_matrix)

    def turn(v):
        return jnp.where(lane % 64 < 32, pltpu.roll(v, 96, 1), pltpu.roll(v, 32, 1))

    def norm_tokens():
        tok_wait()

        def step(i):
            t = Tk[rows(i, 128), :].astype(f32)
            r = lax.rsqrt(jnp.mean(t * t, axis=1, keepdims=True) + epsilon)
            R1[rows(i, 128), :] = jnp.broadcast_to(r, (128, 128))
            Nm[rows(i, 128), :] = (t * r * ga_ref[...]).astype(bf16)

        loop(T // 128, step)

    def project():
        ag_wait(0)

        def step(i):
            r = rows(i, RB)
            PRE[r, :] = dot_nn(Nm[r, :], W[:, pl.ds(0, 2 * QW)])
            cos, sin = CS[r, :], SN[r, :]
            for p in range(3):
                v = PRE[r, pl.ds(128 * p, 128)]
                n = v * lax.rsqrt(head_mean(v * v) + epsilon)
                u = n * (gain_q if p < 2 else gain_k)
                u = (u * cos + turn(u) * sin).astype(bf16)
                if p < 2:
                    u = u * jnp.asarray(0.125, bf16)
                    QS[p, 0, r, :] = u[:, :64]
                    QS[p, 1, r, :] = u[:, 64:]
                else:
                    KS[0, r, :] = u[:, :64]
                    KS[1, r, :] = u[:, 64:]
                    ut = jnp.transpose(u)
                    KT[0, :, r] = ut[:64, :]
                    KT[1, :, r] = ut[64:, :]
            v = PRE[r, pl.ds(384, 128)].astype(bf16)
            VS[0, r, :] = v[:, :64]
            VS[1, r, :] = v[:, 64:]
            vt = jnp.transpose(v)
            VT[0, :, r] = vt[:64, :]
            VT[1, :, r] = vt[64:, :]

        loop(nb, step)

    def attend(i):
        start, width, at = windows[i]
        keys = pl.ds(start, width)
        r = pl.ds(RB * i, RB)

        def step(h):
            q = QS[h, :, r, :].reshape(2 * RB, 64)
            bias = BIAS[pl.ds(at, width), :].astype(f32)
            s = dot_nt(KS[h, keys, :], q) + jnp.concatenate([bias, bias], axis=1)
            e = jnp.exp(s)
            inv = 1.0 / jnp.sum(e, axis=0, keepdims=True)
            INV[h, pl.ds(i, 1), :] = inv
            o = dot_nn(VT[h, :, keys], (e * inv).astype(bf16))
            o = jnp.concatenate([o[:, :RB], o[:, RB:]], axis=0)
            MX[r, pl.ds(pl.multiple_of(h * 128, 128), 128)] = jnp.transpose(o).astype(bf16)

        loop(2, step)

    def attention_out():
        ag_wait(1)
        a_produce(lambda d: dot_nt(MX[rows(d, RB), :], W[:, pl.ds(2 * QW, QW)]))

    def after_attention(h):
        def use(r, at, summed):
            v = Tk[at, :].astype(f32) + summed
            RES[r, :] = v
            n = v * lax.rsqrt(jnp.mean(v * v, axis=1, keepdims=True) + epsilon)
            NF[at, :] = (n * gf_ref[...]).astype(bf16)

        a_total(h, use)
        nf_start(h)

    def ffn(j):
        if j == 0:
            nf_wait()
            nf_done()
            a_done()
        ag_wait(2 + j)

        def step(i):
            r = rows(i, RB)
            n = NF[r, :]
            gate = dot_nn(n, W[:, pl.ds(PW + 2 * FC * j, FC)])
            up = dot_nn(n, W[:, pl.ds(PW + 2 * FC * j + FC, FC)])
            sig = 1.0 / (1.0 + jnp.exp(-gate))
            act = gate * sig
            HID[r, pl.ds(FC * j, FC)] = (act * up).astype(bf16)
            GG[r, pl.ds(2 * FC * j, FC)] = (up * (sig + act * (1.0 - sig))).astype(bf16)
            GG[r, pl.ds(2 * FC * j + FC, FC)] = act.astype(bf16)

        loop(nb, step)

    def grad_weights(what):
        if what < 3:
            if what == 0:
                cot_wait()
                cot_done()
            weight_grad(Ct, [(what, HID.at[:, pl.ds(FC * what, FC)])])
        elif what == 3:
            weight_grad(NF, [(3 + j, GG.at[:, pl.ds(2 * FC * j, 2 * FC)]) for j in range(3)])
        elif what == 6:
            weight_grad(Ct, [(6, MX)])
        else:
            weight_grad(Nm, [(7, GQ)])

    def grad_hidden(j):
        ag_wait(5 + j)

        def step(i):
            r = rows(i, RB)
            gh = dot_nn(Ct[r, :], W[:, pl.ds(down0 + FC * j, FC)])
            a, b = pl.ds(2 * FC * j, FC), pl.ds(2 * FC * j + FC, FC)
            GG[r, a] = (gh * GG[r, a].astype(f32)).astype(bf16)
            GG[r, b] = (gh * GG[r, b].astype(f32)).astype(bf16)

        loop(nb, step)

    def grad_ffn_norm():
        n_produce(lambda d: dot_nt(GG[rows(d, RB), :], W[:, pl.ds(PW, 2 * F)]))

    def after_ffn(h):
        def use(r, at, gy):
            v = RES[r, :]
            inv = lax.rsqrt(jnp.mean(v * v, axis=1, keepdims=True) + epsilon)
            n = v * inv
            VEC[1:2, :] += jnp.sum(gy * n, axis=0, keepdims=True)
            g = gy * gf_ref[...]
            g = inv * (g - n * jnp.mean(g * n, axis=1, keepdims=True))
            Ct[at, :] = (Ct[at, :].astype(f32) + g).astype(bf16)

        n_total(h, use)
        rl_start(h)

    def grad_mixed():
        rl_wait()
        DKV[...] = jnp.zeros(DKV.shape, f32)

        def step(i):
            r = rows(i, RB)
            g = dot_nn(Ct[r, :], W[:, pl.ds(2 * QW, QW)]).astype(bf16)
            for p in range(2):
                DO[p, 0, r, :] = g[:, 128 * p : 128 * p + 64]
                DO[p, 1, r, :] = g[:, 128 * p + 64 : 128 * p + 128]

        loop(nb, step)

    def attend_back(i):
        start, width, at = windows[i]
        keys = pl.ds(start, width)
        r = pl.ds(RB * i, RB)

        def step(h):
            q = QS[h, :, r, :].reshape(2 * RB, 64)
            do = DO[h, :, r, :].reshape(2 * RB, 64)
            bias = BIAS[pl.ds(at, width), :].astype(f32)
            s = dot_nt(KS[h, keys, :], q) + jnp.concatenate([bias, bias], axis=1)
            p = jnp.exp(s) * INV[h, pl.ds(i, 1), :]
            dp = dot_nt(VS[h, keys, :], do)
            ds = (p * (dp - jnp.sum(p * dp, axis=0, keepdims=True))).astype(bf16)
            DKV[h, keys, :] += jnp.concatenate([dot_nn(ds, q), dot_nn(p.astype(bf16), do)], axis=1)
            g = dot_nn(KT[h, :, keys], ds) * 0.125
            g = jnp.concatenate([g[:, :RB], g[:, RB:]], axis=0)
            DQ[r, pl.ds(pl.multiple_of(h * 128, 128), 128)] = jnp.transpose(g)

        loop(2, step)

    def project_back():
        def step(i):
            r = rows(i, RB)
            cos, sin = CS[r, :], SN[r, :]
            for p in range(3):
                if p < 2:
                    g = DQ[r, pl.ds(128 * p, 128)]
                else:
                    g = jnp.concatenate([DKV[0, r, pl.ds(0, 64)], DKV[1, r, pl.ds(0, 64)]], axis=1)
                g = g * cos - turn(g) * sin
                v = PRE[r, pl.ds(128 * p, 128)]
                inv = lax.rsqrt(head_mean(v * v) + epsilon)
                n = v * inv
                s = pl.ds(0 if p < 2 else 128, 128)
                VEC[2:3, s] += jnp.sum(g * n, axis=0, keepdims=True)
                g = g * (gain_q if p < 2 else gain_k)
                GQ[r, pl.ds(128 * p, 128)] = (inv * (g - n * head_mean(g * n))).astype(bf16)
            v = jnp.concatenate([DKV[0, r, pl.ds(64, 64)], DKV[1, r, pl.ds(64, 64)]], axis=1)
            GQ[r, pl.ds(384, 128)] = v.astype(bf16)

        loop(nb, step)

    def gn_core(i, k, xx, cc):
        return rc(
            PN.at[rows(i, RB), pl.ds(pl.multiple_of((xx * 2 + cc) * CW, CW), CW)],
            AC.at[rows(i, RB), pl.ds(pl.multiple_of(xx * CW, CW), CW)],
            gn_s.at[i, k], gn_r.at[i, k], cpeer,
        )

    def gn_x(i):
        return rc(SC.at[rows(i, RB), :], BC.at[rows(i, RB), :], gn_s.at[i, 2], gn_r.at[i, 2], xpeer)

    vec_c = rc(VEC, VC, vec_s.at[0], vec_r.at[0], cpeer)
    vec_x = rc(VEC, VX, vec_s.at[1], vec_r.at[1], xpeer)
    vec_y = rc(VEC, VY, vec_s.at[2], vec_r.at[2], ypeer)

    def vz_copy(k, src):
        return rc(VZ.at[src], VZ.at[src], vz_s.at[k], vz_r.at[k], zdev((z + k) % nz))

    def gn_produce():
        def step(i):
            r = rows(i, RB)
            g = dot_nt(GQ[r, :], W[:, pl.ds(0, 2 * QW)])
            PN[r, :] = g.astype(bf16)
            gn_core(i, 0, 1 - x, 1 - c).start()
            gn_core(i, 1, x, 1 - c).start()
            g = g * (Tk[r, :].astype(f32) * R1[r, pl.ds(0, 1)])
            VEC[0:1, :] += jnp.sum(g, axis=0, keepdims=True)
            s = jnp.sum(g * ga_ref[...], axis=1, keepdims=True)
            VEC[3:4, r] = jnp.transpose(jnp.broadcast_to(s, (RB, 128)))[0:1, :]

        loop(nb, step)
        vec_c.start()

    def gn_middle():
        def step(i):
            r = rows(i, RB)
            gn_core(i, 0, 1 - x, c).wait_recv()
            a = PN[r, pl.ds(pl.multiple_of(((1 - x) * 2 + c) * CW, CW), CW)].astype(f32)
            b = AC[r, pl.ds(pl.multiple_of((1 - x) * CW, CW), CW)].astype(f32)
            SC[r, :] = (a + b).astype(bf16)
            gn_x(i).start()

        loop(nb, step)

    def vec_step(copy, landing, following):
        copy.wait_recv()
        copy.wait_send()
        VEC[...] += landing[...]
        following.start()

    def vec_last():
        vec_y.wait_recv()
        vec_y.wait_send()
        VZ[z] = VEC[...] + VY[...]
        loop(nz, lambda k: vz_copy(k, z).start(), 1)

    gt_copy = pltpu.make_async_copy(DQ, gt_h, out_sem.at[24])
    lo_out = pltpu.make_async_copy(LOC, lo_h, out_sem.at[25])

    def gn_finish():
        def step(i):
            r = rows(i, RB)
            gn_core(i, 1, x, c).wait_recv()
            gn_x(i).wait_recv()
            g = PN[r, mine].astype(f32) + AC[r, pl.ds(pl.multiple_of(x * CW, CW), CW)].astype(f32)
            g = (g + BC[r, :].astype(f32)) * ga_ref[:, mine]
            inv = R1[r, pl.ds(0, 1)]
            s = jnp.transpose(jnp.broadcast_to(VEC[3:4, r], (128, RB)))[:, 0:1] * (1.0 / D)
            n = Tk[r, mine].astype(f32) * inv
            DQ[r, :] = Ct[r, mine].astype(f32) + inv * (g - n * s)

        loop(nb, step)
        gt_copy.start()

    others = [(0, x * 2 + 1 - c, cpeer), (1, (1 - x) * 2 + c, xpeer), (2, (1 - x) * 2 + 1 - c, dpeer)]

    def lo_copy(i, d, dev):
        return rc(
            S0.at[:, pl.ds(pl.multiple_of(d * CW, CW), CW)], LOC.at[rows(col, RB), :], lo_s.at[i], lo_r.at[i], dev
        )

    def branch():
        n_done()
        b_produce(lambda d: dot_nt(HID[rows(d, RB), :], W[:, pl.ds(down0, F)]))

    def block_out():
        def use(r, at, summed):
            S0[r, :] = (RES[r, :] + summed).astype(bf16)

        b_total(0, use)
        b_total(1, use)
        for i, d, dev in others:
            lo_copy(i, d, dev).start()
        LOC[rows(col, RB), :] = S0[:, mine]

    def block_out_wait():
        for i, d, dev in others:
            lo_copy(i, d, dev).wait_recv()
        lo_out.start()

    def finish():
        loop(nz, lambda k: vz_copy(k, (z + nz - k) % nz).wait_recv(), 1)
        gain_ref[...] = lax.fori_loop(1, nz, lambda k, t: t + VZ[k], VZ[0])
        tok_done()
        rl_done()
        b_done()
        for i, d, dev in others:
            lo_copy(i, d, dev).wait_send()

        def gn_done(i):
            gn_core(i, 0, 1 - x, 1 - c).wait_send()
            gn_core(i, 1, x, 1 - c).wait_send()
            gn_x(i).wait_send()

        loop(nb, gn_done)
        loop(nz, lambda k: vz_copy(k, z).wait_send(), 1)
        for ch in range(len(CH)):
            ag_done(ch)
        for ch in range(len(RCH)):
            rs_done(ch)
        gt_copy.wait()
        lo_out.wait()

    steps = {
        "gate_up": load_gate_up, "down": load_down, "toks": start_tokens, "cots": start_cotangent,
        "owny": own_y, "ownz": own_z, "fwd": forward, "tokf": tok_forward, "cotf": cot_forward,
        "tables": tables, "norm": norm_tokens, "project": project, "att": attend, "aprod": attention_out,
        "amid": a_middle, "aft": after_attention, "nff": nf_forward, "ffn": ffn, "wg": grad_weights,
        "gh": grad_hidden, "gnfp": grad_ffn_norm, "gnfm": n_middle, "naft": after_ffn, "rlf": rl_forward,
        "gmix": grad_mixed, "ab": attend_back, "pb": project_back, "gnp": gn_produce, "gnm": gn_middle,
        "vc": lambda: vec_step(vec_c, VC, vec_x), "vx": lambda: vec_step(vec_x, VX, vec_y), "vy": vec_last,
        "gnfin": gn_finish, "brp": branch, "brm": b_middle, "brf": block_out, "lof": block_out_wait,
        "mid": rs_mid, "relay": rs_relay, "pre": rs_pre, "fin": rs_fin, "end": finish,
    }
    for name, *which, who in ORDER:
        if name in ("fwd", "mid"):
            run = functools.partial(steps[name], *which, who == "m")
        else:
            run = functools.partial(steps[name], *which)
        if who == "a" or not tree:
            if who != "e" or name in ("fwd", "mid"):
                run()
        else:

            @pl.when(is_middle if who == "m" else jnp.logical_not(is_middle))
            def _():
                run()


def hand_out(*refs):
    sources, gains, targets, held, sem = refs[:9], refs[9], refs[10:19], refs[23:32], refs[32]
    loads = [pltpu.make_async_copy(a, b, sem.at[0, i]) for i, (a, b) in enumerate(zip(sources, held))]
    stores = [pltpu.make_async_copy(a, b, sem.at[1, i]) for i, (a, b) in enumerate(zip(held, targets))]
    for copy in loads:
        copy.start()
    attn, ffn, query, key = refs[19:23]
    attn[...] = gains[0:1, :]
    ffn[...] = gains[1:2, :]
    query[...] = gains[2:3, 0:64] + gains[2:3, 64:128]
    key[...] = gains[2:3, 128:192] + gains[2:3, 192:256]
    for load, store in zip(loads, stores):
        load.wait()
        store.start()
    for store in stores:
        store.wait()


def per_device(
    n_row, tokens, segment_ids, w_query, key_matrix, value_matrix, w_out, w_gate, w_up, w_down,
    norm_attn, norm_ffn, norm_query, norm_key, cotangent,
):
    T, CW = tokens.shape
    br, QW = w_query.shape
    KW = key_matrix.shape[1]
    F = w_gate.shape[1]
    D = br * n_row
    nz = n_row // 2
    PW = 2 * QW + 2 * KW
    WW = PW + 3 * F
    FC = F // 3
    nb = T // RB
    area = sum(RB * (i + 1) - max(0, RB * i - longest) for i in range(nb))
    chunks = [(0, 2 * QW), (2 * QW, QW)]
    chunks += [(PW + 2 * FC * j, 2 * FC) for j in range(3)] + [(PW + 2 * F + FC * j, FC) for j in range(3)]
    grads = chunks[5:8] + chunks[2:5] + [chunks[1], chunks[0]]
    tree = nz == 4
    ag_pairs, rs_pairs = (AG_PAIRS, RS_PAIRS) if tree else ((), ())
    place, widths = [], [0, 0]
    for ch, (_, width) in enumerate(grads):
        paired = ch in rs_pairs
        place.append(widths[paired])
        widths[paired] += width
    plan = (nz, tree, chunks, grads, ag_pairs, rs_pairs, place)
    single, paired = widths[0], max(widths[1], 128)
    slots = 4 if tree else nz - 1
    vm, sem = pltpu.VMEM, pltpu.SemaphoreType.DMA
    scratch = [
        vm((D, WW), bf16), vm((QW, br), bf16), vm((F, br), bf16), vm((QW, br), f32), vm((F, br), f32),
        vm((D, 3 * F), bf16), vm((nz, br, single), bf16), vm((slots, br, single), bf16),
        vm((br, paired), bf16), vm((4, 2 * br, paired), bf16),
        vm((br, 2 * QW + 2 * F), f32), vm((T, D), bf16), vm((T, D), bf16), vm((T, D), bf16), vm((T, 128), f32),
        vm((T, 2 * QW), f32), vm((2, 2, T, 64), bf16), vm((2, T, 64), bf16), vm((2, T, 64), bf16),
        vm((2, 64, T), bf16), vm((2, 64, T), bf16), vm((2, 2, T, 64), bf16), vm((T, QW), bf16),
        vm((T, D), bf16), vm((2, RB, D), bf16), vm((RB, D), bf16), vm((RB, D), bf16), vm((RB, D), f32),
        vm((T, D), bf16), vm((T, 2 * F), bf16), vm((T, F), bf16),
        vm((T, 128), f32), vm((T, 128), f32), vm((area, RB), bf16), vm((2, 8, 2 * RB), f32),
        vm((T, QW), f32), vm((2, T, 128), f32),
        vm((T, 2 * CW), bf16), vm((T, CW), bf16), vm((T, CW), bf16), vm((T, CW), bf16),
        vm((8, D), f32), vm((8, D), f32), vm((8, D), f32), vm((8, D), f32), vm((nz, 8, D), f32),
        sem((13,)), sem((8, nz)), sem((8, nz)), sem((8, nz)), sem((8, nz)),
        sem((8, nz)), sem((8, nz)), sem((8, nz)), sem((8, nz)),
        sem((4, 2, 3)), sem((4, 2, 3)), sem((3, 4)), sem((3, 4)), sem((nb, 3)), sem((nb, 3)), sem((3,)), sem((3,)),
        sem((3,)), sem((3,)), sem((nz,)), sem((nz,)), sem((26,)),
    ]
    whole, hbm = pl.BlockSpec(memory_space=pltpu.VMEM), pl.BlockSpec(memory_space=pl.ANY)
    shape = jax.ShapeDtypeStruct
    results = (
        shape((T, CW), bf16), shape((T, CW), f32), shape((br, QW), f32), shape((br, KW), f32), shape((br, KW), f32),
        shape((QW, br), f32), shape((br, F), f32), shape((br, F), f32), shape((F, br), f32),
    )
    outs = pl.pallas_call(
        functools.partial(layer_kernel, plan),
        out_shape=results + (shape((8, D), f32),),
        in_specs=[hbm, whole] + [hbm] * 7 + [whole] * 4 + [hbm],
        out_specs=(hbm,) * 9 + (whole,),
        scratch_shapes=scratch,
        compiler_params=pltpu.CompilerParams(
            collective_id=0, has_side_effects=True, vmem_limit_bytes=64 * 2**20
        ),
        name="layer",
    )(
        tokens, segment_ids, w_query, key_matrix, value_matrix, w_out, w_gate, w_up, w_down,
        norm_attn[None], norm_ffn[None], norm_query[None], norm_key[None], cotangent,
    )
    gain = shape((1, D), f32)
    head_gain = shape((1, norm_query.shape[0]), f32)
    outs = pl.pallas_call(
        hand_out,
        out_shape=results + (gain, gain, head_gain, head_gain),
        in_specs=[pl.BlockSpec(memory_space=pltpu.HBM)] * 9 + [whole],
        out_specs=(pl.BlockSpec(memory_space=pltpu.HBM),) * 9 + (whole,) * 4,
        scratch_shapes=[vm(v.shape, v.dtype) for v in results] + [sem((2, 9))],
        compiler_params=pltpu.CompilerParams(vmem_limit_bytes=63 * 2**20),
        name="hand_out",
    )(*outs)
    return outs[:9] + tuple(v[0] for v in outs[9:])


def solution(mesh):
    in_specs = (
        P("row", "col"), P("row", None), P("row", "col"), P("row", "col"), P("row", "col"), P("col", "row"),
        P("row", "col"), P("row", "col"), P("col", "row"), P(), P(), P(), P(), P("row", "col"),
    )
    out_specs = (
        P("row", "col"), P("row", "col"), P("row", "col"), P("row", "col"), P("row", "col"), P("col", "row"),
        P("row", "col"), P("row", "col"), P("col", "row"), P(), P(), P(), P(),
    )
    return jax.shard_map(
        functools.partial(per_device, mesh.shape["row"]),
        mesh=mesh, in_specs=in_specs, out_specs=out_specs, check_vma=False,
    )
```

```python
import functools
import math

import jax
import jax.numpy as jnp
from jax import lax
from jax.experimental import pallas as pl
from jax.experimental.pallas import tpu as pltpu
from jax.sharding import PartitionSpec as P

epsilon = 1e-05
rope_base = 1000000.0
longest = 512
ids = 8
f32, bf16 = jnp.float32, jnp.bfloat16
MESH = pl.DeviceIdType.MESH
RB = 256


def dot_nn(a, b):
    return lax.dot_general(a, b, (((1,), (0,)), ((), ())), preferred_element_type=f32)


def dot_nt(a, b):
    return lax.dot_general(a, b, (((1,), (1,)), ((), ())), preferred_element_type=f32)


def rows(i, n):
    return pl.ds(pl.multiple_of(i * n, n), n)


AG_PAIRS, RS_PAIRS = (5, 6), (0, 1, 2)
ORDER = [
    ("owny", 0, "a"), ("ownz", 0, "a"), ("owny", 1, "a"), ("ownz", 1, "a"), ("gate_up", "a"), ("owny", 2, "a"),
    ("down", "a"), ("owny", 7, "a"), ("fwd", 0, 1, "e"), ("ownz", 2, "a"), ("toks", "a"), ("tables", "a"),
    ("cots", "a"), ("owny", 3, "a"), ("ownz", 7, "a"), ("fwd", 0, 1, "m"), ("fwd", 0, 2, "e"), ("fwd", 0, 2, "m"),
    ("fwd", 0, 3, "e"), ("fwd", 1, 1, "e"), ("fwd", 0, 3, "m"), ("tokf", "a"), ("fwd", 1, 1, "m"),
    ("fwd", 1, 2, "e"), ("fwd", 1, 2, "m"), ("owny", 5, "a"), ("fwd", 1, 3, "m"), ("ownz", 3, "a"), ("norm", "a"),
    ("fwd", 1, 3, "e"), ("fwd", 2, 1, "m"), ("fwd", 2, 2, "m"), ("owny", 4, "a"), ("owny", 6, "a"),
    ("ownz", 4, "a"), ("project", "a"), ("fwd", 2, 3, "m"), ("fwd", 3, 1, "m"), ("att", 0, "a"), ("aprod", 0, "a"),
    ("fwd", 4, 1, "e"), ("fwd", 2, 1, "e"), ("fwd", 3, 2, "m"), ("ownz", 5, "a"), ("amid", "a"), ("fwd", 5, 1, "m"),
    ("fwd", 3, 3, "m"), ("att", 1, "a"), ("fwd", 4, 1, "m"), ("cotf", "a"), ("fwd", 4, 2, "m"), ("fwd", 2, 2, "e"),
    ("aprod", 1, "a"), ("fwd", 4, 3, "m"), ("fwd", 3, 1, "e"), ("fwd", 5, 2, "m"), ("fwd", 7, 1, "m"),
    ("ownz", 6, "a"), ("aft", 0, "a"), ("fwd", 7, 1, "e"), ("fwd", 5, 3, "m"), ("fwd", 2, 3, "e"),
    ("fwd", 7, 2, "m"), ("fwd", 7, 3, "m"), ("fwd", 5, 1, "e"), ("aft", 1, "a"), ("fwd", 3, 2, "e"),
    ("fwd", 5, 2, "e"), ("fwd", 3, 3, "e"), ("fwd", 6, 1, "e"), ("nff", 0, "a"), ("fwd", 4, 2, "e"),
    ("nff", 1, "a"), ("fwd", 4, 3, "e"), ("ffn", 0, 0, "a"), ("fwd", 6, 2, "e"), ("fwd", 6, 1, "m"),
    ("fwd", 6, 2, "m"), ("fwd", 6, 3, "m"), ("ffn", 0, 1, "a"), ("wg", 0, "a"), ("ffn", 1, 0, "a"),
    ("ffn", 1, 1, "a"), ("fwd", 5, 3, "e"), ("wg", 1, "a"), ("fwd", 7, 2, "e"), ("fwd", 6, 3, "e"),
    ("gh", 0, 0, "a"), ("relay", 0, 0, "m"), ("gh", 0, 1, "a"), ("fwd", 7, 3, "e"), ("wg", 3, "a"),
    ("ffn", 2, 0, "a"), ("ffn", 2, 1, "a"), ("wg", 2, "a"), ("gh", 1, 0, "a"), ("gh", 2, 0, "a"), ("gnfp", 0, "a"),
    ("mid", 3, 0, "e"), ("gh", 1, 1, "a"), ("gnfm", "a"), ("relay", 0, 1, "m"), ("gh", 2, 1, "a"),
    ("mid", 3, 0, "m"), ("relay", 1, 0, "m"), ("gnfp", 1, "a"), ("wg", 5, "a"), ("mid", 3, 1, "e"), ("snd", 8, "a"),
    ("naft", 0, "a"), ("wg", 4, "a"), ("mid", 5, 0, "m"), ("relay", 2, 0, "m"), ("relay", 1, 1, "m"),
    ("naft", 1, "a"), ("mid", 5, 1, "m"), ("gmix", 0, "a"), ("mid", 3, 1, "m"), ("mid", 5, 0, "e"), ("ab", 0, "a"),
    ("mid", 5, 2, "m"), ("mid", 3, 2, "e"), ("mid", 5, 1, "e"), ("rlf", 0, "a"), ("rlf", 1, "a"),
    ("mid", 8, 0, "e"), ("mid", 8, 1, "e"), ("relay", 3, 0, "m"), ("relay", 2, 1, "m"), ("relay", 3, 1, "m"),
    ("mid", 5, 2, "e"), ("mid", 8, 0, "m"), ("mid", 3, 2, "m"), ("mid", 8, 2, "e"), ("gmix", 1, "a"), ("brp", "a"),
    ("mid", 4, 0, "e"), ("wg", 6, "a"), ("relay", 5, 0, "m"), ("brm", "a"), ("mid", 8, 1, "m"), ("mid", 4, 0, "m"),
    ("ab", 1, "a"), ("mid", 4, 1, "e"), ("pb", "a"), ("relay", 5, 1, "m"), ("mid", 8, 2, "m"), ("mid", 4, 1, "m"),
    ("gnp", "a"), ("mid", 6, 0, "e"), ("mid", 4, 2, "m"), ("relay", 8, 0, "m"), ("relay", 4, 0, "m"),
    ("wg", 7, "a"), ("mid", 6, 1, "e"), ("gnm", "a"), ("mid", 6, 0, "m"), ("relay", 8, 1, "m"), ("mid", 6, 2, "e"),
    ("brf", "a"), ("relay", 4, 1, "m"), ("mid", 6, 1, "m"), ("mid", 9, 0, "m"), ("mid", 7, 0, "e"),
    ("mid", 7, 0, "m"), ("mid", 6, 2, "m"), ("mid", 9, 0, "e"), ("vc", "a"), ("mid", 7, 1, "e"), ("pre", 2, "e"),
    ("pre", 1, "e"), ("relay", 6, 0, "m"), ("mid", 7, 1, "m"), ("mid", 9, 1, "m"), ("relay", 6, 1, "m"),
    ("fin", 5, "a"), ("pre", 2, "m"), ("mid", 9, 1, "e"), ("relay", 7, 0, "m"), ("pre", 1, "m"), ("mid", 9, 2, "m"),
    ("pre", 0, "e"), ("mid", 7, 2, "m"), ("mid", 4, 2, "e"), ("pre", 0, "m"), ("relay", 9, 0, "m"),
    ("relay", 9, 1, "m"), ("mid", 9, 2, "e"), ("fin", 8, "a"), ("relay", 7, 1, "m"), ("fin", 6, "a"), ("vy", "a"),
    ("fin", 4, "a"), ("mid", 7, 2, "e"), ("fin", 3, "a"), ("fin", 2, "a"), ("fin", 1, "a"), ("fin", 9, "a"),
    ("gnfin", "a"), ("fin", 7, "a"), ("fin", 0, "a"), ("lof", "a"), ("end", "a"),
]


def layer_kernel(
    plan,
    tok_h, seg_ref, wq_h, wk_h, wv_h, wo_h, wg_h, wu_h, wd_h, ga_ref, gf_ref, gq_ref, gk_ref, cot_h,
    lo_h, gt_h, gquery_h, gkey_h, gvalue_h, gout_h, ggate_h, gup_h, gdown_h, gain_ref,
    W, WO, WD, GFO, GFD, G, RY, RZ, RYP, RZP, GF, Tk, Ct, Nm, R1, PRE, QS, KS, VS, KT, VT, DO, MX, PB, A0, B0, S0,
    RES, NF, GG, HID, CS, SN, BIAS, INV, DQ, DKV, AC, BC, SC, LOC, VEC, VCOL, VSUM, VY, VZ,
    loc_sem, agz_s, agz_r, agy_s, agy_r, rsy_s, rsy_r, rsz_s, rsz_r,
    cag_s, cag_r, crs_s, crs_r, gn_s, gn_r, lo_s, lo_r, vec_s, vec_r, vz_s, vz_r, out_sem,
):
    nz, tree, CH, RCH, ag_pairs, rs_pairs, place = plan
    T, D = Tk.shape
    br = RY.shape[1]
    QW, KW = PRE.shape[1] // 2, PRE.shape[1] // 4
    PW = 2 * QW + 2 * KW
    F = HID.shape[1]
    FC = F // 3
    HB = RB // 2
    down0 = PW + 2 * F
    nb = T // RB
    CW = D // 4
    GQ = GG.at[:, pl.ds(PW, 2 * QW)]
    PN = GG.at[:, pl.ds(PW + 2 * QW, D)]
    row, col = lax.axis_index("row"), lax.axis_index("col")
    z, y = row // 2, row % 2
    x, c = col // 2, col % 2
    ypeer = (row + 1 - 2 * y, col)
    cpeer = (row, col + 1 - 2 * c)
    xpeer = (row, (1 - x) * 2 + c)
    dpeer = (row, (1 - x) * 2 + 1 - c)
    partner = z + 1 - 2 * (z % 2)
    is_middle = (z == 1) | (z == 2)
    near, far = 2 - z // 2, 3 - 3 * (z // 2)

    def zdev(zz):
        return (zz * 2 + y, col)

    def zsrc(k):
        return [z, partner, near, far][k] if tree else (z + nz - k) % nz

    def zto(i):
        return [near, far, partner, z][i]

    def rc(src, dst, ss, rs, dev):
        return pltpu.make_async_remote_copy(
            src_ref=src, dst_ref=dst, send_sem=ss, recv_sem=rs, device_id=dev, device_id_type=MESH
        )

    def loop(n, body, first=0):
        def step(i, carry):
            body(i)
            return carry

        lax.fori_loop(first, n, step, 0)

    own = rows(row, br)
    mine = pl.ds(pl.multiple_of(col * CW, CW), CW)
    local = [
        (wq_h, W.at[own, pl.ds(0, QW)]),
        (wk_h, W.at[own, pl.ds(QW, KW)]),
        (wv_h, W.at[own, pl.ds(QW + KW, KW)]),
        (wo_h, WO),
        (tok_h, Tk.at[:, mine]),
        (cot_h, Ct.at[:, mine]),
    ]
    for j in range(3):
        local.append((wg_h.at[:, pl.ds(FC * j, FC)], W.at[own, pl.ds(PW + 2 * FC * j, FC)]))
        local.append((wu_h.at[:, pl.ds(FC * j, FC)], W.at[own, pl.ds(PW + 2 * FC * j + FC, FC)]))
    local.append((wd_h, WD))
    local = [pltpu.make_async_copy(s, d, loc_sem.at[i]) for i, (s, d) in enumerate(local)]

    def wblk(ch, zz, yy):
        start, width = CH[ch]
        return W.at[rows(zz * 2 + yy, br), pl.ds(start, width)]

    def wpair(ch, zz):
        start, width = CH[ch]
        return W.at[rows(zz, 2 * br), pl.ds(start, width)]

    def ag_z(ch, k, src, slot, dev):
        b = wpair(ch, src) if ch in ag_pairs else wblk(ch, src, y)
        return rc(b, b, agz_s.at[ch, k], agz_r.at[ch, slot], zdev(dev))

    def ag_y(ch, k, src, yy):
        b = wblk(ch, src, yy)
        return rc(b, b, agy_s.at[ch, k], agy_r.at[ch, k], ypeer)

    def own_y(ch):
        ag_y(ch, 0, z, y).start()

    def own_z(ch):
        if ch in ag_pairs:
            ag_y(ch, 0, z, 1 - y).wait_recv()
        if tree:
            ag_z(ch, 0, z, 1, partner).start()
            ag_z(ch, 1, z, jnp.where(is_middle, 2, 3), near).start()
        else:
            loop(nz, lambda k: ag_z(ch, k, z, k, (z + k) % nz).start(), 1)

    def forward(ch, k, middle):
        if not tree:
            if k == 3 and middle:

                def step(k):
                    ag_z(ch, k, zsrc(k), k, z).wait_recv()
                    ag_y(ch, k, zsrc(k), y).start()

                loop(nz, step, 1)
            return
        relayed = middle and k >= 2
        if ch in ag_pairs and not relayed:
            return
        ag_z(ch, k, zsrc(k), k, partner).wait_recv()
        if relayed:
            ag_z(ch, k, zsrc(k), k, partner).start()
        if ch not in ag_pairs:
            ag_y(ch, k, zsrc(k), y).start()

    def ag_wait(ch):
        if not tree:
            loop(nz, lambda k: ag_y(ch, k, zsrc(k), 1 - y).wait_recv())
        elif ch in ag_pairs:
            ag_z(ch, 0, partner, 1, partner).wait_recv()

            @pl.when(jnp.logical_not(is_middle))
            def _():
                ag_z(ch, 0, near, 2, partner).wait_recv()
                ag_z(ch, 0, far, 3, partner).wait_recv()

        else:
            for k in range(4):
                ag_y(ch, k, zsrc(k), 1 - y).wait_recv()

    def ag_done(ch):
        if not tree:
            loop(nz, lambda k: ag_y(ch, k, zsrc(k), y).wait_send())
            loop(nz, lambda k: ag_z(ch, k, z, k, z).wait_send(), 1)
            return
        for k in range(1 if ch in ag_pairs else 4):
            ag_y(ch, k, zsrc(k), y).wait_send()
        ag_z(ch, 0, z, 1, partner).wait_send()
        ag_z(ch, 1, z, 2, near).wait_send()

        @pl.when(is_middle)
        def _():
            ag_z(ch, 2, near, 2, partner).wait_send()
            ag_z(ch, 3, far, 3, partner).wait_send()

    def cag(n, block, parts=1):
        def copy(i, d, dev, h):
            return rc(block(d, h), block(d, h), cag_s.at[n, h, i], cag_r.at[n, h, i], dev)

        def start(h=0):
            copy(0, col, cpeer, h).start()
            copy(1, col, xpeer, h).start()

        def forward(h=0):
            copy(1, (1 - x) * 2 + c, xpeer, h).wait_recv()
            copy(2, (1 - x) * 2 + c, cpeer, h).start()

        def wait(far):
            for h in range(parts):
                if far:
                    copy(2, (1 - x) * 2 + 1 - c, cpeer, h).wait_recv()
                else:
                    copy(0, x * 2 + 1 - c, cpeer, h).wait_recv()

        def done():
            for h in range(parts):
                copy(0, col, cpeer, h).wait_send()
                copy(1, col, xpeer, h).wait_send()
                copy(2, (1 - x) * 2 + c, cpeer, h).wait_send()

        return start, forward, wait, done

    def col_block(ref):
        return lambda d, h: ref.at[:, pl.ds(pl.multiple_of(d * CW, CW), CW)]

    def row_block(ref):
        return lambda d, h: ref.at[rows(d * 2 + h, HB), :]

    tok_start, tok_forward, tok_wait, tok_done = cag(0, col_block(Tk))
    cot_start, cot_forward, cot_wait, cot_done = cag(1, col_block(Ct))
    nf_start, nf_forward, nf_wait, nf_done = cag(2, row_block(NF), 2)
    rl_start, rl_forward, rl_wait, rl_done = cag(3, row_block(Ct), 2)

    def crs(n, A, B, S):
        def to_core(i, xx, cc):
            return rc(PB.at[rows(xx * 2 + cc, RB), :], A(xx), crs_s.at[n, i], crs_r.at[n, i], cpeer)

        def to_x(h):
            half = rows(h, HB)
            return rc(S.at[half, :], B.at[half, :], crs_s.at[n, 2 + h], crs_r.at[n, 2 + h], xpeer)

        def produce(half, part):
            def step(i):
                xx = jnp.where(i < 2, 1 - x, x)
                cc = jnp.where(i % 2 == 0, 1 - c, c)
                PB[rows(xx * 2 + cc, RB), :] = part(xx * 2 + cc).astype(bf16)

                @pl.when(i % 2 == 0)
                def _():
                    to_core(i // 2, xx, 1 - c).start()

            loop(2 * half + 2, step, 2 * half)

        def middle():
            to_core(0, 1 - x, c).wait_recv()

            def step(i):
                r = rows(i, 32)
                block = PB[pl.ds(pl.multiple_of(((1 - x) * 2 + c) * RB + i * 32, 32), 32), :]
                S[r, :] = (block.astype(f32) + A(1 - x)[r, :].astype(f32)).astype(bf16)

            for h in range(2):
                loop(HB // 32 * (h + 1), step, HB // 32 * h)
                to_x(h).start()

        def total(h, use):
            if h == 0:
                to_core(1, x, c).wait_recv()
            to_x(h).wait_recv()

            def step(i):
                r = rows(i, 32)
                at = pl.ds(pl.multiple_of(col * RB + i * 32, 32), 32)
                use(r, at, PB[at, :].astype(f32) + A(x)[r, :].astype(f32) + B[r, :].astype(f32))

            loop(HB // 32 * (h + 1), step, HB // 32 * h)

        def done():
            to_core(0, 1 - x, 1 - c).wait_send()
            to_core(1, x, 1 - c).wait_send()
            to_x(0).wait_send()
            to_x(1).wait_send()

        return produce, middle, total, done

    a_produce, a_middle, a_total, a_done = crs(0, lambda i: A0.at[i], B0, S0)
    n_produce, n_middle, n_total, n_done = crs(1, lambda i: A0.at[i], B0, S0)
    b_produce, b_middle, b_total, b_done = crs(
        2, lambda i: NF.at[rows(i, RB), :], NF.at[pl.ds(2 * RB, RB), :], NF.at[pl.ds(3 * RB, RB), :]
    )

    def other_first(half, i):
        return jnp.where(half == 0, 1 - x, x) * 2 + jnp.where(i == 0, 1 - c, c)

    def own_first(half, i):
        return jnp.where(half == 0, x, 1 - x) * 2 + jnp.where(i == 0, c, 1 - c)

    def rows_of_chip(mine_first, half, work):
        for xx in range(2):

            @pl.when(x == (xx if mine_first == (half == 0) else 1 - xx))
            def _():
                work(2 * xx)
                work(2 * xx + 1)

    def gcol(ch):
        start, width = RCH[ch]
        return (G, start - PW, width) if start >= PW else (GG, start, width)

    def gblk(ch, zz, yy):
        ref, start, width = gcol(ch)
        return ref.at[rows(zz * 2 + yy, br), pl.ds(start, width)]

    def part_of(ch):
        return pl.ds(place[ch], RCH[ch][1])

    def rs_y(ch, zz, yy):
        landing = RYP.at[:, part_of(ch)] if ch in rs_pairs else RY.at[zz, :, part_of(ch)]
        return rc(gblk(ch, zz, yy), landing, rsy_s.at[ch, zz], rsy_r.at[ch, zz], ypeer)

    def rs_z(ch, k, zz, slot, dev):
        if ch in rs_pairs:
            ref, start, width = gcol(ch)
            src, dst = ref.at[rows(zz, 2 * br), pl.ds(start, width)], RZP.at[slot, :, part_of(ch)]
        else:
            src, dst = RY.at[zz, :, part_of(ch)], RZ.at[slot, :, part_of(ch)]
        return rc(src, dst, rsz_s.at[ch, k], rsz_r.at[ch, slot], zdev(dev))

    zper = RB // (2 * br)

    def weight_grad(left, pieces):
        def one(i, d):
            lt = jnp.transpose(left[:, rows(d, RB)])
            for ch, right in pieces:
                ref, start, width = gcol(ch)
                ref[rows(d, RB), pl.ds(start, right.shape[1])] = dot_nn(lt, right[...]).astype(bf16)
                if ch not in rs_pairs:
                    loop(zper, lambda s: rs_y(ch, d * zper + s, 1 - y).start())
                elif i == 2:
                    rs_z(ch, 2, d, 2, partner).start()
                elif i < 2:

                    @pl.when(jnp.logical_not(is_middle))
                    def _():
                        rs_z(ch, i, d, i, partner).start()

        if any(ch in rs_pairs for ch, _ in pieces):
            for i in range(4):
                one(i, zto(i))
        elif tree:

            def step(i):
                one(i, jnp.where(i == 0, near, jnp.where(i == 1, far, jnp.where(i == 2, partner, z))))

            loop(4, step)
        else:
            loop(D // RB, lambda i: one(i, (row * br // RB + 1 + i) % (D // RB)))

    def send_grad(ch):
        if tree:
            for i in range(4):
                rs_y(ch, zto(i), 1 - y).start()
        else:
            loop(nz, lambda k: rs_y(ch, k, 1 - y).start())

    def rs_mid(ch, i, middle):
        ref, gstart, width = gcol(ch)

        def one(zz):
            rs_y(ch, zz, y).wait_recv()

            def add(j):
                r = rows(j, 16)
                g = ref[pl.ds(pl.multiple_of((zz * 2 + y) * br + j * 16, 16), 16), pl.ds(gstart, width)]
                t = RY[zz, r, part_of(ch)]
                RY[zz, r, part_of(ch)] = (g.astype(f32) + t.astype(f32)).astype(bf16)

            loop(br // 16, add)

        if not tree:
            if i == 2 and middle:

                def step(k):
                    zz = (z + k) % nz
                    one(zz)
                    rs_z(ch, k, zz, k - 1, zz).start()

                loop(nz, step, 1)
        elif ch not in rs_pairs:
            one(zto(i))
            if i == 2 or not middle:
                rs_z(ch, i, zto(i), i, partner).start()

    def rs_relay(ch, i):
        if not tree:
            return
        zz = zto(i)
        rs_z(ch, i, zz, i, partner).wait_recv()
        ref, gstart, width = gcol(ch)

        def add(j):
            r = rows(j, 16)
            if ch in rs_pairs:
                at = pl.ds(pl.multiple_of(zz * 2 * br + j * 16, 16), 16)
                t = ref[at, pl.ds(gstart, width)].astype(f32) + RZP[i, r, part_of(ch)].astype(f32)
                ref[at, pl.ds(gstart, width)] = t.astype(bf16)
            else:
                t = RY[zz, r, part_of(ch)].astype(f32) + RZ[i, r, part_of(ch)].astype(f32)
                RY[zz, r, part_of(ch)] = t.astype(bf16)

        loop((2 * br if ch in rs_pairs else br) // 16, add)
        rs_z(ch, i, zz, 3, zz).start()

    def rs_pre(ch):
        if ch not in rs_pairs:
            return
        for slot in (2, 3):
            rs_z(ch, 2, z, slot, partner).wait_recv()
        ref, gstart, width = gcol(ch)

        def add(j):
            at = pl.ds(pl.multiple_of((z * 2 + 1 - y) * br + j * 16, 16), 16)
            r = pl.ds(pl.multiple_of((1 - y) * br + j * 16, 16), 16)
            t = ref[at, pl.ds(gstart, width)].astype(f32)
            t = t + RZP[2, r, part_of(ch)].astype(f32) + RZP[3, r, part_of(ch)].astype(f32)
            ref[at, pl.ds(gstart, width)] = t.astype(bf16)

        loop(br // 16, add)
        rs_y(ch, z, 1 - y).start()

    def outs(ch):
        start, width = RCH[ch]
        if start >= down0:
            pairs = [(GFD.at[pl.ds(start - down0, width), :], gdown_h.at[pl.ds(start - down0, width), :])]
        elif start >= PW:
            third = (start - PW) // (2 * FC)
            at = start - PW - 2 * FC * third
            pairs = []
            for target, low in ((ggate_h, 0), (gup_h, FC)):
                first, last = max(at, low), min(at + width, low + FC)
                if first < last:
                    held = GF.at[:, pl.ds(start - 2 * KW + first - at, last - first)]
                    pairs.append((held, target.at[:, pl.ds(third * FC + first - low, last - first)]))
        elif start == 2 * QW:
            pairs = [(GFO, gout_h)]
        elif start == 0:
            pairs = [(GF.at[:, pl.ds(0, QW)], gquery_h)]
        else:
            pairs = [
                (GF.at[:, pl.ds(QW, KW)], gkey_h),
                (GF.at[:, pl.ds(QW + KW, KW)], gvalue_h),
            ]
        return [pltpu.make_async_copy(a, b, out_sem.at[3 * ch + i]) for i, (a, b) in enumerate(pairs)]

    def rs_fin(ch):
        ref, gstart, width = gcol(ch)
        start = RCH[ch][0]
        paired = ch in rs_pairs
        rs_y(ch, z, y).wait_recv()
        if not tree:
            loop(nz - 1, lambda k: rs_z(ch, 0, z, k, z).wait_recv())
        elif not paired:
            for slot in (2, 3):
                rs_z(ch, 0, z, slot, z).wait_recv()

        def total(r0, rn, c0, cn):
            r = pl.ds(r0, rn)
            g = ref[pl.ds(pl.multiple_of(row * br + r0, 16), rn), pl.ds(gstart + c0, cn)]
            part = pl.ds(place[ch] + c0, cn)
            if paired:
                rp = pl.ds(pl.multiple_of(y * br + r0, 16), rn)
                t = RZP[2, rp, part].astype(f32) + RZP[3, rp, part].astype(f32)
                return g.astype(f32) + t + RYP[r, part].astype(f32)
            t = g.astype(f32) + RY[z, r, part].astype(f32)
            if tree:
                return t + (RZ[2, r, part].astype(f32) + RZ[3, r, part].astype(f32))
            return lax.fori_loop(0, nz - 1, lambda k, t: t + RZ[k, r, part].astype(f32), t)

        if start >= down0 or start == 2 * QW:
            for c0 in range(0, width, 128):
                t = jnp.transpose(total(0, br, c0, 128))
                if start >= down0:
                    GFD[pl.ds(start - down0 + c0, 128), :] = t
                else:
                    GFO[pl.ds(c0, 128), :] = t
        else:
            at = start - 2 * KW if start >= PW else start

            def add(i):
                r0 = pl.multiple_of(i * 16, 16)
                GF[pl.ds(r0, 16), pl.ds(at, width)] = total(r0, 16, 0, width)

            loop(br // 16, add)
        for copy in outs(ch):
            copy.start()

    def rs_done(ch):
        if ch in rs_pairs:
            rs_y(ch, z, 1 - y).wait_send()
        else:
            loop(nz, lambda zz: rs_y(ch, zz, 1 - y).wait_send())
        if tree:
            for i in range(3):
                rs_z(ch, i, zto(i), 0, partner).wait_send()
        else:
            loop(nz, lambda k: rs_z(ch, k, z, 0, z).wait_send(), 1)
        for copy in outs(ch):
            copy.wait()

    for copy in local:
        copy.start()
    bar = pltpu.get_barrier_semaphore()
    for dev in (ypeer, cpeer, xpeer, dpeer):
        pl.semaphore_signal(bar, inc=1, device_id=dev, device_id_type=MESH)

    def greet(k):
        pl.semaphore_signal(bar, inc=1, device_id=zdev((z + k) % nz), device_id_type=MESH)

    loop(nz, greet, 1)
    for i in range(4):
        local[i].wait()
    W[own, pl.ds(2 * QW, QW)] = jnp.transpose(WO[...])
    pl.semaphore_wait(bar, 4 + nz - 1)

    def load_gate_up():
        for i in range(6, 12):
            local[i].wait()

    def load_down():
        local[12].wait()
        W[own, pl.ds(down0, F)] = jnp.transpose(WD[...])

    def start_tokens():
        local[4].wait()
        tok_start()

    def start_cotangent():
        local[5].wait()
        cot_start()

    lane = lax.broadcasted_iota(jnp.int32, (1, 128), 1)
    gain_q = jnp.concatenate([gq_ref[...], gq_ref[...]], axis=1)
    gain_k = jnp.concatenate([gk_ref[...], gk_ref[...]], axis=1)
    windows = []
    for i in range(nb):
        start = max(0, RB * i - longest)
        windows.append((start, RB * (i + 1) - start, sum(w for _, w, _ in windows)))

    def tables():
        VEC[...] = jnp.zeros(VEC.shape, f32)
        seg = seg_ref[...]
        first = jnp.zeros((1, T), jnp.int32)
        for d in range(ids):
            count = jnp.sum((seg == d).astype(f32), axis=1, keepdims=True).astype(jnp.int32)
            first = first + jnp.where(seg > d, count, 0)
        place = lax.broadcasted_iota(jnp.int32, (1, T), 1)
        inverse_freq = jnp.exp((lane % 32).astype(f32) * (-2.0 / 64 * math.log(rope_base)))
        CS[...] = jnp.transpose(jnp.broadcast_to((place - first).astype(f32), (128, T)))

        def fill(i):
            angle = CS[rows(i, 128), :] * inverse_freq
            sine = jnp.sin(angle)
            CS[rows(i, 128), :] = jnp.cos(angle)
            SN[rows(i, 128), :] = jnp.where(lane % 64 < 32, -sine, sine)

        loop(T // 128, fill)
        for i, (start, width, at) in enumerate(windows):
            key_place = lax.broadcasted_iota(jnp.int32, (width, RB), 0) + start
            q_place, q_first = place[:, RB * i : RB * (i + 1)], first[:, RB * i : RB * (i + 1)]
            seen = (key_place <= q_place) & (key_place >= q_first)
            BIAS[pl.ds(at, width), :] = jnp.where(seen, 0.0, -1e30).astype(bf16)

    def head_mean(v):
        half_a = lax.broadcasted_iota(jnp.int32, (128, 128), 0) // 64
        half_b = lax.broadcasted_iota(jnp.int32, (128, 128), 1) // 64
        mean_matrix = jnp.where(half_a == half_b, 1.0 / 64, 0.0).astype(bf16)
        high = v.astype(bf16)
        low = (v - high.astype(f32)).astype(bf16)
        return dot_nn(high, mean_matrix) + dot_nn(low, mean_matrix)

    def turn(v):
        return jnp.where(lane % 64 < 32, pltpu.roll(v, 96, 1), pltpu.roll(v, 32, 1))

    def norm_tokens():
        tok_wait(False)
        tok_wait(True)

        def step(i):
            t = Tk[rows(i, 128), :].astype(f32)
            r = lax.rsqrt(jnp.mean(t * t, axis=1, keepdims=True) + epsilon)
            R1[rows(i, 128), :] = jnp.broadcast_to(r, (128, 128))
            Nm[rows(i, 128), :] = (t * r * ga_ref[...]).astype(bf16)

        loop(T // 128, step)

    def project():
        ag_wait(0)

        def step(i):
            r = rows(i, RB)
            PRE[r, :] = dot_nn(Nm[r, :], W[:, pl.ds(0, 2 * QW)])
            cos, sin = CS[r, :], SN[r, :]
            for p in range(3):
                v = PRE[r, pl.ds(128 * p, 128)]
                n = v * lax.rsqrt(head_mean(v * v) + epsilon)
                u = n * (gain_q if p < 2 else gain_k)
                u = (u * cos + turn(u) * sin).astype(bf16)
                if p < 2:
                    u = u * jnp.asarray(0.125, bf16)
                    QS[p, 0, r, :] = u[:, :64]
                    QS[p, 1, r, :] = u[:, 64:]
                else:
                    KS[0, r, :] = u[:, :64]
                    KS[1, r, :] = u[:, 64:]
                    ut = jnp.transpose(u)
                    KT[0, :, r] = ut[:64, :]
                    KT[1, :, r] = ut[64:, :]
            v = PRE[r, pl.ds(384, 128)].astype(bf16)
            VS[0, r, :] = v[:, :64]
            VS[1, r, :] = v[:, 64:]
            vt = jnp.transpose(v)
            VT[0, :, r] = vt[:64, :]
            VT[1, :, r] = vt[64:, :]

        loop(nb, step)

    def attend(i):
        start, width, at = windows[i]
        keys = pl.ds(start, width)
        r = pl.ds(RB * i, RB)

        def step(h):
            q = QS[h, :, r, :].reshape(2 * RB, 64)
            bias = BIAS[pl.ds(at, width), :].astype(f32)
            s = dot_nt(KS[h, keys, :], q) + jnp.concatenate([bias, bias], axis=1)
            e = jnp.exp(s)
            inv = 1.0 / jnp.sum(e, axis=0, keepdims=True)
            INV[h, pl.ds(i, 1), :] = inv
            o = dot_nn(VT[h, :, keys], (e * inv).astype(bf16))
            o = jnp.concatenate([o[:, :RB], o[:, RB:]], axis=0)
            MX[r, pl.ds(pl.multiple_of(h * 128, 128), 128)] = jnp.transpose(o).astype(bf16)

        loop(2, step)

    def attention_out(half):
        if half == 0:
            ag_wait(1)
        a_produce(half, lambda d: dot_nt(MX[rows(d, RB), :], W[:, pl.ds(2 * QW, QW)]))

    def after_attention(h):
        def use(r, at, summed):
            v = Tk[at, :].astype(f32) + summed
            RES[r, :] = v
            n = v * lax.rsqrt(jnp.mean(v * v, axis=1, keepdims=True) + epsilon)
            NF[at, :] = (n * gf_ref[...]).astype(bf16)

        a_total(h, use)
        nf_start(h)

    def ffn(j, half):
        if j == 0:
            nf_wait(half == 1)
        if half == 0:
            ag_wait(2 + j)
        elif j == 0:
            nf_done()

        def step(i):
            r = rows(own_first(half, i), RB)
            n = NF[r, :]
            gate = dot_nn(n, W[:, pl.ds(PW + 2 * FC * j, FC)])
            up = dot_nn(n, W[:, pl.ds(PW + 2 * FC * j + FC, FC)])
            sig = 1.0 / (1.0 + jnp.exp(-gate))
            act = gate * sig
            HID[r, pl.ds(FC * j, FC)] = (act * up).astype(bf16)
            GG[r, pl.ds(2 * FC * j, FC)] = (up * (sig + act * (1.0 - sig))).astype(bf16)
            GG[r, pl.ds(2 * FC * j + FC, FC)] = act.astype(bf16)

        loop(2, step)

    def grad_weights(what):
        if what < 3:
            if what == 0:
                cot_wait(False)
                cot_wait(True)
                cot_done()
            weight_grad(Ct, [(what, HID.at[:, pl.ds(FC * what, FC)])])
        elif what < 6:
            weight_grad(NF, [(what, GG.at[:, pl.ds(2 * FC * (what - 3), 2 * FC)])])
        elif what == 6:
            weight_grad(Ct, [(6, MX)])
        else:
            weight_grad(Nm, [(7, GQ.at[:, pl.ds(0, QW)]), (9, GQ.at[:, pl.ds(QW, 2 * KW)])])

    def grad_hidden(j, half):
        if half == 0:
            ag_wait(5 + j)

        def step(i):
            r = rows(other_first(half, i), RB)
            gh = dot_nn(Ct[r, :], W[:, pl.ds(down0 + FC * j, FC)])
            a, b = pl.ds(2 * FC * j, FC), pl.ds(2 * FC * j + FC, FC)
            GG[r, a] = (gh * GG[r, a].astype(f32)).astype(bf16)
            GG[r, b] = (gh * GG[r, b].astype(f32)).astype(bf16)

        loop(2, step)

    def grad_ffn_norm(half):
        if half == 0:
            a_done()
        n_produce(half, lambda d: dot_nt(GG[rows(d, RB), :], W[:, pl.ds(PW, 2 * F)]))

    def after_ffn(h):
        def use(r, at, gy):
            v = RES[r, :]
            inv = lax.rsqrt(jnp.mean(v * v, axis=1, keepdims=True) + epsilon)
            n = v * inv
            VEC[1:2, :] += jnp.sum(gy * n, axis=0, keepdims=True)
            g = gy * gf_ref[...]
            g = inv * (g - n * jnp.mean(g * n, axis=1, keepdims=True))
            Ct[at, :] = (Ct[at, :].astype(f32) + g).astype(bf16)

        n_total(h, use)
        rl_start(h)

    def grad_mixed(half):
        rl_wait(half == 1)
        if half == 0:
            DKV[...] = jnp.zeros(DKV.shape, f32)

        def step(i):
            r = rows(own_first(half, i), RB)
            g = dot_nn(Ct[r, :], W[:, pl.ds(2 * QW, QW)]).astype(bf16)
            for p in range(2):
                DO[p, 0, r, :] = g[:, 128 * p : 128 * p + 64]
                DO[p, 1, r, :] = g[:, 128 * p + 64 : 128 * p + 128]

        loop(2, step)

    def attend_back(i):
        start, width, at = windows[i]
        keys = pl.ds(start, width)
        r = pl.ds(RB * i, RB)

        def step(h):
            q = QS[h, :, r, :].reshape(2 * RB, 64)
            do = DO[h, :, r, :].reshape(2 * RB, 64)
            bias = BIAS[pl.ds(at, width), :].astype(f32)
            s = dot_nt(KS[h, keys, :], q) + jnp.concatenate([bias, bias], axis=1)
            p = jnp.exp(s) * INV[h, pl.ds(i, 1), :]
            dp = dot_nt(VS[h, keys, :], do)
            ds = (p * (dp - jnp.sum(p * dp, axis=0, keepdims=True))).astype(bf16)
            DKV[h, keys, :] += jnp.concatenate([dot_nn(ds, q), dot_nn(p.astype(bf16), do)], axis=1)
            g = dot_nn(KT[h, :, keys], ds) * 0.125
            g = jnp.concatenate([g[:, :RB], g[:, RB:]], axis=0)
            DQ[r, pl.ds(pl.multiple_of(h * 128, 128), 128)] = jnp.transpose(g)

        loop(2, step)

    def project_back():
        def step(i):
            r = rows(i, RB)
            cos, sin = CS[r, :], SN[r, :]
            for p in range(3):
                if p < 2:
                    g = DQ[r, pl.ds(128 * p, 128)]
                else:
                    g = jnp.concatenate([DKV[0, r, pl.ds(0, 64)], DKV[1, r, pl.ds(0, 64)]], axis=1)
                g = g * cos - turn(g) * sin
                v = PRE[r, pl.ds(128 * p, 128)]
                inv = lax.rsqrt(head_mean(v * v) + epsilon)
                n = v * inv
                s = pl.ds(0 if p < 2 else 128, 128)
                VEC[2:3, s] += jnp.sum(g * n, axis=0, keepdims=True)
                g = g * (gain_q if p < 2 else gain_k)
                GQ[r, pl.ds(128 * p, 128)] = (inv * (g - n * head_mean(g * n))).astype(bf16)
            v = jnp.concatenate([DKV[0, r, pl.ds(64, 64)], DKV[1, r, pl.ds(64, 64)]], axis=1)
            GQ[r, pl.ds(384, 128)] = v.astype(bf16)

        loop(nb, step)

    def gn_core(i, k, xx, cc):
        return rc(
            PN.at[rows(i, RB), pl.ds(pl.multiple_of((xx * 2 + cc) * CW, CW), CW)],
            AC.at[rows(i, RB), pl.ds(pl.multiple_of(xx * CW, CW), CW)],
            gn_s.at[i, k], gn_r.at[i, k], cpeer,
        )

    def gn_x(i):
        return rc(SC.at[rows(i, RB), :], BC.at[rows(i, RB), :], gn_s.at[i, 2], gn_r.at[i, 2], xpeer)

    others = [(0, x * 2 + 1 - c, cpeer), (1, (1 - x) * 2 + c, xpeer), (2, (1 - x) * 2 + 1 - c, dpeer)]
    gains = VY.shape[0]
    vec_y = rc(VSUM.at[pl.ds(0, gains), :], VY, vec_s.at[3], vec_r.at[3], ypeer)

    def vec_copy(i, which, dev):
        return rc(VCOL.at[which], VCOL.at[which], vec_s.at[i], vec_r.at[i], dev)

    def vz_copy(k, src):
        return rc(VZ.at[src], VZ.at[src], vz_s.at[k], vz_r.at[k], zdev((z + k) % nz))

    def gn_produce():
        def step(i):
            r = rows(i, RB)
            g = dot_nt(GQ[r, :], W[:, pl.ds(0, 2 * QW)])
            PN[r, :] = g.astype(bf16)
            gn_core(i, 0, 1 - x, 1 - c).start()
            gn_core(i, 1, x, 1 - c).start()
            g = g * (Tk[r, :].astype(f32) * R1[r, pl.ds(0, 1)])
            VEC[0:1, :] += jnp.sum(g, axis=0, keepdims=True)
            s = jnp.sum(g * ga_ref[...], axis=1, keepdims=True)
            VEC[3:4, r] = jnp.transpose(jnp.broadcast_to(s, (RB, 128)))[0:1, :]

        loop(nb, step)
        for i in range(D // 128):
            s = pl.ds(128 * i, 128)
            VCOL[col, pl.ds(i, 1), :] = VEC[0:1, s]
            VCOL[col, pl.ds(D // 128 + i, 1), :] = VEC[1:2, s]
        for i in range(2):
            VCOL[col, pl.ds(D // 64 + i, 1), :] = VEC[2:3, pl.ds(128 * i, 128)]
        for i in range(T // 128):
            VCOL[col, pl.ds(gains + i, 1), :] = VEC[3:4, pl.ds(128 * i, 128)]
        for i, _, dev in others:
            vec_copy(i, col, dev).start()

    def gn_middle():
        def step(i):
            r = rows(i, RB)
            gn_core(i, 0, 1 - x, c).wait_recv()
            a = PN[r, pl.ds(pl.multiple_of(((1 - x) * 2 + c) * CW, CW), CW)].astype(f32)
            b = AC[r, pl.ds(pl.multiple_of((1 - x) * CW, CW), CW)].astype(f32)
            SC[r, :] = (a + b).astype(bf16)
            gn_x(i).start()

        loop(nb, step)

    def vec_col():
        for i, d, dev in others:
            vec_copy(i, d, dev).wait_recv()
        VSUM[...] = (VCOL[0] + VCOL[1]) + (VCOL[2] + VCOL[3])
        vec_y.start()

    def vec_row():
        vec_y.wait_recv()
        VZ[z] = VSUM[0:gains, :] + VY[...]
        loop(nz, lambda k: vz_copy(k, z).start(), 1)

    gt_copy = pltpu.make_async_copy(DQ, gt_h, out_sem.at[30])
    lo_out = pltpu.make_async_copy(LOC, lo_h, out_sem.at[31])

    def gn_finish():
        def step(i):
            r = rows(i, RB)
            gn_core(i, 1, x, c).wait_recv()
            gn_x(i).wait_recv()
            g = PN[r, mine].astype(f32) + AC[r, pl.ds(pl.multiple_of(x * CW, CW), CW)].astype(f32)
            g = (g + BC[r, :].astype(f32)) * ga_ref[:, mine]
            inv = R1[r, pl.ds(0, 1)]
            s = [VSUM[pl.ds(gains + 2 * i + j, 1), :] for j in range(2)]
            s = jnp.transpose(jnp.broadcast_to(jnp.concatenate(s, axis=1), (128, RB)))[:, 0:1] * (1.0 / D)
            n = Tk[r, mine].astype(f32) * inv
            DQ[r, :] = Ct[r, mine].astype(f32) + inv * (g - n * s)

        for i in range(nb):
            step(i)
        gt_copy.start()

    def lo_copy(i, d, dev):
        return rc(
            S0.at[:, pl.ds(pl.multiple_of(d * CW, CW), CW)], LOC.at[rows(col, RB), :], lo_s.at[i], lo_r.at[i], dev
        )

    def branch():
        n_done()
        for half in range(2):
            b_produce(half, lambda d: dot_nt(HID[rows(d, RB), :], W[:, pl.ds(down0, F)]))

    def block_out():
        def use(r, at, summed):
            S0[r, :] = (RES[r, :] + summed).astype(bf16)

        b_total(0, use)
        b_total(1, use)
        for i, d, dev in others:
            lo_copy(i, d, dev).start()
        LOC[rows(col, RB), :] = S0[:, mine]

    def block_out_wait():
        for i, d, dev in others:
            lo_copy(i, d, dev).wait_recv()
        lo_out.start()

    def finish():
        loop(nz, lambda k: vz_copy(k, (z + nz - k) % nz).wait_recv(), 1)
        gain_ref[...] = lax.fori_loop(1, nz, lambda k, t: t + VZ[k], VZ[0])
        tok_done()
        rl_done()
        b_done()
        for i, d, dev in others:
            lo_copy(i, d, dev).wait_send()
            vec_copy(i, col, dev).wait_send()
        vec_y.wait_send()

        def gn_done(i):
            gn_core(i, 0, 1 - x, 1 - c).wait_send()
            gn_core(i, 1, x, 1 - c).wait_send()
            gn_x(i).wait_send()

        loop(nb, gn_done)
        loop(nz, lambda k: vz_copy(k, z).wait_send(), 1)
        for ch in range(len(CH)):
            ag_done(ch)
        for ch in range(len(RCH)):
            rs_done(ch)
        gt_copy.wait()
        lo_out.wait()

    steps = {
        "gate_up": load_gate_up, "down": load_down, "toks": start_tokens, "cots": start_cotangent,
        "owny": own_y, "ownz": own_z, "fwd": forward, "tokf": tok_forward, "cotf": cot_forward,
        "tables": tables, "norm": norm_tokens, "project": project, "att": lambda half: rows_of_chip(False, half, attend), "aprod": attention_out,
        "amid": a_middle, "aft": after_attention, "nff": nf_forward, "ffn": ffn, "wg": grad_weights,
        "gh": grad_hidden, "gnfp": grad_ffn_norm, "gnfm": n_middle, "naft": after_ffn, "rlf": rl_forward,
        "gmix": grad_mixed, "ab": lambda half: rows_of_chip(True, half, attend_back), "snd": send_grad, "pb": project_back, "gnp": gn_produce, "gnm": gn_middle,
        "vc": vec_col, "vy": vec_row,
        "gnfin": gn_finish, "brp": branch, "brm": b_middle, "brf": block_out, "lof": block_out_wait,
        "mid": rs_mid, "relay": rs_relay, "pre": rs_pre, "fin": rs_fin, "end": finish,
    }
    for name, *which, who in ORDER:
        if name in ("fwd", "mid"):
            run = functools.partial(steps[name], *which, who == "m")
        else:
            run = functools.partial(steps[name], *which)
        if who == "a" or not tree:
            if who != "e" or name in ("fwd", "mid"):
                run()
        else:

            @pl.when(is_middle if who == "m" else jnp.logical_not(is_middle))
            def _():
                run()


def hand_out(*refs):
    sources, gains, targets, held, sem = refs[:9], refs[9], refs[10:19], refs[23:32], refs[32]
    loads = [pltpu.make_async_copy(a, b, sem.at[0, i]) for i, (a, b) in enumerate(zip(sources, held))]
    stores = [pltpu.make_async_copy(a, b, sem.at[1, i]) for i, (a, b) in enumerate(zip(held, targets))]
    for copy in loads:
        copy.start()
    attn, ffn, query, key = refs[19:23]
    n = attn.shape[1] // 128
    for i in range(n):
        attn[:, pl.ds(128 * i, 128)] = gains[pl.ds(i, 1), :]
        ffn[:, pl.ds(128 * i, 128)] = gains[pl.ds(n + i, 1), :]
    query[...] = gains[pl.ds(2 * n, 1), pl.ds(0, 64)] + gains[pl.ds(2 * n, 1), pl.ds(64, 64)]
    key[...] = gains[pl.ds(2 * n + 1, 1), pl.ds(0, 64)] + gains[pl.ds(2 * n + 1, 1), pl.ds(64, 64)]
    for load, store in zip(loads, stores):
        load.wait()
        store.start()
    for store in stores:
        store.wait()


def per_device(
    n_row, tokens, segment_ids, w_query, key_matrix, value_matrix, w_out, w_gate, w_up, w_down,
    norm_attn, norm_ffn, norm_query, norm_key, cotangent,
):
    T, CW = tokens.shape
    br, QW = w_query.shape
    KW = key_matrix.shape[1]
    F = w_gate.shape[1]
    D = br * n_row
    nz = n_row // 2
    PW = 2 * QW + 2 * KW
    WW = PW + 3 * F
    FC = F // 3
    nb = T // RB
    area = sum(RB * (i + 1) - max(0, RB * i - longest) for i in range(nb))
    chunks = [(0, 2 * QW), (2 * QW, QW)]
    chunks += [(PW + 2 * FC * j, 2 * FC) for j in range(3)] + [(PW + 2 * F + FC * j, FC) for j in range(3)]
    start, width = chunks[4]
    last = 128
    grads = chunks[5:8] + chunks[2:4] + [(start, width - last), chunks[1], (0, QW), (start + width - last, last)]
    grads.append((QW, 2 * KW))
    gains = 2 * D // 128 + 8
    tree = nz == 4
    ag_pairs, rs_pairs = (AG_PAIRS, RS_PAIRS) if tree else ((), ())
    place, widths = [], [0, 0]
    for ch, (_, width) in enumerate(grads):
        paired = ch in rs_pairs
        place.append(widths[paired])
        widths[paired] += width
    plan = (nz, tree, chunks, grads, ag_pairs, rs_pairs, place)
    single, paired = widths[0], max(widths[1], 128)
    slots = 4 if tree else nz - 1
    vm, sem = pltpu.VMEM, pltpu.SemaphoreType.DMA
    scratch = [
        vm((D, WW), bf16), vm((QW, br), bf16), vm((F, br), bf16), vm((QW, br), f32), vm((F, br), f32),
        vm((D, 3 * F), bf16), vm((nz, br, single), bf16), vm((slots, br, single), bf16),
        vm((br, paired), bf16), vm((4, 2 * br, paired), bf16),
        vm((br, 2 * QW + 2 * F), f32), vm((T, D), bf16), vm((T, D), bf16), vm((T, D), bf16), vm((T, 128), f32),
        vm((T, 2 * QW), f32), vm((2, 2, T, 64), bf16), vm((2, T, 64), bf16), vm((2, T, 64), bf16),
        vm((2, 64, T), bf16), vm((2, 64, T), bf16), vm((2, 2, T, 64), bf16), vm((T, QW), bf16),
        vm((T, D), bf16), vm((2, RB, D), bf16), vm((RB, D), bf16), vm((RB, D), bf16), vm((RB, D), f32),
        vm((T, D), bf16), vm((T, 2 * F), bf16), vm((T, F), bf16),
        vm((T, 128), f32), vm((T, 128), f32), vm((area, RB), bf16), vm((2, 8, 2 * RB), f32),
        vm((T, QW), f32), vm((2, T, 128), f32),
        vm((T, 2 * CW), bf16), vm((T, CW), bf16), vm((T, CW), bf16), vm((T, CW), bf16),
        vm((8, D), f32), vm((4, gains + T // 128, 128), f32), vm((gains + T // 128, 128), f32), vm((gains, 128), f32),
        vm((nz, gains, 128), f32),
        sem((13,)), sem((8, nz)), sem((8, nz)), sem((8, nz)), sem((8, nz)),
        sem((10, nz)), sem((10, nz)), sem((10, nz)), sem((10, nz)),
        sem((4, 2, 3)), sem((4, 2, 3)), sem((3, 4)), sem((3, 4)), sem((nb, 3)), sem((nb, 3)), sem((3,)), sem((3,)),
        sem((4,)), sem((4,)), sem((nz,)), sem((nz,)), sem((32,)),
    ]
    whole, hbm = pl.BlockSpec(memory_space=pltpu.VMEM), pl.BlockSpec(memory_space=pl.ANY)
    shape = jax.ShapeDtypeStruct
    results = (
        shape((T, CW), bf16), shape((T, CW), f32), shape((br, QW), f32), shape((br, KW), f32), shape((br, KW), f32),
        shape((QW, br), f32), shape((br, F), f32), shape((br, F), f32), shape((F, br), f32),
    )
    outs = pl.pallas_call(
        functools.partial(layer_kernel, plan),
        out_shape=results + (shape((gains, 128), f32),),
        in_specs=[hbm, whole] + [hbm] * 7 + [whole] * 4 + [hbm],
        out_specs=(hbm,) * 9 + (whole,),
        scratch_shapes=scratch,
        compiler_params=pltpu.CompilerParams(
            collective_id=0, has_side_effects=True, vmem_limit_bytes=64 * 2**20
        ),
        name="layer",
    )(
        tokens, segment_ids, w_query, key_matrix, value_matrix, w_out, w_gate, w_up, w_down,
        norm_attn[None], norm_ffn[None], norm_query[None], norm_key[None], cotangent,
    )
    gain = shape((1, D), f32)
    head_gain = shape((1, norm_query.shape[0]), f32)
    outs = pl.pallas_call(
        hand_out,
        out_shape=results + (gain, gain, head_gain, head_gain),
        in_specs=[pl.BlockSpec(memory_space=pltpu.HBM)] * 9 + [whole],
        out_specs=(pl.BlockSpec(memory_space=pltpu.HBM),) * 9 + (whole,) * 4,
        scratch_shapes=[vm(v.shape, v.dtype) for v in results] + [sem((2, 9))],
        compiler_params=pltpu.CompilerParams(vmem_limit_bytes=63 * 2**20),
        name="hand_out",
    )(*outs)
    return outs[:9] + tuple(v[0] for v in outs[9:])


def solution(mesh):
    in_specs = (
        P("row", "col"), P("row", None), P("row", "col"), P("row", "col"), P("row", "col"), P("col", "row"),
        P("row", "col"), P("row", "col"), P("col", "row"), P(), P(), P(), P(), P("row", "col"),
    )
    out_specs = (
        P("row", "col"), P("row", "col"), P("row", "col"), P("row", "col"), P("row", "col"), P("col", "row"),
        P("row", "col"), P("row", "col"), P("col", "row"), P(), P(), P(), P(),
    )
    return jax.shard_map(
        functools.partial(per_device, mesh.shape["row"]),
        mesh=mesh, in_specs=in_specs, out_specs=out_specs, check_vma=False,
    )
```

```python
import functools
import math

import jax
import jax.numpy as jnp
from jax import lax
from jax.experimental import pallas as pl
from jax.experimental.pallas import tpu as pltpu
from jax.sharding import PartitionSpec as P

epsilon = 1e-05
rope_base = 1000000.0
longest = 512
ids = 8
f32, bf16 = jnp.float32, jnp.bfloat16
MESH = pl.DeviceIdType.MESH
RB = 256


def dot_nn(a, b):
    return lax.dot_general(a, b, (((1,), (0,)), ((), ())), preferred_element_type=f32)


def dot_nt(a, b):
    return lax.dot_general(a, b, (((1,), (1,)), ((), ())), preferred_element_type=f32)


def rows(i, n):
    return pl.ds(pl.multiple_of(i * n, n), n)


AG_PAIRS, RS_PAIRS = (5, 6), (0, 1, 2)
ORDER = [
    ("owny", 0, "a"), ("ownz", 0, "a"), ("owny", 1, "a"), ("ownz", 1, "a"), ("gate_up", "a"), ("owny", 2, "a"),
    ("down", "a"), ("owny", 7, "a"), ("fwd", 0, 1, "e"), ("ownz", 2, "a"), ("toks", "a"), ("tables", "a"),
    ("cots", "a"), ("owny", 3, "a"), ("ownz", 7, "a"), ("fwd", 0, 1, "m"), ("fwd", 0, 2, "e"), ("fwd", 0, 2, "m"),
    ("fwd", 0, 3, "e"), ("fwd", 1, 1, "e"), ("fwd", 0, 3, "m"), ("tokf", "a"), ("fwd", 1, 1, "m"),
    ("fwd", 1, 2, "e"), ("fwd", 1, 2, "m"), ("owny", 5, "a"), ("fwd", 1, 3, "m"), ("ownz", 3, "a"), ("norm", "a"),
    ("fwd", 1, 3, "e"), ("fwd", 2, 1, "m"), ("fwd", 2, 2, "m"), ("owny", 4, "a"), ("owny", 6, "a"),
    ("ownz", 4, "a"), ("project", "a"), ("fwd", 2, 3, "m"), ("fwd", 3, 1, "m"), ("att", 0, "a"), ("aprod", 0, "a"),
    ("fwd", 4, 1, "e"), ("fwd", 2, 1, "e"), ("fwd", 3, 2, "m"), ("ownz", 5, "a"), ("amid", "a"), ("fwd", 5, 1, "m"),
    ("fwd", 3, 3, "m"), ("att", 1, "a"), ("fwd", 4, 1, "m"), ("cotf", "a"), ("fwd", 4, 2, "m"), ("fwd", 2, 2, "e"),
    ("aprod", 1, "a"), ("fwd", 4, 3, "m"), ("fwd", 3, 1, "e"), ("fwd", 5, 2, "m"), ("fwd", 7, 1, "m"),
    ("ownz", 6, "a"), ("aft", 0, "a"), ("fwd", 7, 1, "e"), ("fwd", 5, 3, "m"), ("fwd", 2, 3, "e"),
    ("fwd", 7, 2, "m"), ("fwd", 7, 3, "m"), ("fwd", 5, 1, "e"), ("aft", 1, "a"), ("fwd", 3, 2, "e"),
    ("fwd", 5, 2, "e"), ("fwd", 3, 3, "e"), ("fwd", 6, 1, "e"), ("nff", 0, "a"), ("fwd", 4, 2, "e"),
    ("nff", 1, "a"), ("fwd", 4, 3, "e"), ("ffn", 0, 0, "a"), ("fwd", 6, 2, "e"), ("fwd", 6, 1, "m"),
    ("fwd", 6, 2, "m"), ("fwd", 6, 3, "m"), ("ffn", 0, 1, "a"), ("wg", 0, "a"), ("ffn", 1, 0, "a"),
    ("ffn", 1, 1, "a"), ("fwd", 5, 3, "e"), ("wg", 1, "a"), ("fwd", 7, 2, "e"), ("fwd", 6, 3, "e"),
    ("gh", 0, 0, "a"), ("relay", 0, 0, "m"), ("gh", 0, 1, "a"), ("fwd", 7, 3, "e"), ("wg", 3, "a"),
    ("ffn", 2, 0, "a"), ("ffn", 2, 1, "a"), ("wg", 2, "a"), ("gh", 1, 0, "a"), ("gh", 2, 0, "a"), ("gnfp", 0, "a"),
    ("mid", 3, 0, "e"), ("gh", 1, 1, "a"), ("gnfm", "a"), ("relay", 0, 1, "m"), ("gh", 2, 1, "a"),
    ("mid", 3, 0, "m"), ("relay", 1, 0, "m"), ("gnfp", 1, "a"), ("wg", 5, "a"), ("mid", 3, 1, "e"), ("snd", 8, "a"),
    ("naft", 0, "a"), ("wg", 4, "a"), ("mid", 5, 0, "m"), ("relay", 2, 0, "m"), ("relay", 1, 1, "m"),
    ("naft", 1, "a"), ("mid", 5, 1, "m"), ("gmix", 0, "a"), ("mid", 3, 1, "m"), ("mid", 5, 0, "e"), ("ab", 0, "a"),
    ("mid", 5, 2, "m"), ("mid", 3, 2, "e"), ("mid", 5, 1, "e"), ("rlf", 0, "a"), ("rlf", 1, "a"),
    ("mid", 8, 0, "e"), ("mid", 8, 1, "e"), ("relay", 3, 0, "m"), ("relay", 2, 1, "m"), ("relay", 3, 1, "m"),
    ("mid", 5, 2, "e"), ("mid", 8, 0, "m"), ("mid", 3, 2, "m"), ("mid", 8, 2, "e"), ("gmix", 1, "a"), ("brp", "a"),
    ("mid", 4, 0, "e"), ("wg", 6, "a"), ("relay", 5, 0, "m"), ("brm", "a"), ("mid", 8, 1, "m"), ("mid", 4, 0, "m"),
    ("ab", 1, "a"), ("mid", 4, 1, "e"), ("pb", "a"), ("relay", 5, 1, "m"), ("mid", 8, 2, "m"), ("mid", 4, 1, "m"),
    ("gnp", "a"), ("mid", 6, 0, "e"), ("mid", 4, 2, "m"), ("relay", 8, 0, "m"), ("relay", 4, 0, "m"),
    ("wg", 7, "a"), ("mid", 6, 1, "e"), ("gnm", "a"), ("mid", 6, 0, "m"), ("relay", 8, 1, "m"), ("mid", 6, 2, "e"),
    ("brf", "a"), ("relay", 4, 1, "m"), ("mid", 6, 1, "m"), ("mid", 9, 0, "m"), ("mid", 7, 0, "e"),
    ("mid", 7, 0, "m"), ("mid", 6, 2, "m"), ("mid", 9, 0, "e"), ("vc", "a"), ("mid", 7, 1, "e"), ("pre", 2, "e"),
    ("pre", 1, "e"), ("relay", 6, 0, "m"), ("mid", 7, 1, "m"), ("mid", 9, 1, "m"), ("relay", 6, 1, "m"),
    ("fin", 5, "a"), ("pre", 2, "m"), ("mid", 9, 1, "e"), ("relay", 7, 0, "m"), ("pre", 1, "m"), ("mid", 9, 2, "m"),
    ("pre", 0, "e"), ("mid", 7, 2, "m"), ("mid", 4, 2, "e"), ("pre", 0, "m"), ("relay", 9, 0, "m"),
    ("relay", 9, 1, "m"), ("mid", 9, 2, "e"), ("fin", 8, "a"), ("relay", 7, 1, "m"), ("fin", 6, "a"), ("vy", "a"),
    ("fin", 4, "a"), ("mid", 7, 2, "e"), ("fin", 3, "a"), ("fin", 2, "a"), ("fin", 1, "a"), ("fin", 9, "a"),
    ("gnfin", "a"), ("fin", 7, "a"), ("fin", 0, "a"), ("lof", "a"), ("end", "a"),
]


def layer_kernel(
    plan,
    tok_h, seg_ref, wq_h, wk_h, wv_h, wo_h, wg_h, wu_h, wd_h, ga_ref, gf_ref, gq_ref, gk_ref, cot_h,
    lo_h, gt_h, gquery_h, gkey_h, gvalue_h, gout_h, ggate_h, gup_h, gdown_h, gain_ref,
    W, WO, WD, GFO, GFD, G, RY, RZ, RYP, RZP, GF, Tk, Ct, Nm, R1, PRE, QS, KS, VS, KT, VT, DO, MX, PB, A0, B0, S0,
    RES, NF, GG, HID, CS, SN, BIAS, INV, DQ, DKV, AC, BC, SC, LOC, VEC, VCOL, VSUM, VY, VZ,
    loc_sem, agz_s, agz_r, agy_s, agy_r, rsy_s, rsy_r, rsz_s, rsz_r,
    cag_s, cag_r, crs_s, crs_r, gn_s, gn_r, lo_s, lo_r, vec_s, vec_r, vz_s, vz_r, out_sem,
):
    nz, tree, CH, RCH, ag_pairs, rs_pairs, place = plan
    T, D = Tk.shape
    br = RY.shape[1]
    QW, KW = PRE.shape[1] // 2, PRE.shape[1] // 4
    PW = 2 * QW + 2 * KW
    F = HID.shape[1]
    FC = F // 3
    HB = RB // 2
    down0 = PW + 2 * F
    nb = T // RB
    CW = D // 4
    GQ = GG.at[:, pl.ds(PW, 2 * QW)]
    PN = GG.at[:, pl.ds(PW + 2 * QW, D)]
    row, col = lax.axis_index("row"), lax.axis_index("col")
    z, y = row // 2, row % 2
    x, c = col // 2, col % 2
    ypeer = (row + 1 - 2 * y, col)
    cpeer = (row, col + 1 - 2 * c)
    xpeer = (row, (1 - x) * 2 + c)
    dpeer = (row, (1 - x) * 2 + 1 - c)
    partner = z + 1 - 2 * (z % 2)
    is_middle = (z == 1) | (z == 2)
    near, far = 2 - z // 2, 3 - 3 * (z // 2)

    def zdev(zz):
        return (zz * 2 + y, col)

    def zsrc(k):
        return [z, partner, near, far][k] if tree else (z + nz - k) % nz

    def zto(i):
        return [near, far, partner, z][i]

    def rc(src, dst, ss, rs, dev):
        return pltpu.make_async_remote_copy(
            src_ref=src, dst_ref=dst, send_sem=ss, recv_sem=rs, device_id=dev, device_id_type=MESH
        )

    def loop(n, body, first=0):
        def step(i, carry):
            body(i)
            return carry

        lax.fori_loop(first, n, step, 0)

    own = rows(row, br)
    mine = pl.ds(pl.multiple_of(col * CW, CW), CW)
    local = [
        (wq_h, W.at[own, pl.ds(0, QW)]),
        (wk_h, W.at[own, pl.ds(QW, KW)]),
        (wv_h, W.at[own, pl.ds(QW + KW, KW)]),
        (wo_h, WO),
        (tok_h, Tk.at[:, mine]),
        (cot_h, Ct.at[:, mine]),
    ]
    for j in range(3):
        local.append((wg_h.at[:, pl.ds(FC * j, FC)], W.at[own, pl.ds(PW + 2 * FC * j, FC)]))
        local.append((wu_h.at[:, pl.ds(FC * j, FC)], W.at[own, pl.ds(PW + 2 * FC * j + FC, FC)]))
    local.append((wd_h, WD))
    local = [pltpu.make_async_copy(s, d, loc_sem.at[i]) for i, (s, d) in enumerate(local)]

    def wblk(ch, zz, yy):
        start, width = CH[ch]
        return W.at[rows(zz * 2 + yy, br), pl.ds(start, width)]

    def wpair(ch, zz):
        start, width = CH[ch]
        return W.at[rows(zz, 2 * br), pl.ds(start, width)]

    def ag_z(ch, k, src, slot, dev):
        b = wpair(ch, src) if ch in ag_pairs else wblk(ch, src, y)
        return rc(b, b, agz_s.at[ch, k], agz_r.at[ch, slot], zdev(dev))

    def ag_y(ch, k, src, yy):
        b = wblk(ch, src, yy)
        return rc(b, b, agy_s.at[ch, k], agy_r.at[ch, k], ypeer)

    def own_y(ch):
        ag_y(ch, 0, z, y).start()

    def own_z(ch):
        if ch in ag_pairs:
            ag_y(ch, 0, z, 1 - y).wait_recv()
        if tree:
            ag_z(ch, 0, z, 1, partner).start()
            ag_z(ch, 1, z, jnp.where(is_middle, 2, 3), near).start()
        else:
            loop(nz, lambda k: ag_z(ch, k, z, k, (z + k) % nz).start(), 1)

    def forward(ch, k, middle):
        if not tree:
            if k == 3 and middle:

                def step(k):
                    ag_z(ch, k, zsrc(k), k, z).wait_recv()
                    ag_y(ch, k, zsrc(k), y).start()

                loop(nz, step, 1)
            return
        relayed = middle and k >= 2
        if ch in ag_pairs and not relayed:
            return
        ag_z(ch, k, zsrc(k), k, partner).wait_recv()
        if relayed:
            ag_z(ch, k, zsrc(k), k, partner).start()
        if ch not in ag_pairs:
            ag_y(ch, k, zsrc(k), y).start()

    def ag_wait(ch):
        if not tree:
            loop(nz, lambda k: ag_y(ch, k, zsrc(k), 1 - y).wait_recv())
        elif ch in ag_pairs:
            ag_z(ch, 0, partner, 1, partner).wait_recv()

            @pl.when(jnp.logical_not(is_middle))
            def _():
                ag_z(ch, 0, near, 2, partner).wait_recv()
                ag_z(ch, 0, far, 3, partner).wait_recv()

        else:
            for k in range(4):
                ag_y(ch, k, zsrc(k), 1 - y).wait_recv()

    def ag_done(ch):
        if not tree:
            loop(nz, lambda k: ag_y(ch, k, zsrc(k), y).wait_send())
            loop(nz, lambda k: ag_z(ch, k, z, k, z).wait_send(), 1)
            return
        for k in range(1 if ch in ag_pairs else 4):
            ag_y(ch, k, zsrc(k), y).wait_send()
        ag_z(ch, 0, z, 1, partner).wait_send()
        ag_z(ch, 1, z, 2, near).wait_send()

        @pl.when(is_middle)
        def _():
            ag_z(ch, 2, near, 2, partner).wait_send()
            ag_z(ch, 3, far, 3, partner).wait_send()

    def cag(n, block, parts=1):
        def copy(i, d, dev, h):
            return rc(block(d, h), block(d, h), cag_s.at[n, h, i], cag_r.at[n, h, i], dev)

        def start(h=0):
            copy(0, col, cpeer, h).start()
            copy(1, col, xpeer, h).start()

        def forward(h=0):
            copy(1, (1 - x) * 2 + c, xpeer, h).wait_recv()
            copy(2, (1 - x) * 2 + c, cpeer, h).start()

        def wait(far):
            for h in range(parts):
                if far:
                    copy(2, (1 - x) * 2 + 1 - c, cpeer, h).wait_recv()
                else:
                    copy(0, x * 2 + 1 - c, cpeer, h).wait_recv()

        def done():
            for h in range(parts):
                copy(0, col, cpeer, h).wait_send()
                copy(1, col, xpeer, h).wait_send()
                copy(2, (1 - x) * 2 + c, cpeer, h).wait_send()

        return start, forward, wait, done

    def col_block(ref):
        return lambda d, h: ref.at[:, pl.ds(pl.multiple_of(d * CW, CW), CW)]

    def row_block(ref):
        return lambda d, h: ref.at[rows(d * 2 + h, HB), :]

    tok_start, tok_forward, tok_wait, tok_done = cag(0, col_block(Tk))
    cot_start, cot_forward, cot_wait, cot_done = cag(1, col_block(Ct))
    nf_start, nf_forward, nf_wait, nf_done = cag(2, row_block(NF), 2)
    rl_start, rl_forward, rl_wait, rl_done = cag(3, row_block(Ct), 2)

    def crs(n, A, B, S):
        def to_core(i, xx, cc):
            return rc(PB.at[rows(xx * 2 + cc, RB), :], A(xx), crs_s.at[n, i], crs_r.at[n, i], cpeer)

        def to_x(h):
            half = rows(h, HB)
            return rc(S.at[half, :], B.at[half, :], crs_s.at[n, 2 + h], crs_r.at[n, 2 + h], xpeer)

        def produce(half, part):
            def step(i):
                xx = jnp.where(i < 2, 1 - x, x)
                cc = jnp.where(i % 2 == 0, 1 - c, c)
                PB[rows(xx * 2 + cc, RB), :] = part(xx * 2 + cc).astype(bf16)

                @pl.when(i % 2 == 0)
                def _():
                    to_core(i // 2, xx, 1 - c).start()

            loop(2 * half + 2, step, 2 * half)

        def middle():
            to_core(0, 1 - x, c).wait_recv()

            def step(i):
                r = rows(i, 32)
                block = PB[pl.ds(pl.multiple_of(((1 - x) * 2 + c) * RB + i * 32, 32), 32), :]
                S[r, :] = (block.astype(f32) + A(1 - x)[r, :].astype(f32)).astype(bf16)

            for h in range(2):
                loop(HB // 32 * (h + 1), step, HB // 32 * h)
                to_x(h).start()

        def total(h, use):
            if h == 0:
                to_core(1, x, c).wait_recv()
            to_x(h).wait_recv()

            def step(i):
                r = rows(i, 32)
                at = pl.ds(pl.multiple_of(col * RB + i * 32, 32), 32)
                use(r, at, PB[at, :].astype(f32) + A(x)[r, :].astype(f32) + B[r, :].astype(f32))

            loop(HB // 32 * (h + 1), step, HB // 32 * h)

        def done():
            to_core(0, 1 - x, 1 - c).wait_send()
            to_core(1, x, 1 - c).wait_send()
            to_x(0).wait_send()
            to_x(1).wait_send()

        return produce, middle, total, done

    a_produce, a_middle, a_total, a_done = crs(0, lambda i: A0.at[i], B0, S0)
    n_produce, n_middle, n_total, n_done = crs(1, lambda i: A0.at[i], B0, S0)
    b_produce, b_middle, b_total, b_done = crs(
        2, lambda i: NF.at[rows(i, RB), :], NF.at[pl.ds(2 * RB, RB), :], NF.at[pl.ds(3 * RB, RB), :]
    )

    def other_first(half, i):
        return jnp.where(half == 0, 1 - x, x) * 2 + jnp.where(i == 0, 1 - c, c)

    def own_first(half, i):
        return jnp.where(half == 0, x, 1 - x) * 2 + jnp.where(i == 0, c, 1 - c)

    def rows_of_chip(mine_first, half, work):
        for xx in range(2):

            @pl.when(x == (xx if mine_first == (half == 0) else 1 - xx))
            def _():
                work(xx)

    def gcol(ch):
        start, width = RCH[ch]
        return (G, start - PW, width) if start >= PW else (GG, start, width)

    def gblk(ch, zz, yy):
        ref, start, width = gcol(ch)
        return ref.at[rows(zz * 2 + yy, br), pl.ds(start, width)]

    def part_of(ch):
        return pl.ds(place[ch], RCH[ch][1])

    def rs_y(ch, zz, yy):
        landing = RYP.at[:, part_of(ch)] if ch in rs_pairs else RY.at[zz, :, part_of(ch)]
        return rc(gblk(ch, zz, yy), landing, rsy_s.at[ch, zz], rsy_r.at[ch, zz], ypeer)

    def rs_z(ch, k, zz, slot, dev):
        if ch in rs_pairs:
            ref, start, width = gcol(ch)
            src, dst = ref.at[rows(zz, 2 * br), pl.ds(start, width)], RZP.at[slot, :, part_of(ch)]
        else:
            src, dst = RY.at[zz, :, part_of(ch)], RZ.at[slot, :, part_of(ch)]
        return rc(src, dst, rsz_s.at[ch, k], rsz_r.at[ch, slot], zdev(dev))

    zper = RB // (2 * br)

    def weight_grad(left, pieces):
        def one(i, d):
            lt = jnp.transpose(left[:, rows(d, RB)])
            for ch, right in pieces:
                ref, start, width = gcol(ch)
                ref[rows(d, RB), pl.ds(start, right.shape[1])] = dot_nn(lt, right[...]).astype(bf16)
                if ch not in rs_pairs:
                    loop(zper, lambda s: rs_y(ch, d * zper + s, 1 - y).start())
                else:

                    @pl.when((i == 2) | ((i < 2) & jnp.logical_not(is_middle)))
                    def _():
                        rs_z(ch, i, d, i, partner).start()

        if tree:

            def step(i):
                one(i, jnp.where(i == 0, near, jnp.where(i == 1, far, jnp.where(i == 2, partner, z))))

            loop(4, step)
        else:
            loop(D // RB, lambda i: one(i, (row * br // RB + 1 + i) % (D // RB)))

    def send_grad(ch):
        if tree:
            for i in range(4):
                rs_y(ch, zto(i), 1 - y).start()
        else:
            loop(nz, lambda k: rs_y(ch, k, 1 - y).start())

    def rs_mid(ch, i, middle):
        ref, gstart, width = gcol(ch)

        def one(zz):
            rs_y(ch, zz, y).wait_recv()

            def add(j):
                r = rows(j, 16)
                g = ref[pl.ds(pl.multiple_of((zz * 2 + y) * br + j * 16, 16), 16), pl.ds(gstart, width)]
                t = RY[zz, r, part_of(ch)]
                RY[zz, r, part_of(ch)] = (g.astype(f32) + t.astype(f32)).astype(bf16)

            loop(br // 16, add)

        if not tree:
            if i == 2 and middle:

                def step(k):
                    zz = (z + k) % nz
                    one(zz)
                    rs_z(ch, k, zz, k - 1, zz).start()

                loop(nz, step, 1)
        elif ch not in rs_pairs:
            one(zto(i))
            if i == 2 or not middle:
                rs_z(ch, i, zto(i), i, partner).start()

    def rs_relay(ch, i):
        if not tree:
            return
        zz = zto(i)
        rs_z(ch, i, zz, i, partner).wait_recv()
        ref, gstart, width = gcol(ch)

        def add(j):
            r = rows(j, 16)
            if ch in rs_pairs:
                at = pl.ds(pl.multiple_of(zz * 2 * br + j * 16, 16), 16)
                t = ref[at, pl.ds(gstart, width)].astype(f32) + RZP[i, r, part_of(ch)].astype(f32)
                ref[at, pl.ds(gstart, width)] = t.astype(bf16)
            else:
                t = RY[zz, r, part_of(ch)].astype(f32) + RZ[i, r, part_of(ch)].astype(f32)
                RY[zz, r, part_of(ch)] = t.astype(bf16)

        loop((2 * br if ch in rs_pairs else br) // 16, add)
        rs_z(ch, i, zz, 3, zz).start()

    def rs_pre(ch):
        if ch not in rs_pairs:
            return
        for slot in (2, 3):
            rs_z(ch, 2, z, slot, partner).wait_recv()
        ref, gstart, width = gcol(ch)

        def add(j):
            at = pl.ds(pl.multiple_of((z * 2 + 1 - y) * br + j * 16, 16), 16)
            r = pl.ds(pl.multiple_of((1 - y) * br + j * 16, 16), 16)
            t = ref[at, pl.ds(gstart, width)].astype(f32)
            t = t + RZP[2, r, part_of(ch)].astype(f32) + RZP[3, r, part_of(ch)].astype(f32)
            ref[at, pl.ds(gstart, width)] = t.astype(bf16)

        loop(br // 16, add)
        rs_y(ch, z, 1 - y).start()

    def outs(ch):
        start, width = RCH[ch]
        if start >= down0:
            pairs = [(GFD.at[pl.ds(start - down0, width), :], gdown_h.at[pl.ds(start - down0, width), :])]
        elif start >= PW:
            third = (start - PW) // (2 * FC)
            at = start - PW - 2 * FC * third
            pairs = []
            for target, low in ((ggate_h, 0), (gup_h, FC)):
                first, last = max(at, low), min(at + width, low + FC)
                if first < last:
                    held = GF.at[:, pl.ds(start - 2 * KW + first - at, last - first)]
                    pairs.append((held, target.at[:, pl.ds(third * FC + first - low, last - first)]))
        elif start == 2 * QW:
            pairs = [(GFO, gout_h)]
        elif start == 0:
            pairs = [(GF.at[:, pl.ds(0, QW)], gquery_h)]
        else:
            pairs = [
                (GF.at[:, pl.ds(QW, KW)], gkey_h),
                (GF.at[:, pl.ds(QW + KW, KW)], gvalue_h),
            ]
        return [pltpu.make_async_copy(a, b, out_sem.at[3 * ch + i]) for i, (a, b) in enumerate(pairs)]

    def rs_fin(ch):
        ref, gstart, width = gcol(ch)
        start = RCH[ch][0]
        paired = ch in rs_pairs
        rs_y(ch, z, y).wait_recv()
        if not tree:
            loop(nz - 1, lambda k: rs_z(ch, 0, z, k, z).wait_recv())
        elif not paired:
            for slot in (2, 3):
                rs_z(ch, 0, z, slot, z).wait_recv()

        def total(r0, rn, c0, cn):
            r = pl.ds(r0, rn)
            g = ref[pl.ds(pl.multiple_of(row * br + r0, 16), rn), pl.ds(gstart + c0, cn)]
            part = pl.ds(place[ch] + c0, cn)
            if paired:
                rp = pl.ds(pl.multiple_of(y * br + r0, 16), rn)
                t = RZP[2, rp, part].astype(f32) + RZP[3, rp, part].astype(f32)
                return g.astype(f32) + t + RYP[r, part].astype(f32)
            t = g.astype(f32) + RY[z, r, part].astype(f32)
            if tree:
                return t + (RZ[2, r, part].astype(f32) + RZ[3, r, part].astype(f32))
            return lax.fori_loop(0, nz - 1, lambda k, t: t + RZ[k, r, part].astype(f32), t)

        if start >= down0 or start == 2 * QW:
            for c0 in range(0, width, 128):
                t = jnp.transpose(total(0, br, c0, 128))
                if start >= down0:
                    GFD[pl.ds(start - down0 + c0, 128), :] = t
                else:
                    GFO[pl.ds(c0, 128), :] = t
        else:
            at = start - 2 * KW if start >= PW else start

            def add(i):
                r0 = pl.multiple_of(i * 16, 16)
                GF[pl.ds(r0, 16), pl.ds(at, width)] = total(r0, 16, 0, width)

            loop(br // 16, add)
        for copy in outs(ch):
            copy.start()

    def rs_done(ch):
        if ch in rs_pairs:
            rs_y(ch, z, 1 - y).wait_send()
        else:
            loop(nz, lambda zz: rs_y(ch, zz, 1 - y).wait_send())
        if tree:
            for i in range(3):
                rs_z(ch, i, zto(i), 0, partner).wait_send()
        else:
            loop(nz, lambda k: rs_z(ch, k, z, 0, z).wait_send(), 1)
        for copy in outs(ch):
            copy.wait()

    for copy in local:
        copy.start()
    bar = pltpu.get_barrier_semaphore()
    for dev in (ypeer, cpeer, xpeer, dpeer):
        pl.semaphore_signal(bar, inc=1, device_id=dev, device_id_type=MESH)

    def greet(k):
        pl.semaphore_signal(bar, inc=1, device_id=zdev((z + k) % nz), device_id_type=MESH)

    loop(nz, greet, 1)
    for i in range(4):
        local[i].wait()
    W[own, pl.ds(2 * QW, QW)] = jnp.transpose(WO[...])
    pl.semaphore_wait(bar, 4 + nz - 1)

    def load_gate_up():
        for i in range(6, 12):
            local[i].wait()

    def load_down():
        local[12].wait()
        W[own, pl.ds(down0, F)] = jnp.transpose(WD[...])

    def start_tokens():
        local[4].wait()
        tok_start()

    def start_cotangent():
        local[5].wait()
        cot_start()

    lane = lax.broadcasted_iota(jnp.int32, (1, 128), 1)
    gain_q = jnp.concatenate([gq_ref[...], gq_ref[...]], axis=1)
    gain_k = jnp.concatenate([gk_ref[...], gk_ref[...]], axis=1)
    hb = nb // 2
    spans = []
    for half in range(2):
        low = max(0, RB * half * hb - longest)
        if half * RB * hb >= longest:
            spans.append((longest + RB, RB, low, sum(s[0] for s in spans) * hb))
        else:
            spans.append((RB * hb * (half + 1), 0, 0, sum(s[0] for s in spans) * hb))

    def tables():
        VEC[...] = jnp.zeros(VEC.shape, f32)
        seg = seg_ref[...]
        first = jnp.zeros((1, T), jnp.int32)
        for d in range(ids):
            count = jnp.sum((seg == d).astype(f32), axis=1, keepdims=True).astype(jnp.int32)
            first = first + jnp.where(seg > d, count, 0)
        place = lax.broadcasted_iota(jnp.int32, (1, T), 1)
        inverse_freq = jnp.exp((lane % 32).astype(f32) * (-2.0 / 64 * math.log(rope_base)))
        CS[...] = jnp.transpose(jnp.broadcast_to((place - first).astype(f32), (128, T)))

        def fill(i):
            angle = CS[rows(i, 128), :] * inverse_freq
            sine = jnp.sin(angle)
            CS[rows(i, 128), :] = jnp.cos(angle)
            SN[rows(i, 128), :] = jnp.where(lane % 64 < 32, -sine, sine)

        loop(T // 128, fill)
        for i in range(nb):
            width, pace, start, at = spans[i // hb]
            start, at = start + pace * (i % hb), at + width * (i % hb)
            key_place = lax.broadcasted_iota(jnp.int32, (width, RB), 0) + start
            q_place, q_first = place[:, RB * i : RB * (i + 1)], first[:, RB * i : RB * (i + 1)]
            seen = (key_place <= q_place) & (key_place >= q_first)
            BIAS[pl.ds(at, width), :] = jnp.where(seen, 0.0, -1e30).astype(bf16)

    def head_mean(v):
        half_a = lax.broadcasted_iota(jnp.int32, (128, 128), 0) // 64
        half_b = lax.broadcasted_iota(jnp.int32, (128, 128), 1) // 64
        mean_matrix = jnp.where(half_a == half_b, 1.0 / 64, 0.0).astype(bf16)
        high = v.astype(bf16)
        low = (v - high.astype(f32)).astype(bf16)
        return dot_nn(high, mean_matrix) + dot_nn(low, mean_matrix)

    def turn(v):
        return jnp.where(lane % 64 < 32, pltpu.roll(v, 96, 1), pltpu.roll(v, 32, 1))

    def norm_tokens():
        tok_wait(False)
        tok_wait(True)

        def step(i):
            t = Tk[rows(i, 128), :].astype(f32)
            r = lax.rsqrt(jnp.mean(t * t, axis=1, keepdims=True) + epsilon)
            R1[rows(i, 128), :] = jnp.broadcast_to(r, (128, 128))
            Nm[rows(i, 128), :] = (t * r * ga_ref[...]).astype(bf16)

        loop(T // 128, step)

    def project():
        ag_wait(0)

        def step(i):
            r = rows(i, RB)
            PRE[r, :] = dot_nn(Nm[r, :], W[:, pl.ds(0, 2 * QW)])
            cos, sin = CS[r, :], SN[r, :]
            for p in range(3):
                v = PRE[r, pl.ds(128 * p, 128)]
                n = v * lax.rsqrt(head_mean(v * v) + epsilon)
                u = n * (gain_q if p < 2 else gain_k)
                u = (u * cos + turn(u) * sin).astype(bf16)
                if p < 2:
                    u = u * jnp.asarray(0.125, bf16)
                    QS[p, 0, r, :] = u[:, :64]
                    QS[p, 1, r, :] = u[:, 64:]
                else:
                    KS[0, r, :] = u[:, :64]
                    KS[1, r, :] = u[:, 64:]
                    ut = jnp.transpose(u)
                    KT[0, :, r] = ut[:64, :]
                    KT[1, :, r] = ut[64:, :]
            v = PRE[r, pl.ds(384, 128)].astype(bf16)
            VS[0, r, :] = v[:, :64]
            VS[1, r, :] = v[:, 64:]
            vt = jnp.transpose(v)
            VT[0, :, r] = vt[:64, :]
            VT[1, :, r] = vt[64:, :]

        loop(nb, step)

    def per_block(half, work):
        width, pace, low, at = spans[half]

        def step(n):
            i, h = n // 2, n % 2
            keys = pl.ds(pl.multiple_of(low + pace * i, RB), width) if pace else pl.ds(low, width)
            bias = BIAS[pl.ds(pl.multiple_of(at + width * i, RB), width), :].astype(f32)
            work(h, half * hb + i, keys, jnp.concatenate([bias, bias], axis=1), rows(half * hb + i, RB))

        loop(2 * hb, step)

    def attend(half):
        def work(h, i, keys, bias, r):
            q = QS[h, :, r, :].reshape(2 * RB, 64)
            e = jnp.exp(dot_nt(KS[h, keys, :], q) + bias)
            inv = 1.0 / jnp.sum(e, axis=0, keepdims=True)
            INV[h, i] = inv
            o = dot_nn(VT[h, :, keys], (e * inv).astype(bf16))
            o = jnp.concatenate([o[:, :RB], o[:, RB:]], axis=0)
            MX[r, pl.ds(pl.multiple_of(h * 128, 128), 128)] = jnp.transpose(o).astype(bf16)

        per_block(half, work)

    def attention_out(half):
        if half == 0:
            ag_wait(1)
        a_produce(half, lambda d: dot_nt(MX[rows(d, RB), :], W[:, pl.ds(2 * QW, QW)]))

    def after_attention(h):
        def use(r, at, summed):
            v = Tk[at, :].astype(f32) + summed
            RES[r, :] = v
            n = v * lax.rsqrt(jnp.mean(v * v, axis=1, keepdims=True) + epsilon)
            NF[at, :] = (n * gf_ref[...]).astype(bf16)

        a_total(h, use)
        nf_start(h)

    def ffn(j, half):
        if j == 0:
            nf_wait(half == 1)
        if half == 0:
            ag_wait(2 + j)
        elif j == 0:
            nf_done()

        def step(i):
            r = rows(own_first(half, i), RB)
            n = NF[r, :]
            gate = dot_nn(n, W[:, pl.ds(PW + 2 * FC * j, FC)])
            up = dot_nn(n, W[:, pl.ds(PW + 2 * FC * j + FC, FC)])
            sig = 1.0 / (1.0 + jnp.exp(-gate))
            act = gate * sig
            HID[r, pl.ds(FC * j, FC)] = (act * up).astype(bf16)
            GG[r, pl.ds(2 * FC * j, FC)] = (up * (sig + act * (1.0 - sig))).astype(bf16)
            GG[r, pl.ds(2 * FC * j + FC, FC)] = act.astype(bf16)

        loop(2, step)

    def grad_weights(what):
        if what < 3:
            if what == 0:
                cot_wait(False)
                cot_wait(True)
                cot_done()
            weight_grad(Ct, [(what, HID.at[:, pl.ds(FC * what, FC)])])
        elif what < 6:
            weight_grad(NF, [(what, GG.at[:, pl.ds(2 * FC * (what - 3), 2 * FC)])])
        elif what == 6:
            weight_grad(Ct, [(6, MX)])
        else:
            weight_grad(Nm, [(7, GQ.at[:, pl.ds(0, QW)]), (9, GQ.at[:, pl.ds(QW, 2 * KW)])])

    def grad_hidden(j, half):
        if half == 0:
            ag_wait(5 + j)

        def step(i):
            r = rows(other_first(half, i), RB)
            gh = dot_nn(Ct[r, :], W[:, pl.ds(down0 + FC * j, FC)])
            a, b = pl.ds(2 * FC * j, FC), pl.ds(2 * FC * j + FC, FC)
            GG[r, a] = (gh * GG[r, a].astype(f32)).astype(bf16)
            GG[r, b] = (gh * GG[r, b].astype(f32)).astype(bf16)

        loop(2, step)

    def grad_ffn_norm(half):
        if half == 0:
            a_done()
        n_produce(half, lambda d: dot_nt(GG[rows(d, RB), :], W[:, pl.ds(PW, 2 * F)]))

    def after_ffn(h):
        def use(r, at, gy):
            v = RES[r, :]
            inv = lax.rsqrt(jnp.mean(v * v, axis=1, keepdims=True) + epsilon)
            n = v * inv
            VEC[1:2, :] += jnp.sum(gy * n, axis=0, keepdims=True)
            g = gy * gf_ref[...]
            g = inv * (g - n * jnp.mean(g * n, axis=1, keepdims=True))
            Ct[at, :] = (Ct[at, :].astype(f32) + g).astype(bf16)

        n_total(h, use)
        rl_start(h)

    def grad_mixed(half):
        rl_wait(half == 1)
        if half == 0:
            DKV[...] = jnp.zeros(DKV.shape, f32)

        def step(i):
            r = rows(own_first(half, i), RB)
            g = dot_nn(Ct[r, :], W[:, pl.ds(2 * QW, QW)]).astype(bf16)
            for p in range(2):
                DO[p, 0, r, :] = g[:, 128 * p : 128 * p + 64]
                DO[p, 1, r, :] = g[:, 128 * p + 64 : 128 * p + 128]

        loop(2, step)

    def attend_back(half):
        def work(h, i, keys, bias, r):
            q = QS[h, :, r, :].reshape(2 * RB, 64)
            do = DO[h, :, r, :].reshape(2 * RB, 64)
            p = jnp.exp(dot_nt(KS[h, keys, :], q) + bias) * INV[h, i]
            dp = dot_nt(VS[h, keys, :], do)
            ds = (p * (dp - jnp.sum(p * dp, axis=0, keepdims=True))).astype(bf16)
            DKV[h, keys, :] += jnp.concatenate([dot_nn(ds, q), dot_nn(p.astype(bf16), do)], axis=1)
            g = dot_nn(KT[h, :, keys], ds) * 0.125
            g = jnp.concatenate([g[:, :RB], g[:, RB:]], axis=0)
            DQ[r, pl.ds(pl.multiple_of(h * 128, 128), 128)] = jnp.transpose(g)

        per_block(half, work)

    def project_back():
        def step(i):
            r = rows(i, RB)
            cos, sin = CS[r, :], SN[r, :]
            for p in range(3):
                if p < 2:
                    g = DQ[r, pl.ds(128 * p, 128)]
                else:
                    g = jnp.concatenate([DKV[0, r, pl.ds(0, 64)], DKV[1, r, pl.ds(0, 64)]], axis=1)
                g = g * cos - turn(g) * sin
                v = PRE[r, pl.ds(128 * p, 128)]
                inv = lax.rsqrt(head_mean(v * v) + epsilon)
                n = v * inv
                s = pl.ds(0 if p < 2 else 128, 128)
                VEC[2:3, s] += jnp.sum(g * n, axis=0, keepdims=True)
                g = g * (gain_q if p < 2 else gain_k)
                GQ[r, pl.ds(128 * p, 128)] = (inv * (g - n * head_mean(g * n))).astype(bf16)
            v = jnp.concatenate([DKV[0, r, pl.ds(64, 64)], DKV[1, r, pl.ds(64, 64)]], axis=1)
            GQ[r, pl.ds(384, 128)] = v.astype(bf16)

        loop(nb, step)

    def gn_core(i, k, xx, cc):
        return rc(
            PN.at[rows(i, RB), pl.ds(pl.multiple_of((xx * 2 + cc) * CW, CW), CW)],
            AC.at[rows(i, RB), pl.ds(pl.multiple_of(xx * CW, CW), CW)],
            gn_s.at[i, k], gn_r.at[i, k], cpeer,
        )

    def gn_x(i):
        return rc(SC.at[rows(i, RB), :], BC.at[rows(i, RB), :], gn_s.at[i, 2], gn_r.at[i, 2], xpeer)

    others = [(0, x * 2 + 1 - c, cpeer), (1, (1 - x) * 2 + c, xpeer), (2, (1 - x) * 2 + 1 - c, dpeer)]
    gains = VY.shape[0]
    vec_y = rc(VSUM.at[pl.ds(0, gains), :], VY, vec_s.at[3], vec_r.at[3], ypeer)

    def vec_copy(i, which, dev):
        return rc(VCOL.at[which], VCOL.at[which], vec_s.at[i], vec_r.at[i], dev)

    def vz_copy(k, src):
        return rc(VZ.at[src], VZ.at[src], vz_s.at[k], vz_r.at[k], zdev((z + k) % nz))

    def gn_produce():
        def step(i):
            r = rows(i, RB)
            g = dot_nt(GQ[r, :], W[:, pl.ds(0, 2 * QW)])
            PN[r, :] = g.astype(bf16)
            gn_core(i, 0, 1 - x, 1 - c).start()
            gn_core(i, 1, x, 1 - c).start()
            g = g * (Tk[r, :].astype(f32) * R1[r, pl.ds(0, 1)])
            VEC[0:1, :] += jnp.sum(g, axis=0, keepdims=True)
            s = jnp.sum(g * ga_ref[...], axis=1, keepdims=True)
            VEC[3:4, r] = jnp.transpose(jnp.broadcast_to(s, (RB, 128)))[0:1, :]

        loop(nb, step)
        for i in range(D // 128):
            s = pl.ds(128 * i, 128)
            VCOL[col, pl.ds(i, 1), :] = VEC[0:1, s]
            VCOL[col, pl.ds(D // 128 + i, 1), :] = VEC[1:2, s]
        for i in range(2):
            VCOL[col, pl.ds(D // 64 + i, 1), :] = VEC[2:3, pl.ds(128 * i, 128)]
        for i in range(T // 128):
            VCOL[col, pl.ds(gains + i, 1), :] = VEC[3:4, pl.ds(128 * i, 128)]
        for i, _, dev in others:
            vec_copy(i, col, dev).start()

    def gn_middle():
        def step(i):
            r = rows(i, RB)
            gn_core(i, 0, 1 - x, c).wait_recv()
            a = PN[r, pl.ds(pl.multiple_of(((1 - x) * 2 + c) * CW, CW), CW)].astype(f32)
            b = AC[r, pl.ds(pl.multiple_of((1 - x) * CW, CW), CW)].astype(f32)
            SC[r, :] = (a + b).astype(bf16)
            gn_x(i).start()

        loop(nb, step)

    def vec_col():
        for i, d, dev in others:
            vec_copy(i, d, dev).wait_recv()
        VSUM[...] = (VCOL[0] + VCOL[1]) + (VCOL[2] + VCOL[3])
        vec_y.start()

    def vec_row():
        vec_y.wait_recv()
        VZ[z] = VSUM[0:gains, :] + VY[...]
        loop(nz, lambda k: vz_copy(k, z).start(), 1)

    gt_copy = pltpu.make_async_copy(DQ, gt_h, out_sem.at[30])
    lo_out = pltpu.make_async_copy(LOC, lo_h, out_sem.at[31])

    def gn_finish():
        def step(i):
            r = rows(i, RB)
            gn_core(i, 1, x, c).wait_recv()
            gn_x(i).wait_recv()
            g = PN[r, mine].astype(f32) + AC[r, pl.ds(pl.multiple_of(x * CW, CW), CW)].astype(f32)
            g = (g + BC[r, :].astype(f32)) * ga_ref[:, mine]
            inv = R1[r, pl.ds(0, 1)]
            s = [VSUM[pl.ds(gains + 2 * i + j, 1), :] for j in range(2)]
            s = jnp.transpose(jnp.broadcast_to(jnp.concatenate(s, axis=1), (128, RB)))[:, 0:1] * (1.0 / D)
            n = Tk[r, mine].astype(f32) * inv
            DQ[r, :] = Ct[r, mine].astype(f32) + inv * (g - n * s)

        loop(nb, step)
        gt_copy.start()

    def lo_copy(i, d, dev):
        return rc(
            S0.at[:, pl.ds(pl.multiple_of(d * CW, CW), CW)], LOC.at[rows(col, RB), :], lo_s.at[i], lo_r.at[i], dev
        )

    def branch():
        n_done()
        for half in range(2):
            b_produce(half, lambda d: dot_nt(HID[rows(d, RB), :], W[:, pl.ds(down0, F)]))

    def block_out():
        def use(r, at, summed):
            S0[r, :] = (RES[r, :] + summed).astype(bf16)

        b_total(0, use)
        b_total(1, use)
        for i, d, dev in others:
            lo_copy(i, d, dev).start()
        LOC[rows(col, RB), :] = S0[:, mine]

    def block_out_wait():
        for i, d, dev in others:
            lo_copy(i, d, dev).wait_recv()
        lo_out.start()

    def finish():
        loop(nz, lambda k: vz_copy(k, (z + nz - k) % nz).wait_recv(), 1)
        gain_ref[...] = lax.fori_loop(1, nz, lambda k, t: t + VZ[k], VZ[0])
        tok_done()
        rl_done()
        b_done()
        for i, d, dev in others:
            lo_copy(i, d, dev).wait_send()
            vec_copy(i, col, dev).wait_send()
        vec_y.wait_send()

        def gn_done(i):
            gn_core(i, 0, 1 - x, 1 - c).wait_send()
            gn_core(i, 1, x, 1 - c).wait_send()
            gn_x(i).wait_send()

        loop(nb, gn_done)
        loop(nz, lambda k: vz_copy(k, z).wait_send(), 1)
        for ch in range(len(CH)):
            ag_done(ch)
        for ch in range(len(RCH)):
            rs_done(ch)
        gt_copy.wait()
        lo_out.wait()

    steps = {
        "gate_up": load_gate_up, "down": load_down, "toks": start_tokens, "cots": start_cotangent,
        "owny": own_y, "ownz": own_z, "fwd": forward, "tokf": tok_forward, "cotf": cot_forward,
        "tables": tables, "norm": norm_tokens, "project": project, "att": lambda half: rows_of_chip(False, half, attend), "aprod": attention_out,
        "amid": a_middle, "aft": after_attention, "nff": nf_forward, "ffn": ffn, "wg": grad_weights,
        "gh": grad_hidden, "gnfp": grad_ffn_norm, "gnfm": n_middle, "naft": after_ffn, "rlf": rl_forward,
        "gmix": grad_mixed, "ab": lambda half: rows_of_chip(True, half, attend_back), "snd": send_grad, "pb": project_back, "gnp": gn_produce, "gnm": gn_middle,
        "vc": vec_col, "vy": vec_row,
        "gnfin": gn_finish, "brp": branch, "brm": b_middle, "brf": block_out, "lof": block_out_wait,
        "mid": rs_mid, "relay": rs_relay, "pre": rs_pre, "fin": rs_fin, "end": finish,
    }
    for name, *which, who in ORDER:
        if name in ("fwd", "mid"):
            run = functools.partial(steps[name], *which, who == "m")
        else:
            run = functools.partial(steps[name], *which)
        if who == "a" or not tree:
            if who != "e" or name in ("fwd", "mid"):
                run()
        else:

            @pl.when(is_middle if who == "m" else jnp.logical_not(is_middle))
            def _():
                run()


def hand_out(*refs):
    sources, gains, targets, held, sem = refs[:9], refs[9], refs[10:19], refs[23:32], refs[32]
    loads = [pltpu.make_async_copy(a, b, sem.at[0, i]) for i, (a, b) in enumerate(zip(sources, held))]
    stores = [pltpu.make_async_copy(a, b, sem.at[1, i]) for i, (a, b) in enumerate(zip(held, targets))]
    for copy in loads:
        copy.start()
    attn, ffn, query, key = refs[19:23]
    n = attn.shape[1] // 128
    for i in range(n):
        attn[:, pl.ds(128 * i, 128)] = gains[pl.ds(i, 1), :]
        ffn[:, pl.ds(128 * i, 128)] = gains[pl.ds(n + i, 1), :]
    query[...] = gains[pl.ds(2 * n, 1), pl.ds(0, 64)] + gains[pl.ds(2 * n, 1), pl.ds(64, 64)]
    key[...] = gains[pl.ds(2 * n + 1, 1), pl.ds(0, 64)] + gains[pl.ds(2 * n + 1, 1), pl.ds(64, 64)]
    for load, store in zip(loads, stores):
        load.wait()
        store.start()
    for store in stores:
        store.wait()


def per_device(
    n_row, tokens, segment_ids, w_query, key_matrix, value_matrix, w_out, w_gate, w_up, w_down,
    norm_attn, norm_ffn, norm_query, norm_key, cotangent,
):
    T, CW = tokens.shape
    br, QW = w_query.shape
    KW = key_matrix.shape[1]
    F = w_gate.shape[1]
    D = br * n_row
    nz = n_row // 2
    PW = 2 * QW + 2 * KW
    WW = PW + 3 * F
    FC = F // 3
    nb = T // RB
    half = nb // 2 * RB
    area = (half + (longest + RB if half >= longest else 2 * half)) * (nb // 2)
    chunks = [(0, 2 * QW), (2 * QW, QW)]
    chunks += [(PW + 2 * FC * j, 2 * FC) for j in range(3)] + [(PW + 2 * F + FC * j, FC) for j in range(3)]
    start, width = chunks[4]
    last = 128
    grads = chunks[5:8] + chunks[2:4] + [(start, width - last), chunks[1], (0, QW), (start + width - last, last)]
    grads.append((QW, 2 * KW))
    gains = 2 * D // 128 + 8
    tree = nz == 4
    ag_pairs, rs_pairs = (AG_PAIRS, RS_PAIRS) if tree else ((), ())
    place, widths = [], [0, 0]
    for ch, (_, width) in enumerate(grads):
        paired = ch in rs_pairs
        place.append(widths[paired])
        widths[paired] += width
    plan = (nz, tree, chunks, grads, ag_pairs, rs_pairs, place)
    single, paired = widths[0], max(widths[1], 128)
    slots = 4 if tree else nz - 1
    vm, sem = pltpu.VMEM, pltpu.SemaphoreType.DMA
    scratch = [
        vm((D, WW), bf16), vm((QW, br), bf16), vm((F, br), bf16), vm((QW, br), f32), vm((F, br), f32),
        vm((D, 3 * F), bf16), vm((nz, br, single), bf16), vm((slots, br, single), bf16),
        vm((br, paired), bf16), vm((4, 2 * br, paired), bf16),
        vm((br, 2 * QW + 2 * F), f32), vm((T, D), bf16), vm((T, D), bf16), vm((T, D), bf16), vm((T, 128), f32),
        vm((T, 2 * QW), f32), vm((2, 2, T, 64), bf16), vm((2, T, 64), bf16), vm((2, T, 64), bf16),
        vm((2, 64, T), bf16), vm((2, 64, T), bf16), vm((2, 2, T, 64), bf16), vm((T, QW), bf16),
        vm((T, D), bf16), vm((2, RB, D), bf16), vm((RB, D), bf16), vm((RB, D), bf16), vm((RB, D), f32),
        vm((T, D), bf16), vm((T, 2 * F), bf16), vm((T, F), bf16),
        vm((T, 128), f32), vm((T, 128), f32), vm((area, RB), bf16), vm((2, nb, 1, 2 * RB), f32),
        vm((T, QW), f32), vm((2, T, 128), f32),
        vm((T, 2 * CW), bf16), vm((T, CW), bf16), vm((T, CW), bf16), vm((T, CW), bf16),
        vm((8, D), f32), vm((4, gains + T // 128, 128), f32), vm((gains + T // 128, 128), f32), vm((gains, 128), f32),
        vm((nz, gains, 128), f32),
        sem((13,)), sem((8, nz)), sem((8, nz)), sem((8, nz)), sem((8, nz)),
        sem((10, nz)), sem((10, nz)), sem((10, nz)), sem((10, nz)),
        sem((4, 2, 3)), sem((4, 2, 3)), sem((3, 4)), sem((3, 4)), sem((nb, 3)), sem((nb, 3)), sem((3,)), sem((3,)),
        sem((4,)), sem((4,)), sem((nz,)), sem((nz,)), sem((32,)),
    ]
    whole, hbm = pl.BlockSpec(memory_space=pltpu.VMEM), pl.BlockSpec(memory_space=pl.ANY)
    shape = jax.ShapeDtypeStruct
    results = (
        shape((T, CW), bf16), shape((T, CW), f32), shape((br, QW), f32), shape((br, KW), f32), shape((br, KW), f32),
        shape((QW, br), f32), shape((br, F), f32), shape((br, F), f32), shape((F, br), f32),
    )
    outs = pl.pallas_call(
        functools.partial(layer_kernel, plan),
        out_shape=results + (shape((gains, 128), f32),),
        in_specs=[hbm, whole] + [hbm] * 7 + [whole] * 4 + [hbm],
        out_specs=(hbm,) * 9 + (whole,),
        scratch_shapes=scratch,
        compiler_params=pltpu.CompilerParams(
            collective_id=0, has_side_effects=True, vmem_limit_bytes=64 * 2**20
        ),
        name="layer",
    )(
        tokens, segment_ids, w_query, key_matrix, value_matrix, w_out, w_gate, w_up, w_down,
        norm_attn[None], norm_ffn[None], norm_query[None], norm_key[None], cotangent,
    )
    gain = shape((1, D), f32)
    head_gain = shape((1, norm_query.shape[0]), f32)
    outs = pl.pallas_call(
        hand_out,
        out_shape=results + (gain, gain, head_gain, head_gain),
        in_specs=[pl.BlockSpec(memory_space=pltpu.HBM)] * 9 + [whole],
        out_specs=(pl.BlockSpec(memory_space=pltpu.HBM),) * 9 + (whole,) * 4,
        scratch_shapes=[vm(v.shape, v.dtype) for v in results] + [sem((2, 9))],
        compiler_params=pltpu.CompilerParams(vmem_limit_bytes=63 * 2**20),
        name="hand_out",
    )(*outs)
    return outs[:9] + tuple(v[0] for v in outs[9:])


def solution(mesh):
    in_specs = (
        P("row", "col"), P("row", None), P("row", "col"), P("row", "col"), P("row", "col"), P("col", "row"),
        P("row", "col"), P("row", "col"), P("col", "row"), P(), P(), P(), P(), P("row", "col"),
    )
    out_specs = (
        P("row", "col"), P("row", "col"), P("row", "col"), P("row", "col"), P("row", "col"), P("col", "row"),
        P("row", "col"), P("row", "col"), P("col", "row"), P(), P(), P(), P(),
    )
    return jax.shard_map(
        functools.partial(per_device, mesh.shape["row"]),
        mesh=mesh, in_specs=in_specs, out_specs=out_specs, check_vma=False,
    )
```

```python
import functools
import math

import jax
import jax.numpy as jnp
from jax import lax
from jax.experimental import pallas as pl
from jax.experimental.pallas import tpu as pltpu
from jax.sharding import PartitionSpec as P

epsilon = 1e-05
rope_base = 1000000.0
longest = 512
ids = 8
f32, bf16 = jnp.float32, jnp.bfloat16
MESH = pl.DeviceIdType.MESH
RB = 256


def dot_nn(a, b):
    return lax.dot_general(a, b, (((1,), (0,)), ((), ())), preferred_element_type=f32)


def dot_nt(a, b):
    return lax.dot_general(a, b, (((1,), (1,)), ((), ())), preferred_element_type=f32)


def rows(i, n):
    return pl.ds(pl.multiple_of(i * n, n), n)


LAST = 128
AG_PAIRS, RS_PAIRS = (5, 6), (0, 1, 2)
ORDER = [
    ("owny", 0, "a"), ("ownz", 0, "a"), ("out", "a"), ("owny", 1, "a"), ("ownz", 1, "a"), ("gate_up", "a"),
    ("owny", 2, "a"), ("down", "a"), ("owny", 7, "a"), ("fwd", 0, 1, "e"), ("ownz", 2, "a"), ("toks", "a"),
    ("tables", "a"), ("cots", "a"), ("owny", 3, "a"), ("ownz", 7, "a"), ("fwd", 0, 1, "m"), ("fwd", 0, 2, "e"),
    ("fwd", 0, 2, "m"), ("fwd", 0, 3, "e"), ("fwd", 1, 1, "e"), ("fwd", 0, 3, "m"), ("tokf", "a"),
    ("fwd", 1, 1, "m"), ("fwd", 1, 2, "e"), ("fwd", 1, 2, "m"), ("owny", 5, "a"), ("fwd", 1, 3, "m"),
    ("ownz", 3, "a"), ("norm", "a"), ("fwd", 1, 3, "e"), ("fwd", 2, 1, "m"), ("fwd", 2, 2, "m"), ("owny", 4, "a"),
    ("owny", 6, "a"), ("ownz", 4, "a"), ("project", "a"), ("fwd", 2, 3, "m"), ("fwd", 3, 1, "m"), ("att", 0, "a"),
    ("aprod", 0, "a"), ("fwd", 4, 1, "e"), ("fwd", 2, 1, "e"), ("fwd", 3, 2, "m"), ("ownz", 5, "a"), ("amid", "a"),
    ("fwd", 5, 1, "m"), ("fwd", 3, 3, "m"), ("att", 1, "a"), ("fwd", 4, 1, "m"), ("cotf", "a"), ("fwd", 4, 2, "m"),
    ("fwd", 2, 2, "e"), ("aprod", 1, "a"), ("fwd", 4, 3, "m"), ("fwd", 3, 1, "e"), ("fwd", 5, 2, "m"),
    ("fwd", 7, 1, "m"), ("ownz", 6, "a"), ("aft", 0, "a"), ("fwd", 7, 1, "e"), ("fwd", 5, 3, "m"),
    ("fwd", 2, 3, "e"), ("fwd", 7, 2, "m"), ("fwd", 7, 3, "m"), ("fwd", 5, 1, "e"), ("aft", 1, "a"),
    ("fwd", 3, 2, "e"), ("fwd", 5, 2, "e"), ("fwd", 3, 3, "e"), ("fwd", 6, 1, "e"), ("nff", 0, "a"),
    ("fwd", 4, 2, "e"), ("nff", 1, "a"), ("fwd", 4, 3, "e"), ("ffn", 0, 0, "a"), ("fwd", 6, 2, "e"),
    ("fwd", 6, 1, "m"), ("fwd", 6, 2, "m"), ("fwd", 6, 3, "m"), ("ffn", 0, 1, "a"), ("wg", 0, "a"),
    ("ffn", 1, 0, "a"), ("ffn", 1, 1, "a"), ("fwd", 5, 3, "e"), ("wg", 1, "a"), ("fwd", 7, 2, "e"),
    ("fwd", 6, 3, "e"), ("gh", 0, 0, "a"), ("relay", 0, 0, "m"), ("gh", 0, 1, "a"), ("fwd", 7, 3, "e"),
    ("wg", 3, "a"), ("ffn", 2, 0, "a"), ("ffn", 2, 1, "a"), ("wg", 2, "a"), ("gh", 1, 0, "a"), ("gh", 2, 0, "a"),
    ("gnfp", 0, "a"), ("mid", 3, 0, "e"), ("gh", 1, 1, "a"), ("gnfm", "a"), ("relay", 0, 1, "m"), ("gh", 2, 1, "a"),
    ("mid", 3, 0, "m"), ("relay", 1, 0, "m"), ("gnfp", 1, "a"), ("wg", 5, "a"), ("mid", 3, 1, "e"), ("snd", 8, "a"),
    ("naft", 0, "a"), ("wg", 4, "a"), ("mid", 5, 0, "m"), ("relay", 2, 0, "m"), ("relay", 1, 1, "m"),
    ("naft", 1, "a"), ("mid", 5, 1, "m"), ("gmix", 0, "a"), ("mid", 3, 1, "m"), ("mid", 5, 0, "e"), ("ab", 0, "a"),
    ("mid", 5, 2, "m"), ("mid", 3, 2, "e"), ("mid", 5, 1, "e"), ("rlf", 0, "a"), ("rlf", 1, "a"),
    ("mid", 8, 0, "e"), ("mid", 8, 1, "e"), ("relay", 3, 0, "m"), ("relay", 2, 1, "m"), ("relay", 3, 1, "m"),
    ("mid", 5, 2, "e"), ("mid", 8, 0, "m"), ("mid", 3, 2, "m"), ("mid", 8, 2, "e"), ("gmix", 1, "a"), ("brp", "a"),
    ("mid", 4, 0, "e"), ("wg", 6, "a"), ("relay", 5, 0, "m"), ("brm", "a"), ("mid", 8, 1, "m"), ("mid", 4, 0, "m"),
    ("ab", 1, "a"), ("mid", 4, 1, "e"), ("pb", "a"), ("relay", 5, 1, "m"), ("mid", 8, 2, "m"), ("mid", 4, 1, "m"),
    ("gnp", "a"), ("mid", 6, 0, "e"), ("mid", 4, 2, "m"), ("relay", 8, 0, "m"), ("relay", 4, 0, "m"),
    ("wg", 7, "a"), ("mid", 6, 1, "e"), ("gnm", "a"), ("mid", 6, 0, "m"), ("relay", 8, 1, "m"), ("mid", 6, 2, "e"),
    ("brf", "a"), ("relay", 4, 1, "m"), ("mid", 6, 1, "m"), ("mid", 9, 0, "m"), ("mid", 7, 0, "e"),
    ("mid", 7, 0, "m"), ("mid", 6, 2, "m"), ("mid", 9, 0, "e"), ("vc", "a"), ("mid", 7, 1, "e"), ("pre", 2, "e"),
    ("pre", 1, "e"), ("relay", 6, 0, "m"), ("mid", 7, 1, "m"), ("mid", 9, 1, "m"), ("relay", 6, 1, "m"),
    ("fin", 5, "a"), ("pre", 2, "m"), ("mid", 9, 1, "e"), ("relay", 7, 0, "m"), ("pre", 1, "m"), ("mid", 9, 2, "m"),
    ("pre", 0, "e"), ("mid", 7, 2, "m"), ("mid", 4, 2, "e"), ("pre", 0, "m"), ("relay", 9, 0, "m"),
    ("relay", 9, 1, "m"), ("mid", 9, 2, "e"), ("fin", 8, "a"), ("relay", 7, 1, "m"), ("fin", 6, "a"), ("vy", "a"),
    ("fin", 4, "a"), ("mid", 7, 2, "e"), ("fin", 3, "a"), ("fin", 2, "a"), ("fin", 1, "a"), ("fin", 9, "a"),
    ("gnfin", "a"), ("fin", 7, "a"), ("fin", 0, "a"), ("lof", "a"), ("end", "a"),
]


def layer_kernel(
    plan,
    tok_h, seg_h, wq_h, wk_h, wv_h, wo_h, wg_h, wu_h, wd_h, ga_h, gf_h, gq_h, gk_h, cot_h,
    lo_h, gt_h, gquery_h, gkey_h, gvalue_h, gout_h, ggate_h, gup_h, gdown_h, gain_h,
    W, WO, WD, GFO, GFD, G, RY, RZ, RYP, RZP, GF, Tk, Ct, Nm, R1, PRE, QS, KS, VS, KT, VT, DO, MX, PB, A0, B0, S0,
    RES, NF, GG, HID, CS, SN, BIAS, INV, DQ, DKV, AC, BC, SC, LOC, VEC, VCOL, VSUM, VY, VZ,
    seg_ref, ga_ref, gf_ref, gq_ref, gk_ref, gain_ref,
    loc_sem, agz_s, agz_r, agy_s, agy_r, rsy_s, rsy_r, rsz_s, rsz_r,
    cag_s, cag_r, crs_s, crs_r, gn_s, gn_r, lo_s, lo_r, vec_s, vec_r, vz_s, vz_r, out_sem,
):
    nz, tree, CH, RCH, ag_pairs, rs_pairs, place = plan
    T, D = Tk.shape
    br = RY.shape[1]
    QW, KW = PRE.shape[1] // 2, PRE.shape[1] // 4
    PW = 2 * QW + 2 * KW
    F = HID.shape[1]
    FC = F // 3
    HB = RB // 2
    down0 = PW + 2 * F
    nb = T // RB
    CW = D // 4
    GQ = GG.at[:, pl.ds(PW, 2 * QW)]
    PN = GG.at[:, pl.ds(PW + 2 * QW, D)]
    row, col = lax.axis_index("row"), lax.axis_index("col")
    z, y = row // 2, row % 2
    x, c = col // 2, col % 2
    ypeer = (row + 1 - 2 * y, col)
    cpeer = (row, col + 1 - 2 * c)
    xpeer = (row, (1 - x) * 2 + c)
    dpeer = (row, (1 - x) * 2 + 1 - c)
    partner = z + 1 - 2 * (z % 2)
    is_middle = (z == 1) | (z == 2)
    near, far = 2 - z // 2, 3 - 3 * (z // 2)

    def zdev(zz):
        return (zz * 2 + y, col)

    def zsrc(k):
        return [z, partner, near, far][k] if tree else (z + nz - k) % nz

    def zto(i):
        return [near, far, partner, z][i]

    def rc(src, dst, ss, rs, dev):
        return pltpu.make_async_remote_copy(
            src_ref=src, dst_ref=dst, send_sem=ss, recv_sem=rs, device_id=dev, device_id_type=MESH
        )

    def loop(n, body, first=0):
        def step(i, carry):
            body(i)
            return carry

        lax.fori_loop(first, n, step, 0)

    own = rows(row, br)
    mine = pl.ds(pl.multiple_of(col * CW, CW), CW)
    local = [
        (wq_h, W.at[own, pl.ds(0, QW)]),
        (wk_h, W.at[own, pl.ds(QW, KW)]),
        (wv_h, W.at[own, pl.ds(QW + KW, KW)]),
        (wo_h, WO),
        (tok_h, Tk.at[:, mine]),
        (cot_h, Ct.at[:, mine]),
    ]
    for j in range(3):
        local.append((wg_h.at[:, pl.ds(FC * j, FC)], W.at[own, pl.ds(PW + 2 * FC * j, FC)]))
        local.append((wu_h.at[:, pl.ds(FC * j, FC)], W.at[own, pl.ds(PW + 2 * FC * j + FC, FC)]))
    local.append((wd_h, WD))
    local += [(seg_h, seg_ref), (ga_h, ga_ref), (gf_h, gf_ref), (gq_h, gq_ref), (gk_h, gk_ref)]
    local = [pltpu.make_async_copy(s, d, loc_sem.at[i]) for i, (s, d) in enumerate(local)]

    def wblk(ch, zz, yy):
        start, width = CH[ch]
        return W.at[rows(zz * 2 + yy, br), pl.ds(start, width)]

    def wpair(ch, zz):
        start, width = CH[ch]
        return W.at[rows(zz, 2 * br), pl.ds(start, width)]

    def ag_z(ch, k, src, slot, dev):
        b = wpair(ch, src) if ch in ag_pairs else wblk(ch, src, y)
        return rc(b, b, agz_s.at[ch, k], agz_r.at[ch, slot], zdev(dev))

    def ag_y(ch, k, src, yy):
        b = wblk(ch, src, yy)
        return rc(b, b, agy_s.at[ch, k], agy_r.at[ch, k], ypeer)

    def own_y(ch):
        ag_y(ch, 0, z, y).start()

    def own_z(ch):
        if ch in ag_pairs:
            ag_y(ch, 0, z, 1 - y).wait_recv()
        if tree:
            ag_z(ch, 0, z, 1, partner).start()
            ag_z(ch, 1, z, jnp.where(is_middle, 2, 3), near).start()
        else:
            loop(nz, lambda k: ag_z(ch, k, z, k, (z + k) % nz).start(), 1)

    def forward(ch, k, middle):
        if not tree:
            if k == 3 and middle:

                def step(k):
                    ag_z(ch, k, zsrc(k), k, z).wait_recv()
                    ag_y(ch, k, zsrc(k), y).start()

                loop(nz, step, 1)
            return
        relayed = middle and k >= 2
        if ch in ag_pairs and not relayed:
            return
        ag_z(ch, k, zsrc(k), k, partner).wait_recv()
        if relayed:
            ag_z(ch, k, zsrc(k), k, partner).start()
        if ch not in ag_pairs:
            ag_y(ch, k, zsrc(k), y).start()

    def ag_wait(ch):
        if not tree:
            loop(nz, lambda k: ag_y(ch, k, zsrc(k), 1 - y).wait_recv())
        elif ch in ag_pairs:
            ag_z(ch, 0, partner, 1, partner).wait_recv()

            @pl.when(jnp.logical_not(is_middle))
            def _():
                ag_z(ch, 0, near, 2, partner).wait_recv()
                ag_z(ch, 0, far, 3, partner).wait_recv()

        else:
            for k in range(4):
                ag_y(ch, k, zsrc(k), 1 - y).wait_recv()

    def ag_done(ch):
        if not tree:
            loop(nz, lambda k: ag_y(ch, k, zsrc(k), y).wait_send())
            loop(nz, lambda k: ag_z(ch, k, z, k, z).wait_send(), 1)
            return
        for k in range(1 if ch in ag_pairs else 4):
            ag_y(ch, k, zsrc(k), y).wait_send()
        ag_z(ch, 0, z, 1, partner).wait_send()
        ag_z(ch, 1, z, 2, near).wait_send()

        @pl.when(is_middle)
        def _():
            ag_z(ch, 2, near, 2, partner).wait_send()
            ag_z(ch, 3, far, 3, partner).wait_send()

    def cag(n, block, parts=1):
        def copy(i, d, dev, h):
            return rc(block(d, h), block(d, h), cag_s.at[n, h, i], cag_r.at[n, h, i], dev)

        def start(h=0):
            copy(0, col, cpeer, h).start()
            copy(1, col, xpeer, h).start()

        def forward(h=0):
            copy(1, (1 - x) * 2 + c, xpeer, h).wait_recv()
            copy(2, (1 - x) * 2 + c, cpeer, h).start()

        def wait(far):
            for h in range(parts):
                if far:
                    copy(2, (1 - x) * 2 + 1 - c, cpeer, h).wait_recv()
                else:
                    copy(0, x * 2 + 1 - c, cpeer, h).wait_recv()

        def done():
            for h in range(parts):
                copy(0, col, cpeer, h).wait_send()
                copy(1, col, xpeer, h).wait_send()
                copy(2, (1 - x) * 2 + c, cpeer, h).wait_send()

        return start, forward, wait, done

    def col_block(ref):
        return lambda d, h: ref.at[:, pl.ds(pl.multiple_of(d * CW, CW), CW)]

    def row_block(ref):
        return lambda d, h: ref.at[rows(d * 2 + h, HB), :]

    tok_start, tok_forward, tok_wait, tok_done = cag(0, col_block(Tk))
    cot_start, cot_forward, cot_wait, cot_done = cag(1, col_block(Ct))
    nf_start, nf_forward, nf_wait, nf_done = cag(2, row_block(NF), 2)
    rl_start, rl_forward, rl_wait, rl_done = cag(3, row_block(Ct), 2)

    def crs(n, A, B, S):
        def to_core(i, xx, cc):
            return rc(PB.at[rows(xx * 2 + cc, RB), :], A(xx), crs_s.at[n, i], crs_r.at[n, i], cpeer)

        def to_x(h):
            half = rows(h, HB)
            return rc(S.at[half, :], B.at[half, :], crs_s.at[n, 2 + h], crs_r.at[n, 2 + h], xpeer)

        def produce(half, part):
            def step(i):
                xx = jnp.where(i < 2, 1 - x, x)
                cc = jnp.where(i % 2 == 0, 1 - c, c)
                PB[rows(xx * 2 + cc, RB), :] = part(xx * 2 + cc).astype(bf16)

                @pl.when(i % 2 == 0)
                def _():
                    to_core(i // 2, xx, 1 - c).start()

            loop(2 * half + 2, step, 2 * half)

        def middle():
            to_core(0, 1 - x, c).wait_recv()

            def step(i):
                r = rows(i, 32)
                block = PB[pl.ds(pl.multiple_of(((1 - x) * 2 + c) * RB + i * 32, 32), 32), :]
                S[r, :] = (block.astype(f32) + A(1 - x)[r, :].astype(f32)).astype(bf16)

            for h in range(2):
                loop(HB // 32 * (h + 1), step, HB // 32 * h)
                to_x(h).start()

        def total(h, use):
            if h == 0:
                to_core(1, x, c).wait_recv()
            to_x(h).wait_recv()

            def step(i):
                r = rows(i, 32)
                at = pl.ds(pl.multiple_of(col * RB + i * 32, 32), 32)
                use(r, at, PB[at, :].astype(f32) + A(x)[r, :].astype(f32) + B[r, :].astype(f32))

            loop(HB // 32 * (h + 1), step, HB // 32 * h)

        def done():
            to_core(0, 1 - x, 1 - c).wait_send()
            to_core(1, x, 1 - c).wait_send()
            to_x(0).wait_send()
            to_x(1).wait_send()

        return produce, middle, total, done

    a_produce, a_middle, a_total, a_done = crs(0, lambda i: A0.at[i], B0, S0)
    n_produce, n_middle, n_total, n_done = crs(1, lambda i: A0.at[i], B0, S0)
    b_produce, b_middle, b_total, b_done = crs(
        2, lambda i: NF.at[rows(i, RB), :], NF.at[pl.ds(2 * RB, RB), :], NF.at[pl.ds(3 * RB, RB), :]
    )

    def other_first(half, i):
        return jnp.where(half == 0, 1 - x, x) * 2 + jnp.where(i == 0, 1 - c, c)

    def own_first(half, i):
        return jnp.where(half == 0, x, 1 - x) * 2 + jnp.where(i == 0, c, 1 - c)

    def rows_of_chip(mine_first, half, work):
        for xx in range(2):

            @pl.when(x == (xx if mine_first == (half == 0) else 1 - xx))
            def _():
                work(xx)

    def gcol(ch):
        start, width = RCH[ch]
        return (G, start - PW, width) if start >= PW else (GG, start, width)

    def gblk(ch, zz, yy):
        ref, start, width = gcol(ch)
        return ref.at[rows(zz * 2 + yy, br), pl.ds(start, width)]

    def part_of(ch):
        return pl.ds(place[ch], RCH[ch][1])

    def rs_y(ch, zz, yy):
        landing = RYP.at[:, part_of(ch)] if ch in rs_pairs else RY.at[zz, :, part_of(ch)]
        return rc(gblk(ch, zz, yy), landing, rsy_s.at[ch, zz], rsy_r.at[ch, zz], ypeer)

    def rs_z(ch, k, zz, slot, dev):
        if ch in rs_pairs:
            ref, start, width = gcol(ch)
            src, dst = ref.at[rows(zz, 2 * br), pl.ds(start, width)], RZP.at[slot, :, part_of(ch)]
        else:
            src, dst = RY.at[zz, :, part_of(ch)], RZ.at[slot, :, part_of(ch)]
        return rc(src, dst, rsz_s.at[ch, k], rsz_r.at[ch, slot], zdev(dev))

    zper = RB // (2 * br)

    def weight_grad(left, pieces):
        def one(i, d):
            lt = jnp.transpose(left[:, rows(d, RB)])
            for ch, right in pieces:
                ref, start, width = gcol(ch)
                ref[rows(d, RB), pl.ds(start, right.shape[1])] = dot_nn(lt, right[...]).astype(bf16)
                if ch not in rs_pairs:
                    loop(zper, lambda s: rs_y(ch, d * zper + s, 1 - y).start())
                else:

                    @pl.when((i == 2) | ((i < 2) & jnp.logical_not(is_middle)))
                    def _():
                        rs_z(ch, i, d, i, partner).start()

        if tree:

            def step(i):
                one(i, jnp.where(i == 0, near, jnp.where(i == 1, far, jnp.where(i == 2, partner, z))))

            loop(4, step)
        else:
            loop(D // RB, lambda i: one(i, (row * br // RB + 1 + i) % (D // RB)))

    def send_grad(ch):
        if tree:
            for i in range(4):
                if ch not in rs_pairs:
                    rs_y(ch, zto(i), 1 - y).start()
                elif i == 2:
                    rs_z(ch, i, zto(i), i, partner).start()
                elif i < 2:

                    @pl.when(jnp.logical_not(is_middle))
                    def _():
                        rs_z(ch, i, zto(i), i, partner).start()

        else:
            loop(nz, lambda k: rs_y(ch, k, 1 - y).start())

    def rs_mid(ch, i, middle):
        ref, gstart, width = gcol(ch)

        def one(zz):
            rs_y(ch, zz, y).wait_recv()

            def add(j):
                r = rows(j, 16)
                g = ref[pl.ds(pl.multiple_of((zz * 2 + y) * br + j * 16, 16), 16), pl.ds(gstart, width)]
                t = RY[zz, r, part_of(ch)]
                RY[zz, r, part_of(ch)] = (g.astype(f32) + t.astype(f32)).astype(bf16)

            loop(br // 16, add)

        if not tree:
            if i == 2 and middle:

                def step(k):
                    zz = (z + k) % nz
                    one(zz)
                    rs_z(ch, k, zz, k - 1, zz).start()

                loop(nz, step, 1)
        elif ch not in rs_pairs:
            one(zto(i))
            if i == 2 or not middle:
                rs_z(ch, i, zto(i), i, partner).start()

    def rs_relay(ch, i):
        if not tree:
            return
        zz = zto(i)
        rs_z(ch, i, zz, i, partner).wait_recv()
        ref, gstart, width = gcol(ch)

        def add(j):
            r = rows(j, 16)
            if ch in rs_pairs:
                at = pl.ds(pl.multiple_of(zz * 2 * br + j * 16, 16), 16)
                t = ref[at, pl.ds(gstart, width)].astype(f32) + RZP[i, r, part_of(ch)].astype(f32)
                ref[at, pl.ds(gstart, width)] = t.astype(bf16)
            else:
                t = RY[zz, r, part_of(ch)].astype(f32) + RZ[i, r, part_of(ch)].astype(f32)
                RY[zz, r, part_of(ch)] = t.astype(bf16)

        loop((2 * br if ch in rs_pairs else br) // 16, add)
        rs_z(ch, i, zz, 3, zz).start()

    def rs_pre(ch):
        if ch not in rs_pairs:
            return
        for slot in (2, 3):
            rs_z(ch, 2, z, slot, partner).wait_recv()
        ref, gstart, width = gcol(ch)

        def add(j):
            at = pl.ds(pl.multiple_of((z * 2 + 1 - y) * br + j * 16, 16), 16)
            r = pl.ds(pl.multiple_of((1 - y) * br + j * 16, 16), 16)
            t = ref[at, pl.ds(gstart, width)].astype(f32)
            t = t + RZP[2, r, part_of(ch)].astype(f32) + RZP[3, r, part_of(ch)].astype(f32)
            ref[at, pl.ds(gstart, width)] = t.astype(bf16)

        loop(br // 16, add)
        rs_y(ch, z, 1 - y).start()

    def outs(ch):
        start, width = RCH[ch]
        if start >= down0:
            pairs = [(GFD.at[pl.ds(start - down0, width), :], gdown_h.at[pl.ds(start - down0, width), :])]
        elif start >= PW:
            third = (start - PW) // (2 * FC)
            at = start - PW - 2 * FC * third
            pairs = []
            for target, low in ((ggate_h, 0), (gup_h, FC)):
                first, last = max(at, low), min(at + width, low + FC)
                if first < last:
                    held = GF.at[:, pl.ds(start - 2 * KW + first - at, last - first)]
                    pairs.append((held, target.at[:, pl.ds(third * FC + first - low, last - first)]))
        elif start == 2 * QW:
            pairs = [(GFO, gout_h)]
        elif start == 0:
            pairs = [(GF.at[:, pl.ds(0, QW)], gquery_h)]
        else:
            pairs = [
                (GF.at[:, pl.ds(QW, KW)], gkey_h),
                (GF.at[:, pl.ds(QW + KW, KW)], gvalue_h),
            ]
        return [pltpu.make_async_copy(a, b, out_sem.at[3 * ch + i]) for i, (a, b) in enumerate(pairs)]

    def rs_fin(ch):
        ref, gstart, width = gcol(ch)
        start = RCH[ch][0]
        paired = ch in rs_pairs
        rs_y(ch, z, y).wait_recv()
        if not tree:
            loop(nz - 1, lambda k: rs_z(ch, 0, z, k, z).wait_recv())
        elif not paired:
            for slot in (2, 3):
                rs_z(ch, 0, z, slot, z).wait_recv()

        def total(r0, rn, c0, cn):
            r = pl.ds(r0, rn)
            g = ref[pl.ds(pl.multiple_of(row * br + r0, 16), rn), pl.ds(gstart + c0, cn)]
            part = pl.ds(place[ch] + c0, cn)
            if paired:
                rp = pl.ds(pl.multiple_of(y * br + r0, 16), rn)
                t = RZP[2, rp, part].astype(f32) + RZP[3, rp, part].astype(f32)
                return g.astype(f32) + t + RYP[r, part].astype(f32)
            t = g.astype(f32) + RY[z, r, part].astype(f32)
            if tree:
                return t + (RZ[2, r, part].astype(f32) + RZ[3, r, part].astype(f32))
            return lax.fori_loop(0, nz - 1, lambda k, t: t + RZ[k, r, part].astype(f32), t)

        if start >= down0 or start == 2 * QW:
            for c0 in range(0, width, 128):
                t = jnp.transpose(total(0, br, c0, 128))
                if start >= down0:
                    GFD[pl.ds(start - down0 + c0, 128), :] = t
                else:
                    GFO[pl.ds(c0, 128), :] = t
        else:
            at = start - 2 * KW if start >= PW else start

            def add(i):
                r0 = pl.multiple_of(i * 16, 16)
                GF[pl.ds(r0, 16), pl.ds(at, width)] = total(r0, 16, 0, width)

            loop(br // 16, add)
        for copy in outs(ch):
            copy.start()

    def rs_done(ch):
        if ch in rs_pairs:
            rs_y(ch, z, 1 - y).wait_send()
        else:
            loop(nz, lambda zz: rs_y(ch, zz, 1 - y).wait_send())
        if tree:
            for i in range(3):
                rs_z(ch, i, zto(i), 0, partner).wait_send()
        else:
            loop(nz, lambda k: rs_z(ch, k, z, 0, z).wait_send(), 1)
        for copy in outs(ch):
            copy.wait()

    bar = pltpu.get_barrier_semaphore()
    for dev in (ypeer, cpeer, xpeer, dpeer):
        pl.semaphore_signal(bar, inc=1, device_id=dev, device_id_type=MESH)

    def greet(k):
        pl.semaphore_signal(bar, inc=1, device_id=zdev((z + k) % nz), device_id_type=MESH)

    loop(nz, greet, 1)
    for i in (0, 1, 2, 4, 13, 14, 15, 16, 17, 3, 6, 7, 8, 9, 10, 11, 5, 12):
        local[i].start()
    for i in range(3):
        local[i].wait()
    pl.semaphore_wait(bar, 4 + nz - 1)

    def load_out():
        local[3].wait()
        W[own, pl.ds(2 * QW, QW)] = jnp.transpose(WO[...])

    def load_gate_up():
        for i in range(6, 12):
            local[i].wait()

    def load_down():
        local[12].wait()
        W[own, pl.ds(down0, F)] = jnp.transpose(WD[...])

    def start_tokens():
        local[4].wait()
        tok_start()

    def start_cotangent():
        local[5].wait()
        cot_start()

    lane = lax.broadcasted_iota(jnp.int32, (1, 128), 1)

    def head_gain(p):
        gain = (gq_ref if p < 2 else gk_ref)[...]
        return jnp.concatenate([gain, gain], axis=1)

    hb = nb // 2
    spans = []
    for half in range(2):
        low = max(0, RB * half * hb - longest)
        if half * RB * hb >= longest:
            spans.append((longest + RB, RB, low, sum(s[0] for s in spans) * hb))
        else:
            spans.append((RB * hb * (half + 1), 0, 0, sum(s[0] for s in spans) * hb))

    def tables():
        for i in range(13, 18):
            local[i].wait()
        VEC[...] = jnp.zeros(VEC.shape, f32)
        seg = seg_ref[...]
        first = jnp.zeros((1, T), jnp.int32)
        for d in range(ids):
            count = jnp.sum((seg == d).astype(f32), axis=1, keepdims=True).astype(jnp.int32)
            first = first + jnp.where(seg > d, count, 0)
        place = lax.broadcasted_iota(jnp.int32, (1, T), 1)
        inverse_freq = jnp.exp((lane % 32).astype(f32) * (-2.0 / 64 * math.log(rope_base)))
        CS[...] = jnp.transpose(jnp.broadcast_to((place - first).astype(f32), (128, T)))

        def fill(i):
            angle = CS[rows(i, 128), :] * inverse_freq
            sine = jnp.sin(angle)
            CS[rows(i, 128), :] = jnp.cos(angle)
            SN[rows(i, 128), :] = jnp.where(lane % 64 < 32, -sine, sine)

        loop(T // 128, fill)
        for i in range(nb):
            width, pace, start, at = spans[i // hb]
            start, at = start + pace * (i % hb), at + width * (i % hb)
            key_place = lax.broadcasted_iota(jnp.int32, (width, RB), 0) + start
            q_place, q_first = place[:, RB * i : RB * (i + 1)], first[:, RB * i : RB * (i + 1)]
            seen = (key_place <= q_place) & (key_place >= q_first)
            BIAS[pl.ds(at, width), :] = jnp.where(seen, 0.0, -1e30).astype(bf16)

    def head_mean(v):
        half_a = lax.broadcasted_iota(jnp.int32, (128, 128), 0) // 64
        half_b = lax.broadcasted_iota(jnp.int32, (128, 128), 1) // 64
        mean_matrix = jnp.where(half_a == half_b, 1.0 / 64, 0.0).astype(bf16)
        high = v.astype(bf16)
        low = (v - high.astype(f32)).astype(bf16)
        return dot_nn(high, mean_matrix) + dot_nn(low, mean_matrix)

    def turn(v):
        return jnp.where(lane % 64 < 32, pltpu.roll(v, 96, 1), pltpu.roll(v, 32, 1))

    def norm_tokens():
        tok_wait(False)
        tok_wait(True)

        def step(i):
            t = Tk[rows(i, 128), :].astype(f32)
            r = lax.rsqrt(jnp.mean(t * t, axis=1, keepdims=True) + epsilon)
            R1[rows(i, 128), :] = jnp.broadcast_to(r, (128, 128))
            Nm[rows(i, 128), :] = (t * r * ga_ref[...]).astype(bf16)

        loop(T // 128, step)

    def project():
        ag_wait(0)

        def step(i):
            r = rows(i, RB)
            PRE[r, :] = dot_nn(Nm[r, :], W[:, pl.ds(0, 2 * QW)])
            cos, sin = CS[r, :], SN[r, :]
            for p in range(3):
                v = PRE[r, pl.ds(128 * p, 128)]
                n = v * lax.rsqrt(head_mean(v * v) + epsilon)
                u = n * head_gain(p)
                u = (u * cos + turn(u) * sin).astype(bf16)
                if p < 2:
                    u = u * jnp.asarray(0.125, bf16)
                    QS[p, 0, r, :] = u[:, :64]
                    QS[p, 1, r, :] = u[:, 64:]
                else:
                    KS[0, r, :] = u[:, :64]
                    KS[1, r, :] = u[:, 64:]
                    ut = jnp.transpose(u)
                    KT[0, :, r] = ut[:64, :]
                    KT[1, :, r] = ut[64:, :]
            v = PRE[r, pl.ds(384, 128)].astype(bf16)
            VS[0, r, :] = v[:, :64]
            VS[1, r, :] = v[:, 64:]
            vt = jnp.transpose(v)
            VT[0, :, r] = vt[:64, :]
            VT[1, :, r] = vt[64:, :]

        loop(nb, step)

    def per_block(half, work):
        width, pace, low, at = spans[half]

        def step(n):
            i, h = n // 2, n % 2
            keys = pl.ds(pl.multiple_of(low + pace * i, RB), width) if pace else pl.ds(low, width)
            bias = BIAS[pl.ds(pl.multiple_of(at + width * i, RB), width), :].astype(f32)
            work(h, half * hb + i, keys, jnp.concatenate([bias, bias], axis=1), rows(half * hb + i, RB))

        loop(2 * hb, step)

    def attend(half):
        def work(h, i, keys, bias, r):
            q = QS[h, :, r, :].reshape(2 * RB, 64)
            e = jnp.exp(dot_nt(KS[h, keys, :], q) + bias)
            inv = 1.0 / jnp.sum(e, axis=0, keepdims=True)
            INV[h, i] = inv
            o = dot_nn(VT[h, :, keys], (e * inv).astype(bf16))
            o = jnp.concatenate([o[:, :RB], o[:, RB:]], axis=0)
            MX[r, pl.ds(pl.multiple_of(h * 128, 128), 128)] = jnp.transpose(o).astype(bf16)

        per_block(half, work)

    def attention_out(half):
        if half == 0:
            ag_wait(1)
        a_produce(half, lambda d: dot_nt(MX[rows(d, RB), :], W[:, pl.ds(2 * QW, QW)]))

    def after_attention(h):
        def use(r, at, summed):
            v = Tk[at, :].astype(f32) + summed
            RES[r, :] = v
            n = v * lax.rsqrt(jnp.mean(v * v, axis=1, keepdims=True) + epsilon)
            NF[at, :] = (n * gf_ref[...]).astype(bf16)

        a_total(h, use)
        nf_start(h)

    def ffn(j, half):
        if j == 0:
            nf_wait(half == 1)
        if half == 0:
            ag_wait(2 + j)
        elif j == 0:
            nf_done()

        def step(i):
            r = rows(own_first(half, i), RB)
            n = NF[r, :]
            gate = dot_nn(n, W[:, pl.ds(PW + 2 * FC * j, FC)])
            up = dot_nn(n, W[:, pl.ds(PW + 2 * FC * j + FC, FC)])
            sig = 1.0 / (1.0 + jnp.exp(-gate))
            act = gate * sig
            HID[r, pl.ds(FC * j, FC)] = (act * up).astype(bf16)
            GG[r, pl.ds(2 * FC * j, FC)] = (up * (sig + act * (1.0 - sig))).astype(bf16)
            GG[r, pl.ds(2 * FC * j + FC, FC)] = act.astype(bf16)

        loop(2, step)

    def grad_weights(what):
        if what < 3:
            if what == 0:
                cot_wait(False)
                cot_wait(True)
                cot_done()
            weight_grad(Ct, [(what, HID.at[:, pl.ds(FC * what, FC)])])
        elif what < 6:
            weight_grad(NF, [(what, GG.at[:, pl.ds(2 * FC * (what - 3), 2 * FC)])])
        elif what == 6:
            weight_grad(Ct, [(6, MX)])
        else:
            weight_grad(Nm, [(7, GQ.at[:, pl.ds(0, QW)]), (9, GQ.at[:, pl.ds(QW, 2 * KW)])])

    def grad_hidden(j, half):
        if half == 0:
            ag_wait(5 + j)

        def step(i):
            r = rows(other_first(half, i), RB)
            gh = dot_nn(Ct[r, :], W[:, pl.ds(down0 + FC * j, FC)])
            a, b = pl.ds(2 * FC * j, FC), pl.ds(2 * FC * j + FC, FC)
            GG[r, a] = (gh * GG[r, a].astype(f32)).astype(bf16)
            GG[r, b] = (gh * GG[r, b].astype(f32)).astype(bf16)

        loop(2, step)

    def grad_ffn_norm(half):
        if half == 0:
            a_done()
        n_produce(half, lambda d: dot_nt(GG[rows(d, RB), :], W[:, pl.ds(PW, 2 * F)]))

    def after_ffn(h):
        def use(r, at, gy):
            v = RES[r, :]
            inv = lax.rsqrt(jnp.mean(v * v, axis=1, keepdims=True) + epsilon)
            n = v * inv
            VEC[1:2, :] += jnp.sum(gy * n, axis=0, keepdims=True)
            g = gy * gf_ref[...]
            g = inv * (g - n * jnp.mean(g * n, axis=1, keepdims=True))
            Ct[at, :] = (Ct[at, :].astype(f32) + g).astype(bf16)

        n_total(h, use)
        rl_start(h)

    def grad_mixed(half):
        rl_wait(half == 1)
        if half == 0:
            DKV[...] = jnp.zeros(DKV.shape, f32)

        def step(i):
            r = rows(own_first(half, i), RB)
            g = dot_nn(Ct[r, :], W[:, pl.ds(2 * QW, QW)]).astype(bf16)
            for p in range(2):
                DO[p, 0, r, :] = g[:, 128 * p : 128 * p + 64]
                DO[p, 1, r, :] = g[:, 128 * p + 64 : 128 * p + 128]

        loop(2, step)

    def attend_back(half):
        def work(h, i, keys, bias, r):
            q = QS[h, :, r, :].reshape(2 * RB, 64)
            do = DO[h, :, r, :].reshape(2 * RB, 64)
            p = jnp.exp(dot_nt(KS[h, keys, :], q) + bias) * INV[h, i]
            dp = dot_nt(VS[h, keys, :], do)
            ds = (p * (dp - jnp.sum(p * dp, axis=0, keepdims=True))).astype(bf16)
            DKV[h, keys, :] += jnp.concatenate([dot_nn(ds, q), dot_nn(p.astype(bf16), do)], axis=1)
            g = dot_nn(KT[h, :, keys], ds) * 0.125
            g = jnp.concatenate([g[:, :RB], g[:, RB:]], axis=0)
            DQ[r, pl.ds(pl.multiple_of(h * 128, 128), 128)] = jnp.transpose(g)

        per_block(half, work)

    def project_back():
        def step(i):
            r = rows(i, RB)
            cos, sin = CS[r, :], SN[r, :]
            for p in range(3):
                if p < 2:
                    g = DQ[r, pl.ds(128 * p, 128)]
                else:
                    g = jnp.concatenate([DKV[0, r, pl.ds(0, 64)], DKV[1, r, pl.ds(0, 64)]], axis=1)
                g = g * cos - turn(g) * sin
                v = PRE[r, pl.ds(128 * p, 128)]
                inv = lax.rsqrt(head_mean(v * v) + epsilon)
                n = v * inv
                s = pl.ds(0 if p < 2 else 128, 128)
                VEC[2:3, s] += jnp.sum(g * n, axis=0, keepdims=True)
                g = g * head_gain(p)
                GQ[r, pl.ds(128 * p, 128)] = (inv * (g - n * head_mean(g * n))).astype(bf16)
            v = jnp.concatenate([DKV[0, r, pl.ds(64, 64)], DKV[1, r, pl.ds(64, 64)]], axis=1)
            GQ[r, pl.ds(384, 128)] = v.astype(bf16)

        loop(nb, step)

    def gn_core(i, k, xx, cc):
        return rc(
            PN.at[rows(i, RB), pl.ds(pl.multiple_of((xx * 2 + cc) * CW, CW), CW)],
            AC.at[rows(i, RB), pl.ds(pl.multiple_of(xx * CW, CW), CW)],
            gn_s.at[i, k], gn_r.at[i, k], cpeer,
        )

    def gn_x(i):
        return rc(SC.at[rows(i, RB), :], BC.at[rows(i, RB), :], gn_s.at[i, 2], gn_r.at[i, 2], xpeer)

    others = [(0, x * 2 + 1 - c, cpeer), (1, (1 - x) * 2 + c, xpeer), (2, (1 - x) * 2 + 1 - c, dpeer)]
    gains = VY.shape[0]
    vec_y = rc(VSUM.at[pl.ds(0, gains), :], VY, vec_s.at[3], vec_r.at[3], ypeer)

    def vec_copy(i, which, dev):
        return rc(VCOL.at[which], VCOL.at[which], vec_s.at[i], vec_r.at[i], dev)

    def vz_copy(k, src):
        return rc(VZ.at[src], VZ.at[src], vz_s.at[k], vz_r.at[k], zdev((z + k) % nz))

    def gn_produce():
        def step(i):
            r = rows(i, RB)
            g = dot_nt(GQ[r, :], W[:, pl.ds(0, 2 * QW)])
            PN[r, :] = g.astype(bf16)
            gn_core(i, 0, 1 - x, 1 - c).start()
            gn_core(i, 1, x, 1 - c).start()
            g = g * (Tk[r, :].astype(f32) * R1[r, pl.ds(0, 1)])
            VEC[0:1, :] += jnp.sum(g, axis=0, keepdims=True)
            s = jnp.sum(g * ga_ref[...], axis=1, keepdims=True)
            VEC[3:4, r] = jnp.transpose(jnp.broadcast_to(s, (RB, 128)))[0:1, :]

        loop(nb, step)
        for i in range(D // 128):
            s = pl.ds(128 * i, 128)
            VCOL[col, pl.ds(i, 1), :] = VEC[0:1, s]
            VCOL[col, pl.ds(D // 128 + i, 1), :] = VEC[1:2, s]
        for i in range(2):
            VCOL[col, pl.ds(D // 64 + i, 1), :] = VEC[2:3, pl.ds(128 * i, 128)]
        for i in range(T // 128):
            VCOL[col, pl.ds(gains + i, 1), :] = VEC[3:4, pl.ds(128 * i, 128)]
        for i, _, dev in others:
            vec_copy(i, col, dev).start()

    def gn_middle():
        def step(i):
            r = rows(i, RB)
            gn_core(i, 0, 1 - x, c).wait_recv()
            a = PN[r, pl.ds(pl.multiple_of(((1 - x) * 2 + c) * CW, CW), CW)].astype(f32)
            b = AC[r, pl.ds(pl.multiple_of((1 - x) * CW, CW), CW)].astype(f32)
            SC[r, :] = (a + b).astype(bf16)
            gn_x(i).start()

        loop(nb, step)

    def vec_col():
        for i, d, dev in others:
            vec_copy(i, d, dev).wait_recv()
        VSUM[...] = (VCOL[0] + VCOL[1]) + (VCOL[2] + VCOL[3])
        vec_y.start()

    def vec_row():
        vec_y.wait_recv()
        VZ[z] = VSUM[0:gains, :] + VY[...]
        loop(nz, lambda k: vz_copy(k, z).start(), 1)

    gt_copy = pltpu.make_async_copy(DQ, gt_h, out_sem.at[30])
    lo_out = pltpu.make_async_copy(LOC, lo_h, out_sem.at[31])

    def gn_finish():
        def step(i):
            r = rows(i, RB)
            gn_core(i, 1, x, c).wait_recv()
            gn_x(i).wait_recv()
            g = PN[r, mine].astype(f32) + AC[r, pl.ds(pl.multiple_of(x * CW, CW), CW)].astype(f32)
            g = (g + BC[r, :].astype(f32)) * ga_ref[:, mine]
            inv = R1[r, pl.ds(0, 1)]
            s = [VSUM[pl.ds(gains + 2 * i + j, 1), :] for j in range(2)]
            s = jnp.transpose(jnp.broadcast_to(jnp.concatenate(s, axis=1), (128, RB)))[:, 0:1] * (1.0 / D)
            n = Tk[r, mine].astype(f32) * inv
            DQ[r, :] = Ct[r, mine].astype(f32) + inv * (g - n * s)

        loop(nb, step)
        gt_copy.start()

    def lo_copy(i, d, dev):
        return rc(
            S0.at[:, pl.ds(pl.multiple_of(d * CW, CW), CW)], LOC.at[rows(col, RB), :], lo_s.at[i], lo_r.at[i], dev
        )

    def branch():
        n_done()
        for half in range(2):
            b_produce(half, lambda d: dot_nt(HID[rows(d, RB), :], W[:, pl.ds(down0, F)]))

    def block_out():
        def use(r, at, summed):
            S0[r, :] = (RES[r, :] + summed).astype(bf16)

        b_total(0, use)
        b_total(1, use)
        for i, d, dev in others:
            lo_copy(i, d, dev).start()
        LOC[rows(col, RB), :] = S0[:, mine]

    def block_out_wait():
        for i, d, dev in others:
            lo_copy(i, d, dev).wait_recv()
        lo_out.start()

    def finish():
        loop(nz, lambda k: vz_copy(k, (z + nz - k) % nz).wait_recv(), 1)
        gain_ref[...] = lax.fori_loop(1, nz, lambda k, t: t + VZ[k], VZ[0])
        gain_out = pltpu.make_async_copy(gain_ref, gain_h, out_sem.at[32])
        gain_out.start()
        tok_done()
        rl_done()
        b_done()
        for i, d, dev in others:
            lo_copy(i, d, dev).wait_send()
            vec_copy(i, col, dev).wait_send()
        vec_y.wait_send()

        def gn_done(i):
            gn_core(i, 0, 1 - x, 1 - c).wait_send()
            gn_core(i, 1, x, 1 - c).wait_send()
            gn_x(i).wait_send()

        loop(nb, gn_done)
        loop(nz, lambda k: vz_copy(k, z).wait_send(), 1)
        for ch in range(len(CH)):
            ag_done(ch)
        for ch in range(len(RCH)):
            rs_done(ch)
        gt_copy.wait()
        lo_out.wait()
        gain_out.wait()

    steps = {
        "out": load_out, "gate_up": load_gate_up, "down": load_down, "toks": start_tokens, "cots": start_cotangent,
        "owny": own_y, "ownz": own_z, "fwd": forward, "tokf": tok_forward, "cotf": cot_forward,
        "tables": tables, "norm": norm_tokens, "project": project, "att": lambda half: rows_of_chip(False, half, attend), "aprod": attention_out,
        "amid": a_middle, "aft": after_attention, "nff": nf_forward, "ffn": ffn, "wg": grad_weights,
        "gh": grad_hidden, "gnfp": grad_ffn_norm, "gnfm": n_middle, "naft": after_ffn, "rlf": rl_forward,
        "gmix": grad_mixed, "ab": lambda half: rows_of_chip(True, half, attend_back), "snd": send_grad, "pb": project_back, "gnp": gn_produce, "gnm": gn_middle,
        "vc": vec_col, "vy": vec_row,
        "gnfin": gn_finish, "brp": branch, "brm": b_middle, "brf": block_out, "lof": block_out_wait,
        "mid": rs_mid, "relay": rs_relay, "pre": rs_pre, "fin": rs_fin, "end": finish,
    }
    for name, *which, who in ORDER:
        if name in ("fwd", "mid"):
            run = functools.partial(steps[name], *which, who == "m")
        else:
            run = functools.partial(steps[name], *which)
        if who == "a" or not tree:
            if who != "e" or name in ("fwd", "mid"):
                run()
        else:

            @pl.when(is_middle if who == "m" else jnp.logical_not(is_middle))
            def _():
                run()


def hand_out(*refs):
    sources, targets, held, sem = refs[:10], refs[10:23], refs[23:37], refs[37]
    loads = [pltpu.make_async_copy(a, b, sem.at[0, i]) for i, (a, b) in enumerate(zip(sources, held))]
    stores = [pltpu.make_async_copy(a, b, sem.at[1, i]) for i, (a, b) in enumerate(zip(held[:9] + held[10:], targets))]
    gains, attn, ffn, query, key = held[9:]
    for copy in loads[9:] + loads[:9]:
        copy.start()
    loads[9].wait()
    n = attn.shape[1] // 128
    for i in range(n):
        attn[:, pl.ds(128 * i, 128)] = gains[pl.ds(i, 1), :]
        ffn[:, pl.ds(128 * i, 128)] = gains[pl.ds(n + i, 1), :]
    query[...] = gains[pl.ds(2 * n, 1), pl.ds(0, 64)] + gains[pl.ds(2 * n, 1), pl.ds(64, 64)]
    key[...] = gains[pl.ds(2 * n + 1, 1), pl.ds(0, 64)] + gains[pl.ds(2 * n + 1, 1), pl.ds(64, 64)]
    for store in stores[9:]:
        store.start()
    for load, store in zip(loads[:9], stores):
        load.wait()
        store.start()
    for store in stores:
        store.wait()


def per_device(
    n_row, tokens, segment_ids, w_query, key_matrix, value_matrix, w_out, w_gate, w_up, w_down,
    norm_attn, norm_ffn, norm_query, norm_key, cotangent,
):
    T, CW = tokens.shape
    br, QW = w_query.shape
    KW = key_matrix.shape[1]
    F = w_gate.shape[1]
    D = br * n_row
    nz = n_row // 2
    PW = 2 * QW + 2 * KW
    WW = PW + 3 * F
    FC = F // 3
    nb = T // RB
    half = nb // 2 * RB
    area = (half + (longest + RB if half >= longest else 2 * half)) * (nb // 2)
    chunks = [(0, 2 * QW), (2 * QW, QW)]
    chunks += [(PW + 2 * FC * j, 2 * FC) for j in range(3)] + [(PW + 2 * F + FC * j, FC) for j in range(3)]
    start, width = chunks[4]
    last = LAST
    grads = chunks[5:8] + chunks[2:4] + [(start, width - last), chunks[1], (0, QW), (start + width - last, last)]
    grads.append((QW, 2 * KW))
    gains = 2 * D // 128 + 8
    tree = nz == 4
    ag_pairs, rs_pairs = (AG_PAIRS, RS_PAIRS) if tree else ((), ())
    place, widths = [], [0, 0]
    for ch, (_, width) in enumerate(grads):
        paired = ch in rs_pairs
        place.append(widths[paired])
        widths[paired] += width
    plan = (nz, tree, chunks, grads, ag_pairs, rs_pairs, place)
    single, paired = widths[0], max(widths[1], 128)
    slots = 4 if tree else nz - 1
    vm, sem = pltpu.VMEM, pltpu.SemaphoreType.DMA
    scratch = [
        vm((D, WW), bf16), vm((QW, br), bf16), vm((F, br), bf16), vm((QW, br), f32), vm((F, br), f32),
        vm((D, 3 * F), bf16), vm((nz, br, single), bf16), vm((slots, br, single), bf16),
        vm((br, paired), bf16), vm((4, 2 * br, paired), bf16),
        vm((br, 2 * QW + 2 * F), f32), vm((T, D), bf16), vm((T, D), bf16), vm((T, D), bf16), vm((T, 128), f32),
        vm((T, 2 * QW), f32), vm((2, 2, T, 64), bf16), vm((2, T, 64), bf16), vm((2, T, 64), bf16),
        vm((2, 64, T), bf16), vm((2, 64, T), bf16), vm((2, 2, T, 64), bf16), vm((T, QW), bf16),
        vm((T, D), bf16), vm((2, RB, D), bf16), vm((RB, D), bf16), vm((RB, D), bf16), vm((RB, D), f32),
        vm((T, D), bf16), vm((T, 2 * F), bf16), vm((T, F), bf16),
        vm((T, 128), f32), vm((T, 128), f32), vm((area, RB), bf16), vm((2, nb, 1, 2 * RB), f32),
        vm((T, QW), f32), vm((2, T, 128), f32),
        vm((T, 2 * CW), bf16), vm((T, CW), bf16), vm((T, CW), bf16), vm((T, CW), bf16),
        vm((8, D), f32), vm((4, gains + T // 128, 128), f32), vm((gains + T // 128, 128), f32), vm((gains, 128), f32),
        vm((nz, gains, 128), f32), vm((1, T), jnp.int32), vm((1, D), f32), vm((1, D), f32),
        vm((1, norm_query.shape[0]), f32), vm((1, norm_query.shape[0]), f32), vm((gains, 128), f32),
        sem((18,)), sem((8, nz)), sem((8, nz)), sem((8, nz)), sem((8, nz)),
        sem((10, nz)), sem((10, nz)), sem((10, nz)), sem((10, nz)),
        sem((4, 2, 3)), sem((4, 2, 3)), sem((3, 4)), sem((3, 4)), sem((nb, 3)), sem((nb, 3)), sem((3,)), sem((3,)),
        sem((4,)), sem((4,)), sem((nz,)), sem((nz,)), sem((33,)),
    ]
    hbm = pl.BlockSpec(memory_space=pl.ANY)
    shape = jax.ShapeDtypeStruct
    results = (
        shape((T, CW), bf16), shape((T, CW), f32), shape((br, QW), f32), shape((br, KW), f32), shape((br, KW), f32),
        shape((QW, br), f32), shape((br, F), f32), shape((br, F), f32), shape((F, br), f32),
    )
    outs = pl.pallas_call(
        functools.partial(layer_kernel, plan),
        out_shape=results + (shape((gains, 128), f32),),
        in_specs=[hbm] * 14,
        out_specs=(hbm,) * 10,
        scratch_shapes=scratch,
        compiler_params=pltpu.CompilerParams(
            collective_id=0, has_side_effects=True, vmem_limit_bytes=64 * 2**20
        ),
        name="layer",
    )(
        tokens, segment_ids, w_query, key_matrix, value_matrix, w_out, w_gate, w_up, w_down,
        norm_attn[None], norm_ffn[None], norm_query[None], norm_key[None], cotangent,
    )
    gain = shape((1, D), f32)
    head_gain = shape((1, norm_query.shape[0]), f32)
    outs = pl.pallas_call(
        hand_out,
        out_shape=results + (gain, gain, head_gain, head_gain),
        in_specs=[hbm] * 10,
        out_specs=(hbm,) * 13,
        scratch_shapes=[vm(v.shape, v.dtype) for v in results + (shape((gains, 128), f32), gain, gain, head_gain, head_gain)]
        + [sem((2, 13))],
        compiler_params=pltpu.CompilerParams(vmem_limit_bytes=63 * 2**20),
        name="hand_out",
    )(*outs)
    return outs[:9] + tuple(v[0] for v in outs[9:])


def solution(mesh):
    in_specs = (
        P("row", "col"), P("row", None), P("row", "col"), P("row", "col"), P("row", "col"), P("col", "row"),
        P("row", "col"), P("row", "col"), P("col", "row"), P(), P(), P(), P(), P("row", "col"),
    )
    out_specs = (
        P("row", "col"), P("row", "col"), P("row", "col"), P("row", "col"), P("row", "col"), P("col", "row"),
        P("row", "col"), P("row", "col"), P("col", "row"), P(), P(), P(), P(),
    )
    return jax.shard_map(
        functools.partial(per_device, mesh.shape["row"]),
        mesh=mesh, in_specs=in_specs, out_specs=out_specs, check_vma=False,
    )
```

```python
import functools
import math

import jax
import jax.numpy as jnp
from jax import lax
from jax.experimental import pallas as pl
from jax.experimental.pallas import tpu as pltpu
from jax.sharding import PartitionSpec as P

epsilon = 1e-05
rope_base = 1000000.0
longest = 512
ids = 8
f32, bf16 = jnp.float32, jnp.bfloat16
MESH = pl.DeviceIdType.MESH
RB = 256


def dot_nn(a, b):
    return lax.dot_general(a, b, (((1,), (0,)), ((), ())), preferred_element_type=f32)


def dot_nt(a, b):
    return lax.dot_general(a, b, (((1,), (1,)), ((), ())), preferred_element_type=f32)


def rows(i, n):
    return pl.ds(pl.multiple_of(i * n, n), n)


LAST = 128
AG_PAIRS, RS_PAIRS = (5, 6), (0, 1, 2, 8)
ORDER = [
    ("out", "a"), ("owny", 1, "a"), ("ownz", 1, "a"), ("gate_up", "a"), ("owny", 2, "a"), ("owny", 0, "a"),
    ("toks", "a"), ("fwd", 1, 1, "e"), ("ownz", 0, "a"), ("tables", "a"), ("down", "a"), ("owny", 6, "a"),
    ("ownz", 2, "a"), ("fwd", 0, 1, "e"), ("cots", "a"), ("fwd", 0, 1, "m"), ("fwd", 0, 2, "m"), ("fwd", 0, 3, "m"),
    ("fwd", 0, 2, "e"), ("tokf", "a"), ("fwd", 1, 1, "m"), ("fwd", 1, 2, "m"), ("fwd", 0, 3, "e"), ("owny", 5, "a"),
    ("fwd", 1, 3, "m"), ("fwd", 1, 2, "e"), ("ownz", 6, "a"), ("fwd", 6, 1, "e"), ("norm", "a"), ("fwd", 1, 3, "e"),
    ("fwd", 2, 1, "m"), ("owny", 3, "a"), ("ownz", 3, "a"), ("fwd", 2, 1, "e"), ("owny", 4, "a"),
    ("fwd", 2, 2, "m"), ("project", "a"), ("fwd", 6, 2, "e"), ("att", 0, "a"), ("fwd", 2, 3, "m"),
    ("aprod", 0, "a"), ("owny", 7, "a"), ("amid", "a"), ("fwd", 6, 1, "m"), ("att", 1, "a"), ("ownz", 4, "a"),
    ("fwd", 3, 1, "m"), ("fwd", 6, 3, "e"), ("aprod", 1, "a"), ("ownz", 5, "a"), ("fwd", 5, 1, "m"),
    ("fwd", 2, 2, "e"), ("fwd", 3, 2, "m"), ("aft", 0, "a"), ("fwd", 3, 3, "m"), ("fwd", 4, 1, "m"),
    ("fwd", 4, 2, "m"), ("fwd", 5, 1, "e"), ("ownz", 7, "a"), ("fwd", 2, 3, "e"), ("fwd", 3, 1, "e"),
    ("aft", 1, "a"), ("fwd", 4, 3, "m"), ("fwd", 3, 2, "e"), ("fwd", 5, 2, "e"), ("cotf", "a"), ("fwd", 7, 1, "m"),
    ("nff", 0, "a"), ("fwd", 5, 2, "m"), ("fwd", 7, 2, "m"), ("fwd", 3, 3, "e"), ("fwd", 5, 3, "e"),
    ("fwd", 7, 3, "m"), ("fwd", 4, 1, "e"), ("ffn", 0, 0, "a"), ("nff", 1, "a"), ("ffn", 0, 1, "a"),
    ("fwd", 5, 3, "m"), ("fwd", 6, 2, "m"), ("fwd", 6, 3, "m"), ("wg", 0, "a"), ("fwd", 4, 2, "e"),
    ("ffn", 1, 0, "a"), ("fwd", 4, 3, "e"), ("ffn", 1, 1, "a"), ("wg", 1, "a"), ("fwd", 7, 1, "e"),
    ("fwd", 7, 2, "e"), ("fwd", 7, 3, "e"), ("gh", 0, 0, "a"), ("gh", 0, 1, "a"), ("wg", 3, "a"),
    ("ffn", 2, 0, "a"), ("ffn", 2, 1, "a"), ("wg", 2, "a"), ("gh", 1, 0, "a"), ("gh", 2, 0, "a"), ("gnfp", 0, "a"),
    ("mid", 3, 0, "e"), ("relay", 0, 0, "m"), ("gnfm", "a"), ("mid", 3, 1, "e"), ("gh", 1, 1, "a"),
    ("mid", 3, 0, "m"), ("relay", 1, 0, "m"), ("gh", 2, 1, "a"), ("relay", 2, 0, "m"), ("wg", 5, "a"),
    ("gnfp", 1, "a"), ("naft", 0, "a"), ("wg", 4, "a"), ("mid", 3, 1, "m"), ("mid", 5, 0, "e"),
    ("relay", 1, 1, "m"), ("mid", 0, 2, "m"), ("naft", 1, "a"), ("snd", 8, "a"), ("mid", 3, 2, "m"),
    ("mid", 5, 0, "m"), ("gmix", 0, "a"), ("mid", 5, 1, "e"), ("relay", 0, 1, "m"), ("relay", 3, 0, "m"),
    ("ab", 0, "a"), ("rlf", 0, "a"), ("rlf", 1, "a"), ("relay", 3, 1, "m"), ("mid", 3, 2, "e"), ("mid", 4, 0, "e"),
    ("relay", 2, 1, "m"), ("mid", 1, 2, "m"), ("gmix", 1, "a"), ("mid", 5, 1, "m"), ("relay", 5, 0, "m"),
    ("relay", 8, 0, "m"), ("brp", "a"), ("wg", 6, "a"), ("brm", "a"), ("mid", 4, 1, "e"), ("mid", 5, 2, "m"),
    ("ab", 1, "a"), ("relay", 8, 1, "m"), ("pb", "a"), ("mid", 4, 2, "e"), ("relay", 5, 1, "m"), ("mid", 4, 0, "m"),
    ("mid", 4, 1, "m"), ("gnp", "a"), ("mid", 4, 2, "m"), ("relay", 4, 0, "m"), ("relay", 4, 1, "m"),
    ("mid", 6, 0, "e"), ("wg", 7, "a"), ("gnm", "a"), ("mid", 6, 1, "e"), ("mid", 7, 0, "e"), ("mid", 6, 0, "m"),
    ("mid", 9, 0, "e"), ("mid", 9, 0, "m"), ("mid", 6, 2, "e"), ("relay", 6, 0, "m"), ("pre", 0, "e"),
    ("mid", 6, 1, "m"), ("mid", 7, 1, "e"), ("pre", 2, "m"), ("mid", 7, 0, "m"), ("pre", 8, "e"),
    ("mid", 9, 1, "e"), ("mid", 6, 2, "m"), ("mid", 9, 1, "m"), ("relay", 6, 1, "m"), ("mid", 2, 2, "m"),
    ("vc", "a"), ("mid", 8, 2, "m"), ("mid", 5, 2, "e"), ("relay", 9, 0, "m"), ("mid", 9, 2, "m"), ("fin", 3, "a"),
    ("mid", 7, 2, "e"), ("pre", 2, "e"), ("mid", 9, 2, "e"), ("brf", "a"), ("pre", 0, "m"), ("pre", 1, "e"),
    ("relay", 7, 0, "m"), ("pre", 8, "m"), ("mid", 7, 1, "m"), ("mid", 7, 2, "m"), ("relay", 9, 1, "m"),
    ("relay", 7, 1, "m"), ("vy", "a"), ("pre", 1, "m"), ("gnfin", "a"), ("fin", 0, "a"), ("fin", 4, "a"),
    ("fin", 5, "a"), ("fin", 9, "a"), ("fin", 6, "a"), ("fin", 2, "a"), ("fin", 8, "a"), ("lof", "a"),
    ("fin", 7, "a"), ("fin", 1, "a"), ("end", "a"),
]


def layer_kernel(
    plan,
    tok_h, seg_h, wq_h, wk_h, wv_h, wo_h, wg_h, wu_h, wd_h, ga_h, gf_h, gq_h, gk_h, cot_h,
    lo_h, gt_h, gquery_h, gkey_h, gvalue_h, gout_h, ggate_h, gup_h, gdown_h, gain_h,
    W, WO, WD, GFO, GFD, G, RY, RZ, RYP, RZP, GF, Tk, Ct, Nm, R1, PRE, QS, KS, VS, KT, VT, DO, MX, PB, A0, B0, S0,
    RES, NF, GG, HID, CS, SN, BIAS, INV, DQ, DKV, AC, BC, SC, LOC, VEC, VCOL, VSUM, VY, VZ,
    seg_ref, ga_ref, gf_ref, gq_ref, gk_ref, gain_ref,
    loc_sem, agz_s, agz_r, agy_s, agy_r, rsy_s, rsy_r, rsz_s, rsz_r,
    cag_s, cag_r, crs_s, crs_r, gn_s, gn_r, lo_s, lo_r, vec_s, vec_r, vz_s, vz_r, out_sem,
):
    nz, tree, CH, RCH, ag_pairs, rs_pairs, place = plan
    T, D = Tk.shape
    br = RY.shape[1]
    QW, KW = PRE.shape[1] // 2, PRE.shape[1] // 4
    PW = 2 * QW + 2 * KW
    F = HID.shape[1]
    FC = F // 3
    HB = RB // 2
    down0 = PW + 2 * F
    nb = T // RB
    CW = D // 4
    GQ = GG.at[:, pl.ds(PW, 2 * QW)]
    PN = GG.at[:, pl.ds(PW + 2 * QW, D)]
    row, col = lax.axis_index("row"), lax.axis_index("col")
    z, y = row // 2, row % 2
    x, c = col // 2, col % 2
    ypeer = (row + 1 - 2 * y, col)
    cpeer = (row, col + 1 - 2 * c)
    xpeer = (row, (1 - x) * 2 + c)
    dpeer = (row, (1 - x) * 2 + 1 - c)
    partner = z + 1 - 2 * (z % 2)
    is_middle = (z == 1) | (z == 2)
    near, far = 2 - z // 2, 3 - 3 * (z // 2)

    def zdev(zz):
        return (zz * 2 + y, col)

    def zsrc(k):
        return [z, partner, near, far][k] if tree else (z + nz - k) % nz

    def zto(i):
        return [near, far, partner, z][i]

    def rc(src, dst, ss, rs, dev):
        return pltpu.make_async_remote_copy(
            src_ref=src, dst_ref=dst, send_sem=ss, recv_sem=rs, device_id=dev, device_id_type=MESH
        )

    def loop(n, body, first=0):
        def step(i, carry):
            body(i)
            return carry

        lax.fori_loop(first, n, step, 0)

    own = rows(row, br)
    mine = pl.ds(pl.multiple_of(col * CW, CW), CW)
    local = [
        (wq_h, W.at[own, pl.ds(0, QW)]),
        (wk_h, W.at[own, pl.ds(QW, KW)]),
        (wv_h, W.at[own, pl.ds(QW + KW, KW)]),
        (wo_h, WO),
        (tok_h, Tk.at[:, mine]),
        (cot_h, Ct.at[:, mine]),
    ]
    for j in range(3):
        local.append((wg_h.at[:, pl.ds(FC * j, FC)], W.at[own, pl.ds(PW + 2 * FC * j, FC)]))
        local.append((wu_h.at[:, pl.ds(FC * j, FC)], W.at[own, pl.ds(PW + 2 * FC * j + FC, FC)]))
    local.append((wd_h, WD))
    local += [(seg_h, seg_ref), (ga_h, ga_ref), (gf_h, gf_ref), (gq_h, gq_ref), (gk_h, gk_ref)]
    local = [pltpu.make_async_copy(s, d, loc_sem.at[i]) for i, (s, d) in enumerate(local)]

    def wblk(ch, zz, yy):
        start, width = CH[ch]
        return W.at[rows(zz * 2 + yy, br), pl.ds(start, width)]

    def wpair(ch, zz):
        start, width = CH[ch]
        return W.at[rows(zz, 2 * br), pl.ds(start, width)]

    def ag_z(ch, k, src, slot, dev):
        b = wpair(ch, src) if ch in ag_pairs else wblk(ch, src, y)
        return rc(b, b, agz_s.at[ch, k], agz_r.at[ch, slot], zdev(dev))

    def ag_y(ch, k, src, yy):
        b = wblk(ch, src, yy)
        return rc(b, b, agy_s.at[ch, k], agy_r.at[ch, k], ypeer)

    def own_y(ch):
        ag_y(ch, 0, z, y).start()

    def own_z(ch):
        if ch in ag_pairs:
            ag_y(ch, 0, z, 1 - y).wait_recv()
        if tree:
            ag_z(ch, 0, z, 1, partner).start()
            ag_z(ch, 1, z, jnp.where(is_middle, 2, 3), near).start()
        else:
            loop(nz, lambda k: ag_z(ch, k, z, k, (z + k) % nz).start(), 1)

    def forward(ch, k, middle):
        if not tree:
            if k == 3 and middle:

                def step(k):
                    ag_z(ch, k, zsrc(k), k, z).wait_recv()
                    ag_y(ch, k, zsrc(k), y).start()

                loop(nz, step, 1)
            return
        relayed = middle and k >= 2
        if ch in ag_pairs and not relayed:
            return
        ag_z(ch, k, zsrc(k), k, partner).wait_recv()
        if relayed:
            ag_z(ch, k, zsrc(k), k, partner).start()
        if ch not in ag_pairs:
            ag_y(ch, k, zsrc(k), y).start()

    def ag_wait(ch):
        if not tree:
            loop(nz, lambda k: ag_y(ch, k, zsrc(k), 1 - y).wait_recv())
        elif ch in ag_pairs:
            ag_z(ch, 0, partner, 1, partner).wait_recv()

            @pl.when(jnp.logical_not(is_middle))
            def _():
                ag_z(ch, 0, near, 2, partner).wait_recv()
                ag_z(ch, 0, far, 3, partner).wait_recv()

        else:
            for k in range(4):
                ag_y(ch, k, zsrc(k), 1 - y).wait_recv()

    def ag_done(ch):
        if not tree:
            loop(nz, lambda k: ag_y(ch, k, zsrc(k), y).wait_send())
            loop(nz, lambda k: ag_z(ch, k, z, k, z).wait_send(), 1)
            return
        for k in range(1 if ch in ag_pairs else 4):
            ag_y(ch, k, zsrc(k), y).wait_send()
        ag_z(ch, 0, z, 1, partner).wait_send()
        ag_z(ch, 1, z, 2, near).wait_send()

        @pl.when(is_middle)
        def _():
            ag_z(ch, 2, near, 2, partner).wait_send()
            ag_z(ch, 3, far, 3, partner).wait_send()

    def cag(n, block, parts=1):
        def copy(i, d, dev, h):
            return rc(block(d, h), block(d, h), cag_s.at[n, h, i], cag_r.at[n, h, i], dev)

        def start(h=0):
            copy(0, col, cpeer, h).start()
            copy(1, col, xpeer, h).start()

        def forward(h=0):
            copy(1, (1 - x) * 2 + c, xpeer, h).wait_recv()
            copy(2, (1 - x) * 2 + c, cpeer, h).start()

        def wait(far):
            for h in range(parts):
                if far:
                    copy(2, (1 - x) * 2 + 1 - c, cpeer, h).wait_recv()
                else:
                    copy(0, x * 2 + 1 - c, cpeer, h).wait_recv()

        def done():
            for h in range(parts):
                copy(0, col, cpeer, h).wait_send()
                copy(1, col, xpeer, h).wait_send()
                copy(2, (1 - x) * 2 + c, cpeer, h).wait_send()

        return start, forward, wait, done

    def col_block(ref):
        return lambda d, h: ref.at[:, pl.ds(pl.multiple_of(d * CW, CW), CW)]

    def row_block(ref):
        return lambda d, h: ref.at[rows(d * 2 + h, HB), :]

    tok_start, tok_forward, tok_wait, tok_done = cag(0, col_block(Tk))
    cot_start, cot_forward, cot_wait, cot_done = cag(1, col_block(Ct))
    nf_start, nf_forward, nf_wait, nf_done = cag(2, row_block(NF), 2)
    rl_start, rl_forward, rl_wait, rl_done = cag(3, row_block(Ct), 2)

    def crs(n, A, B, S):
        def to_core(i, xx, cc):
            return rc(PB.at[rows(xx * 2 + cc, RB), :], A(xx), crs_s.at[n, i], crs_r.at[n, i], cpeer)

        def to_x(h):
            half = rows(h, HB)
            return rc(S.at[half, :], B.at[half, :], crs_s.at[n, 2 + h], crs_r.at[n, 2 + h], xpeer)

        def produce(half, part):
            def step(i):
                xx = jnp.where(i < 2, 1 - x, x)
                cc = jnp.where(i % 2 == 0, 1 - c, c)
                PB[rows(xx * 2 + cc, RB), :] = part(xx * 2 + cc).astype(bf16)

                @pl.when(i % 2 == 0)
                def _():
                    to_core(i // 2, xx, 1 - c).start()

            loop(2 * half + 2, step, 2 * half)

        def middle():
            to_core(0, 1 - x, c).wait_recv()

            def step(i):
                r = rows(i, 32)
                block = PB[pl.ds(pl.multiple_of(((1 - x) * 2 + c) * RB + i * 32, 32), 32), :]
                S[r, :] = (block.astype(f32) + A(1 - x)[r, :].astype(f32)).astype(bf16)

            for h in range(2):
                loop(HB // 32 * (h + 1), step, HB // 32 * h)
                to_x(h).start()

        def total(h, use):
            if h == 0:
                to_core(1, x, c).wait_recv()
            to_x(h).wait_recv()

            def step(i):
                r = rows(i, 32)
                at = pl.ds(pl.multiple_of(col * RB + i * 32, 32), 32)
                use(r, at, PB[at, :].astype(f32) + A(x)[r, :].astype(f32) + B[r, :].astype(f32))

            loop(HB // 32 * (h + 1), step, HB // 32 * h)

        def done():
            to_core(0, 1 - x, 1 - c).wait_send()
            to_core(1, x, 1 - c).wait_send()
            to_x(0).wait_send()
            to_x(1).wait_send()

        return produce, middle, total, done

    a_produce, a_middle, a_total, a_done = crs(0, lambda i: A0.at[i], B0, S0)
    n_produce, n_middle, n_total, n_done = crs(1, lambda i: A0.at[i], B0, S0)
    b_produce, b_middle, b_total, b_done = crs(
        2, lambda i: NF.at[rows(i, RB), :], NF.at[pl.ds(2 * RB, RB), :], NF.at[pl.ds(3 * RB, RB), :]
    )

    def other_first(half, i):
        return jnp.where(half == 0, 1 - x, x) * 2 + jnp.where(i == 0, 1 - c, c)

    def own_first(half, i):
        return jnp.where(half == 0, x, 1 - x) * 2 + jnp.where(i == 0, c, 1 - c)

    def rows_of_chip(mine_first, half, work):
        for xx in range(2):

            @pl.when(x == (xx if mine_first == (half == 0) else 1 - xx))
            def _():
                work(xx)

    def gcol(ch):
        start, width = RCH[ch]
        return (G, start - PW, width) if start >= PW else (GG, start, width)

    def gblk(ch, zz, yy):
        ref, start, width = gcol(ch)
        return ref.at[rows(zz * 2 + yy, br), pl.ds(start, width)]

    def part_of(ch):
        return pl.ds(place[ch], RCH[ch][1])

    def rs_y(ch, zz, yy):
        landing = RYP.at[:, part_of(ch)] if ch in rs_pairs else RY.at[zz, :, part_of(ch)]
        return rc(gblk(ch, zz, yy), landing, rsy_s.at[ch, zz], rsy_r.at[ch, zz], ypeer)

    def rs_z(ch, k, zz, slot, dev):
        if ch in rs_pairs:
            ref, start, width = gcol(ch)
            src, dst = ref.at[rows(zz, 2 * br), pl.ds(start, width)], RZP.at[slot, :, part_of(ch)]
        else:
            src, dst = RY.at[zz, :, part_of(ch)], RZ.at[slot, :, part_of(ch)]
        return rc(src, dst, rsz_s.at[ch, k], rsz_r.at[ch, slot], zdev(dev))

    zper = RB // (2 * br)

    def weight_grad(left, pieces):
        def one(i, d):
            lt = jnp.transpose(left[:, rows(d, RB)])
            for ch, right in pieces:
                ref, start, width = gcol(ch)
                ref[rows(d, RB), pl.ds(start, right.shape[1])] = dot_nn(lt, right[...]).astype(bf16)
                if ch not in rs_pairs:
                    loop(zper, lambda s: rs_y(ch, d * zper + s, 1 - y).start())
                else:

                    @pl.when((i == 2) | ((i < 2) & jnp.logical_not(is_middle)))
                    def _():
                        rs_z(ch, i, d, i, partner).start()

        if tree:

            def step(i):
                one(i, jnp.where(i == 0, near, jnp.where(i == 1, far, jnp.where(i == 2, partner, z))))

            loop(4, step)
        else:
            loop(D // RB, lambda i: one(i, (row * br // RB + 1 + i) % (D // RB)))

    def send_grad(ch):
        if tree:
            for i in range(4):
                if ch not in rs_pairs:
                    rs_y(ch, zto(i), 1 - y).start()
                elif i == 2:
                    rs_z(ch, i, zto(i), i, partner).start()
                elif i < 2:

                    @pl.when(jnp.logical_not(is_middle))
                    def _():
                        rs_z(ch, i, zto(i), i, partner).start()

        else:
            loop(nz, lambda k: rs_y(ch, k, 1 - y).start())

    def rs_mid(ch, i, middle):
        ref, gstart, width = gcol(ch)

        def one(zz):
            rs_y(ch, zz, y).wait_recv()

            def add(j):
                r = rows(j, 16)
                g = ref[pl.ds(pl.multiple_of((zz * 2 + y) * br + j * 16, 16), 16), pl.ds(gstart, width)]
                t = RY[zz, r, part_of(ch)]
                RY[zz, r, part_of(ch)] = (g.astype(f32) + t.astype(f32)).astype(bf16)

            loop(br // 16, add)

        if not tree:
            if i == 2 and middle:

                def step(k):
                    zz = (z + k) % nz
                    one(zz)
                    rs_z(ch, k, zz, k - 1, zz).start()

                loop(nz, step, 1)
        elif ch not in rs_pairs:
            one(zto(i))
            if i == 2 or not middle:
                rs_z(ch, i, zto(i), i, partner).start()

    def rs_relay(ch, i):
        if not tree:
            return
        zz = zto(i)
        rs_z(ch, i, zz, i, partner).wait_recv()
        ref, gstart, width = gcol(ch)

        def add(j):
            r = rows(j, 16)
            if ch in rs_pairs:
                at = pl.ds(pl.multiple_of(zz * 2 * br + j * 16, 16), 16)
                t = ref[at, pl.ds(gstart, width)].astype(f32) + RZP[i, r, part_of(ch)].astype(f32)
                ref[at, pl.ds(gstart, width)] = t.astype(bf16)
            else:
                t = RY[zz, r, part_of(ch)].astype(f32) + RZ[i, r, part_of(ch)].astype(f32)
                RY[zz, r, part_of(ch)] = t.astype(bf16)

        loop((2 * br if ch in rs_pairs else br) // 16, add)
        rs_z(ch, i, zz, 3, zz).start()

    def rs_pre(ch):
        if ch not in rs_pairs:
            return
        for slot in (2, 3):
            rs_z(ch, 2, z, slot, partner).wait_recv()
        ref, gstart, width = gcol(ch)

        def add(j):
            at = pl.ds(pl.multiple_of((z * 2 + 1 - y) * br + j * 16, 16), 16)
            r = pl.ds(pl.multiple_of((1 - y) * br + j * 16, 16), 16)
            t = ref[at, pl.ds(gstart, width)].astype(f32)
            t = t + RZP[2, r, part_of(ch)].astype(f32) + RZP[3, r, part_of(ch)].astype(f32)
            ref[at, pl.ds(gstart, width)] = t.astype(bf16)

        loop(br // 16, add)
        rs_y(ch, z, 1 - y).start()

    def outs(ch):
        start, width = RCH[ch]
        if start >= down0:
            pairs = [(GFD.at[pl.ds(start - down0, width), :], gdown_h.at[pl.ds(start - down0, width), :])]
        elif start >= PW:
            third = (start - PW) // (2 * FC)
            at = start - PW - 2 * FC * third
            pairs = []
            for target, low in ((ggate_h, 0), (gup_h, FC)):
                first, last = max(at, low), min(at + width, low + FC)
                if first < last:
                    held = GF.at[:, pl.ds(start - 2 * KW + first - at, last - first)]
                    pairs.append((held, target.at[:, pl.ds(third * FC + first - low, last - first)]))
        elif start == 2 * QW:
            pairs = [(GFO, gout_h)]
        elif start == 0:
            pairs = [(GF.at[:, pl.ds(0, QW)], gquery_h)]
        else:
            pairs = [
                (GF.at[:, pl.ds(QW, KW)], gkey_h),
                (GF.at[:, pl.ds(QW + KW, KW)], gvalue_h),
            ]
        return [pltpu.make_async_copy(a, b, out_sem.at[3 * ch + i]) for i, (a, b) in enumerate(pairs)]

    def rs_fin(ch):
        ref, gstart, width = gcol(ch)
        start = RCH[ch][0]
        paired = ch in rs_pairs
        rs_y(ch, z, y).wait_recv()
        if not tree:
            loop(nz - 1, lambda k: rs_z(ch, 0, z, k, z).wait_recv())
        elif not paired:
            for slot in (2, 3):
                rs_z(ch, 0, z, slot, z).wait_recv()

        def total(r0, rn, c0, cn):
            r = pl.ds(r0, rn)
            g = ref[pl.ds(pl.multiple_of(row * br + r0, 16), rn), pl.ds(gstart + c0, cn)]
            part = pl.ds(place[ch] + c0, cn)
            if paired:
                rp = pl.ds(pl.multiple_of(y * br + r0, 16), rn)
                t = RZP[2, rp, part].astype(f32) + RZP[3, rp, part].astype(f32)
                return g.astype(f32) + t + RYP[r, part].astype(f32)
            t = g.astype(f32) + RY[z, r, part].astype(f32)
            if tree:
                return t + (RZ[2, r, part].astype(f32) + RZ[3, r, part].astype(f32))
            return lax.fori_loop(0, nz - 1, lambda k, t: t + RZ[k, r, part].astype(f32), t)

        if start >= down0 or start == 2 * QW:
            for c0 in range(0, width, 128):
                t = jnp.transpose(total(0, br, c0, 128))
                if start >= down0:
                    GFD[pl.ds(start - down0 + c0, 128), :] = t
                else:
                    GFO[pl.ds(c0, 128), :] = t
        else:
            at = start - 2 * KW if start >= PW else start

            def add(i):
                r0 = pl.multiple_of(i * 16, 16)
                GF[pl.ds(r0, 16), pl.ds(at, width)] = total(r0, 16, 0, width)

            loop(br // 16, add)
        for copy in outs(ch):
            copy.start()

    def rs_done(ch):
        if ch in rs_pairs:
            rs_y(ch, z, 1 - y).wait_send()
        else:
            loop(nz, lambda zz: rs_y(ch, zz, 1 - y).wait_send())
        if tree:
            for i in range(3):
                rs_z(ch, i, zto(i), 0, partner).wait_send()
        else:
            loop(nz, lambda k: rs_z(ch, k, z, 0, z).wait_send(), 1)
        for copy in outs(ch):
            copy.wait()

    bar = pltpu.get_barrier_semaphore()
    for dev in (ypeer, cpeer, xpeer, dpeer):
        pl.semaphore_signal(bar, inc=1, device_id=dev, device_id_type=MESH)

    def greet(k):
        pl.semaphore_signal(bar, inc=1, device_id=zdev((z + k) % nz), device_id_type=MESH)

    loop(nz, greet, 1)
    for i in (0, 1, 2, 4, 13, 14, 15, 16, 17, 3, 6, 7, 8, 9, 10, 11, 5, 12):
        local[i].start()
    for i in range(3):
        local[i].wait()
    pl.semaphore_wait(bar, 4 + nz - 1)

    def load_out():
        local[3].wait()
        W[own, pl.ds(2 * QW, QW)] = jnp.transpose(WO[...])

    def load_gate_up():
        for i in range(6, 12):
            local[i].wait()

    def load_down():
        local[12].wait()
        W[own, pl.ds(down0, F)] = jnp.transpose(WD[...])

    def start_tokens():
        local[4].wait()
        tok_start()

    def start_cotangent():
        local[5].wait()
        cot_start()

    lane = lax.broadcasted_iota(jnp.int32, (1, 128), 1)

    def head_gain(p):
        gain = (gq_ref if p < 2 else gk_ref)[...]
        return jnp.concatenate([gain, gain], axis=1)

    hb = nb // 2
    spans = []
    for half in range(2):
        low = max(0, RB * half * hb - longest)
        if half * RB * hb >= longest:
            spans.append((longest + RB, RB, low, sum(s[0] for s in spans) * hb))
        else:
            spans.append((RB * hb * (half + 1), 0, 0, sum(s[0] for s in spans) * hb))

    def tables():
        for i in range(13, 18):
            local[i].wait()
        VEC[...] = jnp.zeros(VEC.shape, f32)
        seg = seg_ref[...]
        first = jnp.zeros((1, T), jnp.int32)
        for d in range(ids):
            count = jnp.sum((seg == d).astype(f32), axis=1, keepdims=True).astype(jnp.int32)
            first = first + jnp.where(seg > d, count, 0)
        place = lax.broadcasted_iota(jnp.int32, (1, T), 1)
        inverse_freq = jnp.exp((lane % 32).astype(f32) * (-2.0 / 64 * math.log(rope_base)))
        CS[...] = jnp.transpose(jnp.broadcast_to((place - first).astype(f32), (128, T)))

        def fill(i):
            angle = CS[rows(i, 128), :] * inverse_freq
            sine = jnp.sin(angle)
            CS[rows(i, 128), :] = jnp.cos(angle)
            SN[rows(i, 128), :] = jnp.where(lane % 64 < 32, -sine, sine)

        loop(T // 128, fill)
        for i in range(nb):
            width, pace, start, at = spans[i // hb]
            start, at = start + pace * (i % hb), at + width * (i % hb)
            key_place = lax.broadcasted_iota(jnp.int32, (width, RB), 0) + start
            q_place, q_first = place[:, RB * i : RB * (i + 1)], first[:, RB * i : RB * (i + 1)]
            seen = (key_place <= q_place) & (key_place >= q_first)
            BIAS[pl.ds(at, width), :] = jnp.where(seen, 0.0, -1e30).astype(bf16)

    def head_mean(v):
        half_a = lax.broadcasted_iota(jnp.int32, (128, 128), 0) // 64
        half_b = lax.broadcasted_iota(jnp.int32, (128, 128), 1) // 64
        mean_matrix = jnp.where(half_a == half_b, 1.0 / 64, 0.0).astype(bf16)
        high = v.astype(bf16)
        low = (v - high.astype(f32)).astype(bf16)
        return dot_nn(high, mean_matrix) + dot_nn(low, mean_matrix)

    def turn(v):
        return jnp.where(lane % 64 < 32, pltpu.roll(v, 96, 1), pltpu.roll(v, 32, 1))

    def norm_tokens():
        tok_wait(False)
        tok_wait(True)

        def step(i):
            t = Tk[rows(i, 128), :].astype(f32)
            r = lax.rsqrt(jnp.mean(t * t, axis=1, keepdims=True) + epsilon)
            R1[rows(i, 128), :] = jnp.broadcast_to(r, (128, 128))
            Nm[rows(i, 128), :] = (t * r * ga_ref[...]).astype(bf16)

        loop(T // 128, step)

    def project():
        ag_wait(0)

        def step(i):
            r = rows(i, RB)
            PRE[r, :] = dot_nn(Nm[r, :], W[:, pl.ds(0, 2 * QW)])
            cos, sin = CS[r, :], SN[r, :]
            for p in range(3):
                v = PRE[r, pl.ds(128 * p, 128)]
                n = v * lax.rsqrt(head_mean(v * v) + epsilon)
                u = n * head_gain(p)
                u = (u * cos + turn(u) * sin).astype(bf16)
                if p < 2:
                    u = u * jnp.asarray(0.125, bf16)
                    QS[p, 0, r, :] = u[:, :64]
                    QS[p, 1, r, :] = u[:, 64:]
                else:
                    KS[0, r, :] = u[:, :64]
                    KS[1, r, :] = u[:, 64:]
                    ut = jnp.transpose(u)
                    KT[0, :, r] = ut[:64, :]
                    KT[1, :, r] = ut[64:, :]
            v = PRE[r, pl.ds(384, 128)].astype(bf16)
            VS[0, r, :] = v[:, :64]
            VS[1, r, :] = v[:, 64:]
            vt = jnp.transpose(v)
            VT[0, :, r] = vt[:64, :]
            VT[1, :, r] = vt[64:, :]

        loop(nb, step)

    def per_block(half, work):
        width, pace, low, at = spans[half]

        def step(n):
            i, h = n // 2, n % 2
            keys = pl.ds(pl.multiple_of(low + pace * i, RB), width) if pace else pl.ds(low, width)
            bias = BIAS[pl.ds(pl.multiple_of(at + width * i, RB), width), :].astype(f32)
            work(h, half * hb + i, keys, jnp.concatenate([bias, bias], axis=1), rows(half * hb + i, RB))

        loop(2 * hb, step)

    def attend(half):
        def work(h, i, keys, bias, r):
            q = QS[h, :, r, :].reshape(2 * RB, 64)
            e = jnp.exp(dot_nt(KS[h, keys, :], q) + bias)
            inv = 1.0 / jnp.sum(e, axis=0, keepdims=True)
            INV[h, i] = inv
            o = dot_nn(VT[h, :, keys], (e * inv).astype(bf16))
            o = jnp.concatenate([o[:, :RB], o[:, RB:]], axis=0)
            MX[r, pl.ds(pl.multiple_of(h * 128, 128), 128)] = jnp.transpose(o).astype(bf16)

        per_block(half, work)

    def attention_out(half):
        if half == 0:
            ag_wait(1)
        a_produce(half, lambda d: dot_nt(MX[rows(d, RB), :], W[:, pl.ds(2 * QW, QW)]))

    def after_attention(h):
        def use(r, at, summed):
            v = Tk[at, :].astype(f32) + summed
            RES[r, :] = v
            n = v * lax.rsqrt(jnp.mean(v * v, axis=1, keepdims=True) + epsilon)
            NF[at, :] = (n * gf_ref[...]).astype(bf16)

        a_total(h, use)
        nf_start(h)

    def ffn(j, half):
        if j == 0:
            nf_wait(half == 1)
        if half == 0:
            ag_wait(2 + j)
        elif j == 0:
            nf_done()

        def step(i):
            r = rows(own_first(half, i), RB)
            n = NF[r, :]
            gate = dot_nn(n, W[:, pl.ds(PW + 2 * FC * j, FC)])
            up = dot_nn(n, W[:, pl.ds(PW + 2 * FC * j + FC, FC)])
            sig = 1.0 / (1.0 + jnp.exp(-gate))
            act = gate * sig
            HID[r, pl.ds(FC * j, FC)] = (act * up).astype(bf16)
            GG[r, pl.ds(2 * FC * j, FC)] = (up * (sig + act * (1.0 - sig))).astype(bf16)
            GG[r, pl.ds(2 * FC * j + FC, FC)] = act.astype(bf16)

        loop(2, step)

    def grad_weights(what):
        if what < 3:
            if what == 0:
                cot_wait(False)
                cot_wait(True)
                cot_done()
            weight_grad(Ct, [(what, HID.at[:, pl.ds(FC * what, FC)])])
        elif what < 6:
            weight_grad(NF, [(what, GG.at[:, pl.ds(2 * FC * (what - 3), 2 * FC)])])
        elif what == 6:
            weight_grad(Ct, [(6, MX)])
        else:
            weight_grad(Nm, [(7, GQ.at[:, pl.ds(0, QW)]), (9, GQ.at[:, pl.ds(QW, 2 * KW)])])

    def grad_hidden(j, half):
        if half == 0:
            ag_wait(5 + j)

        def step(i):
            r = rows(other_first(half, i), RB)
            gh = dot_nn(Ct[r, :], W[:, pl.ds(down0 + FC * j, FC)])
            a, b = pl.ds(2 * FC * j, FC), pl.ds(2 * FC * j + FC, FC)
            GG[r, a] = (gh * GG[r, a].astype(f32)).astype(bf16)
            GG[r, b] = (gh * GG[r, b].astype(f32)).astype(bf16)

        loop(2, step)

    def grad_ffn_norm(half):
        if half == 0:
            a_done()
        n_produce(half, lambda d: dot_nt(GG[rows(d, RB), :], W[:, pl.ds(PW, 2 * F)]))

    def after_ffn(h):
        def use(r, at, gy):
            v = RES[r, :]
            inv = lax.rsqrt(jnp.mean(v * v, axis=1, keepdims=True) + epsilon)
            n = v * inv
            VEC[1:2, :] += jnp.sum(gy * n, axis=0, keepdims=True)
            g = gy * gf_ref[...]
            g = inv * (g - n * jnp.mean(g * n, axis=1, keepdims=True))
            Ct[at, :] = (Ct[at, :].astype(f32) + g).astype(bf16)

        n_total(h, use)
        rl_start(h)

    def grad_mixed(half):
        rl_wait(half == 1)
        if half == 0:
            DKV[...] = jnp.zeros(DKV.shape, f32)

        def step(i):
            r = rows(own_first(half, i), RB)
            g = dot_nn(Ct[r, :], W[:, pl.ds(2 * QW, QW)]).astype(bf16)
            for p in range(2):
                DO[p, 0, r, :] = g[:, 128 * p : 128 * p + 64]
                DO[p, 1, r, :] = g[:, 128 * p + 64 : 128 * p + 128]

        loop(2, step)

    def attend_back(half):
        def work(h, i, keys, bias, r):
            q = QS[h, :, r, :].reshape(2 * RB, 64)
            do = DO[h, :, r, :].reshape(2 * RB, 64)
            p = jnp.exp(dot_nt(KS[h, keys, :], q) + bias) * INV[h, i]
            dp = dot_nt(VS[h, keys, :], do)
            ds = (p * (dp - jnp.sum(p * dp, axis=0, keepdims=True))).astype(bf16)
            DKV[h, keys, :] += jnp.concatenate([dot_nn(ds, q), dot_nn(p.astype(bf16), do)], axis=1)
            g = dot_nn(KT[h, :, keys], ds) * 0.125
            g = jnp.concatenate([g[:, :RB], g[:, RB:]], axis=0)
            DQ[r, pl.ds(pl.multiple_of(h * 128, 128), 128)] = jnp.transpose(g)

        per_block(half, work)

    def project_back():
        def step(i):
            r = rows(i, RB)
            cos, sin = CS[r, :], SN[r, :]
            for p in range(3):
                if p < 2:
                    g = DQ[r, pl.ds(128 * p, 128)]
                else:
                    g = jnp.concatenate([DKV[0, r, pl.ds(0, 64)], DKV[1, r, pl.ds(0, 64)]], axis=1)
                g = g * cos - turn(g) * sin
                v = PRE[r, pl.ds(128 * p, 128)]
                inv = lax.rsqrt(head_mean(v * v) + epsilon)
                n = v * inv
                s = pl.ds(0 if p < 2 else 128, 128)
                VEC[2:3, s] += jnp.sum(g * n, axis=0, keepdims=True)
                g = g * head_gain(p)
                GQ[r, pl.ds(128 * p, 128)] = (inv * (g - n * head_mean(g * n))).astype(bf16)
            v = jnp.concatenate([DKV[0, r, pl.ds(64, 64)], DKV[1, r, pl.ds(64, 64)]], axis=1)
            GQ[r, pl.ds(384, 128)] = v.astype(bf16)

        loop(nb, step)

    def gn_core(i, k, xx, cc):
        return rc(
            PN.at[rows(i, RB), pl.ds(pl.multiple_of((xx * 2 + cc) * CW, CW), CW)],
            AC.at[rows(i, RB), pl.ds(pl.multiple_of(xx * CW, CW), CW)],
            gn_s.at[i, k], gn_r.at[i, k], cpeer,
        )

    def gn_x(i):
        return rc(SC.at[rows(i, RB), :], BC.at[rows(i, RB), :], gn_s.at[i, 2], gn_r.at[i, 2], xpeer)

    others = [(0, x * 2 + 1 - c, cpeer), (1, (1 - x) * 2 + c, xpeer), (2, (1 - x) * 2 + 1 - c, dpeer)]
    gains = VY.shape[0]
    vec_y = rc(VSUM.at[pl.ds(0, gains), :], VY, vec_s.at[3], vec_r.at[3], ypeer)

    def vec_copy(i, which, dev):
        return rc(VCOL.at[which], VCOL.at[which], vec_s.at[i], vec_r.at[i], dev)

    def vz_copy(k, src):
        return rc(VZ.at[src], VZ.at[src], vz_s.at[k], vz_r.at[k], zdev((z + k) % nz))

    def gn_produce():
        def step(i):
            r = rows(i, RB)
            g = dot_nt(GQ[r, :], W[:, pl.ds(0, 2 * QW)])
            PN[r, :] = g.astype(bf16)
            gn_core(i, 0, 1 - x, 1 - c).start()
            gn_core(i, 1, x, 1 - c).start()
            g = g * (Tk[r, :].astype(f32) * R1[r, pl.ds(0, 1)])
            VEC[0:1, :] += jnp.sum(g, axis=0, keepdims=True)
            s = jnp.sum(g * ga_ref[...], axis=1, keepdims=True)
            VEC[3:4, r] = jnp.transpose(jnp.broadcast_to(s, (RB, 128)))[0:1, :]

        loop(nb, step)
        for i in range(D // 128):
            s = pl.ds(128 * i, 128)
            VCOL[col, pl.ds(i, 1), :] = VEC[0:1, s]
            VCOL[col, pl.ds(D // 128 + i, 1), :] = VEC[1:2, s]
        for i in range(2):
            VCOL[col, pl.ds(D // 64 + i, 1), :] = VEC[2:3, pl.ds(128 * i, 128)]
        for i in range(T // 128):
            VCOL[col, pl.ds(gains + i, 1), :] = VEC[3:4, pl.ds(128 * i, 128)]
        for i, _, dev in others:
            vec_copy(i, col, dev).start()

    def gn_middle():
        def step(i):
            r = rows(i, RB)
            gn_core(i, 0, 1 - x, c).wait_recv()
            a = PN[r, pl.ds(pl.multiple_of(((1 - x) * 2 + c) * CW, CW), CW)].astype(f32)
            b = AC[r, pl.ds(pl.multiple_of((1 - x) * CW, CW), CW)].astype(f32)
            SC[r, :] = (a + b).astype(bf16)
            gn_x(i).start()

        loop(nb, step)

    def vec_col():
        for i, d, dev in others:
            vec_copy(i, d, dev).wait_recv()
        VSUM[...] = (VCOL[0] + VCOL[1]) + (VCOL[2] + VCOL[3])
        vec_y.start()

    def vec_row():
        vec_y.wait_recv()
        VZ[z] = VSUM[0:gains, :] + VY[...]
        loop(nz, lambda k: vz_copy(k, z).start(), 1)

    gt_copy = pltpu.make_async_copy(DQ, gt_h, out_sem.at[30])
    lo_out = pltpu.make_async_copy(LOC, lo_h, out_sem.at[31])

    def gn_finish():
        def step(i):
            r = rows(i, RB)
            gn_core(i, 1, x, c).wait_recv()
            gn_x(i).wait_recv()
            g = PN[r, mine].astype(f32) + AC[r, pl.ds(pl.multiple_of(x * CW, CW), CW)].astype(f32)
            g = (g + BC[r, :].astype(f32)) * ga_ref[:, mine]
            inv = R1[r, pl.ds(0, 1)]
            s = [VSUM[pl.ds(gains + 2 * i + j, 1), :] for j in range(2)]
            s = jnp.transpose(jnp.broadcast_to(jnp.concatenate(s, axis=1), (128, RB)))[:, 0:1] * (1.0 / D)
            n = Tk[r, mine].astype(f32) * inv
            DQ[r, :] = Ct[r, mine].astype(f32) + inv * (g - n * s)

        loop(nb, step)
        gt_copy.start()

    def lo_copy(i, d, dev):
        return rc(
            S0.at[:, pl.ds(pl.multiple_of(d * CW, CW), CW)], LOC.at[rows(col, RB), :], lo_s.at[i], lo_r.at[i], dev
        )

    def branch():
        n_done()
        for half in range(2):
            b_produce(half, lambda d: dot_nt(HID[rows(d, RB), :], W[:, pl.ds(down0, F)]))

    def block_out():
        def use(r, at, summed):
            S0[r, :] = (RES[r, :] + summed).astype(bf16)

        b_total(0, use)
        b_total(1, use)
        for i, d, dev in others:
            lo_copy(i, d, dev).start()
        LOC[rows(col, RB), :] = S0[:, mine]

    def block_out_wait():
        for i, d, dev in others:
            lo_copy(i, d, dev).wait_recv()
        lo_out.start()

    def finish():
        loop(nz, lambda k: vz_copy(k, (z + nz - k) % nz).wait_recv(), 1)
        gain_ref[...] = lax.fori_loop(1, nz, lambda k, t: t + VZ[k], VZ[0])
        gain_out = pltpu.make_async_copy(gain_ref, gain_h, out_sem.at[32])
        gain_out.start()
        tok_done()
        rl_done()
        b_done()
        for i, d, dev in others:
            lo_copy(i, d, dev).wait_send()
            vec_copy(i, col, dev).wait_send()
        vec_y.wait_send()

        def gn_done(i):
            gn_core(i, 0, 1 - x, 1 - c).wait_send()
            gn_core(i, 1, x, 1 - c).wait_send()
            gn_x(i).wait_send()

        loop(nb, gn_done)
        loop(nz, lambda k: vz_copy(k, z).wait_send(), 1)
        for ch in range(len(CH)):
            ag_done(ch)
        for ch in range(len(RCH)):
            rs_done(ch)
        gt_copy.wait()
        lo_out.wait()
        gain_out.wait()

    steps = {
        "out": load_out, "gate_up": load_gate_up, "down": load_down, "toks": start_tokens, "cots": start_cotangent,
        "owny": own_y, "ownz": own_z, "fwd": forward, "tokf": tok_forward, "cotf": cot_forward,
        "tables": tables, "norm": norm_tokens, "project": project, "att": lambda half: rows_of_chip(False, half, attend), "aprod": attention_out,
        "amid": a_middle, "aft": after_attention, "nff": nf_forward, "ffn": ffn, "wg": grad_weights,
        "gh": grad_hidden, "gnfp": grad_ffn_norm, "gnfm": n_middle, "naft": after_ffn, "rlf": rl_forward,
        "gmix": grad_mixed, "ab": lambda half: rows_of_chip(True, half, attend_back), "snd": send_grad, "pb": project_back, "gnp": gn_produce, "gnm": gn_middle,
        "vc": vec_col, "vy": vec_row,
        "gnfin": gn_finish, "brp": branch, "brm": b_middle, "brf": block_out, "lof": block_out_wait,
        "mid": rs_mid, "relay": rs_relay, "pre": rs_pre, "fin": rs_fin, "end": finish,
    }
    for name, *which, who in ORDER:
        if name in ("fwd", "mid"):
            run = functools.partial(steps[name], *which, who == "m")
        else:
            run = functools.partial(steps[name], *which)
        if who == "a" or not tree:
            if who != "e" or name in ("fwd", "mid"):
                run()
        else:

            @pl.when(is_middle if who == "m" else jnp.logical_not(is_middle))
            def _():
                run()


def hand_out(*refs):
    sources, targets, held, sem = refs[:10], refs[10:23], refs[23:37], refs[37]
    loads = [pltpu.make_async_copy(a, b, sem.at[0, i]) for i, (a, b) in enumerate(zip(sources, held))]
    stores = [pltpu.make_async_copy(a, b, sem.at[1, i]) for i, (a, b) in enumerate(zip(held[:9] + held[10:], targets))]
    gains, attn, ffn, query, key = held[9:]
    for copy in loads[9:] + loads[:9]:
        copy.start()
    loads[9].wait()
    n = attn.shape[1] // 128
    for i in range(n):
        attn[:, pl.ds(128 * i, 128)] = gains[pl.ds(i, 1), :]
        ffn[:, pl.ds(128 * i, 128)] = gains[pl.ds(n + i, 1), :]
    query[...] = gains[pl.ds(2 * n, 1), pl.ds(0, 64)] + gains[pl.ds(2 * n, 1), pl.ds(64, 64)]
    key[...] = gains[pl.ds(2 * n + 1, 1), pl.ds(0, 64)] + gains[pl.ds(2 * n + 1, 1), pl.ds(64, 64)]
    for store in stores[9:]:
        store.start()
    for load, store in zip(loads[:9], stores):
        load.wait()
        store.start()
    for store in stores:
        store.wait()


def per_device(
    n_row, tokens, segment_ids, w_query, key_matrix, value_matrix, w_out, w_gate, w_up, w_down,
    norm_attn, norm_ffn, norm_query, norm_key, cotangent,
):
    T, CW = tokens.shape
    br, QW = w_query.shape
    KW = key_matrix.shape[1]
    F = w_gate.shape[1]
    D = br * n_row
    nz = n_row // 2
    PW = 2 * QW + 2 * KW
    WW = PW + 3 * F
    FC = F // 3
    nb = T // RB
    half = nb // 2 * RB
    area = (half + (longest + RB if half >= longest else 2 * half)) * (nb // 2)
    chunks = [(0, 2 * QW), (2 * QW, QW)]
    chunks += [(PW + 2 * FC * j, 2 * FC) for j in range(3)] + [(PW + 2 * F + FC * j, FC) for j in range(3)]
    start, width = chunks[4]
    last = LAST
    grads = chunks[5:8] + chunks[2:4] + [(start, width - last), chunks[1], (0, QW), (start + width - last, last)]
    grads.append((QW, 2 * KW))
    gains = 2 * D // 128 + 8
    tree = nz == 4
    ag_pairs, rs_pairs = (AG_PAIRS, RS_PAIRS) if tree else ((), ())
    place, widths = [], [0, 0]
    for ch, (_, width) in enumerate(grads):
        paired = ch in rs_pairs
        place.append(widths[paired])
        widths[paired] += width
    plan = (nz, tree, chunks, grads, ag_pairs, rs_pairs, place)
    single, paired = widths[0], max(widths[1], 128)
    slots = 4 if tree else nz - 1
    vm, sem = pltpu.VMEM, pltpu.SemaphoreType.DMA
    scratch = [
        vm((D, WW), bf16), vm((QW, br), bf16), vm((F, br), bf16), vm((QW, br), f32), vm((F, br), f32),
        vm((D, 3 * F), bf16), vm((nz, br, single), bf16), vm((slots, br, single), bf16),
        vm((br, paired), bf16), vm((4, 2 * br, paired), bf16),
        vm((br, 2 * QW + 2 * F), f32), vm((T, D), bf16), vm((T, D), bf16), vm((T, D), bf16), vm((T, 128), f32),
        vm((T, 2 * QW), f32), vm((2, 2, T, 64), bf16), vm((2, T, 64), bf16), vm((2, T, 64), bf16),
        vm((2, 64, T), bf16), vm((2, 64, T), bf16), vm((2, 2, T, 64), bf16), vm((T, QW), bf16),
        vm((T, D), bf16), vm((2, RB, D), bf16), vm((RB, D), bf16), vm((RB, D), bf16), vm((RB, D), f32),
        vm((T, D), bf16), vm((T, 2 * F), bf16), vm((T, F), bf16),
        vm((T, 128), f32), vm((T, 128), f32), vm((area, RB), bf16), vm((2, nb, 1, 2 * RB), f32),
        vm((T, QW), f32), vm((2, T, 128), f32),
        vm((T, 2 * CW), bf16), vm((T, CW), bf16), vm((T, CW), bf16), vm((T, CW), bf16),
        vm((8, D), f32), vm((4, gains + T // 128, 128), f32), vm((gains + T // 128, 128), f32), vm((gains, 128), f32),
        vm((nz, gains, 128), f32), vm((1, T), jnp.int32), vm((1, D), f32), vm((1, D), f32),
        vm((1, norm_query.shape[0]), f32), vm((1, norm_query.shape[0]), f32), vm((gains, 128), f32),
        sem((18,)), sem((8, nz)), sem((8, nz)), sem((8, nz)), sem((8, nz)),
        sem((10, nz)), sem((10, nz)), sem((10, nz)), sem((10, nz)),
        sem((4, 2, 3)), sem((4, 2, 3)), sem((3, 4)), sem((3, 4)), sem((nb, 3)), sem((nb, 3)), sem((3,)), sem((3,)),
        sem((4,)), sem((4,)), sem((nz,)), sem((nz,)), sem((33,)),
    ]
    hbm = pl.BlockSpec(memory_space=pl.ANY)
    shape = jax.ShapeDtypeStruct
    results = (
        shape((T, CW), bf16), shape((T, CW), f32), shape((br, QW), f32), shape((br, KW), f32), shape((br, KW), f32),
        shape((QW, br), f32), shape((br, F), f32), shape((br, F), f32), shape((F, br), f32),
    )
    outs = pl.pallas_call(
        functools.partial(layer_kernel, plan),
        out_shape=results + (shape((gains, 128), f32),),
        in_specs=[hbm] * 14,
        out_specs=(hbm,) * 10,
        scratch_shapes=scratch,
        compiler_params=pltpu.CompilerParams(
            collective_id=0, has_side_effects=True, vmem_limit_bytes=64 * 2**20
        ),
        name="layer",
    )(
        tokens, segment_ids, w_query, key_matrix, value_matrix, w_out, w_gate, w_up, w_down,
        norm_attn[None], norm_ffn[None], norm_query[None], norm_key[None], cotangent,
    )
    gain = shape((1, D), f32)
    head_gain = shape((1, norm_query.shape[0]), f32)
    outs = pl.pallas_call(
        hand_out,
        out_shape=results + (gain, gain, head_gain, head_gain),
        in_specs=[hbm] * 10,
        out_specs=(hbm,) * 13,
        scratch_shapes=[vm(v.shape, v.dtype) for v in results + (shape((gains, 128), f32), gain, gain, head_gain, head_gain)]
        + [sem((2, 13))],
        compiler_params=pltpu.CompilerParams(vmem_limit_bytes=63 * 2**20),
        name="hand_out",
    )(*outs)
    return outs[:9] + tuple(v[0] for v in outs[9:])


def solution(mesh):
    in_specs = (
        P("row", "col"), P("row", None), P("row", "col"), P("row", "col"), P("row", "col"), P("col", "row"),
        P("row", "col"), P("row", "col"), P("col", "row"), P(), P(), P(), P(), P("row", "col"),
    )
    out_specs = (
        P("row", "col"), P("row", "col"), P("row", "col"), P("row", "col"), P("row", "col"), P("col", "row"),
        P("row", "col"), P("row", "col"), P("col", "row"), P(), P(), P(), P(),
    )
    return jax.shard_map(
        functools.partial(per_device, mesh.shape["row"]),
        mesh=mesh, in_specs=in_specs, out_specs=out_specs, check_vma=False,
    )
```

```python
import functools
import math

import jax
import jax.numpy as jnp
from jax import lax
from jax.experimental import pallas as pl
from jax.experimental.pallas import tpu as pltpu
from jax.sharding import PartitionSpec as P

epsilon = 1e-05
rope_base = 1000000.0
longest = 512
ids = 8
f32, bf16 = jnp.float32, jnp.bfloat16
MESH = pl.DeviceIdType.MESH
RB = 256


def dot_nn(a, b):
    return lax.dot_general(a, b, (((1,), (0,)), ((), ())), preferred_element_type=f32)


def dot_nt(a, b):
    return lax.dot_general(a, b, (((1,), (1,)), ((), ())), preferred_element_type=f32)


def rows(i, n):
    return pl.ds(pl.multiple_of(i * n, n), n)


LAST = 128
AG_PAIRS, RS_PAIRS = (5, 6), (0, 1, 2, 8)
ORDER = [
    ("out", "a"), ("owny", 1, "a"), ("ownz", 1, "a"), ("gate_up", "a"), ("owny", 2, "a"), ("owny", 0, "a"),
    ("toks", "a"), ("fwd", 1, 1, "e"), ("ownz", 0, "a"), ("tables", "a"), ("down", "a"), ("owny", 6, "a"),
    ("ownz", 2, "a"), ("fwd", 0, 1, "e"), ("cots", "a"), ("fwd", 0, 1, "m"), ("fwd", 0, 2, "m"), ("fwd", 0, 3, "m"),
    ("fwd", 0, 2, "e"), ("tokf", "a"), ("fwd", 1, 1, "m"), ("fwd", 1, 2, "m"), ("fwd", 0, 3, "e"), ("owny", 5, "a"),
    ("fwd", 1, 3, "m"), ("fwd", 1, 2, "e"), ("ownz", 6, "a"), ("fwd", 6, 1, "e"), ("norm", "a"), ("fwd", 1, 3, "e"),
    ("fwd", 2, 1, "m"), ("owny", 3, "a"), ("ownz", 3, "a"), ("fwd", 2, 1, "e"), ("owny", 4, "a"),
    ("fwd", 2, 2, "m"), ("project", "a"), ("fwd", 6, 2, "e"), ("att", 0, "a"), ("fwd", 2, 3, "m"),
    ("aprod", 0, "a"), ("owny", 7, "a"), ("amid", "a"), ("fwd", 6, 1, "m"), ("att", 1, "a"), ("ownz", 4, "a"),
    ("fwd", 3, 1, "m"), ("fwd", 6, 3, "e"), ("aprod", 1, "a"), ("ownz", 5, "a"), ("fwd", 5, 1, "m"),
    ("fwd", 2, 2, "e"), ("fwd", 3, 2, "m"), ("aft", 0, "a"), ("fwd", 3, 3, "m"), ("fwd", 4, 1, "m"),
    ("fwd", 4, 2, "m"), ("fwd", 5, 1, "e"), ("ownz", 7, "a"), ("fwd", 2, 3, "e"), ("fwd", 3, 1, "e"),
    ("aft", 1, "a"), ("fwd", 4, 3, "m"), ("fwd", 3, 2, "e"), ("fwd", 5, 2, "e"), ("cotf", "a"), ("fwd", 7, 1, "m"),
    ("nff", 0, "a"), ("fwd", 5, 2, "m"), ("fwd", 7, 2, "m"), ("fwd", 3, 3, "e"), ("fwd", 5, 3, "e"),
    ("fwd", 7, 3, "m"), ("fwd", 4, 1, "e"), ("ffn", 0, 0, "a"), ("nff", 1, "a"), ("ffn", 0, 1, "a"),
    ("fwd", 5, 3, "m"), ("fwd", 6, 2, "m"), ("fwd", 6, 3, "m"), ("wg", 0, "a"), ("fwd", 4, 2, "e"),
    ("ffn", 1, 0, "a"), ("fwd", 4, 3, "e"), ("ffn", 1, 1, "a"), ("wg", 1, "a"), ("fwd", 7, 1, "e"),
    ("fwd", 7, 2, "e"), ("fwd", 7, 3, "e"), ("gh", 0, 0, "a"), ("gh", 0, 1, "a"), ("wg", 3, "a"),
    ("ffn", 2, 0, "a"), ("ffn", 2, 1, "a"), ("wg", 2, "a"), ("gh", 1, 0, "a"), ("gh", 2, 0, "a"), ("gnfp", 0, "a"),
    ("mid", 3, 0, "e"), ("relay", 0, 0, "m"), ("gnfm", "a"), ("mid", 3, 1, "e"), ("gh", 1, 1, "a"),
    ("mid", 3, 0, "m"), ("relay", 1, 0, "m"), ("gh", 2, 1, "a"), ("relay", 2, 0, "m"), ("wg", 5, "a"),
    ("gnfp", 1, "a"), ("naft", 0, "a"), ("wg", 4, "a"), ("mid", 3, 1, "m"), ("mid", 5, 0, "e"),
    ("relay", 1, 1, "m"), ("mid", 0, 2, "m"), ("naft", 1, "a"), ("snd", 8, "a"), ("mid", 3, 2, "m"),
    ("mid", 5, 0, "m"), ("gmix", 0, "a"), ("mid", 5, 1, "e"), ("relay", 0, 1, "m"), ("relay", 3, 0, "m"),
    ("ab", 0, "a"), ("rlf", 0, "a"), ("rlf", 1, "a"), ("relay", 3, 1, "m"), ("mid", 3, 2, "e"), ("mid", 4, 0, "e"),
    ("relay", 2, 1, "m"), ("mid", 1, 2, "m"), ("gmix", 1, "a"), ("mid", 5, 1, "m"), ("relay", 5, 0, "m"),
    ("relay", 8, 0, "m"), ("brp", "a"), ("wg", 6, "a"), ("brm", "a"), ("mid", 4, 1, "e"), ("mid", 5, 2, "m"),
    ("ab", 1, "a"), ("relay", 8, 1, "m"), ("pb", "a"), ("mid", 4, 2, "e"), ("relay", 5, 1, "m"), ("mid", 4, 0, "m"),
    ("mid", 4, 1, "m"), ("gnp", "a"), ("mid", 4, 2, "m"), ("relay", 4, 0, "m"), ("relay", 4, 1, "m"),
    ("mid", 6, 0, "e"), ("wg", 7, "a"), ("gnm", "a"), ("mid", 6, 1, "e"), ("mid", 7, 0, "e"), ("mid", 6, 0, "m"),
    ("mid", 9, 0, "e"), ("mid", 9, 0, "m"), ("mid", 6, 2, "e"), ("relay", 6, 0, "m"), ("pre", 0, "e"),
    ("mid", 6, 1, "m"), ("mid", 7, 1, "e"), ("pre", 2, "m"), ("mid", 7, 0, "m"), ("pre", 8, "e"),
    ("mid", 9, 1, "e"), ("mid", 6, 2, "m"), ("mid", 9, 1, "m"), ("relay", 6, 1, "m"), ("mid", 2, 2, "m"),
    ("vc", "a"), ("mid", 8, 2, "m"), ("mid", 5, 2, "e"), ("relay", 9, 0, "m"), ("mid", 9, 2, "m"), ("fin", 3, "a"),
    ("mid", 7, 2, "e"), ("pre", 2, "e"), ("mid", 9, 2, "e"), ("brf", "a"), ("pre", 0, "m"), ("pre", 1, "e"),
    ("relay", 7, 0, "m"), ("pre", 8, "m"), ("mid", 7, 1, "m"), ("mid", 7, 2, "m"), ("relay", 9, 1, "m"),
    ("relay", 7, 1, "m"), ("vy", "a"), ("pre", 1, "m"), ("gnfin", "a"), ("fin", 0, "a"), ("fin", 4, "a"),
    ("fin", 5, "a"), ("fin", 9, "a"), ("fin", 6, "a"), ("fin", 2, "a"), ("fin", 8, "a"), ("lof", "a"),
    ("fin", 7, "a"), ("fin", 1, "a"), ("end", "a"),
]


def layer_kernel(
    plan,
    tok_h, seg_h, wq_h, wk_h, wv_h, wo_h, wg_h, wu_h, wd_h, ga_h, gf_h, gq_h, gk_h, cot_h,
    lo_h, gt_h, gquery_h, gkey_h, gvalue_h, gout_h, ggate_h, gup_h, gdown_h, gain_h,
    W, WO, WD, GFO, GFD, G, RY, RZ, RYP, RZP, GF, Tk, Ct, Nm, R1, PRE, QS, KS, VS, KT, VT, DO, MX, PB, A0, B0, S0,
    RES, NF, GG, HID, CS, SN, BIAS, INV, DQ, DKV, AC, BC, SC, LOC, VEC, VCOL, VSUM, VY, VZ,
    seg_ref, ga_ref, gf_ref, gq_ref, gk_ref, gain_ref,
    loc_sem, agz_s, agz_r, agy_s, agy_r, rsy_s, rsy_r, rsz_s, rsz_r,
    cag_s, cag_r, crs_s, crs_r, gn_s, gn_r, lo_s, lo_r, vec_s, vec_r, vz_s, vz_r, out_sem,
):
    nz, tree, CH, RCH, ag_pairs, rs_pairs, place = plan
    T, D = Tk.shape
    br = RY.shape[1]
    QW, KW = PRE.shape[1] // 2, PRE.shape[1] // 4
    PW = 2 * QW + 2 * KW
    F = HID.shape[1]
    FC = F // 3
    HB = RB // 2
    down0 = PW + 2 * F
    nb = T // RB
    CW = D // 4
    GQ = GG.at[:, pl.ds(PW, 2 * QW)]
    PN = GG.at[:, pl.ds(PW + 2 * QW, D)]
    row, col = lax.axis_index("row"), lax.axis_index("col")
    z, y = row // 2, row % 2
    x, c = col // 2, col % 2
    ypeer = (row + 1 - 2 * y, col)
    cpeer = (row, col + 1 - 2 * c)
    xpeer = (row, (1 - x) * 2 + c)
    dpeer = (row, (1 - x) * 2 + 1 - c)
    partner = z + 1 - 2 * (z % 2)
    is_middle = (z == 1) | (z == 2)
    near, far = 2 - z // 2, 3 - 3 * (z // 2)

    def zdev(zz):
        return (zz * 2 + y, col)

    def zsrc(k):
        return [z, partner, near, far][k] if tree else (z + nz - k) % nz

    def zto(i):
        return [near, far, partner, z][i]

    def rc(src, dst, ss, rs, dev):
        return pltpu.make_async_remote_copy(
            src_ref=src, dst_ref=dst, send_sem=ss, recv_sem=rs, device_id=dev, device_id_type=MESH
        )

    def loop(n, body, first=0):
        def step(i, carry):
            body(i)
            return carry

        lax.fori_loop(first, n, step, 0)

    own = rows(row, br)
    mine = pl.ds(pl.multiple_of(col * CW, CW), CW)
    local = [
        (wq_h, W.at[own, pl.ds(0, QW)]),
        (wk_h, W.at[own, pl.ds(QW, KW)]),
        (wv_h, W.at[own, pl.ds(QW + KW, KW)]),
        (wo_h, WO),
        (tok_h, Tk.at[:, mine]),
        (cot_h, Ct.at[:, mine]),
    ]
    for j in range(3):
        local.append((wg_h.at[:, pl.ds(FC * j, FC)], W.at[own, pl.ds(PW + 2 * FC * j, FC)]))
        local.append((wu_h.at[:, pl.ds(FC * j, FC)], W.at[own, pl.ds(PW + 2 * FC * j + FC, FC)]))
    local.append((wd_h, WD))
    local += [(seg_h, seg_ref), (ga_h, ga_ref), (gf_h, gf_ref), (gq_h, gq_ref), (gk_h, gk_ref)]
    local = [pltpu.make_async_copy(s, d, loc_sem.at[i]) for i, (s, d) in enumerate(local)]

    def wblk(ch, zz, yy):
        start, width = CH[ch]
        return W.at[rows(zz * 2 + yy, br), pl.ds(start, width)]

    def wpair(ch, zz):
        start, width = CH[ch]
        return W.at[rows(zz, 2 * br), pl.ds(start, width)]

    def ag_z(ch, k, src, slot, dev):
        b = wpair(ch, src) if ch in ag_pairs else wblk(ch, src, y)
        return rc(b, b, agz_s.at[ch, k], agz_r.at[ch, slot], zdev(dev))

    def ag_y(ch, k, src, yy):
        b = wblk(ch, src, yy)
        return rc(b, b, agy_s.at[ch, k], agy_r.at[ch, k], ypeer)

    def own_y(ch):
        ag_y(ch, 0, z, y).start()

    def own_z(ch):
        if ch in ag_pairs:
            ag_y(ch, 0, z, 1 - y).wait_recv()
        if tree:
            ag_z(ch, 0, z, 1, partner).start()
            ag_z(ch, 1, z, jnp.where(is_middle, 2, 3), near).start()
        else:
            loop(nz, lambda k: ag_z(ch, k, z, k, (z + k) % nz).start(), 1)

    def forward(ch, k, middle):
        if not tree:
            if k == 3 and middle:

                def step(k):
                    ag_z(ch, k, zsrc(k), k, z).wait_recv()
                    ag_y(ch, k, zsrc(k), y).start()

                loop(nz, step, 1)
            return
        relayed = middle and k >= 2
        if ch in ag_pairs and not relayed:
            return
        ag_z(ch, k, zsrc(k), k, partner).wait_recv()
        if relayed:
            ag_z(ch, k, zsrc(k), k, partner).start()
        if ch not in ag_pairs:
            ag_y(ch, k, zsrc(k), y).start()

    def ag_wait(ch):
        if not tree:
            loop(nz, lambda k: ag_y(ch, k, zsrc(k), 1 - y).wait_recv())
        elif ch in ag_pairs:
            ag_z(ch, 0, partner, 1, partner).wait_recv()

            @pl.when(jnp.logical_not(is_middle))
            def _():
                ag_z(ch, 0, near, 2, partner).wait_recv()
                ag_z(ch, 0, far, 3, partner).wait_recv()

        else:
            for k in range(4):
                ag_y(ch, k, zsrc(k), 1 - y).wait_recv()

    def ag_done(ch):
        if not tree:
            loop(nz, lambda k: ag_y(ch, k, zsrc(k), y).wait_send())
            loop(nz, lambda k: ag_z(ch, k, z, k, z).wait_send(), 1)
            return
        for k in range(1 if ch in ag_pairs else 4):
            ag_y(ch, k, zsrc(k), y).wait_send()
        ag_z(ch, 0, z, 1, partner).wait_send()
        ag_z(ch, 1, z, 2, near).wait_send()

        @pl.when(is_middle)
        def _():
            ag_z(ch, 2, near, 2, partner).wait_send()
            ag_z(ch, 3, far, 3, partner).wait_send()

    def cag(n, block, parts=1):
        def copy(i, d, dev, h):
            return rc(block(d, h), block(d, h), cag_s.at[n, h, i], cag_r.at[n, h, i], dev)

        def start(h=0):
            copy(0, col, cpeer, h).start()
            copy(1, col, xpeer, h).start()

        def forward(h=0):
            copy(1, (1 - x) * 2 + c, xpeer, h).wait_recv()
            copy(2, (1 - x) * 2 + c, cpeer, h).start()

        def wait(far):
            for h in range(parts):
                if far:
                    copy(2, (1 - x) * 2 + 1 - c, cpeer, h).wait_recv()
                else:
                    copy(0, x * 2 + 1 - c, cpeer, h).wait_recv()

        def done():
            for h in range(parts):
                copy(0, col, cpeer, h).wait_send()
                copy(1, col, xpeer, h).wait_send()
                copy(2, (1 - x) * 2 + c, cpeer, h).wait_send()

        return start, forward, wait, done

    def col_block(ref):
        return lambda d, h: ref.at[:, pl.ds(pl.multiple_of(d * CW, CW), CW)]

    def row_block(ref):
        return lambda d, h: ref.at[rows(d * 2 + h, HB), :]

    tok_start, tok_forward, tok_wait, tok_done = cag(0, col_block(Tk))
    cot_start, cot_forward, cot_wait, cot_done = cag(1, col_block(Ct))
    nf_start, nf_forward, nf_wait, nf_done = cag(2, row_block(NF), 2)
    rl_start, rl_forward, rl_wait, rl_done = cag(3, row_block(Ct), 2)

    def crs(n, A, B, S):
        def to_core(i, xx, cc):
            return rc(PB.at[rows(xx * 2 + cc, RB), :], A(xx), crs_s.at[n, i], crs_r.at[n, i], cpeer)

        def to_x(h):
            half = rows(h, HB)
            return rc(S.at[half, :], B.at[half, :], crs_s.at[n, 2 + h], crs_r.at[n, 2 + h], xpeer)

        def produce(half, part):
            def step(i):
                xx = jnp.where(i < 2, 1 - x, x)
                cc = jnp.where(i % 2 == 0, 1 - c, c)
                PB[rows(xx * 2 + cc, RB), :] = part(xx * 2 + cc).astype(bf16)

                @pl.when(i % 2 == 0)
                def _():
                    to_core(i // 2, xx, 1 - c).start()

            loop(2 * half + 2, step, 2 * half)

        def middle():
            to_core(0, 1 - x, c).wait_recv()

            def step(i):
                r = rows(i, 32)
                block = PB[pl.ds(pl.multiple_of(((1 - x) * 2 + c) * RB + i * 32, 32), 32), :]
                S[r, :] = (block.astype(f32) + A(1 - x)[r, :].astype(f32)).astype(bf16)

            for h in range(2):
                loop(HB // 32 * (h + 1), step, HB // 32 * h)
                to_x(h).start()

        def total(h, use):
            if h == 0:
                to_core(1, x, c).wait_recv()
            to_x(h).wait_recv()

            def step(i):
                r = rows(i, 32)
                at = pl.ds(pl.multiple_of(col * RB + i * 32, 32), 32)
                use(r, at, PB[at, :].astype(f32) + A(x)[r, :].astype(f32) + B[r, :].astype(f32))

            loop(HB // 32 * (h + 1), step, HB // 32 * h)

        def done():
            to_core(0, 1 - x, 1 - c).wait_send()
            to_core(1, x, 1 - c).wait_send()
            to_x(0).wait_send()
            to_x(1).wait_send()

        return produce, middle, total, done

    a_produce, a_middle, a_total, a_done = crs(0, lambda i: A0.at[i], B0, S0)
    n_produce, n_middle, n_total, n_done = crs(1, lambda i: A0.at[i], B0, S0)
    b_produce, b_middle, b_total, b_done = crs(
        2, lambda i: NF.at[rows(i, RB), :], NF.at[pl.ds(2 * RB, RB), :], NF.at[pl.ds(3 * RB, RB), :]
    )

    def other_first(half, i):
        return jnp.where(half == 0, 1 - x, x) * 2 + jnp.where(i == 0, 1 - c, c)

    def own_first(half, i):
        return jnp.where(half == 0, x, 1 - x) * 2 + jnp.where(i == 0, c, 1 - c)

    def rows_of_chip(mine_first, half, work):
        for xx in range(2):

            @pl.when(x == (xx if mine_first == (half == 0) else 1 - xx))
            def _():
                work(xx)

    def gcol(ch):
        start, width = RCH[ch]
        return (G, start - PW, width) if start >= PW else (GG, start, width)

    def gblk(ch, zz, yy):
        ref, start, width = gcol(ch)
        return ref.at[rows(zz * 2 + yy, br), pl.ds(start, width)]

    def part_of(ch):
        return pl.ds(place[ch], RCH[ch][1])

    def rs_y(ch, zz, yy):
        landing = RYP.at[:, part_of(ch)] if ch in rs_pairs else RY.at[zz, :, part_of(ch)]
        return rc(gblk(ch, zz, yy), landing, rsy_s.at[ch, zz], rsy_r.at[ch, zz], ypeer)

    def rs_z(ch, k, zz, slot, dev):
        if ch in rs_pairs:
            ref, start, width = gcol(ch)
            src, dst = ref.at[rows(zz, 2 * br), pl.ds(start, width)], RZP.at[slot, :, part_of(ch)]
        else:
            src, dst = RY.at[zz, :, part_of(ch)], RZ.at[slot, :, part_of(ch)]
        return rc(src, dst, rsz_s.at[ch, k], rsz_r.at[ch, slot], zdev(dev))

    zper = RB // (2 * br)

    def weight_grad(left, pieces):
        def one(i, d):
            lt = jnp.transpose(left[:, rows(d, RB)])
            for ch, right in pieces:
                ref, start, width = gcol(ch)
                ref[rows(d, RB), pl.ds(start, right.shape[1])] = dot_nn(lt, right[...]).astype(bf16)
                if ch not in rs_pairs:
                    loop(zper, lambda s: rs_y(ch, d * zper + s, 1 - y).start())
                else:

                    @pl.when((i == 2) | ((i < 2) & jnp.logical_not(is_middle)))
                    def _():
                        rs_z(ch, i, d, i, partner).start()

        if tree:

            def step(i):
                one(i, jnp.where(i == 0, near, jnp.where(i == 1, far, jnp.where(i == 2, partner, z))))

            loop(4, step)
        else:
            loop(D // RB, lambda i: one(i, (row * br // RB + 1 + i) % (D // RB)))

    def send_grad(ch):
        if tree:
            for i in range(4):
                if ch not in rs_pairs:
                    rs_y(ch, zto(i), 1 - y).start()
                elif i == 2:
                    rs_z(ch, i, zto(i), i, partner).start()
                elif i < 2:

                    @pl.when(jnp.logical_not(is_middle))
                    def _():
                        rs_z(ch, i, zto(i), i, partner).start()

        else:
            loop(nz, lambda k: rs_y(ch, k, 1 - y).start())

    def rs_mid(ch, i, middle):
        ref, gstart, width = gcol(ch)

        def one(zz):
            rs_y(ch, zz, y).wait_recv()

            def add(j):
                r = rows(j, 16)
                g = ref[pl.ds(pl.multiple_of((zz * 2 + y) * br + j * 16, 16), 16), pl.ds(gstart, width)]
                t = RY[zz, r, part_of(ch)]
                RY[zz, r, part_of(ch)] = (g.astype(f32) + t.astype(f32)).astype(bf16)

            loop(br // 16, add)

        if not tree:
            if i == 2 and middle:

                def step(k):
                    zz = (z + k) % nz
                    one(zz)
                    rs_z(ch, k, zz, k - 1, zz).start()

                loop(nz, step, 1)
        elif ch not in rs_pairs:
            one(zto(i))
            if i == 2 or not middle:
                rs_z(ch, i, zto(i), i, partner).start()

    def rs_relay(ch, i):
        if not tree:
            return
        zz = zto(i)
        rs_z(ch, i, zz, i, partner).wait_recv()
        ref, gstart, width = gcol(ch)

        def add(j):
            r = rows(j, 16)
            if ch in rs_pairs:
                at = pl.ds(pl.multiple_of(zz * 2 * br + j * 16, 16), 16)
                t = ref[at, pl.ds(gstart, width)].astype(f32) + RZP[i, r, part_of(ch)].astype(f32)
                ref[at, pl.ds(gstart, width)] = t.astype(bf16)
            else:
                t = RY[zz, r, part_of(ch)].astype(f32) + RZ[i, r, part_of(ch)].astype(f32)
                RY[zz, r, part_of(ch)] = t.astype(bf16)

        loop((2 * br if ch in rs_pairs else br) // 16, add)
        rs_z(ch, i, zz, 3, zz).start()

    def rs_pre(ch):
        if ch not in rs_pairs:
            return
        for slot in (2, 3):
            rs_z(ch, 2, z, slot, partner).wait_recv()
        ref, gstart, width = gcol(ch)

        def add(j):
            at = pl.ds(pl.multiple_of((z * 2 + 1 - y) * br + j * 16, 16), 16)
            r = pl.ds(pl.multiple_of((1 - y) * br + j * 16, 16), 16)
            t = ref[at, pl.ds(gstart, width)].astype(f32)
            t = t + RZP[2, r, part_of(ch)].astype(f32) + RZP[3, r, part_of(ch)].astype(f32)
            ref[at, pl.ds(gstart, width)] = t.astype(bf16)

        loop(br // 16, add)
        rs_y(ch, z, 1 - y).start()

    def outs(ch):
        start, width = RCH[ch]
        if start >= down0:
            pairs = [(GFD.at[pl.ds(start - down0, width), :], gdown_h.at[pl.ds(start - down0, width), :])]
        elif start >= PW:
            third = (start - PW) // (2 * FC)
            at = start - PW - 2 * FC * third
            pairs = []
            for target, low in ((ggate_h, 0), (gup_h, FC)):
                first, last = max(at, low), min(at + width, low + FC)
                if first < last:
                    held = GF.at[:, pl.ds(start - 2 * KW + first - at, last - first)]
                    pairs.append((held, target.at[:, pl.ds(third * FC + first - low, last - first)]))
        elif start == 2 * QW:
            pairs = [(GFO, gout_h)]
        elif start == 0:
            pairs = [(GF.at[:, pl.ds(0, QW)], gquery_h)]
        else:
            pairs = [
                (GF.at[:, pl.ds(QW, KW)], gkey_h),
                (GF.at[:, pl.ds(QW + KW, KW)], gvalue_h),
            ]
        return [pltpu.make_async_copy(a, b, out_sem.at[3 * ch + i]) for i, (a, b) in enumerate(pairs)]

    def rs_fin(ch):
        ref, gstart, width = gcol(ch)
        start = RCH[ch][0]
        paired = ch in rs_pairs
        rs_y(ch, z, y).wait_recv()
        if not tree:
            loop(nz - 1, lambda k: rs_z(ch, 0, z, k, z).wait_recv())
        elif not paired:
            for slot in (2, 3):
                rs_z(ch, 0, z, slot, z).wait_recv()

        def total(r0, rn, c0, cn):
            r = pl.ds(r0, rn)
            g = ref[pl.ds(pl.multiple_of(row * br + r0, 16), rn), pl.ds(gstart + c0, cn)]
            part = pl.ds(place[ch] + c0, cn)
            if paired:
                rp = pl.ds(pl.multiple_of(y * br + r0, 16), rn)
                t = RZP[2, rp, part].astype(f32) + RZP[3, rp, part].astype(f32)
                return g.astype(f32) + t + RYP[r, part].astype(f32)
            t = g.astype(f32) + RY[z, r, part].astype(f32)
            if tree:
                return t + (RZ[2, r, part].astype(f32) + RZ[3, r, part].astype(f32))
            return lax.fori_loop(0, nz - 1, lambda k, t: t + RZ[k, r, part].astype(f32), t)

        if start >= down0 or start == 2 * QW:
            for c0 in range(0, width, 128):
                t = jnp.transpose(total(0, br, c0, 128))
                if start >= down0:
                    GFD[pl.ds(start - down0 + c0, 128), :] = t
                else:
                    GFO[pl.ds(c0, 128), :] = t
        else:
            at = start - 2 * KW if start >= PW else start

            def add(i):
                r0 = pl.multiple_of(i * 16, 16)
                GF[pl.ds(r0, 16), pl.ds(at, width)] = total(r0, 16, 0, width)

            loop(br // 16, add)
        for copy in outs(ch):
            copy.start()

    def rs_done(ch):
        if ch in rs_pairs:
            rs_y(ch, z, 1 - y).wait_send()
        else:
            loop(nz, lambda zz: rs_y(ch, zz, 1 - y).wait_send())
        if tree:
            for i in range(3):
                rs_z(ch, i, zto(i), 0, partner).wait_send()
        else:
            loop(nz, lambda k: rs_z(ch, k, z, 0, z).wait_send(), 1)
        for copy in outs(ch):
            copy.wait()

    bar = pltpu.get_barrier_semaphore()
    for dev in (ypeer, cpeer, xpeer, dpeer):
        pl.semaphore_signal(bar, inc=1, device_id=dev, device_id_type=MESH)

    def greet(k):
        pl.semaphore_signal(bar, inc=1, device_id=zdev((z + k) % nz), device_id_type=MESH)

    loop(nz, greet, 1)
    for i in (0, 1, 2, 4, 13, 14, 15, 16, 17, 3, 6, 7, 8, 9, 10, 11, 5, 12):
        local[i].start()
    for i in range(3):
        local[i].wait()
    pl.semaphore_wait(bar, 4 + nz - 1)

    def load_out():
        local[3].wait()
        W[own, pl.ds(2 * QW, QW)] = jnp.transpose(WO[...])

    def load_gate_up():
        for i in range(6, 12):
            local[i].wait()

    def load_down():
        local[12].wait()
        W[own, pl.ds(down0, F)] = jnp.transpose(WD[...])

    def start_tokens():
        local[4].wait()
        tok_start()

    def start_cotangent():
        local[5].wait()
        cot_start()

    lane = lax.broadcasted_iota(jnp.int32, (1, 128), 1)

    def head_gain(p):
        gain = (gq_ref if p < 2 else gk_ref)[...]
        return jnp.concatenate([gain, gain], axis=1)

    hb = nb // 2
    spans = []
    for half in range(2):
        low = max(0, RB * half * hb - longest)
        if half * RB * hb >= longest:
            spans.append((longest + RB, RB, low, sum(s[0] for s in spans) * hb))
        else:
            spans.append((RB * hb * (half + 1), 0, 0, sum(s[0] for s in spans) * hb))

    def tables():
        for i in range(13, 18):
            local[i].wait()
        VEC[...] = jnp.zeros(VEC.shape, f32)
        seg = seg_ref[...]
        first = jnp.zeros((1, T), jnp.int32)
        for d in range(ids):
            count = jnp.sum((seg == d).astype(f32), axis=1, keepdims=True).astype(jnp.int32)
            first = first + jnp.where(seg > d, count, 0)
        place = lax.broadcasted_iota(jnp.int32, (1, T), 1)
        inverse_freq = jnp.exp((lane % 32).astype(f32) * (-2.0 / 64 * math.log(rope_base)))
        CS[...] = jnp.transpose(jnp.broadcast_to((place - first).astype(f32), (128, T)))

        def fill(i):
            angle = CS[rows(i, 128), :] * inverse_freq
            sine = jnp.sin(angle)
            CS[rows(i, 128), :] = jnp.cos(angle)
            SN[rows(i, 128), :] = jnp.where(lane % 64 < 32, -sine, sine)

        loop(T // 128, fill)
        for i in range(nb):
            width, pace, start, at = spans[i // hb]
            start, at = start + pace * (i % hb), at + width * (i % hb)
            key_place = lax.broadcasted_iota(jnp.int32, (width, RB), 0) + start
            q_place, q_first = place[:, RB * i : RB * (i + 1)], first[:, RB * i : RB * (i + 1)]
            seen = (key_place <= q_place) & (key_place >= q_first)
            BIAS[pl.ds(at, width), :] = jnp.where(seen, 0.0, -1e30).astype(bf16)

    def head_mean(v):
        half_a = lax.broadcasted_iota(jnp.int32, (128, 128), 0) // 64
        half_b = lax.broadcasted_iota(jnp.int32, (128, 128), 1) // 64
        mean_matrix = jnp.where(half_a == half_b, 1.0 / 64, 0.0).astype(bf16)
        high = v.astype(bf16)
        low = (v - high.astype(f32)).astype(bf16)
        return dot_nn(high, mean_matrix) + dot_nn(low, mean_matrix)

    def turn(v):
        return jnp.where(lane % 64 < 32, pltpu.roll(v, 96, 1), pltpu.roll(v, 32, 1))

    def norm_tokens():
        tok_wait(False)
        tok_wait(True)

        def step(i):
            t = Tk[rows(i, 128), :].astype(f32)
            r = lax.rsqrt(jnp.mean(t * t, axis=1, keepdims=True) + epsilon)
            R1[rows(i, 128), :] = jnp.broadcast_to(r, (128, 128))
            Nm[rows(i, 128), :] = (t * r * ga_ref[...]).astype(bf16)

        loop(T // 128, step)

    def project():
        ag_wait(0)

        def step(i):
            r = rows(i, RB)
            PRE[r, :] = dot_nn(Nm[r, :], W[:, pl.ds(0, 2 * QW)])
            cos, sin = CS[r, :], SN[r, :]
            for p in range(3):
                v = PRE[r, pl.ds(128 * p, 128)]
                n = v * lax.rsqrt(head_mean(v * v) + epsilon)
                u = n * head_gain(p)
                u = (u * cos + turn(u) * sin).astype(bf16)
                if p < 2:
                    u = u * jnp.asarray(0.125, bf16)
                    QS[p, 0, r, :] = u[:, :64]
                    QS[p, 1, r, :] = u[:, 64:]
                else:
                    KS[0, r, :] = u[:, :64]
                    KS[1, r, :] = u[:, 64:]
                    ut = jnp.transpose(u)
                    KT[0, :, r] = ut[:64, :]
                    KT[1, :, r] = ut[64:, :]
            v = PRE[r, pl.ds(384, 128)].astype(bf16)
            VS[0, r, :] = v[:, :64]
            VS[1, r, :] = v[:, 64:]
            vt = jnp.transpose(v)
            VT[0, :, r] = vt[:64, :]
            VT[1, :, r] = vt[64:, :]

        loop(nb, step)

    def per_block(half, work):
        width, pace, low, at = spans[half]

        def step(n):
            i, h = n // 2, n % 2
            keys = pl.ds(pl.multiple_of(low + pace * i, RB), width) if pace else pl.ds(low, width)
            bias = BIAS[pl.ds(pl.multiple_of(at + width * i, RB), width), :].astype(f32)
            work(h, half * hb + i, keys, jnp.concatenate([bias, bias], axis=1), rows(half * hb + i, RB))

        loop(2 * hb, step)

    def attend(half):
        def work(h, i, keys, bias, r):
            q = QS[h, :, r, :].reshape(2 * RB, 64)
            e = jnp.exp(dot_nt(KS[h, keys, :], q) + bias)
            inv = 1.0 / jnp.sum(e, axis=0, keepdims=True)
            INV[h, i] = inv
            o = dot_nn(VT[h, :, keys], (e * inv).astype(bf16))
            o = jnp.concatenate([o[:, :RB], o[:, RB:]], axis=0)
            MX[r, pl.ds(pl.multiple_of(h * 128, 128), 128)] = jnp.transpose(o).astype(bf16)

        per_block(half, work)

    def attention_out(half):
        if half == 0:
            ag_wait(1)
        a_produce(half, lambda d: dot_nt(MX[rows(d, RB), :], W[:, pl.ds(2 * QW, QW)]))

    def after_attention(h):
        def use(r, at, summed):
            v = Tk[at, :].astype(f32) + summed
            RES[r, :] = v
            n = v * lax.rsqrt(jnp.mean(v * v, axis=1, keepdims=True) + epsilon)
            NF[at, :] = (n * gf_ref[...]).astype(bf16)

        a_total(h, use)
        nf_start(h)

    def ffn(j, half):
        if j == 0:
            nf_wait(half == 1)
        if half == 0:
            ag_wait(2 + j)
        elif j == 0:
            nf_done()

        def step(i):
            r = rows(own_first(half, i), RB)
            n = NF[r, :]
            gate = dot_nn(n, W[:, pl.ds(PW + 2 * FC * j, FC)])
            up = dot_nn(n, W[:, pl.ds(PW + 2 * FC * j + FC, FC)])
            sig = 1.0 / (1.0 + jnp.exp(-gate))
            act = gate * sig
            HID[r, pl.ds(FC * j, FC)] = (act * up).astype(bf16)
            GG[r, pl.ds(2 * FC * j, FC)] = (up * (sig + act * (1.0 - sig))).astype(bf16)
            GG[r, pl.ds(2 * FC * j + FC, FC)] = act.astype(bf16)

        loop(2, step)

    def grad_weights(what):
        if what < 3:
            if what == 0:
                cot_wait(False)
                cot_wait(True)
                cot_done()
            weight_grad(Ct, [(what, HID.at[:, pl.ds(FC * what, FC)])])
        elif what < 6:
            weight_grad(NF, [(what, GG.at[:, pl.ds(2 * FC * (what - 3), 2 * FC)])])
        elif what == 6:
            weight_grad(Ct, [(6, MX)])
        else:
            weight_grad(Nm, [(7, GQ.at[:, pl.ds(0, QW)]), (9, GQ.at[:, pl.ds(QW, 2 * KW)])])

    def grad_hidden(j, half):
        if half == 0:
            ag_wait(5 + j)

        def step(i):
            r = rows(other_first(half, i), RB)
            gh = dot_nn(Ct[r, :], W[:, pl.ds(down0 + FC * j, FC)])
            a, b = pl.ds(2 * FC * j, FC), pl.ds(2 * FC * j + FC, FC)
            GG[r, a] = (gh * GG[r, a].astype(f32)).astype(bf16)
            GG[r, b] = (gh * GG[r, b].astype(f32)).astype(bf16)

        loop(2, step)

    def grad_ffn_norm(half):
        if half == 0:
            a_done()
        n_produce(half, lambda d: dot_nt(GG[rows(d, RB), :], W[:, pl.ds(PW, 2 * F)]))

    def after_ffn(h):
        def use(r, at, gy):
            v = RES[r, :]
            inv = lax.rsqrt(jnp.mean(v * v, axis=1, keepdims=True) + epsilon)
            n = v * inv
            VEC[1:2, :] += jnp.sum(gy * n, axis=0, keepdims=True)
            g = gy * gf_ref[...]
            g = inv * (g - n * jnp.mean(g * n, axis=1, keepdims=True))
            Ct[at, :] = (Ct[at, :].astype(f32) + g).astype(bf16)

        n_total(h, use)
        rl_start(h)

    def grad_mixed(half):
        rl_wait(half == 1)
        if half == 0:
            DKV[...] = jnp.zeros(DKV.shape, f32)

        def step(i):
            r = rows(own_first(half, i), RB)
            g = dot_nn(Ct[r, :], W[:, pl.ds(2 * QW, QW)]).astype(bf16)
            for p in range(2):
                DO[p, 0, r, :] = g[:, 128 * p : 128 * p + 64]
                DO[p, 1, r, :] = g[:, 128 * p + 64 : 128 * p + 128]

        loop(2, step)

    def attend_back(half):
        def work(h, i, keys, bias, r):
            q = QS[h, :, r, :].reshape(2 * RB, 64)
            do = DO[h, :, r, :].reshape(2 * RB, 64)
            p = jnp.exp(dot_nt(KS[h, keys, :], q) + bias) * INV[h, i]
            dp = dot_nt(VS[h, keys, :], do)
            ds = (p * (dp - jnp.sum(p * dp, axis=0, keepdims=True))).astype(bf16)
            DKV[h, keys, :] += jnp.concatenate([dot_nn(ds, q), dot_nn(p.astype(bf16), do)], axis=1)
            g = dot_nn(KT[h, :, keys], ds) * 0.125
            g = jnp.concatenate([g[:, :RB], g[:, RB:]], axis=0)
            DQ[r, pl.ds(pl.multiple_of(h * 128, 128), 128)] = jnp.transpose(g)

        per_block(half, work)

    def project_back():
        def step(i):
            r = rows(i, RB)
            cos, sin = CS[r, :], SN[r, :]
            for p in range(3):
                if p < 2:
                    g = DQ[r, pl.ds(128 * p, 128)]
                else:
                    g = jnp.concatenate([DKV[0, r, pl.ds(0, 64)], DKV[1, r, pl.ds(0, 64)]], axis=1)
                g = g * cos - turn(g) * sin
                v = PRE[r, pl.ds(128 * p, 128)]
                inv = lax.rsqrt(head_mean(v * v) + epsilon)
                n = v * inv
                s = pl.ds(0 if p < 2 else 128, 128)
                VEC[2:3, s] += jnp.sum(g * n, axis=0, keepdims=True)
                g = g * head_gain(p)
                GQ[r, pl.ds(128 * p, 128)] = (inv * (g - n * head_mean(g * n))).astype(bf16)
            v = jnp.concatenate([DKV[0, r, pl.ds(64, 64)], DKV[1, r, pl.ds(64, 64)]], axis=1)
            GQ[r, pl.ds(384, 128)] = v.astype(bf16)

        loop(nb, step)

    def gn_core(i, k, xx, cc):
        return rc(
            PN.at[rows(i, RB), pl.ds(pl.multiple_of((xx * 2 + cc) * CW, CW), CW)],
            AC.at[rows(i, RB), pl.ds(pl.multiple_of(xx * CW, CW), CW)],
            gn_s.at[i, k], gn_r.at[i, k], cpeer,
        )

    def gn_x(i):
        return rc(SC.at[rows(i, RB), :], BC.at[rows(i, RB), :], gn_s.at[i, 2], gn_r.at[i, 2], xpeer)

    others = [(0, x * 2 + 1 - c, cpeer), (1, (1 - x) * 2 + c, xpeer), (2, (1 - x) * 2 + 1 - c, dpeer)]
    gains = VY.shape[0]
    vec_y = rc(VSUM.at[pl.ds(0, gains), :], VY, vec_s.at[3], vec_r.at[3], ypeer)

    def vec_copy(i, which, dev):
        return rc(VCOL.at[which], VCOL.at[which], vec_s.at[i], vec_r.at[i], dev)

    def vz_copy(k, src):
        return rc(VZ.at[src], VZ.at[src], vz_s.at[k], vz_r.at[k], zdev((z + k) % nz))

    def gn_produce():
        def step(i):
            r = rows(i, RB)
            g = dot_nt(GQ[r, :], W[:, pl.ds(0, 2 * QW)])
            PN[r, :] = g.astype(bf16)
            gn_core(i, 0, 1 - x, 1 - c).start()
            gn_core(i, 1, x, 1 - c).start()
            g = g * (Tk[r, :].astype(f32) * R1[r, pl.ds(0, 1)])
            VEC[0:1, :] += jnp.sum(g, axis=0, keepdims=True)
            s = jnp.sum(g * ga_ref[...], axis=1, keepdims=True)
            VEC[3:4, r] = jnp.transpose(jnp.broadcast_to(s, (RB, 128)))[0:1, :]

        loop(nb, step)
        for i in range(D // 128):
            s = pl.ds(128 * i, 128)
            VCOL[col, pl.ds(i, 1), :] = VEC[0:1, s]
            VCOL[col, pl.ds(D // 128 + i, 1), :] = VEC[1:2, s]
        for i in range(2):
            VCOL[col, pl.ds(D // 64 + i, 1), :] = VEC[2:3, pl.ds(128 * i, 128)]
        for i in range(T // 128):
            VCOL[col, pl.ds(gains + i, 1), :] = VEC[3:4, pl.ds(128 * i, 128)]
        for i, _, dev in others:
            vec_copy(i, col, dev).start()

    def gn_middle():
        def step(i):
            r = rows(i, RB)
            gn_core(i, 0, 1 - x, c).wait_recv()
            a = PN[r, pl.ds(pl.multiple_of(((1 - x) * 2 + c) * CW, CW), CW)].astype(f32)
            b = AC[r, pl.ds(pl.multiple_of((1 - x) * CW, CW), CW)].astype(f32)
            SC[r, :] = (a + b).astype(bf16)
            gn_x(i).start()

        loop(nb, step)

    def vec_col():
        for i, d, dev in others:
            vec_copy(i, d, dev).wait_recv()
        VSUM[...] = (VCOL[0] + VCOL[1]) + (VCOL[2] + VCOL[3])
        vec_y.start()

    def vec_row():
        vec_y.wait_recv()
        VZ[z] = VSUM[0:gains, :] + VY[...]
        loop(nz, lambda k: vz_copy(k, z).start(), 1)

    gt_copy = pltpu.make_async_copy(DQ, gt_h, out_sem.at[30])
    lo_out = pltpu.make_async_copy(LOC, lo_h, out_sem.at[31])

    def gn_finish():
        def step(i):
            r = rows(i, RB)
            gn_core(i, 1, x, c).wait_recv()
            gn_x(i).wait_recv()
            g = PN[r, mine].astype(f32) + AC[r, pl.ds(pl.multiple_of(x * CW, CW), CW)].astype(f32)
            g = (g + BC[r, :].astype(f32)) * ga_ref[:, mine]
            inv = R1[r, pl.ds(0, 1)]
            s = [VSUM[pl.ds(gains + 2 * i + j, 1), :] for j in range(2)]
            s = jnp.transpose(jnp.broadcast_to(jnp.concatenate(s, axis=1), (128, RB)))[:, 0:1] * (1.0 / D)
            n = Tk[r, mine].astype(f32) * inv
            DQ[r, :] = Ct[r, mine].astype(f32) + inv * (g - n * s)

        loop(nb, step)
        gt_copy.start()

    def lo_copy(i, d, dev):
        return rc(
            S0.at[:, pl.ds(pl.multiple_of(d * CW, CW), CW)], LOC.at[rows(col, RB), :], lo_s.at[i], lo_r.at[i], dev
        )

    def branch():
        n_done()
        for half in range(2):
            b_produce(half, lambda d: dot_nt(HID[rows(d, RB), :], W[:, pl.ds(down0, F)]))

    def block_out():
        def use(r, at, summed):
            S0[r, :] = (RES[r, :] + summed).astype(bf16)

        b_total(0, use)
        b_total(1, use)
        for i, d, dev in others:
            lo_copy(i, d, dev).start()
        LOC[rows(col, RB), :] = S0[:, mine]

    def block_out_wait():
        for i, d, dev in others:
            lo_copy(i, d, dev).wait_recv()
        lo_out.start()

    def finish():
        loop(nz, lambda k: vz_copy(k, (z + nz - k) % nz).wait_recv(), 1)
        gain_ref[...] = lax.fori_loop(1, nz, lambda k, t: t + VZ[k], VZ[0])
        gain_out = pltpu.make_async_copy(gain_ref, gain_h, out_sem.at[32])
        gain_out.start()
        rl_done()
        b_done()
        for i, d, dev in others:
            lo_copy(i, d, dev).wait_send()
            vec_copy(i, col, dev).wait_send()
        vec_y.wait_send()

        def gn_done(i):
            gn_core(i, 0, 1 - x, 1 - c).wait_send()
            gn_core(i, 1, x, 1 - c).wait_send()
            gn_x(i).wait_send()

        loop(nb, gn_done)
        loop(nz, lambda k: vz_copy(k, z).wait_send(), 1)
        for ch in range(len(RCH)):
            rs_done(ch)
        gt_copy.wait()
        lo_out.wait()
        gain_out.wait()

    def gather_rest(half):
        if half == 0:
            tok_done()
            for ch in range(len(CH)):
                ag_done(ch)
        rl_forward(half)

    steps = {
        "out": load_out, "gate_up": load_gate_up, "down": load_down, "toks": start_tokens, "cots": start_cotangent,
        "owny": own_y, "ownz": own_z, "fwd": forward, "tokf": tok_forward, "cotf": cot_forward,
        "tables": tables, "norm": norm_tokens, "project": project, "att": lambda half: rows_of_chip(False, half, attend), "aprod": attention_out,
        "amid": a_middle, "aft": after_attention, "nff": nf_forward, "ffn": ffn, "wg": grad_weights,
        "gh": grad_hidden, "gnfp": grad_ffn_norm, "gnfm": n_middle, "naft": after_ffn, "rlf": gather_rest,
        "gmix": grad_mixed, "ab": lambda half: rows_of_chip(True, half, attend_back), "snd": send_grad, "pb": project_back, "gnp": gn_produce, "gnm": gn_middle,
        "vc": vec_col, "vy": vec_row,
        "gnfin": gn_finish, "brp": branch, "brm": b_middle, "brf": block_out, "lof": block_out_wait,
        "mid": rs_mid, "relay": rs_relay, "pre": rs_pre, "fin": rs_fin, "end": finish,
    }
    for name, *which, who in ORDER:
        if name in ("fwd", "mid"):
            run = functools.partial(steps[name], *which, who == "m")
        else:
            run = functools.partial(steps[name], *which)
        if who == "a" or not tree:
            if who != "e" or name in ("fwd", "mid"):
                run()
        else:

            @pl.when(is_middle if who == "m" else jnp.logical_not(is_middle))
            def _():
                run()


def hand_out(*refs):
    sources, targets, held, sem = refs[:10], refs[10:23], refs[23:37], refs[37]
    loads = [pltpu.make_async_copy(a, b, sem.at[0, i]) for i, (a, b) in enumerate(zip(sources, held))]
    stores = [pltpu.make_async_copy(a, b, sem.at[1, i]) for i, (a, b) in enumerate(zip(held[:9] + held[10:], targets))]
    gains, attn, ffn, query, key = held[9:]
    for copy in loads[9:] + loads[:9]:
        copy.start()
    loads[9].wait()
    n = attn.shape[1] // 128
    for i in range(n):
        attn[:, pl.ds(128 * i, 128)] = gains[pl.ds(i, 1), :]
        ffn[:, pl.ds(128 * i, 128)] = gains[pl.ds(n + i, 1), :]
    query[...] = gains[pl.ds(2 * n, 1), pl.ds(0, 64)] + gains[pl.ds(2 * n, 1), pl.ds(64, 64)]
    key[...] = gains[pl.ds(2 * n + 1, 1), pl.ds(0, 64)] + gains[pl.ds(2 * n + 1, 1), pl.ds(64, 64)]
    for store in stores[9:]:
        store.start()
    for load, store in zip(loads[:9], stores):
        load.wait()
        store.start()
    for store in stores:
        store.wait()


def per_device(
    n_row, tokens, segment_ids, w_query, key_matrix, value_matrix, w_out, w_gate, w_up, w_down,
    norm_attn, norm_ffn, norm_query, norm_key, cotangent,
):
    T, CW = tokens.shape
    br, QW = w_query.shape
    KW = key_matrix.shape[1]
    F = w_gate.shape[1]
    D = br * n_row
    nz = n_row // 2
    PW = 2 * QW + 2 * KW
    WW = PW + 3 * F
    FC = F // 3
    nb = T // RB
    half = nb // 2 * RB
    area = (half + (longest + RB if half >= longest else 2 * half)) * (nb // 2)
    chunks = [(0, 2 * QW), (2 * QW, QW)]
    chunks += [(PW + 2 * FC * j, 2 * FC) for j in range(3)] + [(PW + 2 * F + FC * j, FC) for j in range(3)]
    start, width = chunks[4]
    last = LAST
    grads = chunks[5:8] + chunks[2:4] + [(start, width - last), chunks[1], (0, QW), (start + width - last, last)]
    grads.append((QW, 2 * KW))
    gains = 2 * D // 128 + 8
    tree = nz == 4
    ag_pairs, rs_pairs = (AG_PAIRS, RS_PAIRS) if tree else ((), ())
    place, widths = [], [0, 0]
    for ch, (_, width) in enumerate(grads):
        paired = ch in rs_pairs
        place.append(widths[paired])
        widths[paired] += width
    plan = (nz, tree, chunks, grads, ag_pairs, rs_pairs, place)
    single, paired = widths[0], max(widths[1], 128)
    slots = 4 if tree else nz - 1
    vm, sem = pltpu.VMEM, pltpu.SemaphoreType.DMA
    scratch = [
        vm((D, WW), bf16), vm((QW, br), bf16), vm((F, br), bf16), vm((QW, br), f32), vm((F, br), f32),
        vm((D, 3 * F), bf16), vm((nz, br, single), bf16), vm((slots, br, single), bf16),
        vm((br, paired), bf16), vm((4, 2 * br, paired), bf16),
        vm((br, 2 * QW + 2 * F), f32), vm((T, D), bf16), vm((T, D), bf16), vm((T, D), bf16), vm((T, 128), f32),
        vm((T, 2 * QW), f32), vm((2, 2, T, 64), bf16), vm((2, T, 64), bf16), vm((2, T, 64), bf16),
        vm((2, 64, T), bf16), vm((2, 64, T), bf16), vm((2, 2, T, 64), bf16), vm((T, QW), bf16),
        vm((T, D), bf16), vm((2, RB, D), bf16), vm((RB, D), bf16), vm((RB, D), bf16), vm((RB, D), f32),
        vm((T, D), bf16), vm((T, 2 * F), bf16), vm((T, F), bf16),
        vm((T, 128), f32), vm((T, 128), f32), vm((area, RB), bf16), vm((2, nb, 1, 2 * RB), f32),
        vm((T, QW), f32), vm((2, T, 128), f32),
        vm((T, 2 * CW), bf16), vm((T, CW), bf16), vm((T, CW), bf16), vm((T, CW), bf16),
        vm((8, D), f32), vm((4, gains + T // 128, 128), f32), vm((gains + T // 128, 128), f32), vm((gains, 128), f32),
        vm((nz, gains, 128), f32), vm((1, T), jnp.int32), vm((1, D), f32), vm((1, D), f32),
        vm((1, norm_query.shape[0]), f32), vm((1, norm_query.shape[0]), f32), vm((gains, 128), f32),
        sem((18,)), sem((8, nz)), sem((8, nz)), sem((8, nz)), sem((8, nz)),
        sem((10, nz)), sem((10, nz)), sem((10, nz)), sem((10, nz)),
        sem((4, 2, 3)), sem((4, 2, 3)), sem((3, 4)), sem((3, 4)), sem((nb, 3)), sem((nb, 3)), sem((3,)), sem((3,)),
        sem((4,)), sem((4,)), sem((nz,)), sem((nz,)), sem((33,)),
    ]
    hbm = pl.BlockSpec(memory_space=pl.ANY)
    shape = jax.ShapeDtypeStruct
    results = (
        shape((T, CW), bf16), shape((T, CW), f32), shape((br, QW), f32), shape((br, KW), f32), shape((br, KW), f32),
        shape((QW, br), f32), shape((br, F), f32), shape((br, F), f32), shape((F, br), f32),
    )
    outs = pl.pallas_call(
        functools.partial(layer_kernel, plan),
        out_shape=results + (shape((gains, 128), f32),),
        in_specs=[hbm] * 14,
        out_specs=(hbm,) * 10,
        scratch_shapes=scratch,
        compiler_params=pltpu.CompilerParams(
            collective_id=0, has_side_effects=True, vmem_limit_bytes=64 * 2**20
        ),
        name="layer",
    )(
        tokens, segment_ids, w_query, key_matrix, value_matrix, w_out, w_gate, w_up, w_down,
        norm_attn[None], norm_ffn[None], norm_query[None], norm_key[None], cotangent,
    )
    gain = shape((1, D), f32)
    head_gain = shape((1, norm_query.shape[0]), f32)
    outs = pl.pallas_call(
        hand_out,
        out_shape=results + (gain, gain, head_gain, head_gain),
        in_specs=[hbm] * 10,
        out_specs=(hbm,) * 13,
        scratch_shapes=[vm(v.shape, v.dtype) for v in results + (shape((gains, 128), f32), gain, gain, head_gain, head_gain)]
        + [sem((2, 13))],
        compiler_params=pltpu.CompilerParams(vmem_limit_bytes=63 * 2**20),
        name="hand_out",
    )(*outs)
    return outs[:9] + tuple(v[0] for v in outs[9:])


def solution(mesh):
    in_specs = (
        P("row", "col"), P("row", None), P("row", "col"), P("row", "col"), P("row", "col"), P("col", "row"),
        P("row", "col"), P("row", "col"), P("col", "row"), P(), P(), P(), P(), P("row", "col"),
    )
    out_specs = (
        P("row", "col"), P("row", "col"), P("row", "col"), P("row", "col"), P("row", "col"), P("col", "row"),
        P("row", "col"), P("row", "col"), P("col", "row"), P(), P(), P(), P(),
    )
    return jax.shard_map(
        functools.partial(per_device, mesh.shape["row"]),
        mesh=mesh, in_specs=in_specs, out_specs=out_specs, check_vma=False,
    )
```
